32 devices in a mesh: ctx: 8 (over z, core), shard: 4 (over y, x).
Axes of the slice: x: 2, y: 2, z: 4, core: 2. Of those that a mesh axis runs over, the one named last changes fastest.
Arguments:
- tokens: float32 [8, 1024, 1536], P('shard', 'ctx'), may hold values from -6 to 6
- cotangent: float32 [8, 1024, 1536], P('shard', 'ctx'), may hold values from -6 to 6
- norm_gains: float32 [2, 1536], replicated, may hold values from 0.5 to 1.5
- router: float32 [1536, 4], replicated, may hold values from -0.15625 to 0.15625
- dense_weight: float32 [128, 192, 256], P(('ctx', 'shard')), may hold values from -0.15625 to 0.15625
- expert_weight: float32 [4, 96, 192, 256], P('shard', 'ctx'), may hold values from -0.15625 to 0.15625
- routes: int32 [8, 1024, 2], P('shard', 'ctx'), may hold values from 0 to 3, all different within a row; in each aligned block of 128 rows (0 to 127, 128 to 255, ..., all dimensions but the last counted through in order) at most 128 rows name the same one
- assign: int32 [8, 2], replicated, may hold values from 0 to 15, as said below
- dense_order: int32 [128], replicated, may hold values from 0 to 127, each once
- expert_order: int32 [96], replicated, may hold values from 0 to 95, each once
- dense_moment: float32 [128, 192, 256], P(('ctx', 'shard')), may hold values from -6 to 6
- dense_second: float32 [128, 192, 256], P(('ctx', 'shard')), may hold values from 1 to 30
- dense_left: float32 [128, 192, 192], P(('ctx', 'shard'))
- dense_right: float32 [128, 256, 256], P(('ctx', 'shard'))
- expert_moment: float32 [4, 96, 192, 256], P('shard', 'ctx'), may hold values from -18 to 18
- expert_second: float32 [4, 96, 192, 256], P('shard', 'ctx'), may hold values from 10 to 300
- expert_left: float32 [4, 96, 192, 192], P('shard', 'ctx')
- expert_right: float32 [4, 96, 256, 256], P('shard', 'ctx')
- gains_moment: float32 [2, 1536], replicated, may hold values from -30 to 30
- gains_second: float32 [2, 1536], replicated, may hold values from 10 to 1000
- router_moment: float32 [1536, 4], replicated, may hold values from -30 to 30
- router_second: float32 [1536, 4], replicated, may hold values from 10 to 1000
Outputs:
- output: float32 [8, 1024, 1536], P('shard', 'ctx')
- input_grad: float32 [8, 1024, 1536], P('shard', 'ctx')
- dense_grad: float32 [128, 192, 256], P(('ctx', 'shard'))
- dense_new: float32 [128, 192, 256], P(('ctx', 'shard'))
- dense_moment_new: float32 [128, 192, 256], P(('ctx', 'shard'))
- dense_second_new: float32 [128, 192, 256], P(('ctx', 'shard'))
- expert_grad: float32 [4, 96, 192, 256], P('shard', 'ctx')
- expert_new: float32 [4, 96, 192, 256], P('shard', 'ctx')
- expert_moment_new: float32 [4, 96, 192, 256], P('shard', 'ctx')
- expert_second_new: float32 [4, 96, 192, 256], P('shard', 'ctx')
- gains_grad: float32 [2, 1536], replicated
- gains_new: float32 [2, 1536], replicated
- gains_moment_new: float32 [2, 1536], replicated
- gains_second_new: float32 [2, 1536], replicated
- router_grad: float32 [1536, 4], replicated
- router_new: float32 [1536, 4], replicated
- router_moment_new: float32 [1536, 4], replicated
- router_second_new: float32 [1536, 4], replicated
The draws below stay inside these ranges and needn't reach their ends.
Inputs may be any that keep to these rules, and one draw needn't show every extreme that they name: `assign`: row c names causal blocks b and 15 - b; every causal block is named once. `routes`: in each aligned block of 128 rows of a sequence, no expert is named more than 128 times. `dense_order`: each block number once. `expert_order`: each block number once.
All inputs are finite; a program needn't handle non-finite values.
Results may differ from the reference program's by a relative error of at most 0.015.
Values may be sent and summed in bfloat16 or wider, within the bound.
No kernel may reach another device: no remote copies, remote signals or barrier semaphores. Data moves between devices by JAX's collectives and lax.ppermute only.
A program may use at most 192 MiB of HBM per device.

```python
import math
import jax
import jax.numpy as jnp
import numpy as np
from jax import lax

D = 1536
HEADS = 24
KVH = 8
HD = 64
FF = 1024
BR = 192
BC = 256
BLK = 64
EXPERTS = 4
CAUSAL = 16
L = 1024
SEQS = 8
MOST = 128
QW = 1536
KVW = 512
COLS = 4096
NB_DENSE = 128
EXP_BLOCKS = 96
KEYBLK = 512


def draw_assign(key, part):
    half_count = CAUSAL // 2
    first_blocks = jax.random.permutation(key, half_count).astype(jnp.int32)
    return jnp.stack([first_blocks, CAUSAL - 1 - first_blocks], axis=1)


def near_identity(key, count_shape, order_size):
    perturb = jax.random.normal(key, count_shape + (order_size, order_size), jnp.float32)
    return jnp.eye(order_size, dtype=jnp.float32) + perturb * (0.5 / math.sqrt(order_size))


def draw_dense_left(key, part):
    return near_identity(jax.random.fold_in(key, 101), (NB_DENSE,), BR)


def draw_dense_right(key, part):
    return near_identity(jax.random.fold_in(key, 202), (NB_DENSE,), BC)


def draw_expert_left(key, part):
    return near_identity(jax.random.fold_in(key, 303), (EXPERTS, EXP_BLOCKS), BR)


def draw_expert_right(key, part):
    return near_identity(jax.random.fold_in(key, 404), (EXPERTS, EXP_BLOCKS), BC)


def levels(rng, extent, split, smallest, high):
    def one(position, blocks):
        draws = jax.random.uniform(jax.random.fold_in(jax.random.fold_in(rng, 6), position), (blocks,), jnp.float32, smallest / len(split), high / len(split))
        return jnp.repeat(jnp.exp(draws), extent[position] // blocks).reshape((-1,) + (1,) * (len(extent) - position - 1))

    loudness = one(*split[0])
    for cut in split[1:]:
        loudness = loudness * one(*cut)
    return loudness


def assign_block(own_key, own, number, rows, number_of, top, most, skew):
    ranking = jax.random.permutation(own_key, number_of)
    heavy_load, usual = shares(number_of, rows * top, most, skew, True), shares(number_of, rows * top, most, skew, False)
    places = jnp.arange(number_of)

    def named(lengths, rotation):
        used = int((lengths > 0).sum())
        fixed = max(1, used // 4)
        shifted = fixed + (places - fixed + rotation * (used - fixed)) % max(1, number_of - fixed)
        return jnp.zeros((number_of,), jnp.int32).at[ranking[jnp.where(places < fixed, places, shifted)]].set(jnp.asarray(lengths, jnp.int32))

    lengths = jnp.where(number % 4 == 0, named(heavy_load, number // 4), named(usual, number - number // 4 - 1))
    mixed = jax.random.permutation(jax.random.fold_in(own, 3), number_of)
    source_of, taker = mixed[0:number_of // 2 * 2:2], mixed[1:number_of // 2 * 2:2]
    room = jnp.minimum(lengths[source_of] - 1, most - lengths[taker]) // 2
    room = jnp.where((source_of == ranking[0]) | (taker == ranking[0]) | (lengths[taker] == 0), 0, jnp.maximum(room, 0))
    shifted = jax.random.randint(jax.random.fold_in(own, 4), (number_of // 2,), 0, 1 << 20) % (room + 1)
    lengths = lengths.at[source_of].add(-shifted).at[taker].add(shifted)
    members = jnp.searchsorted(jnp.cumsum(lengths), jnp.arange(rows * top), side="right").astype(jnp.int32)
    table = members.reshape(top, rows).T
    table = table[jax.random.permutation(jax.random.fold_in(own, 1), rows)]
    rotation = jax.random.randint(jax.random.fold_in(own, 2), (rows, 1), 0, top)
    return jnp.take_along_axis(table, (jnp.arange(top)[None, :] + rotation) % top, axis=1)


def shares(number_of, total, limit, slope, full):
    loads = [(1 << 20) // math.isqrt(grade ** slope) + 1 for grade in range(1, number_of + 1)]
    largest = limit if full else min(limit, max(-(-total // number_of), total * loads[0] // sum(loads)))
    least = 1 if total - largest >= number_of - 1 else 0
    holding, spare = [largest] + [least] * (number_of - 1), total - largest - least * (number_of - 1)
    while spare > 0:
        free = [i for i in range(1, number_of) if holding[i] < largest] or [i for i in range(1, number_of) if holding[i] < limit]
        whole, left = sum([loads[i] for i in free]), spare
        for i in free:
            more = min(limit - holding[i], max(1, left * loads[i] // whole), spare)
            holding[i] = holding[i] + more
            spare = spare - more
    return np.array(holding)


def noise(key, dims, scale, bound, cuts=(), kind=jnp.bfloat16):
    level = levels(key, dims, cuts, -0.22, 0.18) if cuts else 1.0
    entries = jax.random.normal(key, dims, jnp.float32) * scale * level
    return jnp.minimum(jnp.maximum(entries, -bound), bound).astype(kind)


def setup_inputs(seed: int = 0) -> dict:
    key_of = jax.random.split(jax.random.key(seed), 23)
    tokens = noise(key_of[0], (SEQS, L, D), 1.0, 6.0, ((0, 4), (1, 8)), jnp.float32)
    cotangent = noise(key_of[1], (SEQS, L, D), 1.0, 6.0, ((0, 4), (1, 8)), jnp.float32)
    norm_gains = jnp.clip(1.0 + 0.1 * jax.random.normal(key_of[2], (2, D), jnp.float32), 0.5, 1.5)
    router = noise(key_of[3], (D, EXPERTS), D ** -0.5, 0.15625, (), jnp.float32)
    dense_weight = noise(key_of[4], (NB_DENSE, BR, BC), D ** -0.5, 0.15625, ((0, 32),), jnp.float32)
    expert_weight = noise(key_of[5], (EXPERTS, EXP_BLOCKS, BR, BC), D ** -0.5, 0.15625, ((0, 4), (1, 8)), jnp.float32)
    routes_keys = jax.random.split(jax.random.fold_in(key_of[6], 1), SEQS * L // (2 * BLK))
    routes_turns = jax.random.permutation(jax.random.fold_in(key_of[6], 3), SEQS * L // (2 * BLK))
    routes = jax.vmap(lambda own, number: assign_block(jax.random.fold_in(key_of[6], 2), own, number, 2 * BLK, EXPERTS, 2, MOST, 2))(routes_keys, routes_turns).reshape((SEQS, L, 2))
    assign = draw_assign(jax.random.fold_in(key_of[22], 71), 0)
    dense_order = jax.random.permutation(key_of[8], NB_DENSE).astype(jnp.int32)
    expert_order = jax.random.permutation(key_of[9], EXP_BLOCKS).astype(jnp.int32)
    dense_moment = noise(key_of[10], (NB_DENSE, BR, BC), 1.0, 6.0, ((0, 32),), jnp.float32)
    dense_second = jnp.clip(jnp.exp(math.log(30.0) - 3.4011974 * jax.random.uniform(key_of[11], (NB_DENSE, BR, BC), jnp.float32) ** levels(key_of[11], (NB_DENSE, BR, BC), ((0, 32),), -0.2, 0.2)), 1.0, 30.0)
    dense_left = draw_dense_left(jax.random.fold_in(key_of[22], 71), 0)
    dense_right = draw_dense_right(jax.random.fold_in(key_of[22], 71), 0)
    expert_moment = noise(key_of[14], (EXPERTS, EXP_BLOCKS, BR, BC), 3.0, 18.0, ((0, 4), (1, 8)), jnp.float32)
    expert_second = jnp.clip(jnp.exp(math.log(300.0) - 3.4011974 * jax.random.uniform(key_of[15], (EXPERTS, EXP_BLOCKS, BR, BC), jnp.float32) ** levels(key_of[15], (EXPERTS, EXP_BLOCKS, BR, BC), ((0, 4), (1, 8)), -0.2, 0.2)), 10.0, 300.0)
    expert_left = draw_expert_left(jax.random.fold_in(key_of[22], 71), 0)
    expert_right = draw_expert_right(jax.random.fold_in(key_of[22], 71), 0)
    gains_moment = noise(key_of[18], (2, D), 5.0, 30.0, (), jnp.float32)
    gains_second = jnp.clip(jnp.exp(jax.random.uniform(key_of[19], (2, D), jnp.float32, math.log(10.0), math.log(1000.0))), 10.0, 1000.0)
    router_moment = noise(key_of[20], (D, EXPERTS), 5.0, 30.0, (), jnp.float32)
    router_second = jnp.clip(jnp.exp(jax.random.uniform(key_of[21], (D, EXPERTS), jnp.float32, math.log(10.0), math.log(1000.0))), 10.0, 1000.0)
    return {"tokens": tokens, "cotangent": cotangent, "norm_gains": norm_gains, "router": router, "dense_weight": dense_weight, "expert_weight": expert_weight, "routes": routes, "assign": assign, "dense_order": dense_order, "expert_order": expert_order, "dense_moment": dense_moment, "dense_second": dense_second, "dense_left": dense_left, "dense_right": dense_right, "expert_moment": expert_moment, "expert_second": expert_second, "expert_left": expert_left, "expert_right": expert_right, "gains_moment": gains_moment, "gains_second": gains_second, "router_moment": router_moment, "router_second": router_second}


@jax.custom_vjp
def low(v):
    return lax.optimization_barrier(v.astype(jnp.bfloat16)).astype(jnp.float32)

@jax.custom_vjp
def low_back(v):
    return v

def low_keep(v):
    return (low(v), None)

def low_pass(kept, grad):
    return (grad,)

def back_keep(v):
    return (v, None)

def back_low(kept, grad):
    return (low(grad),)
low.defvjp(low_keep, low_pass)
low_back.defvjp(back_keep, back_low)
norm_eps = 1e-06
beta_one = 0.9
beta_two = 0.95
rate = 0.01
gain_rate = 0.5
adam_eps = 1e-08
masked_score = -1e+30
highest = lax.Precision.HIGHEST

def product(left_side, right_side):
    return jnp.dot(left_side, right_side, precision=highest, preferred_element_type=jnp.float32)

def rms_norm(inputs, gain):
    return inputs * lax.rsqrt(lax.optimization_barrier(jnp.mean(inputs * inputs, axis=-1, keepdims=True)) + norm_eps) * gain

def soft_max(scores):
    largest = lax.optimization_barrier(jnp.max(scores, axis=-1, keepdims=True))
    raised = jnp.exp(scores - largest)
    return raised / lax.optimization_barrier(jnp.sum(raised, axis=-1, keepdims=True))

def token_positions(assign):
    row_ids = jnp.arange(2 * BLK, dtype=jnp.int32)
    return (assign[:, row_ids // BLK] * BLK + row_ids % BLK).reshape(L)

def dense_full(blocks, slot_order):
    placed = jnp.zeros_like(blocks).at[slot_order].set(blocks)
    shaped = placed.reshape(D // BR, COLS // BC, BR, BC)
    return shaped.transpose(0, 2, 1, 3).reshape(D, COLS)

def dense_blocks(matrix, slot_order):
    shaped = matrix.reshape(D // BR, BR, COLS // BC, BC).transpose(0, 2, 1, 3)
    return shaped.reshape(NB_DENSE, BR, BC)[slot_order]

def expert_full(blocks, slot_order):
    placed = jnp.zeros_like(blocks).at[:, slot_order].set(blocks)
    shaped = placed.reshape(EXPERTS, 3, D // BR, FF // BC, BR, BC)
    return shaped.transpose(0, 1, 2, 4, 3, 5).reshape(EXPERTS, 3, D, FF)

def expert_blocks(matrix, slot_order):
    shaped = matrix.reshape(EXPERTS, 3, D // BR, BR, FF // BC, BC).transpose(0, 1, 2, 4, 3, 5)
    return shaped.reshape(EXPERTS, EXP_BLOCKS, BR, BC)[:, slot_order]

def attention(query_rows, key_rows, value_rows, positions):
    score_scale = HD ** (-0.5)
    key_heads = key_rows.reshape(L, KVH, HD)
    value_heads = value_rows.reshape(L, KVH, HD)

    def one_block(pieces):
        rows_block, rows_pos = pieces
        query_heads = rows_block.reshape(KEYBLK, KVH, HEADS // KVH, HD)
        scores = low_back(jnp.einsum('qkgd,nkd->kgqn', query_heads, key_heads, precision=highest) * score_scale)
        scores = jnp.where(positions[None, None, None, :] <= rows_pos[None, None, :, None], scores, masked_score)
        chance = low(soft_max(scores))
        mixture = jnp.einsum('kgqn,nkd->qkgd', chance, value_heads, precision=highest)
        return mixture.reshape(KEYBLK, QW)
    blocks = lax.map(jax.checkpoint(one_block), (query_rows.reshape(L // KEYBLK, KEYBLK, QW), positions.reshape(L // KEYBLK, KEYBLK)))
    return blocks.reshape(L, QW)

def layer(inputs, seq_routes, positions, gain_rows, weights, router, experts):
    normed_one = low(rms_norm(inputs, gain_rows[0]))
    query_map = low(weights[:, :QW])
    key_map = low(weights[:, QW:QW + KVW])
    value_map = low(weights[:, QW + KVW:QW + 2 * KVW])
    out_map = low(weights[:, QW + 2 * KVW:])
    query_rows = low(low_back(product(normed_one, query_map)))
    key_rows = low(low_back(product(normed_one, key_map)))
    value_rows = low(low_back(product(normed_one, value_map)))
    attended = low(low_back(attention(query_rows, key_rows, value_rows, positions)))
    after_attn = inputs + low_back(product(attended, out_map.T))
    normed_two = low(rms_norm(after_attn, gain_rows[1]))
    router_probs = soft_max(product(normed_two, low(router)))
    chosen = lax.optimization_barrier(jnp.sum((seq_routes[:, :, None] == jnp.arange(EXPERTS, dtype=jnp.int32)).astype(jnp.float32), axis=1))
    mixing = router_probs * chosen

    def one_expert(running, pieces):
        matrices, mix_col = pieces
        matrices = low(matrices)
        expert_in = low_back(normed_two)
        gate_pre = low_back(product(expert_in, matrices[0]))
        up_pre = low_back(product(expert_in, matrices[1]))
        hidden = low(gate_pre * jax.nn.sigmoid(gate_pre) * up_pre)
        result = low(low_back(product(hidden, matrices[2].T)))
        return (running + mix_col[:, None] * result, None)
    mixed_out, _ = lax.scan(jax.checkpoint(one_expert), jnp.zeros_like(inputs), (experts, mixing.T))
    return after_attn + mixed_out

def soap(weight, gradient, moment, second, left_basis, right_basis):
    rotated = jnp.matmul(jnp.matmul(jnp.swapaxes(left_basis, -1, -2), gradient, precision=highest), right_basis, precision=highest)
    moment_new = beta_one * moment + (1.0 - beta_one) * rotated
    second_new = beta_two * second + (1.0 - beta_two) * rotated * rotated
    direction = moment_new / (jnp.sqrt(second_new) + adam_eps)
    rotated_back = jnp.matmul(jnp.matmul(left_basis, direction, precision=highest), jnp.swapaxes(right_basis, -1, -2), precision=highest)
    return (weight - rate * rotated_back, moment_new, second_new)

def adam(weight, gradient, moment, second, step_rate):
    moment_new = beta_one * moment + (1.0 - beta_one) * gradient
    second_new = beta_two * second + (1.0 - beta_two) * gradient * gradient
    return (weight - step_rate * moment_new / (jnp.sqrt(second_new) + adam_eps), moment_new, second_new)

def reference(tokens, cotangent, norm_gains, router, dense_weight, expert_weight, routes, assign, dense_order, expert_order, dense_moment, dense_second, dense_left, dense_right, expert_moment, expert_second, expert_left, expert_right, gains_moment, gains_second, router_moment, router_second):
    positions = token_positions(assign)
    weights = dense_full(dense_weight, dense_order)
    experts = expert_full(expert_weight, expert_order)

    def forward(inputs, gain_rows, weight_matrix, router_matrix, expert_mats):

        def one_seq(carried, pieces):
            seq_inputs, seq_routes = pieces
            return (carried, layer(seq_inputs, seq_routes, positions, gain_rows, weight_matrix, router_matrix, expert_mats))
        _, results = lax.scan(one_seq, jnp.zeros((), jnp.float32), (inputs, routes))
        return results
    output, pullback = jax.vjp(forward, tokens, norm_gains, weights, router, experts)
    input_grad, gains_grad, weights_grad, router_grad, experts_grad = pullback(cotangent)
    dense_grad = dense_blocks(weights_grad, dense_order)
    expert_grad = expert_blocks(experts_grad, expert_order)
    dense_new, dense_moment_new, dense_second_new = soap(dense_weight, dense_grad, dense_moment, dense_second, dense_left, dense_right)
    expert_new, expert_moment_new, expert_second_new = soap(expert_weight, expert_grad, expert_moment, expert_second, expert_left, expert_right)
    gains_new, gains_moment_new, gains_second_new = adam(norm_gains, gains_grad, gains_moment, gains_second, gain_rate)
    router_new, router_moment_new, router_second_new = adam(router, router_grad, router_moment, router_second, rate)
    return (output, input_grad, dense_grad, dense_new, dense_moment_new, dense_second_new, expert_grad, expert_new, expert_moment_new, expert_second_new, gains_grad, gains_new, gains_moment_new, gains_second_new, router_grad, router_new, router_moment_new, router_second_new)
```

```python
import functools

import jax
import jax.numpy as jnp
from jax import lax
from jax.experimental import pallas as pl
from jax.experimental.pallas import tpu as pltpu
from jax.sharding import PartitionSpec as P

HEADS = 24
KVH = 8
HD = 64
FF = 1024
BR = 192
BC = 256
LANES = 128

norm_eps = 1e-06
beta_one = 0.9
beta_two = 0.95
rate = 0.01
gain_rate = 0.5
adam_eps = 1e-08
masked_score = -1e30
low_type = jnp.bfloat16
MIB = 1 << 20

NN = (((1,), (0,)), ((), ()))
NT = (((1,), (1,)), ((), ()))
TN = (((0,), (0,)), ((), ()))

in_vmem = pl.BlockSpec(memory_space=pltpu.VMEM)
in_smem = pl.BlockSpec(memory_space=pltpu.SMEM)
in_any = pl.BlockSpec(memory_space=pl.ANY)


def dot(left_side, right_side, dims=NN):
    return lax.dot_general(left_side, right_side, dims, preferred_element_type=jnp.float32)


def call(kernel, out_shapes, in_specs, out_specs, scratch, flops, moved, limit):
    return pl.pallas_call(
        kernel,
        out_shape=out_shapes,
        in_specs=in_specs,
        out_specs=out_specs,
        scratch_shapes=scratch,
        compiler_params=pltpu.CompilerParams(vmem_limit_bytes=limit * MIB),
        cost_estimate=pl.CostEstimate(flops=flops, bytes_accessed=moved, transcendentals=0),
    )


def shaped(dims, kind):
    return jax.ShapeDtypeStruct(dims, kind)


def inverse_order(slot_order):
    count = slot_order.shape[0]
    numbers = jnp.arange(count, dtype=jnp.int32)
    return jnp.sum(
        jnp.where(slot_order[None, :] == numbers[:, None], numbers[None, :], 0), axis=1
    ).astype(jnp.int32)


def wait_bytes(landed, semaphore):
    pltpu.make_async_copy(landed, landed, semaphore).wait()


def unit_rows(rows, gain):
    inverse = lax.rsqrt(jnp.mean(rows * rows, axis=-1, keepdims=True) + norm_eps)
    return rows * inverse * gain, inverse


def unit_back(rows, gain, inverse, gradient):
    unit = rows * inverse
    scaled = gradient * gain
    inner = jnp.mean(scaled * unit, axis=-1, keepdims=True)
    return inverse * (scaled - unit * inner), jnp.sum(gradient * unit, axis=0, keepdims=True)


def lane_ids(dims):
    return lax.broadcasted_iota(jnp.int32, dims, len(dims) - 1)


def half_turn(tile):
    return pltpu.roll(tile, HD, 1)


def stack_heads(ref, pair, scale=None):
    base = pair * (3 * LANES)
    tiles = [
        ref[:, pl.ds(pl.multiple_of(base + LANES * t, LANES), LANES)].astype(jnp.float32)
        for t in range(3)
    ]
    if scale is not None:
        tiles = [t * scale for t in tiles]
    lower = lane_ids(tiles[0].shape) < HD
    first = [tiles[0], half_turn(tiles[0]), tiles[1]]
    second = [tiles[1], half_turn(tiles[2]), tiles[2]]
    return (
        jnp.concatenate([jnp.where(lower, t, 0.0) for t in first], axis=0),
        jnp.concatenate([jnp.where(lower, 0.0, t) for t in second], axis=0),
    )


def unstack_heads(ref, pair, first, second):
    rows = first.shape[0] // 3
    base = pair * (3 * LANES)
    lower = lane_ids((rows, LANES)) < HD
    tiles = (
        jnp.where(lower, first[:rows], half_turn(first[rows : 2 * rows])),
        jnp.where(lower, first[2 * rows :], second[:rows]),
        jnp.where(lower, half_turn(second[rows : 2 * rows]), second[2 * rows :]),
    )
    for t in range(3):
        ref[:, pl.ds(pl.multiple_of(base + LANES * t, LANES), LANES)] = tiles[t].astype(ref.dtype)


def project_kernel(order_ref, x_ref, gain_ref, w_ref, h_ref, q_ref, kv_ref, held, sems):
    row_groups = x_ref.shape[-1] // BR
    groups = held.shape[0]
    q_groups = q_ref.shape[-1] // BC
    all_groups = w_ref.shape[0] // row_groups
    micros = x_ref.shape[0]
    rows = x_ref.shape[1]

    @pl.loop(0, groups)
    def _(b):
        for a in range(row_groups):
            pltpu.make_async_copy(
                w_ref.at[order_ref[a * all_groups + b]], held.at[b, pl.ds(a * BR, BR)], sems.at[b]
            ).start()

    for m in range(micros):
        h_ref[pl.ds(m * rows, rows), :] = unit_rows(x_ref[m], gain_ref[0:1])[0].astype(low_type)

    @pl.loop(0, q_groups)
    def _(b):
        wait_bytes(held.at[b], sems.at[b])
        made = dot(h_ref[...], held[b]).astype(low_type)
        for m in range(micros):
            q_ref[m, :, pl.ds(pl.multiple_of(b * BC, BC), BC)] = made[m * rows : (m + 1) * rows]

    @pl.loop(q_groups, groups)
    def _(b):
        wait_bytes(held.at[b], sems.at[b])
        made = dot(h_ref[...], held[b]).astype(low_type)
        for m in range(micros):
            kv_ref[m, :, pl.ds(pl.multiple_of((b - q_groups) * BC, BC), BC)] = made[
                m * rows : (m + 1) * rows
            ]


def project(order, x, gains, w):
    micros, rows, width = x.shape
    groups = (HEADS + 2 * KVH) * HD // BC
    return call(
        project_kernel,
        (
            shaped((micros * rows, width), low_type),
            shaped((micros, rows, HEADS * HD), low_type),
            shaped((micros, rows, 2 * KVH * HD), low_type),
        ),
        [in_smem, in_vmem, in_vmem, in_any],
        (in_vmem, in_vmem, in_vmem),
        [pltpu.VMEM((groups, width, BC), low_type), pltpu.SemaphoreType.DMA((groups,))],
        2 * micros * rows * width * groups * BC,
        groups * width * BC * 2,
        24,
    )(order, x, gains, w)


def start_matrix(order_ref, w_ref, held, sem, first_group, all_groups):
    row_groups = held.shape[0] // BR
    groups = held.shape[1] // BC

    @pl.loop(0, row_groups)
    def _(a):
        for b in range(groups):
            pltpu.make_async_copy(
                w_ref.at[order_ref[a * all_groups + first_group + b]],
                held.at[pl.ds(pl.multiple_of(a * BR, 64), BR), pl.ds(b * BC, BC)],
                sem,
            ).start()


def attend_kernel(
    all_groups, order_ref, q_ref, kv_ref, rpos_ref, kpos_ref, x_ref, gain_ref, w_ref,
    ob_ref, log_ref, x2_ref, h2_ref, bias, held, sem,
):
    rows = q_ref.shape[0]
    in_groups = (HEADS + 2 * KVH) * HD // BC
    start_matrix(order_ref, w_ref, held, sem, in_groups, all_groups)
    bias[...] = jnp.where(kpos_ref[...] <= rpos_ref[...], 0.0, masked_score)
    log_ref[...] = jnp.zeros_like(log_ref)
    length = kv_ref.shape[0]

    @pl.loop(0, KVH // 2)
    def _(pair):
        lane = pl.multiple_of(pair * LANES, LANES)
        keys = kv_ref[:, pl.ds(lane, LANES)]
        values = kv_ref[:, pl.ds(pl.multiple_of(lane + KVH * HD, LANES), LANES)]
        stacked = stack_heads(q_ref, pair, HD**-0.5)
        mixed = []
        for part in range(2):
            scores = dot(stacked[part].astype(low_type), keys, NT)
            scores = (scores.reshape(3, rows, length) + bias[...][None]).reshape(3 * rows, length)
            largest = jnp.max(scores, axis=-1, keepdims=True)
            raised = jnp.exp(scores - largest)
            summed = jnp.sum(raised, axis=-1, keepdims=True)
            mixed.append(dot(raised.astype(low_type), values) / summed)
            log_ref[...] = jnp.where(
                lane_ids(log_ref.shape) == 2 * pair + part, largest + jnp.log(summed), log_ref[...]
            )
        unstack_heads(ob_ref, pair, mixed[0], mixed[1])

    wait_bytes(held, sem)
    for n in range(held.shape[0] // BC):
        cut = slice(n * BC, (n + 1) * BC)
        x2_ref[:, cut] = x_ref[:, cut] + dot(ob_ref[...], held[cut, :], NT)
    h2_ref[...] = unit_rows(x2_ref[...], gain_ref[1:2])[0].astype(low_type)


def attend(order, q, kv, rows_pos, key_pos, x, gains, w):
    rows, width = q.shape
    length = kv.shape[0]
    model = x.shape[1]
    return call(
        functools.partial(attend_kernel, w.shape[0] * BR // model),
        (
            shaped((rows, width), low_type),
            shaped((3 * rows, LANES), jnp.float32),
            shaped((rows, model), jnp.float32),
            shaped((rows, model), low_type),
        ),
        [in_smem] + [in_vmem] * 6 + [in_any],
        (in_vmem,) * 4,
        [
            pltpu.VMEM((rows, length), jnp.float32),
            pltpu.VMEM((model, width), low_type),
            pltpu.SemaphoreType.DMA,
        ],
        16 * rows * length * width,
        8 * MIB,
        40,
    )(order, q, kv, rows_pos, key_pos, x, gains, w)


def router_parts(h2, router, experts):
    logits = dot(h2, router)
    logits = jnp.where(lane_ids(logits.shape) < experts, logits, masked_score)
    raised = jnp.exp(logits - jnp.max(logits, axis=-1, keepdims=True))
    return raised / jnp.sum(raised, axis=-1, keepdims=True)


def expert_kernel(sources, micro, order_ref, me_ref, router_ref, *refs):
    h_parts = refs[:sources]
    c_parts = refs[sources : 2 * sources]
    w_ref = refs[2 * sources]
    outs = refs[2 * sources + 1 :]
    back_refs = outs[:sources]
    out_refs = outs[sources : 2 * sources]
    z_ref, dg_ref, du_ref, dy_ref, xs_ref = outs[2 * sources : 2 * sources + 5]
    cs, held, chance, load_sem, w_sems = outs[2 * sources + 5 :]
    rows, width = h_parts[0].shape
    row_groups = width // BR
    col_groups = FF // BC
    for j in range(sources):
        pltpu.make_async_copy(h_parts[j], xs_ref.at[pl.ds(j * rows, rows)], load_sem.at[0]).start()
        pltpu.make_async_copy(
            c_parts[j].at[pl.ds(micro * rows, rows)], cs.at[pl.ds(j * rows, rows)], load_sem.at[1]
        ).start()
    for k in (0, 1, 2):

        @pl.loop(0, row_groups)
        def _(a):
            for b in range(col_groups):
                pltpu.make_async_copy(
                    w_ref.at[order_ref[(k * row_groups + a) * col_groups + b]],
                    held.at[k, pl.ds(pl.multiple_of(a * BR, 64), BR), pl.ds(b * BC, BC)],
                    w_sems.at[k],
                ).start()

    wait_bytes(xs_ref, load_sem.at[0])
    wait_bytes(cs, load_sem.at[1])
    me = me_ref[0]
    probs = router_parts(xs_ref[...], router_ref[...], sources)
    hits = cs[:, width:].astype(jnp.float32)
    mine = lane_ids(hits.shape) == me
    hit = jnp.sum(jnp.where(mine, hits, 0.0), axis=-1, keepdims=True)
    weight = jnp.sum(jnp.where(mine, probs, 0.0), axis=-1, keepdims=True) * hit
    dy_ref[...] = (weight * cs[:, :width].astype(jnp.float32)).astype(low_type)
    chance[...] = jnp.zeros_like(chance)
    for k in (0, 1, 2):
        wait_bytes(held.at[k], w_sems.at[k])

    @pl.loop(0, col_groups)
    def _(b):
        cut = pl.ds(pl.multiple_of(b * BC, BC), BC)
        gate = dot(xs_ref[...], held[0, :, cut])
        up = dot(xs_ref[...], held[1, :, cut])
        down = dot(cs[:, :width], held[2, :, cut])
        sig = jax.nn.sigmoid(gate)
        act = gate * sig
        hidden = act * up
        z_ref[:, cut] = hidden.astype(low_type)
        chance[...] += jnp.sum(down * hidden, axis=-1, keepdims=True)
        down = down * weight
        dg_ref[:, cut] = (down * up * sig * (1.0 + gate * (1.0 - sig))).astype(low_type)
        du_ref[:, cut] = (down * act).astype(low_type)

    for n in range(width // BC):
        cut = slice(n * BC, (n + 1) * BC)
        back = dot(dg_ref[...], held[0, cut, :], NT) + dot(du_ref[...], held[1, cut, :], NT)
        for j in range(sources):
            back_refs[j][:, cut] = back[j * rows : (j + 1) * rows].astype(low_type)
    told = chance[...] * hit
    high_part = told.astype(low_type)
    low_part = (told - high_part.astype(jnp.float32)).astype(low_type)
    lanes = lane_ids((sources * rows, LANES))
    tail = jnp.where(lanes == 0, high_part, jnp.where(lanes == 1, low_part, jnp.zeros_like(low_part)))
    for j in range(sources):
        back_refs[j][:, width:] = tail[j * rows : (j + 1) * rows]
    for n in range(width // BC):
        cut = slice(n * BC, (n + 1) * BC)
        made = dot(z_ref[...], held[2, cut, :], NT) * weight
        for j in range(sources):
            out_refs[j][:, cut] = made[j * rows : (j + 1) * rows].astype(low_type)


def run_expert(micro, order, me, router, h_parts, c_parts, w):
    sources = len(h_parts)
    rows, width = h_parts[0].shape
    total = sources * rows
    return call(
        functools.partial(expert_kernel, sources, micro),
        tuple(
            [shaped((rows, width + LANES), low_type)] * sources
            + [shaped((rows, width), low_type)] * sources
            + [shaped((total, FF), low_type)] * 3
            + [shaped((total, width), low_type)] * 2
        ),
        [in_smem, in_smem, in_vmem] + [in_any] * (2 * sources + 1),
        tuple([in_vmem] * (2 * sources + 5)),
        [
            pltpu.VMEM((total, width + LANES), low_type),
            pltpu.VMEM((3, width, FF), low_type),
            pltpu.VMEM((total, 1), jnp.float32),
            pltpu.SemaphoreType.DMA((2,)),
            pltpu.SemaphoreType.DMA((3,)),
        ],
        12 * total * width * FF,
        20 * MIB,
        56,
    )(order, me, router, *h_parts, *c_parts, w)


def outer_kernel(place, pairs, order_ref, *refs):
    count = len(pairs)
    micros = len(refs[:-3]) // (2 * count)
    lefts = refs[: count * micros]
    rights = refs[count * micros : 2 * count * micros]
    out_ref, stage, sems = refs[-3:]
    span = 2 * BR
    steps = []
    for k in range(count):
        for p in range(lefts[k * micros].shape[-1] // span):
            steps.append((k, p))

    def wait_stage(slot, cols):
        wait_bytes(stage.at[slot, :, pl.ds(0, cols)], sems.at[slot])

    used = [None, None]
    for n, (k, p) in enumerate(steps):
        slot = n % 2
        cols = rights[k * micros].shape[-1]
        if used[slot] is not None:
            wait_stage(slot, used[slot])
        used[slot] = cols
        cut = slice(p * span, (p + 1) * span)
        for c in range(0, cols, 512):
            part = slice(c, c + 512)
            made = sum(
                dot(lefts[k * micros + m][:, cut], rights[k * micros + m][:, part], TN)
                for m in range(micros)
            )
            stage[slot, :, part] = made.astype(low_type)
        first, row_step = place(k)
        for half in range(2):
            for b in range(cols // BC):
                pltpu.make_async_copy(
                    stage.at[slot, pl.ds(half * BR, BR), pl.ds(b * BC, BC)],
                    out_ref.at[order_ref[first + (2 * p + half) * row_step + b]],
                    sems.at[slot],
                ).start()
    for slot in range(2):
        if used[slot] is not None:
            wait_stage(slot, used[slot])


def outer_blocks(order, place, lefts, rights, blocks):
    pairs = [(l[0].shape[-1], r[0].shape[-1]) for l, r in zip(lefts, rights)]
    widest = max(r for _, r in pairs)
    rows = sum(l.shape[0] for l in lefts[0])
    flat = [l for group in lefts for l in group] + [r for group in rights for r in group]
    return call(
        functools.partial(outer_kernel, place, pairs),
        shaped((blocks, BR, BC), low_type),
        [in_smem] + [in_vmem] * len(flat),
        in_any,
        [pltpu.VMEM((2, 2 * BR, widest), low_type), pltpu.SemaphoreType.DMA((2,))],
        2 * rows * blocks * BR * BC,
        blocks * BR * BC * 2 + sum(f.size * 2 for f in flat),
        48,
    )(order, *flat)


def merge_kernel(
    all_groups, sources, order_ref, me_ref, x2_ref, cot_ref, h2_ref, gain_ref, router_ref, w_ref, *refs
):
    back_refs = refs[:sources]
    dx_ref, da_ref, do_ref, stat_ref, held, sem = refs[sources:]
    rows, width = x2_ref.shape
    in_groups = (HEADS + 2 * KVH) * HD // BC
    start_matrix(order_ref, w_ref, held, sem, in_groups, all_groups)
    lanes = lane_ids((rows, LANES))
    prob_grad = jnp.zeros((rows, LANES), jnp.float32)
    gathered = jnp.zeros((rows, width), jnp.float32)
    for j in range(sources):
        tail = back_refs[j][:, width:].astype(jnp.float32)
        told = jnp.sum(tail, axis=-1, keepdims=True)
        expert = jnp.bitwise_xor(me_ref[0], j)
        prob_grad = prob_grad + jnp.where(lanes == expert, told, 0.0)
        gathered = gathered + back_refs[j][:, :width].astype(jnp.float32)
    h2 = h2_ref[...]
    probs = router_parts(h2, router_ref[...], sources)
    logit_grad = probs * (prob_grad - jnp.sum(probs * prob_grad, axis=-1, keepdims=True))
    high_part = logit_grad.astype(low_type)
    low_part = (logit_grad - high_part.astype(jnp.float32)).astype(low_type)
    router_grad = dot(high_part, h2, TN) + dot(low_part, h2, TN)
    gathered = gathered + dot(high_part, router_ref[...], NT) + dot(low_part, router_ref[...], NT)
    x2 = x2_ref[...]
    inverse = lax.rsqrt(jnp.mean(x2 * x2, axis=-1, keepdims=True) + norm_eps)
    moe_grad, gain_grad = unit_back(x2, gain_ref[1:2], inverse, gathered)
    after = cot_ref[...] + moe_grad
    dx_ref[...] = after
    da_ref[...] = after.astype(low_type)
    experts_up = stat_ref.shape[0] - 8
    stat_ref[:experts_up] = router_grad[:experts_up]
    stat_ref[experts_up:] = jnp.broadcast_to(gain_grad, (8, width))
    wait_bytes(held, sem)
    for n in range(held.shape[1] // BC):
        cut = slice(n * BC, (n + 1) * BC)
        do_ref[:, cut] = dot(da_ref[...], held[:, cut]).astype(low_type)


def merge(order, me, x2, cot, h2, gains, router, w, backs):
    rows, width = x2.shape
    sources = len(backs)
    experts_up = -(-sources // 8) * 8
    return call(
        functools.partial(merge_kernel, w.shape[0] * BR // width, sources),
        (
            shaped((rows, width), jnp.float32),
            shaped((rows, width), low_type),
            shaped((rows, HEADS * HD), low_type),
            shaped((experts_up + 8, width), jnp.float32),
        ),
        [in_smem, in_smem] + [in_vmem] * 5 + [in_any] + [in_vmem] * sources,
        (in_vmem,) * 4,
        [pltpu.VMEM((width, HEADS * HD), low_type), pltpu.SemaphoreType.DMA],
        2 * rows * width * HEADS * HD,
        10 * MIB,
        40,
    )(order, me, x2, cot, h2, gains, router, w, *backs)


def attend_back_kernel(
    q_ref, kv_ref, rpos_ref, kpos_ref, ob_ref, log_ref, do_ref, dq_ref, dkv_ref, bias
):
    rows = q_ref.shape[0]
    length = kv_ref.shape[0]
    bias[...] = jnp.where(kpos_ref[...] <= rpos_ref[...], 0.0, masked_score)

    @pl.loop(0, KVH // 2)
    def _(pair):
        lane = pl.multiple_of(pair * LANES, LANES)
        value_lane = pl.multiple_of(lane + KVH * HD, LANES)
        keys = kv_ref[:, pl.ds(lane, LANES)]
        values = kv_ref[:, pl.ds(value_lane, LANES)]
        queries = stack_heads(q_ref, pair, HD**-0.5)
        grads = stack_heads(do_ref, pair)
        mixes = stack_heads(ob_ref, pair)
        query_grads = []
        key_grad = value_grad = None
        for part in range(2):
            query = queries[part].astype(low_type)
            grad = grads[part].astype(low_type)
            log_total = jnp.sum(
                jnp.where(lane_ids(log_ref.shape) == 2 * pair + part, log_ref[...], 0.0),
                axis=-1,
                keepdims=True,
            )
            delta = jnp.sum(grads[part] * mixes[part], axis=-1, keepdims=True)
            scores = dot(query, keys, NT)
            scores = (scores.reshape(3, rows, length) + bias[...][None]).reshape(3 * rows, length)
            chance = jnp.exp(scores - log_total)
            prob_grad = dot(grad, values, NT)
            score_grad = (chance * (prob_grad - delta)).astype(low_type)
            value_term = dot(chance.astype(low_type), grad, TN)
            key_term = dot(score_grad, query, TN)
            key_grad = key_term if part == 0 else key_grad + key_term
            value_grad = value_term if part == 0 else value_grad + value_term
            query_grads.append(dot(score_grad, keys) * HD**-0.5)
        unstack_heads(dq_ref, pair, query_grads[0], query_grads[1])
        dkv_ref[:, pl.ds(lane, LANES)] = key_grad.astype(low_type)
        dkv_ref[:, pl.ds(value_lane, LANES)] = value_grad.astype(low_type)


def attend_back(q, kv, rows_pos, key_pos, ob, log_total, do):
    rows, width = q.shape
    length = kv.shape[0]
    return call(
        attend_back_kernel,
        (shaped((rows, width), low_type), shaped(kv.shape, low_type)),
        [in_vmem] * 7,
        (in_vmem,) * 2,
        [pltpu.VMEM((rows, length), jnp.float32)],
        40 * rows * length * width,
        8 * MIB,
        48,
    )(q, kv, rows_pos, key_pos, ob, log_total, do)


def input_kernel(all_groups, order_ref, x_ref, gain_ref, w_ref, *refs):
    micros = x_ref.shape[0]
    rows = x_ref.shape[1]
    dx_refs = refs[:micros]
    dq_refs = refs[micros : 2 * micros]
    dkv_refs = refs[2 * micros : 3 * micros]
    out_ref, stat_ref, grad, held, sem = refs[3 * micros :]
    start_matrix(order_ref, w_ref, held, sem, 0, all_groups)
    q_width = dq_refs[0].shape[-1]
    wait_bytes(held, sem)
    for n in range(held.shape[0] // BC):
        cut = slice(n * BC, (n + 1) * BC)
        for m in range(micros):
            grad[m, :, cut] = dot(dq_refs[m][...], held[cut, :q_width], NT) + dot(
                dkv_refs[m][...], held[cut, q_width:], NT
            )
    total = jnp.zeros((1, x_ref.shape[-1]), jnp.float32)
    for m in range(micros):
        x = x_ref[m]
        inverse = lax.rsqrt(jnp.mean(x * x, axis=-1, keepdims=True) + norm_eps)
        term, gain_grad = unit_back(x, gain_ref[0:1], inverse, grad[m])
        out_ref[m] = dx_refs[m][...] + term
        total = total + gain_grad
    stat_ref[...] = jnp.broadcast_to(total, stat_ref.shape)


def input_back(order, x, gains, w, dxs, dqs, dkvs):
    micros, rows, width = x.shape
    in_width = (HEADS + 2 * KVH) * HD
    return call(
        functools.partial(input_kernel, w.shape[0] * BR // width),
        (shaped(x.shape, jnp.float32), shaped((8, width), jnp.float32)),
        [in_smem, in_vmem, in_vmem, in_any] + [in_vmem] * (3 * micros),
        (in_vmem,) * 2,
        [
            pltpu.VMEM(x.shape, jnp.float32),
            pltpu.VMEM((width, in_width), low_type),
            pltpu.SemaphoreType.DMA,
        ],
        2 * micros * rows * width * in_width,
        14 * MIB,
        40,
    )(order, x, gains, w, *dxs, *dqs, *dkvs)


def rotate_kernel(
    b_ref, g_ref, m_ref, s_ref, l_ref, r_ref, grad_ref, new_ref, moment_ref, second_ref
):
    gradient = g_ref[0].astype(jnp.float32)
    grad_ref[0] = gradient
    left = l_ref[0].astype(low_type)
    right = r_ref[0].astype(low_type)
    rotated = dot(dot(left, gradient.astype(low_type), TN).astype(low_type), right)
    moment = beta_one * m_ref[0] + (1.0 - beta_one) * rotated
    second = beta_two * s_ref[0] + (1.0 - beta_two) * rotated * rotated
    moment_ref[0] = moment
    second_ref[0] = second
    direction = (moment / (jnp.sqrt(second) + adam_eps)).astype(low_type)
    turned = dot(dot(left, direction).astype(low_type), right, NT)
    new_ref[0] = b_ref[0] - rate * turned


def rotate(weight, gradient, moment, second, left, right):
    count = weight.shape[0]

    def spec(rows, cols):
        return pl.BlockSpec((1, rows, cols), lambda i: (i, 0, 0))

    block = spec(BR, BC)
    return pl.pallas_call(
        rotate_kernel,
        grid=(count,),
        out_shape=(shaped(weight.shape, jnp.float32),) * 4,
        in_specs=[block] * 4 + [spec(BR, BR), spec(BC, BC)],
        out_specs=(block,) * 4,
        compiler_params=pltpu.CompilerParams(vmem_limit_bytes=24 * MIB),
        cost_estimate=pl.CostEstimate(
            flops=4 * count * BR * BC * (BR + BC),
            bytes_accessed=count * 2 * MIB,
            transcendentals=0,
        ),
    )(weight, gradient, moment, second, left, right)


def adam(weight, gradient, moment, second, step_rate):
    moment_new = beta_one * moment + (1.0 - beta_one) * gradient
    second_new = beta_two * second + (1.0 - beta_two) * gradient * gradient
    return (
        weight - step_rate * moment_new / (jnp.sqrt(second_new) + adam_eps),
        moment_new,
        second_new,
    )


def to_partner(array, offset):
    if offset == 0:
        return array
    count = lax.axis_size("shard")
    return lax.ppermute(array, "shard", [(i, i ^ offset) for i in range(count)])


def shards(
    tokens,
    cotangent,
    norm_gains,
    router,
    dense_weight,
    expert_weight,
    routes,
    assign,
    dense_order,
    expert_order,
    dense_moment,
    dense_second,
    dense_left,
    dense_right,
    expert_moment,
    expert_second,
    expert_left,
    expert_right,
    gains_moment,
    gains_second,
    router_moment,
    router_second,
):
    ctx_count = lax.axis_size("ctx")
    shard_count = lax.axis_size("shard")
    micros, rows, width = tokens.shape
    span = rows // 2
    length = rows * ctx_count
    dense_groups = (2 * HEADS + 2 * KVH) * HD // BC
    in_groups = (HEADS + 2 * KVH) * HD // BC
    row_groups = width // BR
    ff_groups = FF // BC
    dense_blocks = row_groups * dense_groups
    expert_blocks = 3 * row_groups * ff_groups

    dense_inverse = inverse_order(dense_order)
    expert_inverse = inverse_order(expert_order)
    row_ids = jnp.arange(rows, dtype=jnp.int32)
    all_pos = (assign[:, row_ids // span] * span + row_ids % span).reshape(length)
    rows_pos = lax.dynamic_slice_in_dim(all_pos, lax.axis_index("ctx") * rows, rows)
    rows_pos = rows_pos.reshape(rows, 1)
    key_pos = all_pos.reshape(1, length)
    me = lax.axis_index("shard").astype(jnp.int32).reshape(1)
    router_pad = jnp.pad(router.astype(low_type), ((0, 0), (0, LANES - shard_count)))

    dense_all = lax.all_gather(dense_weight.astype(low_type), ("ctx", "shard"), axis=0, tiled=True)
    expert_all = lax.all_gather(expert_weight[0].astype(low_type), "ctx", axis=0, tiled=True)

    lanes = jnp.arange(LANES, dtype=jnp.int32)
    hits = jnp.sum((routes[..., None] == lanes).astype(low_type), axis=2)
    cot_rows = jnp.concatenate([cotangent.astype(low_type), hits], axis=2)
    cot_rows = cot_rows.reshape(micros * rows, width + LANES)
    cot_parts = [to_partner(cot_rows, j) for j in range(shard_count)]

    h1, q, kv = project(dense_inverse, tokens, norm_gains, dense_all)
    kv_all = [lax.all_gather(kv[m], "ctx", axis=0, tiled=True) for m in range(micros)]
    obs, logs, x2s, h2s = [], [], [], []
    for m in range(micros):
        ob, log_total, x2, h2 = attend(
            dense_inverse, q[m], kv_all[m], rows_pos, key_pos, tokens[m], norm_gains, dense_all
        )
        obs.append(ob)
        logs.append(log_total)
        x2s.append(x2)
        h2s.append(h2)

    outputs, backs = [], []
    zs, dgs, dus, dys, xs = [], [], [], [], []
    for m in range(micros):
        h_parts = [to_partner(h2s[m], j) for j in range(shard_count)]
        made = run_expert(m, expert_inverse, me, router_pad, h_parts, cot_parts, expert_all)
        back = made[:shard_count]
        out = made[shard_count : 2 * shard_count]
        z, dg, du, dy, x = made[2 * shard_count :]
        zs.append(z)
        dgs.append(dg)
        dus.append(du)
        dys.append(dy)
        xs.append(x)
        backs.append([to_partner(back[j], j) for j in range(shard_count)])
        arrived = [to_partner(out[j], j) for j in range(shard_count)]
        total = x2s[m]
        for part in arrived:
            total = total + part.astype(jnp.float32)
        outputs.append(total)

    expert_slots = inverse_slots = expert_inverse
    expert_term = outer_blocks(
        expert_slots,
        lambda k: (k * row_groups * ff_groups, ff_groups),
        [xs, xs, dys],
        [dgs, dus, zs],
        expert_blocks,
    )
    expert_sum = lax.psum_scatter(expert_term, "ctx", scatter_dimension=0, tiled=True)

    dxs, das, dqs, dkvs, stats = [], [], [], [], []
    for m in range(micros):
        dx, da, do, stat = merge(
            dense_inverse, me, x2s[m], cotangent[m], h2s[m], norm_gains, router_pad, dense_all, backs[m]
        )
        dq, dkv_part = attend_back(q[m], kv_all[m], rows_pos, key_pos, obs[m], logs[m], do)
        dkv = lax.psum_scatter(dkv_part, "ctx", scatter_dimension=0, tiled=True)
        dxs.append(dx)
        das.append(da)
        dqs.append(dq)
        dkvs.append(dkv)
        stats.append(stat)

    h1s = [h1[m * rows : (m + 1) * rows] for m in range(micros)]
    q_groups = HEADS * HD // BC
    starts = (0, q_groups, in_groups)
    dense_term = outer_blocks(
        dense_inverse,
        lambda k: (starts[k], dense_groups),
        [h1s, h1s, das],
        [dqs, dkvs, obs],
        dense_blocks,
    )
    dense_sum = lax.psum_scatter(dense_term, ("ctx", "shard"), scatter_dimension=0, tiled=True)
    input_grad, gain_stat = input_back(
        dense_inverse, tokens, norm_gains, dense_all, dxs, dqs, dkvs
    )
    experts_up = stats[0].shape[0] - 8
    stat_rows = jnp.concatenate(
        [sum(stats)[: experts_up + 1], gain_stat[: 7]], axis=0
    )
    stat_rows = lax.psum(stat_rows, ("ctx", "shard"))
    router_grad = stat_rows[:shard_count].T
    gains_grad = jnp.stack([stat_rows[experts_up + 1], stat_rows[experts_up]])

    expert_grad, expert_new, expert_moment_new, expert_second_new = rotate(
        expert_weight[0], expert_sum, expert_moment[0], expert_second[0], expert_left[0], expert_right[0]
    )
    dense_grad, dense_new, dense_moment_new, dense_second_new = rotate(
        dense_weight, dense_sum, dense_moment, dense_second, dense_left, dense_right
    )
    gains_new, gains_moment_new, gains_second_new = adam(
        norm_gains, gains_grad, gains_moment, gains_second, gain_rate
    )
    router_new, router_moment_new, router_second_new = adam(
        router, router_grad, router_moment, router_second, rate
    )
    return (
        jnp.stack(outputs),
        input_grad,
        dense_grad,
        dense_new,
        dense_moment_new,
        dense_second_new,
        expert_grad[None],
        expert_new[None],
        expert_moment_new[None],
        expert_second_new[None],
        gains_grad,
        gains_new,
        gains_moment_new,
        gains_second_new,
        router_grad,
        router_new,
        router_moment_new,
        router_second_new,
    )


def solution(mesh):
    rows_spec = P("shard", "ctx", None)
    dense_spec = P(("ctx", "shard"), None, None)
    expert_spec = P("shard", "ctx", None, None)
    in_specs = (
        (rows_spec, rows_spec, P(), P(), dense_spec, expert_spec, rows_spec, P(), P(), P())
        + (dense_spec,) * 4
        + (expert_spec,) * 4
        + (P(),) * 4
    )
    out_specs = (rows_spec,) * 2 + (dense_spec,) * 4 + (expert_spec,) * 4 + (P(),) * 8
    return jax.shard_map(shards, mesh=mesh, in_specs=in_specs, out_specs=out_specs, check_vma=False)
```

```python
import functools

import jax
import jax.numpy as jnp
from jax import lax
from jax.experimental import pallas as pl
from jax.experimental.pallas import tpu as pltpu
from jax.sharding import PartitionSpec as P

HEADS = 24
KVH = 8
HD = 64
FF = 1024
BR = 192
BC = 256
LANES = 128

norm_eps = 1e-06
beta_one = 0.9
beta_two = 0.95
rate = 0.01
gain_rate = 0.5
adam_eps = 1e-08
masked_score = -1e30
low_type = jnp.bfloat16
MIB = 1 << 20

NN = (((1,), (0,)), ((), ()))
NT = (((1,), (1,)), ((), ()))
TN = (((0,), (0,)), ((), ()))

in_vmem = pl.BlockSpec(memory_space=pltpu.VMEM)
in_smem = pl.BlockSpec(memory_space=pltpu.SMEM)
in_any = pl.BlockSpec(memory_space=pl.ANY)


def dot(left_side, right_side, dims=NN):
    return lax.dot_general(left_side, right_side, dims, preferred_element_type=jnp.float32)


def call(kernel, out_shapes, in_specs, out_specs, scratch, flops, moved, limit):
    return pl.pallas_call(
        kernel,
        out_shape=out_shapes,
        in_specs=in_specs,
        out_specs=out_specs,
        scratch_shapes=scratch,
        compiler_params=pltpu.CompilerParams(vmem_limit_bytes=limit * MIB),
        cost_estimate=pl.CostEstimate(flops=flops, bytes_accessed=moved, transcendentals=0),
    )


def shaped(dims, kind):
    return jax.ShapeDtypeStruct(dims, kind)


def inverse_order(slot_order):
    count = slot_order.shape[0]
    numbers = jnp.arange(count, dtype=jnp.int32)
    return jnp.sum(
        jnp.where(slot_order[None, :] == numbers[:, None], numbers[None, :], 0), axis=1
    ).astype(jnp.int32)


def wait_bytes(landed, semaphore):
    pltpu.make_async_copy(landed, landed, semaphore).wait()


def unit_rows(rows, gain):
    inverse = lax.rsqrt(jnp.mean(rows * rows, axis=-1, keepdims=True) + norm_eps)
    return rows * inverse * gain, inverse


def unit_back(rows, gain, inverse, gradient):
    unit = rows * inverse
    scaled = gradient * gain
    inner = jnp.mean(scaled * unit, axis=-1, keepdims=True)
    return inverse * (scaled - unit * inner), jnp.sum(gradient * unit, axis=0, keepdims=True)


def lane_ids(dims):
    return lax.broadcasted_iota(jnp.int32, dims, len(dims) - 1)


def half_turn(tile):
    return pltpu.roll(tile, HD, 1)


def stack_heads(ref, pair, scale=None):
    base = pair * (3 * LANES)
    tiles = [
        ref[:, pl.ds(pl.multiple_of(base + LANES * t, LANES), LANES)].astype(jnp.float32)
        for t in range(3)
    ]
    if scale is not None:
        tiles = [t * scale for t in tiles]
    lower = lane_ids(tiles[0].shape) < HD
    first = [tiles[0], half_turn(tiles[0]), tiles[1]]
    second = [tiles[1], half_turn(tiles[2]), tiles[2]]
    return (
        jnp.concatenate([jnp.where(lower, t, 0.0) for t in first], axis=0),
        jnp.concatenate([jnp.where(lower, 0.0, t) for t in second], axis=0),
    )


def unstack_heads(ref, pair, first, second):
    rows = first.shape[0] // 3
    base = pair * (3 * LANES)
    lower = lane_ids((rows, LANES)) < HD
    tiles = (
        jnp.where(lower, first[:rows], half_turn(first[rows : 2 * rows])),
        jnp.where(lower, first[2 * rows :], second[:rows]),
        jnp.where(lower, half_turn(second[rows : 2 * rows]), second[2 * rows :]),
    )
    for t in range(3):
        ref[:, pl.ds(pl.multiple_of(base + LANES * t, LANES), LANES)] = tiles[t].astype(ref.dtype)


def project_kernel(
    pieces, chips, members, slots, all_groups, order_ref, me_ref, x_ref, gain_ref, *refs
):
    piece_refs = refs[: len(pieces)]
    h_ref, q_ref, kv_ref, win_ref, wout_ref, held, sems, out_sems = refs[len(pieces) :]
    groups = held.shape[1] // BC
    q_groups = q_ref.shape[-1] // BC
    micros, rows = x_ref.shape[:2]
    ctx, shard = me_ref[0], me_ref[1]
    chip, core = lax.div(ctx, 2), lax.rem(ctx, 2)

    for ref, (other_core, offset, first, cut) in zip(piece_refs, pieces):

        @pl.loop(0, ref.shape[0])
        def _(i):
            source = lax.rem(chip - (first + lax.div(i, slots)) + chips, chips) * 2
            source = source + jnp.bitwise_xor(core, other_core)
            source = source * members + jnp.bitwise_xor(shard, offset)
            number = order_ref[source * slots + lax.rem(i, slots)]
            a, b = lax.div(number, all_groups), lax.rem(number, all_groups)
            down = pl.ds(pl.multiple_of(a * BR + cut, 32), ref.shape[1])

            @pl.when(b < groups)
            def _():
                across = pl.ds(pl.multiple_of(b * BC, BC), BC)
                pltpu.make_async_copy(ref.at[i], held.at[down, across], sems.at[b]).start()

            @pl.when(b >= groups)
            def _():
                across = pl.ds(pl.multiple_of((b - groups) * BC, BC), BC)
                pltpu.make_async_copy(ref.at[i], wout_ref.at[down, across], out_sems.at[0]).start()

    for m in range(micros):
        h_ref[pl.ds(m * rows, rows), :] = unit_rows(x_ref[m], gain_ref[0:1])[0].astype(low_type)

    def make(b):
        across = pl.ds(pl.multiple_of(b * BC, BC), BC)
        wait_bytes(held.at[:, across], sems.at[b])
        pltpu.make_async_copy(held.at[:, across], win_ref.at[:, across], out_sems.at[1]).start()
        return dot(h_ref[...], held[:, across]).astype(low_type)

    @pl.loop(0, q_groups)
    def _(b):
        made = make(b)
        for m in range(micros):
            q_ref[m, :, pl.ds(pl.multiple_of(b * BC, BC), BC)] = made[m * rows : (m + 1) * rows]

    @pl.loop(q_groups, groups)
    def _(b):
        made = make(b)
        for m in range(micros):
            kv_ref[m, :, pl.ds(pl.multiple_of((b - q_groups) * BC, BC), BC)] = made[
                m * rows : (m + 1) * rows
            ]

    wait_bytes(wout_ref, out_sems.at[0])
    wait_bytes(win_ref, out_sems.at[1])


def project(pieces, arrays, chips, members, slots, order, me, x, gains):
    micros, rows, width = x.shape
    in_width = (HEADS + 2 * KVH) * HD
    out_width = HEADS * HD
    return call(
        functools.partial(
            project_kernel, pieces, chips, members, slots, (in_width + out_width) // BC
        ),
        (
            shaped((micros * rows, width), low_type),
            shaped((micros, rows, HEADS * HD), low_type),
            shaped((micros, rows, 2 * KVH * HD), low_type),
            shaped((width, in_width), low_type),
            shaped((width, out_width), low_type),
        ),
        [in_smem, in_smem, in_vmem, in_vmem] + [in_any] * len(arrays),
        (in_vmem, in_vmem, in_vmem, in_any, in_any),
        [
            pltpu.VMEM((width, in_width), low_type),
            pltpu.SemaphoreType.DMA((in_width // BC,)),
            pltpu.SemaphoreType.DMA((2,)),
        ],
        2 * micros * rows * width * in_width,
        2 * width * in_width * 2,
        24,
    )(order, me, x, gains, *arrays)


def load_keys(parts, held, sem):
    start = 0
    for part in parts:
        count = part.shape[0]
        pltpu.make_async_copy(part, held.at[pl.ds(start, count)], sem).start()
        start += count


def attend_kernel(count, q_ref, rpos_ref, kpos_ref, x_ref, gain_ref, w_ref, *refs):
    parts = refs[:count]
    ob_ref, log_ref, x2_ref, h2_ref, bias, kv_ref, held, sems = refs[count:]
    rows = q_ref.shape[0]
    load_keys(parts, kv_ref, sems.at[0])
    pltpu.make_async_copy(w_ref, held, sems.at[1]).start()
    bias[...] = jnp.where(kpos_ref[...] <= rpos_ref[...], 0.0, masked_score)
    log_ref[...] = jnp.zeros_like(log_ref)
    length = kv_ref.shape[0]
    wait_bytes(kv_ref, sems.at[0])

    @pl.loop(0, KVH // 2)
    def _(pair):
        lane = pl.multiple_of(pair * LANES, LANES)
        keys = kv_ref[:, pl.ds(lane, LANES)]
        values = kv_ref[:, pl.ds(pl.multiple_of(lane + KVH * HD, LANES), LANES)]
        stacked = stack_heads(q_ref, pair, HD**-0.5)
        mixed = []
        for part in range(2):
            scores = dot(stacked[part].astype(low_type), keys, NT)
            scores = (scores.reshape(3, rows, length) + bias[...][None]).reshape(3 * rows, length)
            largest = jnp.max(scores, axis=-1, keepdims=True)
            raised = jnp.exp(scores - largest)
            summed = jnp.sum(raised, axis=-1, keepdims=True)
            mixed.append(dot(raised.astype(low_type), values) / summed)
            log_ref[...] = jnp.where(
                lane_ids(log_ref.shape) == 2 * pair + part, largest + jnp.log(summed), log_ref[...]
            )
        unstack_heads(ob_ref, pair, mixed[0], mixed[1])

    wait_bytes(held, sems.at[1])
    for n in range(held.shape[0] // BC):
        cut = slice(n * BC, (n + 1) * BC)
        x2_ref[:, cut] = x_ref[:, cut] + dot(ob_ref[...], held[cut, :], NT)
    h2_ref[...] = unit_rows(x2_ref[...], gain_ref[1:2])[0].astype(low_type)


def attend(q, kv_parts, rows_pos, key_pos, x, gains, w):
    rows, width = q.shape
    length = key_pos.shape[1]
    model = x.shape[1]
    return call(
        functools.partial(attend_kernel, len(kv_parts)),
        (
            shaped((rows, width), low_type),
            shaped((3 * rows, LANES), jnp.float32),
            shaped((rows, model), jnp.float32),
            shaped((rows, model), low_type),
        ),
        [in_vmem] * 5 + [in_any] * (1 + len(kv_parts)),
        (in_vmem,) * 4,
        [
            pltpu.VMEM((rows, length), jnp.float32),
            pltpu.VMEM((length, kv_parts[0].shape[1]), low_type),
            pltpu.VMEM((model, width), low_type),
            pltpu.SemaphoreType.DMA((2,)),
        ],
        16 * rows * length * width,
        8 * MIB,
        40,
    )(q, rows_pos, key_pos, x, gains, w, *kv_parts)


def router_parts(h2, router, experts):
    logits = dot(h2, router)
    logits = jnp.where(lane_ids(logits.shape) < experts, logits, masked_score)
    raised = jnp.exp(logits - jnp.max(logits, axis=-1, keepdims=True))
    return raised / jnp.sum(raised, axis=-1, keepdims=True)


def expert_kernel(sources, micro, order_ref, me_ref, router_ref, *refs):
    h_parts = refs[:sources]
    c_parts = refs[sources : 2 * sources]
    w_ref = refs[2 * sources]
    outs = refs[2 * sources + 1 :]
    back_refs = outs[:sources]
    out_refs = outs[sources : 2 * sources]
    z_ref, dg_ref, du_ref, dy_ref, xs_ref = outs[2 * sources : 2 * sources + 5]
    cs, held, chance, load_sem, w_sems = outs[2 * sources + 5 :]
    rows, width = h_parts[0].shape
    row_groups = width // BR
    col_groups = FF // BC
    for j in range(sources):
        pltpu.make_async_copy(h_parts[j], xs_ref.at[pl.ds(j * rows, rows)], load_sem.at[0]).start()
        pltpu.make_async_copy(
            c_parts[j].at[pl.ds(micro * rows, rows)], cs.at[pl.ds(j * rows, rows)], load_sem.at[1]
        ).start()
    for k in (0, 1, 2):

        @pl.loop(0, row_groups)
        def _(a):
            for b in range(col_groups):
                pltpu.make_async_copy(
                    w_ref.at[order_ref[(k * row_groups + a) * col_groups + b]],
                    held.at[k, pl.ds(pl.multiple_of(a * BR, 64), BR), pl.ds(b * BC, BC)],
                    w_sems.at[k],
                ).start()

    wait_bytes(xs_ref, load_sem.at[0])
    wait_bytes(cs, load_sem.at[1])
    me = me_ref[1]
    probs = router_parts(xs_ref[...], router_ref[...], sources)
    hits = cs[:, width:].astype(jnp.float32)
    mine = lane_ids(hits.shape) == me
    hit = jnp.sum(jnp.where(mine, hits, 0.0), axis=-1, keepdims=True)
    weight = jnp.sum(jnp.where(mine, probs, 0.0), axis=-1, keepdims=True) * hit
    dy_ref[...] = (weight * cs[:, :width].astype(jnp.float32)).astype(low_type)
    chance[...] = jnp.zeros_like(chance)
    for k in (0, 1, 2):
        wait_bytes(held.at[k], w_sems.at[k])

    @pl.loop(0, col_groups)
    def _(b):
        cut = pl.ds(pl.multiple_of(b * BC, BC), BC)
        gate = dot(xs_ref[...], held[0, :, cut])
        up = dot(xs_ref[...], held[1, :, cut])
        down = dot(cs[:, :width], held[2, :, cut])
        sig = jax.nn.sigmoid(gate)
        act = gate * sig
        hidden = act * up
        z_ref[:, cut] = hidden.astype(low_type)
        chance[...] += jnp.sum(down * hidden, axis=-1, keepdims=True)
        down = down * weight
        dg_ref[:, cut] = (down * up * sig * (1.0 + gate * (1.0 - sig))).astype(low_type)
        du_ref[:, cut] = (down * act).astype(low_type)

    for n in range(width // BC):
        cut = slice(n * BC, (n + 1) * BC)
        back = dot(dg_ref[...], held[0, cut, :], NT) + dot(du_ref[...], held[1, cut, :], NT)
        for j in range(sources):
            back_refs[j][:, cut] = back[j * rows : (j + 1) * rows].astype(low_type)
    told = chance[...] * hit
    high_part = told.astype(low_type)
    low_part = (told - high_part.astype(jnp.float32)).astype(low_type)
    lanes = lane_ids((sources * rows, LANES))
    tail = jnp.where(lanes == 0, high_part, jnp.where(lanes == 1, low_part, jnp.zeros_like(low_part)))
    for j in range(sources):
        back_refs[j][:, width:] = tail[j * rows : (j + 1) * rows]
    for n in range(width // BC):
        cut = slice(n * BC, (n + 1) * BC)
        made = dot(z_ref[...], held[2, cut, :], NT) * weight
        for j in range(sources):
            out_refs[j][:, cut] = made[j * rows : (j + 1) * rows].astype(low_type)


def run_expert(micro, order, me, router, h_parts, c_parts, w):
    sources = len(h_parts)
    rows, width = h_parts[0].shape
    total = sources * rows
    return call(
        functools.partial(expert_kernel, sources, micro),
        tuple(
            [shaped((rows, width + LANES), low_type)] * sources
            + [shaped((rows, width), low_type)] * sources
            + [shaped((total, FF), low_type)] * 3
            + [shaped((total, width), low_type)] * 2
        ),
        [in_smem, in_smem, in_vmem] + [in_any] * (2 * sources + 1),
        tuple([in_vmem] * (2 * sources + 5)),
        [
            pltpu.VMEM((total, width + LANES), low_type),
            pltpu.VMEM((3, width, FF), low_type),
            pltpu.VMEM((total, 1), jnp.float32),
            pltpu.SemaphoreType.DMA((2,)),
            pltpu.SemaphoreType.DMA((3,)),
        ],
        12 * total * width * FF,
        20 * MIB,
        56,
    )(order, me, router, *h_parts, *c_parts, w)


def outer_kernel(place, pairs, order_ref, *refs):
    count = len(pairs)
    micros = len(refs[:-3]) // (2 * count)
    lefts = refs[: count * micros]
    rights = refs[count * micros : 2 * count * micros]
    out_ref, stage, sems = refs[-3:]
    span = 2 * BR
    steps = []
    for k in range(count):
        for p in range(lefts[k * micros].shape[-1] // span):
            steps.append((k, p))

    def wait_stage(slot, cols):
        wait_bytes(stage.at[slot, :, pl.ds(0, cols)], sems.at[slot])

    used = [None, None]
    for n, (k, p) in enumerate(steps):
        slot = n % 2
        cols = rights[k * micros].shape[-1]
        if used[slot] is not None:
            wait_stage(slot, used[slot])
        used[slot] = cols
        cut = slice(p * span, (p + 1) * span)
        for c in range(0, cols, 512):
            part = slice(c, c + 512)
            made = sum(
                dot(lefts[k * micros + m][:, cut], rights[k * micros + m][:, part], TN)
                for m in range(micros)
            )
            stage[slot, :, part] = made.astype(low_type)
        first, row_step = place(k)
        for half in range(2):
            for b in range(cols // BC):
                pltpu.make_async_copy(
                    stage.at[slot, pl.ds(half * BR, BR), pl.ds(b * BC, BC)],
                    out_ref.at[order_ref[first + (2 * p + half) * row_step + b]],
                    sems.at[slot],
                ).start()
    for slot in range(2):
        if used[slot] is not None:
            wait_stage(slot, used[slot])


def outer_blocks(order, place, lefts, rights, blocks):
    pairs = [(l[0].shape[-1], r[0].shape[-1]) for l, r in zip(lefts, rights)]
    widest = max(r for _, r in pairs)
    rows = sum(l.shape[0] for l in lefts[0])
    flat = [l for group in lefts for l in group] + [r for group in rights for r in group]
    return call(
        functools.partial(outer_kernel, place, pairs),
        shaped((blocks, BR, BC), low_type),
        [in_smem] + [in_vmem] * len(flat),
        in_any,
        [pltpu.VMEM((2, 2 * BR, widest), low_type), pltpu.SemaphoreType.DMA((2,))],
        2 * rows * blocks * BR * BC,
        blocks * BR * BC * 2 + sum(f.size * 2 for f in flat),
        48,
    )(order, *flat)


def xor_plan(members, offset):
    if members != 4:
        return list(range(1, members)), [0]
    first = 1 if offset % 2 else 2
    return [first, 3], [0, 3 - first]


def slots_kernel(
    counts, chips, members, slots, all_groups, in_groups, order_ref, me_ref, *refs
):
    lists = []
    for count in counts:
        lists.append(refs[:count])
        refs = refs[count:]
    outs = refs[: 2 * chips]
    lefts, turned, rights, sems = refs[2 * chips :]
    ctx, shard = me_ref[0], me_ref[1]
    chip, core = lax.div(ctx, 2), lax.rem(ctx, 2)
    h_width = lefts.shape[2]
    q_width = lists[2][0].shape[1]
    kv_width = lists[3][0].shape[1]
    total = rights.shape[0]
    targets = (
        (lefts.at[0], 0, h_width, 0),
        (lefts.at[1], 0, h_width, 1),
        (rights, 0, q_width, 2),
        (rights, q_width, kv_width, 2),
        (rights, q_width + kv_width, q_width, 2),
    )
    for group, (target, lane, lanes, sem) in zip(lists, targets):
        start = 0
        for ref in group:
            pltpu.make_async_copy(
                ref, target.at[pl.ds(start, ref.shape[0]), pl.ds(lane, lanes)], sems.at[sem]
            ).start()
            start += ref.shape[0]
    for side in range(2):
        wait_bytes(lefts.at[side], sems.at[side])
        for r in range(0, total, LANES):
            turned[side, :, r : r + LANES] = lefts[side, r : r + LANES, :].T
    wait_bytes(rights, sems.at[2])
    for offset in range(chips):
        there = lax.rem(chip - offset + chips, chips) * 2 + core
        for out, hops in zip(outs[2 * offset : 2 * offset + 2], xor_plan(members, offset)):
            for place, hop in enumerate(hops):
                base = (there * members + jnp.bitwise_xor(shard, hop)) * slots

                @pl.loop(0, slots)
                def _(i):
                    number = order_ref[base + i]
                    a, b = lax.div(number, all_groups), lax.rem(number, all_groups)
                    side = (b >= in_groups).astype(jnp.int32)
                    out[place * slots + i] = dot(
                        turned[side, pl.ds(pl.multiple_of(a * BR, 64), BR), :],
                        rights[:, pl.ds(pl.multiple_of(b * BC, BC), BC)],
                    ).astype(low_type)


def slot_blocks(chips, members, slots, order, me, h1, da, dq, dkv, ob):
    lists = (h1, da, dq, dkv, ob)
    total = sum(part.shape[0] for part in h1)
    width = h1[0].shape[1]
    in_width = dq[0].shape[1] + dkv[0].shape[1]
    all_width = in_width + ob[0].shape[1]
    outs = []
    for offset in range(chips):
        for hops in xor_plan(members, offset):
            outs.append(shaped((len(hops) * slots, BR, BC), low_type))
    made = call(
        functools.partial(
            slots_kernel,
            tuple(len(group) for group in lists),
            chips,
            members,
            slots,
            all_width // BC,
            in_width // BC,
        ),
        tuple(outs),
        [in_smem, in_smem] + [in_any] * sum(len(group) for group in lists),
        (in_vmem,) * len(outs),
        [
            pltpu.VMEM((2, total, width), low_type),
            pltpu.VMEM((2, width, total), low_type),
            pltpu.VMEM((total, all_width), low_type),
            pltpu.SemaphoreType.DMA((3,)),
        ],
        2 * total * chips * members * slots * BR * BC,
        16 * MIB,
        40,
    )(order, me, *[part for group in lists for part in group])
    return [(made[2 * offset], made[2 * offset + 1]) for offset in range(chips)]


def merge_kernel(
    sources, me_ref, x2_ref, cot_ref, h2_ref, gain_ref, router_ref, w_ref, *refs
):
    back_refs = refs[:sources]
    dx_ref, da_ref, do_ref, stat_ref, held, sem = refs[sources:]
    rows, width = x2_ref.shape
    pltpu.make_async_copy(w_ref, held, sem).start()
    lanes = lane_ids((rows, LANES))
    prob_grad = jnp.zeros((rows, LANES), jnp.float32)
    gathered = jnp.zeros((rows, width), jnp.float32)
    for j in range(sources):
        tail = back_refs[j][:, width:].astype(jnp.float32)
        told = jnp.sum(tail, axis=-1, keepdims=True)
        expert = jnp.bitwise_xor(me_ref[1], j)
        prob_grad = prob_grad + jnp.where(lanes == expert, told, 0.0)
        gathered = gathered + back_refs[j][:, :width].astype(jnp.float32)
    h2 = h2_ref[...]
    probs = router_parts(h2, router_ref[...], sources)
    logit_grad = probs * (prob_grad - jnp.sum(probs * prob_grad, axis=-1, keepdims=True))
    high_part = logit_grad.astype(low_type)
    low_part = (logit_grad - high_part.astype(jnp.float32)).astype(low_type)
    router_grad = dot(high_part, h2, TN) + dot(low_part, h2, TN)
    gathered = gathered + dot(high_part, router_ref[...], NT) + dot(low_part, router_ref[...], NT)
    x2 = x2_ref[...]
    inverse = lax.rsqrt(jnp.mean(x2 * x2, axis=-1, keepdims=True) + norm_eps)
    moe_grad, gain_grad = unit_back(x2, gain_ref[1:2], inverse, gathered)
    after = cot_ref[...] + moe_grad
    dx_ref[...] = after
    da_ref[...] = after.astype(low_type)
    experts_up = stat_ref.shape[0] - 8
    stat_ref[:experts_up] = router_grad[:experts_up]
    stat_ref[experts_up:] = jnp.broadcast_to(gain_grad, (8, width))
    wait_bytes(held, sem)
    for n in range(held.shape[1] // BC):
        cut = slice(n * BC, (n + 1) * BC)
        do_ref[:, cut] = dot(da_ref[...], held[:, cut]).astype(low_type)


def merge(me, x2, cot, h2, gains, router, w, backs):
    rows, width = x2.shape
    sources = len(backs)
    experts_up = -(-sources // 8) * 8
    return call(
        functools.partial(merge_kernel, sources),
        (
            shaped((rows, width), jnp.float32),
            shaped((rows, width), low_type),
            shaped((rows, HEADS * HD), low_type),
            shaped((experts_up + 8, width), jnp.float32),
        ),
        [in_smem] + [in_vmem] * 5 + [in_any] + [in_vmem] * sources,
        (in_vmem,) * 4,
        [pltpu.VMEM((width, HEADS * HD), low_type), pltpu.SemaphoreType.DMA],
        2 * rows * width * HEADS * HD,
        10 * MIB,
        40,
    )(me, x2, cot, h2, gains, router, w, *backs)


def attend_back_kernel(count, q_ref, rpos_ref, kpos_ref, ob_ref, log_ref, do_ref, *refs):
    parts = refs[:count]
    dq_ref, own_ref, other_ref, bias, kv_ref, sem = refs[count:]
    rows = q_ref.shape[0]
    load_keys(parts, kv_ref, sem)
    length = kv_ref.shape[0]
    bias[...] = jnp.where(kpos_ref[...] <= rpos_ref[...], 0.0, masked_score)
    wait_bytes(kv_ref, sem)

    @pl.loop(0, KVH // 2)
    def _(pair):
        lane = pl.multiple_of(pair * LANES, LANES)
        value_lane = pl.multiple_of(lane + KVH * HD, LANES)
        keys = kv_ref[:, pl.ds(lane, LANES)]
        values = kv_ref[:, pl.ds(value_lane, LANES)]
        queries = stack_heads(q_ref, pair, HD**-0.5)
        grads = stack_heads(do_ref, pair)
        mixes = stack_heads(ob_ref, pair)
        query_grads = []
        key_grad = value_grad = None
        for part in range(2):
            query = queries[part].astype(low_type)
            grad = grads[part].astype(low_type)
            log_total = jnp.sum(
                jnp.where(lane_ids(log_ref.shape) == 2 * pair + part, log_ref[...], 0.0),
                axis=-1,
                keepdims=True,
            )
            delta = jnp.sum(grads[part] * mixes[part], axis=-1, keepdims=True)
            scores = dot(query, keys, NT)
            scores = (scores.reshape(3, rows, length) + bias[...][None]).reshape(3 * rows, length)
            chance = jnp.exp(scores - log_total)
            prob_grad = dot(grad, values, NT)
            score_grad = (chance * (prob_grad - delta)).astype(low_type)
            value_term = dot(chance.astype(low_type), grad, TN)
            key_term = dot(score_grad, query, TN)
            key_grad = key_term if part == 0 else key_grad + key_term
            value_grad = value_term if part == 0 else value_grad + value_term
            query_grads.append(dot(score_grad, keys) * HD**-0.5)
        unstack_heads(dq_ref, pair, query_grads[0], query_grads[1])
        half = length // 2
        for ref, cut in ((own_ref, slice(0, half)), (other_ref, slice(half, length))):
            ref[:, pl.ds(lane, LANES)] = key_grad[cut].astype(low_type)
            ref[:, pl.ds(value_lane, LANES)] = value_grad[cut].astype(low_type)


def attend_back(q, kv_parts, rows_pos, key_pos, ob, log_total, do):
    rows, width = q.shape
    length = key_pos.shape[1]
    kv_width = kv_parts[0].shape[1]
    return call(
        functools.partial(attend_back_kernel, len(kv_parts)),
        (shaped((rows, width), low_type),) + (shaped((length // 2, kv_width), low_type),) * 2,
        [in_vmem] * 6 + [in_any] * len(kv_parts),
        (in_vmem,) * 3,
        [
            pltpu.VMEM((rows, length), jnp.float32),
            pltpu.VMEM((length, kv_width), low_type),
            pltpu.SemaphoreType.DMA,
        ],
        40 * rows * length * width,
        8 * MIB,
        48,
    )(q, rows_pos, key_pos, ob, log_total, do, *kv_parts)


def input_kernel(x_ref, gain_ref, w_ref, *refs):
    micros = x_ref.shape[0]
    rows = x_ref.shape[1]
    dx_refs = refs[:micros]
    dq_refs = refs[micros : 2 * micros]
    dkv_refs = refs[2 * micros : 3 * micros]
    out_ref, stat_ref, grad, held, sem = refs[3 * micros :]
    pltpu.make_async_copy(w_ref, held, sem).start()
    q_width = dq_refs[0].shape[-1]
    wait_bytes(held, sem)
    for n in range(held.shape[0] // BC):
        cut = slice(n * BC, (n + 1) * BC)
        for m in range(micros):
            grad[m, :, cut] = dot(dq_refs[m][...], held[cut, :q_width], NT) + dot(
                dkv_refs[m][...], held[cut, q_width:], NT
            )
    total = jnp.zeros((1, x_ref.shape[-1]), jnp.float32)
    for m in range(micros):
        x = x_ref[m]
        inverse = lax.rsqrt(jnp.mean(x * x, axis=-1, keepdims=True) + norm_eps)
        term, gain_grad = unit_back(x, gain_ref[0:1], inverse, grad[m])
        out_ref[m] = dx_refs[m][...] + term
        total = total + gain_grad
    stat_ref[...] = jnp.broadcast_to(total, stat_ref.shape)


def input_back(x, gains, w, dxs, dqs, dkvs):
    micros, rows, width = x.shape
    in_width = (HEADS + 2 * KVH) * HD
    return call(
        input_kernel,
        (shaped(x.shape, jnp.float32), shaped((8, width), jnp.float32)),
        [in_vmem, in_vmem, in_any] + [in_vmem] * (3 * micros),
        (in_vmem,) * 2,
        [
            pltpu.VMEM(x.shape, jnp.float32),
            pltpu.VMEM((width, in_width), low_type),
            pltpu.SemaphoreType.DMA,
        ],
        2 * micros * rows * width * in_width,
        14 * MIB,
        40,
    )(x, gains, w, *dxs, *dqs, *dkvs)


def rotate_kernel(
    b_ref, g_ref, m_ref, s_ref, l_ref, r_ref, grad_ref, new_ref, moment_ref, second_ref
):
    gradient = g_ref[0].astype(jnp.float32)
    grad_ref[0] = gradient
    left = l_ref[0].astype(low_type)
    right = r_ref[0].astype(low_type)
    rotated = dot(dot(left, gradient.astype(low_type), TN).astype(low_type), right)
    moment = beta_one * m_ref[0] + (1.0 - beta_one) * rotated
    second = beta_two * s_ref[0] + (1.0 - beta_two) * rotated * rotated
    moment_ref[0] = moment
    second_ref[0] = second
    direction = (moment / (jnp.sqrt(second) + adam_eps)).astype(low_type)
    turned = dot(dot(left, direction).astype(low_type), right, NT)
    new_ref[0] = b_ref[0] - rate * turned


def rotate(weight, gradient, moment, second, left, right):
    count = weight.shape[0]

    def spec(rows, cols):
        return pl.BlockSpec((1, rows, cols), lambda i: (i, 0, 0))

    block = spec(BR, BC)
    return pl.pallas_call(
        rotate_kernel,
        grid=(count,),
        out_shape=(shaped(weight.shape, jnp.float32),) * 4,
        in_specs=[block] * 4 + [spec(BR, BR), spec(BC, BC)],
        out_specs=(block,) * 4,
        compiler_params=pltpu.CompilerParams(vmem_limit_bytes=24 * MIB),
        cost_estimate=pl.CostEstimate(
            flops=4 * count * BR * BC * (BR + BC),
            bytes_accessed=count * 2 * MIB,
            transcendentals=0,
        ),
    )(weight, gradient, moment, second, left, right)


def adam(weight, gradient, moment, second, step_rate):
    moment_new = beta_one * moment + (1.0 - beta_one) * gradient
    second_new = beta_two * second + (1.0 - beta_two) * gradient * gradient
    return (
        weight - step_rate * moment_new / (jnp.sqrt(second_new) + adam_eps),
        moment_new,
        second_new,
    )


def to_partner(array, offset):
    if offset == 0:
        return array
    count = lax.axis_size("shard")
    return lax.ppermute(array, "shard", [(i, i ^ offset) for i in range(count)])


def to_ctx(array, offset):
    count = lax.axis_size("ctx")
    return lax.ppermute(array, "ctx", [(i, i ^ offset) for i in range(count)])


def to_next_chip(array):
    count = lax.axis_size("ctx")
    return lax.ppermute(array, "ctx", [(i, (i + 2) % count) for i in range(count)])


def chip_ring(array, chips):
    parts = [array]
    for _ in range(chips - 1):
        parts.append(to_next_chip(parts[-1]))
    return parts


def wide(array):
    return array.astype(jnp.float32)


def ring_sum(parts, chips):
    total = None
    for offset in list(range(1, chips)) + [0]:
        total = parts[offset] if total is None else wide(to_next_chip(total)) + parts[offset]
        if offset != 0:
            total = total.astype(low_type)
    return total


def gather_weights(blocks, chips, members):
    parts = chip_ring(blocks, chips)
    groups = [(0, parts[0])]
    if chips > 1:
        groups.append((1, jnp.concatenate(parts[1:], axis=0)))
    pieces, arrays = [], []

    def add(array, offset, first, cut):
        pieces.append((0, offset, first, cut))
        arrays.append(array)

    for first, group in groups:
        add(group, 0, first, 0)
        if members == 4:
            by_one, by_two = to_partner(group, 1), to_partner(group, 2)
            add(by_one, 1, first, 0)
            add(by_two, 2, first, 0)
            half = BR // 2
            add(to_partner(by_one[:, :half], 2), 3, first, 0)
            add(to_partner(by_two[:, half:], 1), 3, first, half)
        else:
            for offset in range(1, members):
                add(to_partner(group, offset), offset, first, 0)
    swapped = [to_ctx(array, 1) for array in arrays]
    return pieces + [(1,) + piece[1:] for piece in pieces], arrays + swapped


def sum_slots(made, chips, members, slots):
    sums = []
    for offset in range(chips):
        sent, kept = made[offset]
        hops, keeps = xor_plan(members, offset)
        total = wide(kept[:slots])
        if members == 4:
            first, second = hops[0], keeps[1]
            got = to_partner(sent, first)
            total = total + wide(got[:slots])
            relay = (wide(kept[slots:]) + wide(got[slots:])).astype(low_type)
            total = total + wide(to_partner(relay, second))
        else:
            for place, hop in enumerate(hops):
                total = total + wide(to_partner(sent[place * slots : (place + 1) * slots], hop))
        sums.append(total)
    return ring_sum(sums, chips)


def sum_all(array):
    step = 1
    while step < lax.axis_size("ctx"):
        array = array + to_ctx(array, step)
        step *= 2
    step = 1
    while step < lax.axis_size("shard"):
        array = array + to_partner(array, step)
        step *= 2
    return array


def shards(
    tokens,
    cotangent,
    norm_gains,
    router,
    dense_weight,
    expert_weight,
    routes,
    assign,
    dense_order,
    expert_order,
    dense_moment,
    dense_second,
    dense_left,
    dense_right,
    expert_moment,
    expert_second,
    expert_left,
    expert_right,
    gains_moment,
    gains_second,
    router_moment,
    router_second,
):
    ctx_count = lax.axis_size("ctx")
    shard_count = lax.axis_size("shard")
    chips = ctx_count // 2
    micros, rows, width = tokens.shape
    slots = dense_weight.shape[0]
    span = rows // 2
    row_groups = width // BR
    ff_groups = FF // BC
    expert_blocks = 3 * row_groups * ff_groups

    expert_inverse = inverse_order(expert_order)
    ctx = lax.axis_index("ctx").astype(jnp.int32)
    me = jnp.stack([ctx, lax.axis_index("shard").astype(jnp.int32)])
    row_ids = jnp.arange(rows, dtype=jnp.int32)
    all_pos = assign[:, row_ids // span] * span + row_ids % span
    ring_ids = (ctx // 2 - jnp.arange(chips, dtype=jnp.int32)) % chips * 2
    key_ids = jnp.concatenate([ring_ids + ctx % 2, ring_ids + (1 - ctx % 2)])
    key_pos = all_pos[key_ids].reshape(1, rows * ctx_count)
    rows_pos = all_pos[ctx].reshape(rows, 1)
    router_pad = jnp.pad(router.astype(low_type), ((0, 0), (0, LANES - shard_count)))

    expert_all = lax.all_gather(expert_weight[0].astype(low_type), "ctx", axis=0, tiled=True)
    pieces, arrays = gather_weights(dense_weight.astype(low_type), chips, shard_count)

    lanes = jnp.arange(LANES, dtype=jnp.int32)
    hits = jnp.sum((routes[..., None] == lanes).astype(low_type), axis=2)
    cot_rows = jnp.concatenate([cotangent.astype(low_type), hits], axis=2)
    cot_rows = cot_rows.reshape(micros * rows, width + LANES)
    cot_parts = [to_partner(cot_rows, j) for j in range(shard_count)]

    h1, q, kv, w_in, w_out = project(
        pieces, arrays, chips, shard_count, slots, dense_order, me, tokens, norm_gains
    )
    h1_other = to_ctx(h1, 1)
    kvs, obs, logs, x2s, h2s = [], [], [], [], []
    for m in range(micros):
        parts = chip_ring(kv[m], chips)
        parts = parts + [to_ctx(part, 1) for part in parts]
        ob, log_total, x2, h2 = attend(
            q[m], parts, rows_pos, key_pos, tokens[m], norm_gains, w_out
        )
        kvs.append(parts)
        obs.append(ob)
        logs.append(log_total)
        x2s.append(x2)
        h2s.append(h2)

    backs, outs = [], []
    zs, dgs, dus, dys, xs = [], [], [], [], []
    for m in range(micros):
        h_parts = [to_partner(h2s[m], j) for j in range(shard_count)]
        made = run_expert(m, expert_inverse, me, router_pad, h_parts, cot_parts, expert_all)
        back = made[:shard_count]
        outs.append(made[shard_count : 2 * shard_count])
        z, dg, du, dy, x = made[2 * shard_count :]
        zs.append(z)
        dgs.append(dg)
        dus.append(du)
        dys.append(dy)
        xs.append(x)
        backs.append([to_partner(back[j], j) for j in range(shard_count)])

    expert_term = outer_blocks(
        expert_inverse,
        lambda k: (k * row_groups * ff_groups, ff_groups),
        [xs, xs, dys],
        [dgs, dus, zs],
        expert_blocks,
    )
    expert_sum = lax.psum_scatter(expert_term, "ctx", scatter_dimension=0, tiled=True)

    dxs, das, dqs, dkvs, stats = [], [], [], [], []
    for m in range(micros):
        dx, da, do, stat = merge(
            me, x2s[m], cotangent[m], h2s[m], norm_gains, router_pad, w_out, backs[m]
        )
        dq, dkv_own, dkv_other = attend_back(
            q[m], kvs[m], rows_pos, key_pos, obs[m], logs[m], do
        )
        got = to_ctx(dkv_other, 1)
        dkv = ring_sum(
            [
                wide(dkv_own[o * rows : (o + 1) * rows]) + wide(got[o * rows : (o + 1) * rows])
                for o in range(chips)
            ],
            chips,
        ).astype(low_type)
        dxs.append(dx)
        das.append(da)
        dqs.append(dq)
        dkvs.append(dkv)
        stats.append(stat)

    def both_cores(parts):
        return parts + [to_ctx(part, 1) for part in parts]

    made = slot_blocks(
        chips,
        shard_count,
        slots,
        dense_order,
        me,
        [h1, h1_other],
        both_cores(das),
        both_cores(dqs),
        both_cores(dkvs),
        both_cores(obs),
    )
    dense_sum = sum_slots(made, chips, shard_count, slots)
    input_grad, gain_stat = input_back(tokens, norm_gains, w_in, dxs, dqs, dkvs)
    experts_up = stats[0].shape[0] - 8
    stat_rows = jnp.concatenate([sum(stats)[: experts_up + 1], gain_stat[:7]], axis=0)
    stat_rows = sum_all(stat_rows)
    router_grad = stat_rows[:shard_count].T
    gains_grad = jnp.stack([stat_rows[experts_up + 1], stat_rows[experts_up]])

    outputs = []
    for m in range(micros):
        total = x2s[m]
        for j in range(shard_count):
            total = total + wide(to_partner(outs[m][j], j))
        outputs.append(total)

    expert_grad, expert_new, expert_moment_new, expert_second_new = rotate(
        expert_weight[0], expert_sum, expert_moment[0], expert_second[0], expert_left[0], expert_right[0]
    )
    dense_grad, dense_new, dense_moment_new, dense_second_new = rotate(
        dense_weight, dense_sum, dense_moment, dense_second, dense_left, dense_right
    )
    gains_new, gains_moment_new, gains_second_new = adam(
        norm_gains, gains_grad, gains_moment, gains_second, gain_rate
    )
    router_new, router_moment_new, router_second_new = adam(
        router, router_grad, router_moment, router_second, rate
    )
    return (
        jnp.stack(outputs),
        input_grad,
        dense_grad,
        dense_new,
        dense_moment_new,
        dense_second_new,
        expert_grad[None],
        expert_new[None],
        expert_moment_new[None],
        expert_second_new[None],
        gains_grad,
        gains_new,
        gains_moment_new,
        gains_second_new,
        router_grad,
        router_new,
        router_moment_new,
        router_second_new,
    )


def solution(mesh):
    rows_spec = P("shard", "ctx", None)
    dense_spec = P(("ctx", "shard"), None, None)
    expert_spec = P("shard", "ctx", None, None)
    in_specs = (
        (rows_spec, rows_spec, P(), P(), dense_spec, expert_spec, rows_spec, P(), P(), P())
        + (dense_spec,) * 4
        + (expert_spec,) * 4
        + (P(),) * 4
    )
    out_specs = (rows_spec,) * 2 + (dense_spec,) * 4 + (expert_spec,) * 4 + (P(),) * 8
    return jax.shard_map(shards, mesh=mesh, in_specs=in_specs, out_specs=out_specs, check_vma=False)
```

```python
import functools

import jax
import jax.numpy as jnp
from jax import lax
from jax.experimental import pallas as pl
from jax.experimental.pallas import tpu as pltpu
from jax.sharding import PartitionSpec as P

HEADS = 24
KVH = 8
HD = 64
FF = 1024
BR = 192
BC = 256
LANES = 128

norm_eps = 1e-06
beta_one = 0.9
beta_two = 0.95
rate = 0.01
gain_rate = 0.5
adam_eps = 1e-08
masked_score = -1e30
low_type = jnp.bfloat16
MIB = 1 << 20
VMEM_LIMIT = 60 * MIB

NN = (((1,), (0,)), ((), ()))
NT = (((1,), (1,)), ((), ()))
TN = (((0,), (0,)), ((), ()))

in_vmem = pl.BlockSpec(memory_space=pltpu.VMEM)
in_smem = pl.BlockSpec(memory_space=pltpu.SMEM)
in_any = pl.BlockSpec(memory_space=pl.ANY)


def dot(left_side, right_side, dims=NN):
    return lax.dot_general(left_side, right_side, dims, preferred_element_type=jnp.float32)


def call(kernel, out_shapes, in_specs, out_specs, scratch, flops, moved):
    return pl.pallas_call(
        kernel,
        out_shape=out_shapes,
        in_specs=in_specs,
        out_specs=out_specs,
        scratch_shapes=scratch,
        compiler_params=pltpu.CompilerParams(vmem_limit_bytes=VMEM_LIMIT),
        cost_estimate=pl.CostEstimate(flops=flops, bytes_accessed=moved, transcendentals=0),
    )


def shaped(dims, kind):
    return jax.ShapeDtypeStruct(dims, kind)


def inverse_order(slot_order):
    count = slot_order.shape[0]
    numbers = jnp.arange(count, dtype=jnp.int32)
    return jnp.sum(
        jnp.where(slot_order[None, :] == numbers[:, None], numbers[None, :], 0), axis=1
    ).astype(jnp.int32)


def wait_bytes(landed, semaphore):
    pltpu.make_async_copy(landed, landed, semaphore).wait()


def unit_rows(rows, gain):
    inverse = lax.rsqrt(jnp.mean(rows * rows, axis=-1, keepdims=True) + norm_eps)
    return rows * inverse * gain, inverse


def unit_back(rows, gain, inverse, gradient):
    unit = rows * inverse
    scaled = gradient * gain
    inner = jnp.mean(scaled * unit, axis=-1, keepdims=True)
    return inverse * (scaled - unit * inner), jnp.sum(gradient * unit, axis=0, keepdims=True)


def lane_ids(dims):
    return lax.broadcasted_iota(jnp.int32, dims, len(dims) - 1)


def half_turn(tile):
    return pltpu.roll(tile, HD, 1)


def stack_heads(ref, pair, scale=None):
    base = pair * (3 * LANES)
    tiles = [
        ref[:, pl.ds(pl.multiple_of(base + LANES * t, LANES), LANES)].astype(jnp.float32)
        for t in range(3)
    ]
    if scale is not None:
        tiles = [t * scale for t in tiles]
    lower = lane_ids(tiles[0].shape) < HD
    first = [tiles[0], half_turn(tiles[0]), tiles[1]]
    second = [tiles[1], half_turn(tiles[2]), tiles[2]]
    return (
        jnp.concatenate([jnp.where(lower, t, 0.0) for t in first], axis=0),
        jnp.concatenate([jnp.where(lower, 0.0, t) for t in second], axis=0),
    )


def unstack_heads(ref, pair, first, second):
    rows = first.shape[0] // 3
    base = pair * (3 * LANES)
    lower = lane_ids((rows, LANES)) < HD
    tiles = (
        jnp.where(lower, first[:rows], half_turn(first[rows : 2 * rows])),
        jnp.where(lower, first[2 * rows :], second[:rows]),
        jnp.where(lower, half_turn(second[rows : 2 * rows]), second[2 * rows :]),
    )
    for t in range(3):
        ref[:, pl.ds(pl.multiple_of(base + LANES * t, LANES), LANES)] = tiles[t].astype(ref.dtype)


def project_kernel(
    pieces, chips, members, slots, all_groups, order_ref, me_ref, x_ref, gain_ref, *refs
):
    piece_refs = refs[: len(pieces)]
    h_ref, q_ref, kv_ref, win_ref, wout_ref, held, sems, out_sems = refs[len(pieces) :]
    groups = held.shape[1] // BC
    q_groups = q_ref.shape[-1] // BC
    micros, rows = x_ref.shape[:2]
    ctx, shard = me_ref[0], me_ref[1]
    chip, core = lax.div(ctx, 2), lax.rem(ctx, 2)

    for ref, (other_core, offset, first, cut) in zip(piece_refs, pieces):

        @pl.loop(0, ref.shape[0])
        def _(i):
            source = lax.rem(chip - (first + lax.div(i, slots)) + chips, chips) * 2
            source = source + jnp.bitwise_xor(core, other_core)
            source = source * members + jnp.bitwise_xor(shard, offset)
            number = order_ref[source * slots + lax.rem(i, slots)]
            a, b = lax.div(number, all_groups), lax.rem(number, all_groups)
            down = pl.ds(pl.multiple_of(a * BR + cut, 32), ref.shape[1])

            @pl.when(b < groups)
            def _():
                across = pl.ds(pl.multiple_of(b * BC, BC), BC)
                pltpu.make_async_copy(ref.at[i], held.at[down, across], sems.at[b]).start()

            @pl.when(b >= groups)
            def _():
                across = pl.ds(pl.multiple_of((b - groups) * BC, BC), BC)
                pltpu.make_async_copy(ref.at[i], wout_ref.at[down, across], out_sems.at[0]).start()

    for m in range(micros):
        h_ref[pl.ds(m * rows, rows), :] = unit_rows(x_ref[m], gain_ref[0:1])[0].astype(low_type)

    def make(b):
        across = pl.ds(pl.multiple_of(b * BC, BC), BC)
        wait_bytes(held.at[:, across], sems.at[b])
        pltpu.make_async_copy(held.at[:, across], win_ref.at[:, across], out_sems.at[1]).start()
        return dot(h_ref[...], held[:, across]).astype(low_type)

    @pl.loop(0, q_groups)
    def _(b):
        made = make(b)
        for m in range(micros):
            q_ref[m, :, pl.ds(pl.multiple_of(b * BC, BC), BC)] = made[m * rows : (m + 1) * rows]

    @pl.loop(q_groups, groups)
    def _(b):
        made = make(b)
        for m in range(micros):
            kv_ref[m, :, pl.ds(pl.multiple_of((b - q_groups) * BC, BC), BC)] = made[
                m * rows : (m + 1) * rows
            ]

    wait_bytes(wout_ref, out_sems.at[0])
    wait_bytes(win_ref, out_sems.at[1])


def project(pieces, arrays, chips, members, slots, order, me, x, gains):
    micros, rows, width = x.shape
    in_width = (HEADS + 2 * KVH) * HD
    out_width = HEADS * HD
    return call(
        functools.partial(
            project_kernel, pieces, chips, members, slots, (in_width + out_width) // BC
        ),
        (
            shaped((micros * rows, width), low_type),
            shaped((micros, rows, HEADS * HD), low_type),
            shaped((micros, rows, 2 * KVH * HD), low_type),
            shaped((width, in_width), low_type),
            shaped((width, out_width), low_type),
        ),
        [in_smem, in_smem, in_vmem, in_vmem] + [in_any] * len(arrays),
        (in_vmem, in_vmem, in_vmem, in_any, in_any),
        [
            pltpu.VMEM((width, in_width), low_type),
            pltpu.SemaphoreType.DMA((in_width // BC,)),
            pltpu.SemaphoreType.DMA((2,)),
        ],
        2 * micros * rows * width * in_width,
        2 * width * in_width * 2,
    )(order, me, x, gains, *arrays)


def load_keys(parts, held, sem):
    start = 0
    for part in parts:
        count = part.shape[0]
        pltpu.make_async_copy(part, held.at[pl.ds(start, count)], sem).start()
        start += count


def attend_kernel(count, q_ref, rpos_ref, kpos_ref, x_ref, gain_ref, w_ref, *refs):
    parts = refs[:count]
    ob_ref, log_ref, x2_ref, h2_ref, bias, kv_ref, held, sems = refs[count:]
    rows = q_ref.shape[0]
    load_keys(parts, kv_ref, sems.at[0])
    pltpu.make_async_copy(w_ref, held, sems.at[1]).start()
    bias[...] = jnp.where(kpos_ref[...] <= rpos_ref[...], 0.0, masked_score)
    log_ref[...] = jnp.zeros_like(log_ref)
    length = kv_ref.shape[0]
    wait_bytes(kv_ref, sems.at[0])

    @pl.loop(0, KVH // 2)
    def _(pair):
        lane = pl.multiple_of(pair * LANES, LANES)
        keys = kv_ref[:, pl.ds(lane, LANES)]
        values = kv_ref[:, pl.ds(pl.multiple_of(lane + KVH * HD, LANES), LANES)]
        stacked = stack_heads(q_ref, pair, HD**-0.5)
        mixed = []
        for part in range(2):
            scores = dot(stacked[part].astype(low_type), keys, NT)
            scores = (scores.reshape(3, rows, length) + bias[...][None]).reshape(3 * rows, length)
            largest = jnp.max(scores, axis=-1, keepdims=True)
            raised = jnp.exp(scores - largest)
            summed = jnp.sum(raised, axis=-1, keepdims=True)
            mixed.append(dot(raised.astype(low_type), values) / summed)
            log_ref[...] = jnp.where(
                lane_ids(log_ref.shape) == 2 * pair + part, largest + jnp.log(summed), log_ref[...]
            )
        unstack_heads(ob_ref, pair, mixed[0], mixed[1])

    wait_bytes(held, sems.at[1])
    for n in range(held.shape[0] // BC):
        cut = slice(n * BC, (n + 1) * BC)
        x2_ref[:, cut] = x_ref[:, cut] + dot(ob_ref[...], held[cut, :], NT)
    h2_ref[...] = unit_rows(x2_ref[...], gain_ref[1:2])[0].astype(low_type)


def attend(q, kv_parts, rows_pos, key_pos, x, gains, w):
    rows, width = q.shape
    length = key_pos.shape[1]
    model = x.shape[1]
    return call(
        functools.partial(attend_kernel, len(kv_parts)),
        (
            shaped((rows, width), low_type),
            shaped((3 * rows, LANES), jnp.float32),
            shaped((rows, model), jnp.float32),
            shaped((rows, model), low_type),
        ),
        [in_vmem] * 5 + [in_any] * (1 + len(kv_parts)),
        (in_vmem,) * 4,
        [
            pltpu.VMEM((rows, length), jnp.float32),
            pltpu.VMEM((length, kv_parts[0].shape[1]), low_type),
            pltpu.VMEM((model, width), low_type),
            pltpu.SemaphoreType.DMA((2,)),
        ],
        16 * rows * length * width,
        8 * MIB,
    )(q, rows_pos, key_pos, x, gains, w, *kv_parts)


def router_parts(h2, router, experts):
    logits = dot(h2, router)
    logits = jnp.where(lane_ids(logits.shape) < experts, logits, masked_score)
    raised = jnp.exp(logits - jnp.max(logits, axis=-1, keepdims=True))
    return raised / jnp.sum(raised, axis=-1, keepdims=True)


def expert_kernel(sources, micro, order_ref, me_ref, router_ref, *refs):
    h_parts = refs[:sources]
    c_parts = refs[sources : 2 * sources]
    w_ref = refs[2 * sources]
    outs = refs[2 * sources + 1 :]
    back_refs = outs[:sources]
    out_refs = outs[sources : 2 * sources]
    z_ref, dg_ref, du_ref, dy_ref, xs_ref = outs[2 * sources : 2 * sources + 5]
    cs, held, chance, load_sem, w_sems = outs[2 * sources + 5 :]
    rows, width = h_parts[0].shape
    row_groups = width // BR
    col_groups = FF // BC
    for j in range(sources):
        pltpu.make_async_copy(h_parts[j], xs_ref.at[pl.ds(j * rows, rows)], load_sem.at[0]).start()
        pltpu.make_async_copy(
            c_parts[j].at[pl.ds(micro * rows, rows)], cs.at[pl.ds(j * rows, rows)], load_sem.at[1]
        ).start()
    for k in (0, 1, 2):

        @pl.loop(0, row_groups)
        def _(a):
            for b in range(col_groups):
                pltpu.make_async_copy(
                    w_ref.at[order_ref[(k * row_groups + a) * col_groups + b]],
                    held.at[k, pl.ds(pl.multiple_of(a * BR, 64), BR), pl.ds(b * BC, BC)],
                    w_sems.at[k],
                ).start()

    wait_bytes(xs_ref, load_sem.at[0])
    wait_bytes(cs, load_sem.at[1])
    me = me_ref[1]
    probs = router_parts(xs_ref[...], router_ref[...], sources)
    hits = cs[:, width:].astype(jnp.float32)
    mine = lane_ids(hits.shape) == me
    hit = jnp.sum(jnp.where(mine, hits, 0.0), axis=-1, keepdims=True)
    weight = jnp.sum(jnp.where(mine, probs, 0.0), axis=-1, keepdims=True) * hit
    dy_ref[...] = (weight * cs[:, :width].astype(jnp.float32)).astype(low_type)
    chance[...] = jnp.zeros_like(chance)
    for k in (0, 1, 2):
        wait_bytes(held.at[k], w_sems.at[k])

    @pl.loop(0, col_groups)
    def _(b):
        cut = pl.ds(pl.multiple_of(b * BC, BC), BC)
        gate = dot(xs_ref[...], held[0, :, cut])
        up = dot(xs_ref[...], held[1, :, cut])
        down = dot(cs[:, :width], held[2, :, cut])
        sig = jax.nn.sigmoid(gate)
        act = gate * sig
        hidden = act * up
        z_ref[:, cut] = hidden.astype(low_type)
        chance[...] += jnp.sum(down * hidden, axis=-1, keepdims=True)
        down = down * weight
        dg_ref[:, cut] = (down * up * sig * (1.0 + gate * (1.0 - sig))).astype(low_type)
        du_ref[:, cut] = (down * act).astype(low_type)

    for n in range(width // BC):
        cut = slice(n * BC, (n + 1) * BC)
        back = dot(dg_ref[...], held[0, cut, :], NT) + dot(du_ref[...], held[1, cut, :], NT)
        for j in range(sources):
            back_refs[j][:, cut] = back[j * rows : (j + 1) * rows].astype(low_type)
    told = chance[...] * hit
    high_part = told.astype(low_type)
    low_part = (told - high_part.astype(jnp.float32)).astype(low_type)
    lanes = lane_ids((sources * rows, LANES))
    tail = jnp.where(lanes == 0, high_part, jnp.where(lanes == 1, low_part, jnp.zeros_like(low_part)))
    for j in range(sources):
        back_refs[j][:, width:] = tail[j * rows : (j + 1) * rows]
    for n in range(width // BC):
        cut = slice(n * BC, (n + 1) * BC)
        made = dot(z_ref[...], held[2, cut, :], NT) * weight
        for j in range(sources):
            out_refs[j][:, cut] = made[j * rows : (j + 1) * rows].astype(low_type)


def run_expert(micro, order, me, router, h_parts, c_parts, w):
    sources = len(h_parts)
    rows, width = h_parts[0].shape
    total = sources * rows
    return call(
        functools.partial(expert_kernel, sources, micro),
        tuple(
            [shaped((rows, width + LANES), low_type)] * sources
            + [shaped((rows, width), low_type)] * sources
            + [shaped((total, FF), low_type)] * 3
            + [shaped((total, width), low_type)] * 2
        ),
        [in_smem, in_smem, in_vmem] + [in_any] * (2 * sources + 1),
        tuple([in_vmem] * (2 * sources + 5)),
        [
            pltpu.VMEM((total, width + LANES), low_type),
            pltpu.VMEM((3, width, FF), low_type),
            pltpu.VMEM((total, 1), jnp.float32),
            pltpu.SemaphoreType.DMA((2,)),
            pltpu.SemaphoreType.DMA((3,)),
        ],
        12 * total * width * FF,
        20 * MIB,
    )(order, me, router, *h_parts, *c_parts, w)


def outer_kernel(place, pairs, order_ref, *refs):
    count = len(pairs)
    micros = len(refs[:-3]) // (2 * count)
    lefts = refs[: count * micros]
    rights = refs[count * micros : 2 * count * micros]
    out_ref, stage, sems = refs[-3:]
    span = 2 * BR
    steps = []
    for k in range(count):
        for p in range(lefts[k * micros].shape[-1] // span):
            steps.append((k, p))

    def wait_stage(slot, cols):
        wait_bytes(stage.at[slot, :, pl.ds(0, cols)], sems.at[slot])

    used = [None, None]
    for n, (k, p) in enumerate(steps):
        slot = n % 2
        cols = rights[k * micros].shape[-1]
        if used[slot] is not None:
            wait_stage(slot, used[slot])
        used[slot] = cols
        cut = slice(p * span, (p + 1) * span)
        for c in range(0, cols, 512):
            part = slice(c, c + 512)
            made = sum(
                dot(lefts[k * micros + m][:, cut], rights[k * micros + m][:, part], TN)
                for m in range(micros)
            )
            stage[slot, :, part] = made.astype(low_type)
        first, row_step = place(k)
        for half in range(2):
            for b in range(cols // BC):
                pltpu.make_async_copy(
                    stage.at[slot, pl.ds(half * BR, BR), pl.ds(b * BC, BC)],
                    out_ref.at[order_ref[first + (2 * p + half) * row_step + b]],
                    sems.at[slot],
                ).start()
    for slot in range(2):
        if used[slot] is not None:
            wait_stage(slot, used[slot])


def outer_blocks(order, place, lefts, rights, blocks):
    pairs = [(l[0].shape[-1], r[0].shape[-1]) for l, r in zip(lefts, rights)]
    widest = max(r for _, r in pairs)
    rows = sum(l.shape[0] for l in lefts[0])
    flat = [l for group in lefts for l in group] + [r for group in rights for r in group]
    return call(
        functools.partial(outer_kernel, place, pairs),
        shaped((blocks, BR, BC), low_type),
        [in_smem] + [in_vmem] * len(flat),
        in_any,
        [pltpu.VMEM((2, 2 * BR, widest), low_type), pltpu.SemaphoreType.DMA((2,))],
        2 * rows * blocks * BR * BC,
        blocks * BR * BC * 2 + sum(f.size * 2 for f in flat),
    )(order, *flat)


def xor_plan(members, offset):
    if members != 4:
        return list(range(1, members)), [0]
    first = 1 if offset % 2 else 2
    return [first, 3], [0, 3 - first]


def slots_kernel(
    counts, chips, members, slots, all_groups, in_groups, order_ref, me_ref, *refs
):
    lists = []
    for count in counts:
        lists.append(refs[:count])
        refs = refs[count:]
    outs = refs[: 2 * chips]
    lefts, turned, rights, sems = refs[2 * chips :]
    ctx, shard = me_ref[0], me_ref[1]
    chip, core = lax.div(ctx, 2), lax.rem(ctx, 2)
    h_width = lefts.shape[2]
    q_width = lists[2][0].shape[1]
    kv_width = lists[3][0].shape[1]
    total = rights.shape[0]
    targets = (
        (lefts.at[0], 0, h_width, 0),
        (lefts.at[1], 0, h_width, 1),
        (rights, 0, q_width, 2),
        (rights, q_width, kv_width, 2),
        (rights, q_width + kv_width, q_width, 2),
    )
    for group, (target, lane, lanes, sem) in zip(lists, targets):
        start = 0
        for ref in group:
            pltpu.make_async_copy(
                ref, target.at[pl.ds(start, ref.shape[0]), pl.ds(lane, lanes)], sems.at[sem]
            ).start()
            start += ref.shape[0]
    for side in range(2):
        wait_bytes(lefts.at[side], sems.at[side])
        for r in range(0, total, LANES):
            turned[side, :, r : r + LANES] = lefts[side, r : r + LANES, :].T
    wait_bytes(rights, sems.at[2])
    for offset in range(chips):
        there = lax.rem(chip - offset + chips, chips) * 2 + core
        for out, hops in zip(outs[2 * offset : 2 * offset + 2], xor_plan(members, offset)):
            for place, hop in enumerate(hops):
                base = (there * members + jnp.bitwise_xor(shard, hop)) * slots

                @pl.loop(0, slots)
                def _(i):
                    number = order_ref[base + i]
                    a, b = lax.div(number, all_groups), lax.rem(number, all_groups)
                    side = (b >= in_groups).astype(jnp.int32)
                    out[place * slots + i] = dot(
                        turned[side, pl.ds(pl.multiple_of(a * BR, 64), BR), :],
                        rights[:, pl.ds(pl.multiple_of(b * BC, BC), BC)],
                    ).astype(low_type)


def slot_blocks(chips, members, slots, order, me, h1, da, dq, dkv, ob):
    lists = (h1, da, dq, dkv, ob)
    total = sum(part.shape[0] for part in h1)
    width = h1[0].shape[1]
    in_width = dq[0].shape[1] + dkv[0].shape[1]
    all_width = in_width + ob[0].shape[1]
    outs = []
    for offset in range(chips):
        for hops in xor_plan(members, offset):
            outs.append(shaped((len(hops) * slots, BR, BC), low_type))
    made = call(
        functools.partial(
            slots_kernel,
            tuple(len(group) for group in lists),
            chips,
            members,
            slots,
            all_width // BC,
            in_width // BC,
        ),
        tuple(outs),
        [in_smem, in_smem] + [in_any] * sum(len(group) for group in lists),
        (in_vmem,) * len(outs),
        [
            pltpu.VMEM((2, total, width), low_type),
            pltpu.VMEM((2, width, total), low_type),
            pltpu.VMEM((total, all_width), low_type),
            pltpu.SemaphoreType.DMA((3,)),
        ],
        2 * total * chips * members * slots * BR * BC,
        16 * MIB,
    )(order, me, *[part for group in lists for part in group])
    return [(made[2 * offset], made[2 * offset + 1]) for offset in range(chips)]


def merge_kernel(
    sources, me_ref, x2_ref, cot_ref, h2_ref, gain_ref, router_ref, w_ref, *refs
):
    back_refs = refs[:sources]
    dx_ref, da_ref, do_ref, stat_ref, held, sem = refs[sources:]
    rows, width = x2_ref.shape
    pltpu.make_async_copy(w_ref, held, sem).start()
    lanes = lane_ids((rows, LANES))
    prob_grad = jnp.zeros((rows, LANES), jnp.float32)
    gathered = jnp.zeros((rows, width), jnp.float32)
    for j in range(sources):
        tail = back_refs[j][:, width:].astype(jnp.float32)
        told = jnp.sum(tail, axis=-1, keepdims=True)
        expert = jnp.bitwise_xor(me_ref[1], j)
        prob_grad = prob_grad + jnp.where(lanes == expert, told, 0.0)
        gathered = gathered + back_refs[j][:, :width].astype(jnp.float32)
    h2 = h2_ref[...]
    probs = router_parts(h2, router_ref[...], sources)
    logit_grad = probs * (prob_grad - jnp.sum(probs * prob_grad, axis=-1, keepdims=True))
    high_part = logit_grad.astype(low_type)
    low_part = (logit_grad - high_part.astype(jnp.float32)).astype(low_type)
    router_grad = dot(high_part, h2, TN) + dot(low_part, h2, TN)
    gathered = gathered + dot(high_part, router_ref[...], NT) + dot(low_part, router_ref[...], NT)
    x2 = x2_ref[...]
    inverse = lax.rsqrt(jnp.mean(x2 * x2, axis=-1, keepdims=True) + norm_eps)
    moe_grad, gain_grad = unit_back(x2, gain_ref[1:2], inverse, gathered)
    after = cot_ref[...] + moe_grad
    dx_ref[...] = after
    da_ref[...] = after.astype(low_type)
    experts_up = stat_ref.shape[0] - 8
    stat_ref[:experts_up] = router_grad[:experts_up]
    stat_ref[experts_up:] = jnp.broadcast_to(gain_grad, (8, width))
    wait_bytes(held, sem)
    for n in range(held.shape[1] // BC):
        cut = slice(n * BC, (n + 1) * BC)
        do_ref[:, cut] = dot(da_ref[...], held[:, cut]).astype(low_type)


def merge(me, x2, cot, h2, gains, router, w, backs):
    rows, width = x2.shape
    sources = len(backs)
    experts_up = -(-sources // 8) * 8
    return call(
        functools.partial(merge_kernel, sources),
        (
            shaped((rows, width), jnp.float32),
            shaped((rows, width), low_type),
            shaped((rows, HEADS * HD), low_type),
            shaped((experts_up + 8, width), jnp.float32),
        ),
        [in_smem] + [in_vmem] * 5 + [in_any] + [in_vmem] * sources,
        (in_vmem,) * 4,
        [pltpu.VMEM((width, HEADS * HD), low_type), pltpu.SemaphoreType.DMA],
        2 * rows * width * HEADS * HD,
        10 * MIB,
    )(me, x2, cot, h2, gains, router, w, *backs)


def attend_back_kernel(count, q_ref, rpos_ref, kpos_ref, ob_ref, log_ref, do_ref, *refs):
    parts = refs[:count]
    dq_ref, own_ref, other_ref, bias, kv_ref, sem = refs[count:]
    rows = q_ref.shape[0]
    load_keys(parts, kv_ref, sem)
    length = kv_ref.shape[0]
    bias[...] = jnp.where(kpos_ref[...] <= rpos_ref[...], 0.0, masked_score)
    wait_bytes(kv_ref, sem)

    @pl.loop(0, KVH // 2)
    def _(pair):
        lane = pl.multiple_of(pair * LANES, LANES)
        value_lane = pl.multiple_of(lane + KVH * HD, LANES)
        keys = kv_ref[:, pl.ds(lane, LANES)]
        values = kv_ref[:, pl.ds(value_lane, LANES)]
        queries = stack_heads(q_ref, pair, HD**-0.5)
        grads = stack_heads(do_ref, pair)
        mixes = stack_heads(ob_ref, pair)
        query_grads = []
        key_grad = value_grad = None
        for part in range(2):
            query = queries[part].astype(low_type)
            grad = grads[part].astype(low_type)
            log_total = jnp.sum(
                jnp.where(lane_ids(log_ref.shape) == 2 * pair + part, log_ref[...], 0.0),
                axis=-1,
                keepdims=True,
            )
            delta = jnp.sum(grads[part] * mixes[part], axis=-1, keepdims=True)
            scores = dot(query, keys, NT)
            scores = (scores.reshape(3, rows, length) + bias[...][None]).reshape(3 * rows, length)
            chance = jnp.exp(scores - log_total)
            prob_grad = dot(grad, values, NT)
            score_grad = (chance * (prob_grad - delta)).astype(low_type)
            value_term = dot(chance.astype(low_type), grad, TN)
            key_term = dot(score_grad, query, TN)
            key_grad = key_term if part == 0 else key_grad + key_term
            value_grad = value_term if part == 0 else value_grad + value_term
            query_grads.append(dot(score_grad, keys) * HD**-0.5)
        unstack_heads(dq_ref, pair, query_grads[0], query_grads[1])
        half = length // 2
        for ref, cut in ((own_ref, slice(0, half)), (other_ref, slice(half, length))):
            ref[:, pl.ds(lane, LANES)] = key_grad[cut].astype(low_type)
            ref[:, pl.ds(value_lane, LANES)] = value_grad[cut].astype(low_type)


def attend_back(q, kv_parts, rows_pos, key_pos, ob, log_total, do):
    rows, width = q.shape
    length = key_pos.shape[1]
    kv_width = kv_parts[0].shape[1]
    return call(
        functools.partial(attend_back_kernel, len(kv_parts)),
        (shaped((rows, width), low_type),) + (shaped((length // 2, kv_width), low_type),) * 2,
        [in_vmem] * 6 + [in_any] * len(kv_parts),
        (in_vmem,) * 3,
        [
            pltpu.VMEM((rows, length), jnp.float32),
            pltpu.VMEM((length, kv_width), low_type),
            pltpu.SemaphoreType.DMA,
        ],
        40 * rows * length * width,
        8 * MIB,
    )(q, rows_pos, key_pos, ob, log_total, do, *kv_parts)


def query_back_kernel(w_ref, *refs):
    micros = (len(refs) - 3) // 2
    dq_refs, out_refs = refs[:micros], refs[micros : 2 * micros]
    rows_ref, held, sem = refs[2 * micros :]
    rows = dq_refs[0].shape[0]
    copy = pltpu.make_async_copy(w_ref.at[:, pl.ds(0, held.shape[1])], held, sem)
    copy.start()
    for m in range(micros):
        rows_ref[m * rows : (m + 1) * rows] = dq_refs[m][...]
    copy.wait()
    for n in range(held.shape[0] // BC):
        cut = slice(n * BC, (n + 1) * BC)
        made = dot(rows_ref[...], held[cut, :], NT)
        for m in range(micros):
            out_refs[m][:, cut] = made[m * rows : (m + 1) * rows]


def query_back(w, dqs):
    micros = len(dqs)
    rows, q_width = dqs[0].shape
    width = w.shape[0]
    return call(
        query_back_kernel,
        tuple([shaped((rows, width), jnp.float32)] * micros),
        [in_any] + [in_vmem] * micros,
        tuple([in_vmem] * micros),
        [
            pltpu.VMEM((micros * rows, q_width), low_type),
            pltpu.VMEM((width, q_width), low_type),
            pltpu.SemaphoreType.DMA,
        ],
        2 * micros * rows * width * q_width,
        7 * MIB,
    )(w, *dqs)


def input_kernel(x_ref, gain_ref, w_ref, *refs):
    micros, rows = x_ref.shape[:2]
    dx_refs = refs[:micros]
    part_refs = refs[micros : 2 * micros]
    dkv_refs = refs[2 * micros : 3 * micros]
    out_ref, stat_ref, rows_ref, grad, held, sem = refs[3 * micros :]
    kv_width = held.shape[1]
    copy = pltpu.make_async_copy(
        w_ref.at[:, pl.ds(w_ref.shape[1] - kv_width, kv_width)], held, sem
    )
    copy.start()
    for m in range(micros):
        rows_ref[m * rows : (m + 1) * rows] = dkv_refs[m][...]
    copy.wait()
    for n in range(held.shape[0] // BC):
        cut = slice(n * BC, (n + 1) * BC)
        made = dot(rows_ref[...], held[cut, :], NT)
        for m in range(micros):
            grad[m, :, cut] = part_refs[m][:, cut] + made[m * rows : (m + 1) * rows]
    total = jnp.zeros((1, x_ref.shape[-1]), jnp.float32)
    for m in range(micros):
        x = x_ref[m]
        inverse = lax.rsqrt(jnp.mean(x * x, axis=-1, keepdims=True) + norm_eps)
        term, gain_grad = unit_back(x, gain_ref[0:1], inverse, grad[m])
        out_ref[m] = dx_refs[m][...] + term
        total = total + gain_grad
    stat_ref[...] = jnp.broadcast_to(total, stat_ref.shape)


def input_back(x, gains, w, dxs, parts, dkvs):
    micros, rows, width = x.shape
    kv_width = dkvs[0].shape[1]
    return call(
        input_kernel,
        (shaped(x.shape, jnp.float32), shaped((8, width), jnp.float32)),
        [in_vmem, in_vmem, in_any] + [in_vmem] * (3 * micros),
        (in_vmem,) * 2,
        [
            pltpu.VMEM((micros * rows, kv_width), low_type),
            pltpu.VMEM(x.shape, jnp.float32),
            pltpu.VMEM((width, kv_width), low_type),
            pltpu.SemaphoreType.DMA,
        ],
        2 * micros * rows * width * kv_width,
        14 * MIB,
    )(x, gains, w, *dxs, *parts, *dkvs)


def rotate_kernel(
    b_ref, g_ref, m_ref, s_ref, l_ref, r_ref, grad_ref, new_ref, moment_ref, second_ref
):
    gradient = g_ref[0].astype(jnp.float32)
    grad_ref[0] = gradient
    left = l_ref[0].astype(low_type)
    right = r_ref[0].astype(low_type)
    rotated = dot(dot(left, gradient.astype(low_type), TN).astype(low_type), right)
    moment = beta_one * m_ref[0] + (1.0 - beta_one) * rotated
    second = beta_two * s_ref[0] + (1.0 - beta_two) * rotated * rotated
    moment_ref[0] = moment
    second_ref[0] = second
    direction = (moment / (jnp.sqrt(second) + adam_eps)).astype(low_type)
    turned = dot(dot(left, direction).astype(low_type), right, NT)
    new_ref[0] = b_ref[0] - rate * turned


def rotate(weight, gradient, moment, second, left, right):
    count = weight.shape[0]

    def spec(rows, cols):
        return pl.BlockSpec((1, rows, cols), lambda i: (i, 0, 0))

    block = spec(BR, BC)
    return pl.pallas_call(
        rotate_kernel,
        grid=(count,),
        out_shape=(shaped(weight.shape, jnp.float32),) * 4,
        in_specs=[block] * 4 + [spec(BR, BR), spec(BC, BC)],
        out_specs=(block,) * 4,
        compiler_params=pltpu.CompilerParams(vmem_limit_bytes=VMEM_LIMIT),
        cost_estimate=pl.CostEstimate(
            flops=4 * count * BR * BC * (BR + BC),
            bytes_accessed=count * 2 * MIB,
            transcendentals=0,
        ),
    )(weight, gradient, moment, second, left, right)


def adam(weight, gradient, moment, second, step_rate):
    moment_new = beta_one * moment + (1.0 - beta_one) * gradient
    second_new = beta_two * second + (1.0 - beta_two) * gradient * gradient
    return (
        weight - step_rate * moment_new / (jnp.sqrt(second_new) + adam_eps),
        moment_new,
        second_new,
    )


def to_partner(array, offset):
    if offset == 0:
        return array
    count = lax.axis_size("shard")
    return lax.ppermute(array, "shard", [(i, i ^ offset) for i in range(count)])


def to_ctx(array, offset):
    count = lax.axis_size("ctx")
    return lax.ppermute(array, "ctx", [(i, i ^ offset) for i in range(count)])


def to_chip(array, offset):
    count = lax.axis_size("ctx")
    return lax.ppermute(array, "ctx", [(i, (i + 2 * offset) % count) for i in range(count)])


def after(value, *others):
    return lax.optimization_barrier((value, others))[0]


def from_chips(array, chips):
    return [array] + [to_chip(array, offset) for offset in range(1, chips)]


def wide(array):
    return array.astype(jnp.float32)


def sum_to_chips(parts):
    total = wide(parts[0])
    for offset in range(1, len(parts)):
        total = total + wide(to_chip(parts[offset], -offset))
    return total


def gather_weights(blocks, chips, members):
    parts = from_chips(blocks, chips)
    pieces, arrays = [], []

    def add(array, offset, first, cut):
        pieces.append((0, offset, first, cut))
        arrays.append(array)
        pieces.append((1, offset, first, cut))
        arrays.append(to_ctx(array, 1))
        return array

    add(blocks, 0, 0, 0)
    for offset in range(1, members):
        add(to_partner(blocks, offset), offset, 0, 0)
    near = list(arrays)
    if chips > 1:
        far = after(jnp.concatenate(parts[1:], axis=0), *near)
        add(far, 0, 1, 0)
        if members == 4:
            by_one = add(to_partner(far, 1), 1, 1, 0)
            by_two = add(to_partner(far, 2), 2, 1, 0)
            half = BR // 2
            add(to_partner(by_one[:, :half], 2), 3, 1, 0)
            add(to_partner(by_two[:, half:], 1), 3, 1, half)
        else:
            for offset in range(1, members):
                add(to_partner(far, offset), offset, 1, 0)
    return near + parts[1:], pieces, arrays


def sum_slots(made, chips, members, slots):
    sums, first_got = [], []
    for offset in range(chips):
        sent, kept = made[offset]
        hops, keeps = xor_plan(members, offset)
        total = wide(kept[:slots])
        if members == 4:
            first, second = hops[0], keeps[1]
            got = to_partner(sent, first)
            total = total + wide(got[:slots])
            relay = (wide(kept[slots:]) + wide(got[slots:])).astype(low_type)
            total = total + wide(to_partner(relay, second))
        else:
            for place, hop in enumerate(hops):
                got = to_partner(sent[place * slots : (place + 1) * slots], hop)
                total = total + wide(got)
        sums.append(total if offset == 0 else total.astype(low_type))
        first_got.append(got)
    return sums, first_got


def sum_all(array):
    step = 1
    while step < lax.axis_size("ctx"):
        array = array + to_ctx(array, step)
        step *= 2
    step = 1
    while step < lax.axis_size("shard"):
        array = array + to_partner(array, step)
        step *= 2
    return array


def shards(
    tokens,
    cotangent,
    norm_gains,
    router,
    dense_weight,
    expert_weight,
    routes,
    assign,
    dense_order,
    expert_order,
    dense_moment,
    dense_second,
    dense_left,
    dense_right,
    expert_moment,
    expert_second,
    expert_left,
    expert_right,
    gains_moment,
    gains_second,
    router_moment,
    router_second,
):
    ctx_count = lax.axis_size("ctx")
    shard_count = lax.axis_size("shard")
    chips = ctx_count // 2
    micros, rows, width = tokens.shape
    slots = dense_weight.shape[0]
    span = rows // 2
    row_groups = width // BR
    ff_groups = FF // BC
    expert_blocks = 3 * row_groups * ff_groups

    expert_inverse = inverse_order(expert_order)
    ctx = lax.axis_index("ctx").astype(jnp.int32)
    me = jnp.stack([ctx, lax.axis_index("shard").astype(jnp.int32)])
    row_ids = jnp.arange(rows, dtype=jnp.int32)
    all_pos = assign[:, row_ids // span] * span + row_ids % span
    ring_ids = (ctx // 2 - jnp.arange(chips, dtype=jnp.int32)) % chips * 2
    key_ids = jnp.concatenate([ring_ids + ctx % 2, ring_ids + (1 - ctx % 2)])
    key_pos = all_pos[key_ids].reshape(1, rows * ctx_count)
    rows_pos = all_pos[ctx].reshape(rows, 1)
    router_pad = jnp.pad(router.astype(low_type), ((0, 0), (0, LANES - shard_count)))

    far, pieces, arrays = gather_weights(dense_weight.astype(low_type), chips, shard_count)
    expert_low = after(expert_weight[0].astype(low_type), *far)
    expert_all = lax.all_gather(expert_low, "ctx", axis=0, tiled=True)

    lanes = jnp.arange(LANES, dtype=jnp.int32)
    hits = jnp.sum((routes[..., None] == lanes).astype(low_type), axis=2)
    cot_rows = jnp.concatenate([cotangent.astype(low_type), hits], axis=2)
    cot_rows = cot_rows.reshape(micros * rows, width + LANES)
    cot_rows = after(cot_rows, *arrays[::2])
    cot_parts = [to_partner(cot_rows, j) for j in range(shard_count)]

    h1, q, kv, w_in, w_out = project(
        pieces, arrays, chips, shard_count, slots, dense_order, me, tokens, norm_gains
    )
    h1_other = to_ctx(h1, 1)
    kvs, obs, logs, x2s, h2s = [], [], [], [], []
    chip_kv = []
    for m in range(micros):
        own = kv[m] if m == 0 else after(kv[m], chip_kv[m - 1][1 % chips])
        chip_kv.append(from_chips(own, chips))
    for m in range(micros):
        query = q[m] if m == 0 else after(q[m], obs[m - 1])
        parts = chip_kv[m]
        swapped = parts if m == 0 else after(parts, obs[m - 1])
        kvs.append(parts + [to_ctx(part, 1) for part in swapped])
        ob, log_total, x2, h2 = attend(
            query, kvs[m], rows_pos, key_pos, tokens[m], norm_gains, w_out
        )
        obs.append(ob)
        logs.append(log_total)
        x2s.append(x2)
        h2s.append(h2)
    ob_others = [to_ctx(ob, 1) for ob in obs]

    h_parts = []
    for m in range(micros):
        own = after(h2s[m], *(cot_parts if m == 0 else h_parts[m - 1]))
        h_parts.append([own] + [to_partner(own, j) for j in range(1, shard_count)])
    outs, sent = [], []
    zs, dgs, dus, dys, xs = [], [], [], [], []
    for m in range(micros):
        here = after(me, h2s[-1], h1_other, *ob_others) if m == 0 else after(me, zs[-1])
        made = run_expert(m, expert_inverse, here, router_pad, h_parts[m], cot_parts, expert_all)
        sent.append(made[:shard_count])
        outs.append(made[shard_count : 2 * shard_count])
        z, dg, du, dy, x = made[2 * shard_count :]
        zs.append(z)
        dgs.append(dg)
        dus.append(du)
        dys.append(dy)
        xs.append(x)
    backs = [[to_partner(sent[m][j], j) for j in range(shard_count)] for m in range(micros)]
    arrived = []
    for m in range(micros):
        own = [after(part, *(arrived[-1] if arrived else backs[-1])) for part in outs[m]]
        arrived.append([to_partner(own[j], j) for j in range(shard_count)])

    dxs, das, dqs, stats, own_grads, far_grads = [], [], [], [], [], []
    for m in range(micros):
        here = after(me, zs[-1] if m == 0 else dqs[-1])
        dx, da, do, stat = merge(
            here, x2s[m], cotangent[m], h2s[m], norm_gains, router_pad, w_out, backs[m]
        )
        dq, dkv_own, dkv_other = attend_back(
            q[m], kvs[m], rows_pos, key_pos, obs[m], logs[m], do
        )
        got = to_ctx(dkv_other, 1)
        parts = []
        for o in range(chips):
            cut = slice(o * rows, (o + 1) * rows)
            part = wide(dkv_own[cut]) + wide(got[cut])
            parts.append(part if o == 0 else part.astype(low_type))
        own_grads.append(parts[0])
        far_grads.append(parts[1:])
        dxs.append(dx)
        das.append(da)
        dqs.append(dq)
        stats.append(stat)

    dkvs = [
        sum_to_chips([own_grads[m]] + far_grads[m]).astype(low_type) for m in range(micros)
    ]

    def other_core(parts):
        return [to_ctx(part, 1) for part in parts]

    da_others, dq_others = other_core(das), other_core(dqs)
    expert_term = outer_blocks(
        after(expert_inverse, dqs[-1], dkvs[0], arrived[0]),
        lambda k: (k * row_groups * ff_groups, ff_groups),
        [xs, xs, dys],
        [dgs, dus, zs],
        expert_blocks,
    )
    parts_back = query_back(after(w_in, expert_term), dqs)
    expert_sum = lax.psum_scatter(
        after(expert_term, dkvs[-1]), "ctx", scatter_dimension=0, tiled=True
    )
    here = after(me, arrived[-1], parts_back)
    made = slot_blocks(
        chips,
        shard_count,
        slots,
        dense_order,
        here,
        [h1, h1_other],
        das + da_others,
        dqs + dq_others,
        dkvs + other_core(dkvs),
        obs + ob_others,
    )
    sums, got = sum_slots(made, chips, shard_count, slots)
    dense_sum = sum_to_chips(sums)
    input_grad, gain_stat = input_back(
        after(tokens, *got[:2]), norm_gains, w_in, dxs, parts_back, dkvs
    )
    experts_up = stats[0].shape[0] - 8
    stat_rows = jnp.concatenate([sum(stats)[: experts_up + 1], gain_stat[:7]], axis=0)
    stat_rows = sum_all(stat_rows)
    router_grad = stat_rows[:shard_count].T
    gains_grad = jnp.stack([stat_rows[experts_up + 1], stat_rows[experts_up]])

    outputs = []
    for m in range(micros):
        total = x2s[m]
        for j in range(shard_count):
            total = total + wide(arrived[m][j])
        outputs.append(total)

    expert_grad, expert_new, expert_moment_new, expert_second_new = rotate(
        expert_weight[0], after(expert_sum, *sums), expert_moment[0], expert_second[0], expert_left[0], expert_right[0]
    )
    dense_grad, dense_new, dense_moment_new, dense_second_new = rotate(
        dense_weight, after(dense_sum, expert_new), dense_moment, dense_second, dense_left, dense_right
    )
    gains_new, gains_moment_new, gains_second_new = adam(
        norm_gains, gains_grad, gains_moment, gains_second, gain_rate
    )
    router_new, router_moment_new, router_second_new = adam(
        router, router_grad, router_moment, router_second, rate
    )
    return (
        jnp.stack(outputs),
        input_grad,
        dense_grad,
        dense_new,
        dense_moment_new,
        dense_second_new,
        expert_grad[None],
        expert_new[None],
        expert_moment_new[None],
        expert_second_new[None],
        gains_grad,
        gains_new,
        gains_moment_new,
        gains_second_new,
        router_grad,
        router_new,
        router_moment_new,
        router_second_new,
    )


def solution(mesh):
    rows_spec = P("shard", "ctx", None)
    dense_spec = P(("ctx", "shard"), None, None)
    expert_spec = P("shard", "ctx", None, None)
    in_specs = (
        (rows_spec, rows_spec, P(), P(), dense_spec, expert_spec, rows_spec, P(), P(), P())
        + (dense_spec,) * 4
        + (expert_spec,) * 4
        + (P(),) * 4
    )
    out_specs = (rows_spec,) * 2 + (dense_spec,) * 4 + (expert_spec,) * 4 + (P(),) * 8
    return jax.shard_map(shards, mesh=mesh, in_specs=in_specs, out_specs=out_specs, check_vma=False)
```

```python
import functools

import jax
import jax.numpy as jnp
from jax import lax
from jax.experimental import pallas as pl
from jax.experimental.pallas import tpu as pltpu
from jax.sharding import PartitionSpec as P

HEADS = 24
KVH = 8
HD = 64
FF = 1024
BR = 192
BC = 256
LANES = 128

norm_eps = 1e-06
beta_one = 0.9
beta_two = 0.95
rate = 0.01
gain_rate = 0.5
adam_eps = 1e-08
masked_score = -1e30
low_type = jnp.bfloat16
MIB = 1 << 20

NN = (((1,), (0,)), ((), ()))
NT = (((1,), (1,)), ((), ()))
TN = (((0,), (0,)), ((), ()))

in_vmem = pl.BlockSpec(memory_space=pltpu.VMEM)
in_smem = pl.BlockSpec(memory_space=pltpu.SMEM)
in_any = pl.BlockSpec(memory_space=pl.ANY)


def dot(left_side, right_side, dims=NN):
    return lax.dot_general(left_side, right_side, dims, preferred_element_type=jnp.float32)


def call(kernel, out_shapes, in_specs, out_specs, scratch, flops, moved, limit):
    return pl.pallas_call(
        kernel,
        out_shape=out_shapes,
        in_specs=in_specs,
        out_specs=out_specs,
        scratch_shapes=scratch,
        compiler_params=pltpu.CompilerParams(vmem_limit_bytes=limit * MIB),
        cost_estimate=pl.CostEstimate(flops=flops, bytes_accessed=moved, transcendentals=0),
    )


def shaped(dims, kind):
    return jax.ShapeDtypeStruct(dims, kind)


def inverse_order(slot_order):
    count = slot_order.shape[0]
    numbers = jnp.arange(count, dtype=jnp.int32)
    return jnp.sum(
        jnp.where(slot_order[None, :] == numbers[:, None], numbers[None, :], 0), axis=1
    ).astype(jnp.int32)


def wait_bytes(landed, semaphore):
    pltpu.make_async_copy(landed, landed, semaphore).wait()


def unit_rows(rows, gain):
    inverse = lax.rsqrt(jnp.mean(rows * rows, axis=-1, keepdims=True) + norm_eps)
    return rows * inverse * gain, inverse


def unit_back(rows, gain, inverse, gradient):
    unit = rows * inverse
    scaled = gradient * gain
    inner = jnp.mean(scaled * unit, axis=-1, keepdims=True)
    return inverse * (scaled - unit * inner), jnp.sum(gradient * unit, axis=0, keepdims=True)


def lane_ids(dims):
    return lax.broadcasted_iota(jnp.int32, dims, len(dims) - 1)


def half_turn(tile):
    return pltpu.roll(tile, HD, 1)


def stack_heads(ref, pair, scale=None):
    base = pair * (3 * LANES)
    tiles = [
        ref[:, pl.ds(pl.multiple_of(base + LANES * t, LANES), LANES)].astype(jnp.float32)
        for t in range(3)
    ]
    if scale is not None:
        tiles = [t * scale for t in tiles]
    lower = lane_ids(tiles[0].shape) < HD
    first = [tiles[0], half_turn(tiles[0]), tiles[1]]
    second = [tiles[1], half_turn(tiles[2]), tiles[2]]
    return (
        jnp.concatenate([jnp.where(lower, t, 0.0) for t in first], axis=0),
        jnp.concatenate([jnp.where(lower, 0.0, t) for t in second], axis=0),
    )


def unstack_heads(ref, pair, first, second):
    rows = first.shape[0] // 3
    base = pair * (3 * LANES)
    lower = lane_ids((rows, LANES)) < HD
    tiles = (
        jnp.where(lower, first[:rows], half_turn(first[rows : 2 * rows])),
        jnp.where(lower, first[2 * rows :], second[:rows]),
        jnp.where(lower, half_turn(second[rows : 2 * rows]), second[2 * rows :]),
    )
    for t in range(3):
        ref[:, pl.ds(pl.multiple_of(base + LANES * t, LANES), LANES)] = tiles[t].astype(ref.dtype)


def project_kernel(
    pieces, chips, members, slots, all_groups, micros, order_ref, me_ref, *refs
):
    x_refs = refs[:micros]
    gain_ref = refs[micros]
    piece_refs = refs[micros + 1 : micros + 1 + len(pieces)]
    refs = refs[micros + 1 + len(pieces) :]
    h_ref = refs[0]
    kv_refs = refs[1 : 1 + micros]
    win_ref, wout_ref, held, held_out, sems, out_sems = refs[1 + micros :]
    groups = held.shape[1] // BC
    kv_groups = kv_refs[0].shape[-1] // BC
    rows = x_refs[0].shape[0]
    ctx, shard = me_ref[0], me_ref[1]
    chip, core = lax.div(ctx, 2), lax.rem(ctx, 2)

    for ref, (other_core, offset, first, cut) in zip(piece_refs, pieces):

        @pl.loop(0, ref.shape[0])
        def _(i):
            source = lax.rem(chip - (first + lax.div(i, slots)) + chips, chips) * 2
            source = source + jnp.bitwise_xor(core, other_core)
            source = source * members + jnp.bitwise_xor(shard, offset)
            number = order_ref[source * slots + lax.rem(i, slots)]
            a, b = lax.div(number, all_groups), lax.rem(number, all_groups)
            down = pl.ds(pl.multiple_of(a * BR + cut, 32), ref.shape[1])

            @pl.when(b < groups)
            def _():
                across = pl.ds(pl.multiple_of(b * BC, BC), BC)
                pltpu.make_async_copy(ref.at[i], held.at[down, across], sems.at[b]).start()

            @pl.when(b >= groups)
            def _():
                across = pl.ds(pl.multiple_of((b - groups) * BC, BC), BC)
                pltpu.make_async_copy(ref.at[i], held_out.at[down, across], sems.at[groups]).start()

    for m in range(micros):
        h_ref[m * rows : (m + 1) * rows, :] = unit_rows(x_refs[m][...], gain_ref[0:1])[0].astype(
            low_type
        )
    q_groups = groups - kv_groups

    @pl.loop(0, kv_groups)
    def _(b):
        across = pl.ds(pl.multiple_of((q_groups + b) * BC, BC), BC)
        wait_bytes(held.at[:, across], sems.at[q_groups + b])
        made = dot(h_ref[...], held[:, across]).astype(low_type)
        for m in range(micros):
            kv_refs[m][:, pl.ds(pl.multiple_of(b * BC, BC), BC)] = made[m * rows : (m + 1) * rows]

    @pl.loop(0, q_groups)
    def _(b):
        across = pl.ds(pl.multiple_of(b * BC, BC), BC)
        wait_bytes(held.at[:, across], sems.at[b])

    wait_bytes(held_out, sems.at[groups])
    copies = [
        pltpu.make_async_copy(held, win_ref, out_sems.at[0]),
        pltpu.make_async_copy(held_out, wout_ref, out_sems.at[1]),
    ]
    for copy in copies:
        copy.start()
    for copy in copies:
        copy.wait()


def project(pieces, arrays, chips, members, slots, order, me, xs, gains):
    micros = len(xs)
    rows, width = xs[0].shape
    in_width = (HEADS + 2 * KVH) * HD
    out_width = HEADS * HD
    kv_width = 2 * KVH * HD
    made = call(
        functools.partial(
            project_kernel, pieces, chips, members, slots, (in_width + out_width) // BC, micros
        ),
        tuple(
            [shaped((micros * rows, width), low_type)]
            + [shaped((rows, kv_width), low_type)] * micros
            + [shaped((width, in_width), low_type), shaped((width, out_width), low_type)]
        ),
        [in_smem, in_smem] + [in_vmem] * (micros + 1) + [in_any] * len(arrays),
        tuple([in_vmem] * (1 + micros) + [in_any, in_any]),
        [
            pltpu.VMEM((width, in_width), low_type),
            pltpu.VMEM((width, out_width), low_type),
            pltpu.SemaphoreType.DMA((in_width // BC + 1,)),
            pltpu.SemaphoreType.DMA((2,)),
        ],
        2 * micros * rows * width * kv_width,
        4 * width * (in_width + out_width),
        24,
    )(order, me, *xs, gains, *arrays)
    return made[0], made[1 : 1 + micros], made[1 + micros], made[2 + micros]


def query_kernel(h_ref, w_ref, *refs):
    q_refs = refs[:-2]
    held, sems = refs[-2:]
    groups = held.shape[1] // BC
    rows = q_refs[0].shape[0]

    def copy(b):
        across = pl.ds(pl.multiple_of(b * BC, BC), BC)
        return pltpu.make_async_copy(w_ref.at[:, across], held.at[:, across], sems.at[b])

    @pl.loop(0, groups)
    def _(b):
        copy(b).start()

    @pl.loop(0, groups)
    def _(b):
        copy(b).wait()
        across = pl.ds(pl.multiple_of(b * BC, BC), BC)
        made = dot(h_ref[...], held[:, across]).astype(low_type)
        for m, ref in enumerate(q_refs):
            ref[:, across] = made[m * rows : (m + 1) * rows]


def make_queries(h, w, micros):
    total, width = h.shape
    q_width = HEADS * HD
    return call(
        query_kernel,
        tuple([shaped((total // micros, q_width), low_type)] * micros),
        [in_vmem, in_any],
        tuple([in_vmem] * micros),
        [pltpu.VMEM((width, q_width), low_type), pltpu.SemaphoreType.DMA((q_width // BC,))],
        2 * total * width * q_width,
        2 * width * q_width,
        16,
    )(h, w)


def load_keys(parts, held, sem):
    start = 0
    for part in parts:
        count = part.shape[0]
        pltpu.make_async_copy(part, held.at[pl.ds(start, count)], sem).start()
        start += count


def attend_kernel(count, q_ref, rpos_ref, kpos_ref, x_ref, gain_ref, w_ref, *refs):
    parts = refs[:count]
    ob_ref, log_ref, x2_ref, h2_ref, bias, kv_ref, held, sems = refs[count:]
    rows = q_ref.shape[0]
    load_keys(parts, kv_ref, sems.at[0])
    pltpu.make_async_copy(w_ref, held, sems.at[1]).start()
    bias[...] = jnp.where(kpos_ref[...] <= rpos_ref[...], 0.0, masked_score)
    log_ref[...] = jnp.zeros_like(log_ref)
    length = kv_ref.shape[0]
    wait_bytes(kv_ref, sems.at[0])

    @pl.loop(0, KVH // 2)
    def _(pair):
        lane = pl.multiple_of(pair * LANES, LANES)
        keys = kv_ref[:, pl.ds(lane, LANES)]
        values = kv_ref[:, pl.ds(pl.multiple_of(lane + KVH * HD, LANES), LANES)]
        stacked = stack_heads(q_ref, pair, HD**-0.5)
        mixed = []
        for part in range(2):
            scores = dot(stacked[part].astype(low_type), keys, NT)
            scores = (scores.reshape(3, rows, length) + bias[...][None]).reshape(3 * rows, length)
            largest = jnp.max(scores, axis=-1, keepdims=True)
            raised = jnp.exp(scores - largest)
            summed = jnp.sum(raised, axis=-1, keepdims=True)
            mixed.append(dot(raised.astype(low_type), values) / summed)
            log_ref[...] = jnp.where(
                lane_ids(log_ref.shape) == 2 * pair + part, largest + jnp.log(summed), log_ref[...]
            )
        unstack_heads(ob_ref, pair, mixed[0], mixed[1])

    wait_bytes(held, sems.at[1])
    for n in range(held.shape[0] // BC):
        cut = slice(n * BC, (n + 1) * BC)
        x2_ref[:, cut] = x_ref[:, cut] + dot(ob_ref[...], held[cut, :], NT)
    h2_ref[...] = unit_rows(x2_ref[...], gain_ref[1:2])[0].astype(low_type)


def attend(q, kv_parts, rows_pos, key_pos, x, gains, w):
    rows, width = q.shape
    length = key_pos.shape[1]
    model = x.shape[1]
    return call(
        functools.partial(attend_kernel, len(kv_parts)),
        (
            shaped((rows, width), low_type),
            shaped((3 * rows, LANES), jnp.float32),
            shaped((rows, model), jnp.float32),
            shaped((rows, model), low_type),
        ),
        [in_vmem] * 5 + [in_any] * (1 + len(kv_parts)),
        (in_vmem,) * 4,
        [
            pltpu.VMEM((rows, length), jnp.float32),
            pltpu.VMEM((length, kv_parts[0].shape[1]), low_type),
            pltpu.VMEM((model, width), low_type),
            pltpu.SemaphoreType.DMA((2,)),
        ],
        16 * rows * length * width,
        8 * MIB,
        32,
    )(q, rows_pos, key_pos, x, gains, w, *kv_parts)


def router_parts(h2, router, experts):
    logits = dot(h2, router)
    logits = jnp.where(lane_ids(logits.shape) < experts, logits, masked_score)
    raised = jnp.exp(logits - jnp.max(logits, axis=-1, keepdims=True))
    return raised / jnp.sum(raised, axis=-1, keepdims=True)


def expert_kernel(sources, micro, order_ref, me_ref, router_ref, *refs):
    h_parts = refs[:sources]
    c_parts = refs[sources : 2 * sources]
    w_ref = refs[2 * sources]
    outs = refs[2 * sources + 1 :]
    back_refs = outs[:sources]
    z_ref, dg_ref, du_ref, cs, xs_ref = outs[sources : sources + 5]
    held, chance, load_sem, w_sems = outs[sources + 5 :]
    rows, width = h_parts[0].shape
    row_groups = width // BR
    col_groups = FF // BC
    for j in range(sources):
        pltpu.make_async_copy(h_parts[j], xs_ref.at[pl.ds(j * rows, rows)], load_sem.at[0]).start()
        pltpu.make_async_copy(
            c_parts[j].at[pl.ds(micro * rows, rows)], cs.at[pl.ds(j * rows, rows)], load_sem.at[1]
        ).start()
    for b in range(col_groups):

        @pl.loop(0, row_groups)
        def _(a):
            for k in range(3):
                pltpu.make_async_copy(
                    w_ref.at[order_ref[(k * row_groups + a) * col_groups + b]],
                    held.at[k, pl.ds(pl.multiple_of(a * BR, 64), BR), pl.ds(b * BC, BC)],
                    w_sems.at[b],
                ).start()

    wait_bytes(xs_ref, load_sem.at[0])
    wait_bytes(cs, load_sem.at[1])
    me = me_ref[1]
    probs = router_parts(xs_ref[...], router_ref[...], sources)
    hits = cs[:, width:].astype(jnp.float32)
    mine = lane_ids(hits.shape) == me
    hit = jnp.sum(jnp.where(mine, hits, 0.0), axis=-1, keepdims=True)
    weight = jnp.sum(jnp.where(mine, probs, 0.0), axis=-1, keepdims=True) * hit
    chance[...] = jnp.zeros_like(chance)

    @pl.loop(0, col_groups)
    def _(b):
        cut = pl.ds(pl.multiple_of(b * BC, BC), BC)
        wait_bytes(held.at[:, :, cut], w_sems.at[b])
        gate = dot(xs_ref[...], held[0, :, cut])
        up = dot(xs_ref[...], held[1, :, cut])
        down = dot(cs[:, :width], held[2, :, cut])
        sig = jax.nn.sigmoid(gate)
        act = gate * sig
        hidden = act * up
        chance[...] += jnp.sum(down * hidden, axis=-1, keepdims=True)
        z_ref[:, cut] = (hidden * weight).astype(low_type)
        down = down * weight
        dg_ref[:, cut] = (down * up * (sig + act * (1.0 - sig))).astype(low_type)
        du_ref[:, cut] = (down * act).astype(low_type)

    for n in range(width // BC):
        cut = slice(n * BC, (n + 1) * BC)
        back = dot(dg_ref[...], held[0, cut, :], NT) + dot(du_ref[...], held[1, cut, :], NT)
        for j in range(sources):
            back_refs[j][:, cut] = back[j * rows : (j + 1) * rows].astype(low_type)
    told = chance[...] * hit
    high_part = told.astype(low_type)
    low_part = (told - high_part.astype(jnp.float32)).astype(low_type)
    lanes = lane_ids((sources * rows, LANES))
    tail = jnp.where(lanes == 0, high_part, jnp.where(lanes == 1, low_part, jnp.zeros_like(low_part)))
    for j in range(sources):
        back_refs[j][:, width:] = tail[j * rows : (j + 1) * rows]


def run_expert(micro, order, me, router, h_parts, c_parts, w):
    sources = len(h_parts)
    rows, width = h_parts[0].shape
    total = sources * rows
    return call(
        functools.partial(expert_kernel, sources, micro),
        tuple(
            [shaped((rows, width + LANES), low_type)] * sources
            + [shaped((total, FF), low_type)] * 3
            + [shaped((total, width + LANES), low_type), shaped((total, width), low_type)]
        ),
        [in_smem, in_smem, in_vmem] + [in_any] * (2 * sources + 1),
        tuple([in_vmem] * (sources + 5)),
        [
            pltpu.VMEM((3, width, FF), low_type),
            pltpu.VMEM((total, 1), jnp.float32),
            pltpu.SemaphoreType.DMA((2,)),
            pltpu.SemaphoreType.DMA((FF // BC,)),
        ],
        10 * total * width * FF,
        20 * MIB,
        44,
    )(order, me, router, *h_parts, *c_parts, w)


def produce_kernel(sources, order_ref, w_ref, *refs):
    out_refs = refs[-3 - sources : -3]
    z_refs = refs[: -3 - sources]
    zs, held, sem = refs[-3:]
    width = held.shape[0]
    total = z_refs[0].shape[0]
    rows = total // sources
    row_groups, col_groups = width // BR, FF // BC

    @pl.loop(0, row_groups)
    def _(a):
        for b in range(col_groups):
            pltpu.make_async_copy(
                w_ref.at[order_ref[(2 * row_groups + a) * col_groups + b]],
                held.at[pl.ds(pl.multiple_of(a * BR, 64), BR), pl.ds(b * BC, BC)],
                sem,
            ).start()

    for m, z_ref in enumerate(z_refs):
        zs[m * total : (m + 1) * total] = z_ref[...]
    wait_bytes(held, sem)
    for n in range(width // BC):
        cut = slice(n * BC, (n + 1) * BC)
        made = dot(zs[...], held[cut, :], NT).astype(low_type)
        for m in range(len(z_refs)):
            for j in range(sources):
                start = m * total + j * rows
                out_refs[j][m * rows : (m + 1) * rows, cut] = made[start : start + rows]


def produce(order, w, zs, sources, width):
    micros = len(zs)
    total = zs[0].shape[0]
    return call(
        functools.partial(produce_kernel, sources),
        tuple([shaped((micros * total // sources, width), low_type)] * sources),
        [in_smem, in_any] + [in_vmem] * micros,
        tuple([in_vmem] * sources),
        [
            pltpu.VMEM((micros * total, FF), low_type),
            pltpu.VMEM((width, FF), low_type),
            pltpu.SemaphoreType.DMA,
        ],
        2 * micros * total * width * FF,
        8 * MIB,
        24,
    )(order, w, *zs)


def outer_kernel(place, widths, order_ref, *refs):
    count = len(widths)
    micros = len(refs[:-3]) // (2 * count)
    lefts = refs[: count * micros]
    rights = refs[count * micros : 2 * count * micros]
    out_ref, stage, sems = refs[-3:]
    span = 2 * BR
    steps = []
    for k in range(count):
        for p in range(widths[k] // span):
            steps.append((k, p))

    def wait_stage(slot, cols):
        wait_bytes(stage.at[slot, :, pl.ds(0, cols)], sems.at[slot])

    used = [None, None]
    for n, (k, p) in enumerate(steps):
        slot = n % 2
        cols = rights[k * micros].shape[-1]
        if used[slot] is not None:
            wait_stage(slot, used[slot])
        used[slot] = cols
        cut = slice(p * span, (p + 1) * span)
        for c in range(0, cols, 512):
            part = slice(c, c + 512)
            made = sum(
                dot(lefts[k * micros + m][:, cut], rights[k * micros + m][:, part], TN)
                for m in range(micros)
            )
            stage[slot, :, part] = made.astype(low_type)
        first, row_step = place(k)
        for half in range(2):
            for b in range(cols // BC):
                pltpu.make_async_copy(
                    stage.at[slot, pl.ds(half * BR, BR), pl.ds(b * BC, BC)],
                    out_ref.at[order_ref[first + (2 * p + half) * row_step + b]],
                    sems.at[slot],
                ).start()
    for slot in range(2):
        if used[slot] is not None:
            wait_stage(slot, used[slot])


def outer_blocks(order, place, widths, lefts, rights, blocks):
    widest = max(r[0].shape[-1] for r in rights)
    rows = sum(l.shape[0] for l in lefts[0])
    flat = [l for group in lefts for l in group] + [r for group in rights for r in group]
    return call(
        functools.partial(outer_kernel, place, widths),
        shaped((blocks, BR, BC), low_type),
        [in_smem] + [in_vmem] * len(flat),
        in_any,
        [pltpu.VMEM((2, 2 * BR, widest), low_type), pltpu.SemaphoreType.DMA((2,))],
        2 * rows * blocks * BR * BC,
        blocks * BR * BC * 2 + sum(f.size * 2 for f in flat),
        40,
    )(order, *flat)


def xor_plan(members, offset):
    if members != 4:
        return list(range(1, members)), [0]
    first = 1 if offset % 2 else 2
    return [first, 3], [0, 3 - first]


def slots_kernel(
    counts, chips, members, slots, all_groups, in_groups, order_ref, me_ref, *refs
):
    lists = []
    for count in counts:
        lists.append(refs[:count])
        refs = refs[count:]
    outs = refs[: 2 * chips]
    lefts, turned, rights, sems = refs[2 * chips :]
    ctx, shard = me_ref[0], me_ref[1]
    chip, core = lax.div(ctx, 2), lax.rem(ctx, 2)
    h_width = lefts.shape[2]
    q_width = lists[2][0].shape[1]
    kv_width = lists[3][0].shape[1]
    total = rights.shape[0]
    targets = (
        (lefts.at[0], 0, h_width, 0),
        (lefts.at[1], 0, h_width, 1),
        (rights, 0, q_width, 2),
        (rights, q_width, kv_width, 2),
        (rights, q_width + kv_width, q_width, 2),
    )
    for group, (target, lane, lanes, sem) in zip(lists, targets):
        start = 0
        for ref in group:
            pltpu.make_async_copy(
                ref, target.at[pl.ds(start, ref.shape[0]), pl.ds(lane, lanes)], sems.at[sem]
            ).start()
            start += ref.shape[0]
    for side in range(2):
        wait_bytes(lefts.at[side], sems.at[side])
        for r in range(0, total, LANES):
            turned[side, :, r : r + LANES] = lefts[side, r : r + LANES, :].T
    wait_bytes(rights, sems.at[2])
    for offset in range(chips):
        there = lax.rem(chip - offset + chips, chips) * 2 + core
        for out, hops in zip(outs[2 * offset : 2 * offset + 2], xor_plan(members, offset)):
            for place, hop in enumerate(hops):
                base = (there * members + jnp.bitwise_xor(shard, hop)) * slots

                @pl.loop(0, slots)
                def _(i):
                    number = order_ref[base + i]
                    a, b = lax.div(number, all_groups), lax.rem(number, all_groups)
                    side = (b >= in_groups).astype(jnp.int32)
                    out[place * slots + i] = dot(
                        turned[side, pl.ds(pl.multiple_of(a * BR, 64), BR), :],
                        rights[:, pl.ds(pl.multiple_of(b * BC, BC), BC)],
                    ).astype(low_type)


def slot_blocks(chips, members, slots, order, me, h1, da, dq, dkv, ob):
    lists = (h1, da, dq, dkv, ob)
    total = sum(part.shape[0] for part in h1)
    width = h1[0].shape[1]
    in_width = dq[0].shape[1] + dkv[0].shape[1]
    all_width = in_width + ob[0].shape[1]
    outs = []
    for offset in range(chips):
        for hops in xor_plan(members, offset):
            outs.append(shaped((len(hops) * slots, BR, BC), low_type))
    made = call(
        functools.partial(
            slots_kernel,
            tuple(len(group) for group in lists),
            chips,
            members,
            slots,
            all_width // BC,
            in_width // BC,
        ),
        tuple(outs),
        [in_smem, in_smem] + [in_any] * sum(len(group) for group in lists),
        (in_vmem,) * len(outs),
        [
            pltpu.VMEM((2, total, width), low_type),
            pltpu.VMEM((2, width, total), low_type),
            pltpu.VMEM((total, all_width), low_type),
            pltpu.SemaphoreType.DMA((3,)),
        ],
        2 * total * chips * members * slots * BR * BC,
        16 * MIB,
        28,
    )(order, me, *[part for group in lists for part in group])
    return [(made[2 * offset], made[2 * offset + 1]) for offset in range(chips)]


def merge_kernel(
    sources, me_ref, x2_ref, cot_ref, h2_ref, gain_ref, router_ref, w_ref, *refs
):
    back_refs = refs[:sources]
    dx_ref, da_ref, do_ref, stat_ref, held, sem = refs[sources:]
    rows, width = x2_ref.shape
    pltpu.make_async_copy(w_ref, held, sem).start()
    lanes = lane_ids((rows, LANES))
    prob_grad = jnp.zeros((rows, LANES), jnp.float32)
    gathered = jnp.zeros((rows, width), jnp.float32)
    for j in range(sources):
        tail = back_refs[j][:, width:].astype(jnp.float32)
        told = jnp.sum(tail, axis=-1, keepdims=True)
        expert = jnp.bitwise_xor(me_ref[1], j)
        prob_grad = prob_grad + jnp.where(lanes == expert, told, 0.0)
        gathered = gathered + back_refs[j][:, :width].astype(jnp.float32)
    h2 = h2_ref[...]
    probs = router_parts(h2, router_ref[...], sources)
    logit_grad = probs * (prob_grad - jnp.sum(probs * prob_grad, axis=-1, keepdims=True))
    high_part = logit_grad.astype(low_type)
    low_part = (logit_grad - high_part.astype(jnp.float32)).astype(low_type)
    router_grad = dot(high_part, h2, TN) + dot(low_part, h2, TN)
    gathered = gathered + dot(high_part, router_ref[...], NT) + dot(low_part, router_ref[...], NT)
    x2 = x2_ref[...]
    inverse = lax.rsqrt(jnp.mean(x2 * x2, axis=-1, keepdims=True) + norm_eps)
    moe_grad, gain_grad = unit_back(x2, gain_ref[1:2], inverse, gathered)
    after = cot_ref[...] + moe_grad
    dx_ref[...] = after
    da_ref[...] = after.astype(low_type)
    experts_up = stat_ref.shape[0] - 8
    stat_ref[:experts_up] = router_grad[:experts_up]
    stat_ref[experts_up:] = jnp.broadcast_to(gain_grad, (8, width))
    wait_bytes(held, sem)
    for n in range(held.shape[1] // BC):
        cut = slice(n * BC, (n + 1) * BC)
        do_ref[:, cut] = dot(da_ref[...], held[:, cut]).astype(low_type)


def merge(me, x2, cot, h2, gains, router, w, backs):
    rows, width = x2.shape
    sources = len(backs)
    experts_up = -(-sources // 8) * 8
    return call(
        functools.partial(merge_kernel, sources),
        (
            shaped((rows, width), jnp.float32),
            shaped((rows, width), low_type),
            shaped((rows, HEADS * HD), low_type),
            shaped((experts_up + 8, width), jnp.float32),
        ),
        [in_smem] + [in_vmem] * 5 + [in_any] + [in_vmem] * sources,
        (in_vmem,) * 4,
        [pltpu.VMEM((width, HEADS * HD), low_type), pltpu.SemaphoreType.DMA],
        2 * rows * width * HEADS * HD,
        10 * MIB,
        24,
    )(me, x2, cot, h2, gains, router, w, *backs)


def attend_back_kernel(count, q_ref, rpos_ref, kpos_ref, ob_ref, log_ref, do_ref, *refs):
    parts = refs[:count]
    dq_ref, own_ref, other_ref, bias, kv_ref, sem = refs[count:]
    rows = q_ref.shape[0]
    load_keys(parts, kv_ref, sem)
    length = kv_ref.shape[0]
    bias[...] = jnp.where(kpos_ref[...] <= rpos_ref[...], 0.0, masked_score)
    wait_bytes(kv_ref, sem)

    @pl.loop(0, KVH // 2)
    def _(pair):
        lane = pl.multiple_of(pair * LANES, LANES)
        value_lane = pl.multiple_of(lane + KVH * HD, LANES)
        keys = kv_ref[:, pl.ds(lane, LANES)]
        values = kv_ref[:, pl.ds(value_lane, LANES)]
        queries = stack_heads(q_ref, pair, HD**-0.5)
        grads = stack_heads(do_ref, pair)
        mixes = stack_heads(ob_ref, pair)
        query_grads = []
        key_grad = value_grad = None
        for part in range(2):
            query = queries[part].astype(low_type)
            grad = grads[part].astype(low_type)
            log_total = jnp.sum(
                jnp.where(lane_ids(log_ref.shape) == 2 * pair + part, log_ref[...], 0.0),
                axis=-1,
                keepdims=True,
            )
            delta = jnp.sum(grads[part] * mixes[part], axis=-1, keepdims=True)
            scores = dot(query, keys, NT)
            scores = (scores.reshape(3, rows, length) + bias[...][None]).reshape(3 * rows, length)
            chance = jnp.exp(scores - log_total)
            prob_grad = dot(grad, values, NT)
            score_grad = (chance * (prob_grad - delta)).astype(low_type)
            value_term = dot(chance.astype(low_type), grad, TN)
            key_term = dot(score_grad, query, TN)
            key_grad = key_term if part == 0 else key_grad + key_term
            value_grad = value_term if part == 0 else value_grad + value_term
            query_grads.append(dot(score_grad, keys) * HD**-0.5)
        unstack_heads(dq_ref, pair, query_grads[0], query_grads[1])
        half = length // 2
        for ref, cut in ((own_ref, slice(0, half)), (other_ref, slice(half, length))):
            ref[:, pl.ds(lane, LANES)] = key_grad[cut].astype(low_type)
            ref[:, pl.ds(value_lane, LANES)] = value_grad[cut].astype(low_type)


def attend_back(q, kv_parts, rows_pos, key_pos, ob, log_total, do):
    rows, width = q.shape
    length = key_pos.shape[1]
    kv_width = kv_parts[0].shape[1]
    return call(
        functools.partial(attend_back_kernel, len(kv_parts)),
        (shaped((rows, width), low_type),) + (shaped((length // 2, kv_width), low_type),) * 2,
        [in_vmem] * 6 + [in_any] * len(kv_parts),
        (in_vmem,) * 3,
        [
            pltpu.VMEM((rows, length), jnp.float32),
            pltpu.VMEM((length, kv_width), low_type),
            pltpu.SemaphoreType.DMA,
        ],
        40 * rows * length * width,
        8 * MIB,
        40,
    )(q, rows_pos, key_pos, ob, log_total, do, *kv_parts)


def query_back_kernel(w_ref, *refs):
    micros = (len(refs) - 3) // 2
    dq_refs, out_refs = refs[:micros], refs[micros : 2 * micros]
    rows_ref, held, sem = refs[2 * micros :]
    rows = dq_refs[0].shape[0]
    copy = pltpu.make_async_copy(w_ref.at[:, pl.ds(0, held.shape[1])], held, sem)
    copy.start()
    for m in range(micros):
        rows_ref[m * rows : (m + 1) * rows] = dq_refs[m][...]
    copy.wait()
    for n in range(held.shape[0] // BC):
        cut = slice(n * BC, (n + 1) * BC)
        made = dot(rows_ref[...], held[cut, :], NT)
        for m in range(micros):
            out_refs[m][:, cut] = made[m * rows : (m + 1) * rows]


def query_back(w, dqs):
    micros = len(dqs)
    rows, q_width = dqs[0].shape
    width = w.shape[0]
    return call(
        query_back_kernel,
        tuple([shaped((rows, width), jnp.float32)] * micros),
        [in_any] + [in_vmem] * micros,
        tuple([in_vmem] * micros),
        [
            pltpu.VMEM((micros * rows, q_width), low_type),
            pltpu.VMEM((width, q_width), low_type),
            pltpu.SemaphoreType.DMA,
        ],
        2 * micros * rows * width * q_width,
        7 * MIB,
        16,
    )(w, *dqs)


def input_kernel(x_ref, gain_ref, w_ref, *refs):
    micros, rows = x_ref.shape[:2]
    dx_refs = refs[:micros]
    part_refs = refs[micros : 2 * micros]
    dkv_refs = refs[2 * micros : 3 * micros]
    out_ref, stat_ref, rows_ref, grad, held, sem = refs[3 * micros :]
    kv_width = held.shape[1]
    copy = pltpu.make_async_copy(
        w_ref.at[:, pl.ds(w_ref.shape[1] - kv_width, kv_width)], held, sem
    )
    copy.start()
    for m in range(micros):
        rows_ref[m * rows : (m + 1) * rows] = dkv_refs[m][...]
    copy.wait()
    for n in range(held.shape[0] // BC):
        cut = slice(n * BC, (n + 1) * BC)
        made = dot(rows_ref[...], held[cut, :], NT)
        for m in range(micros):
            grad[m, :, cut] = part_refs[m][:, cut] + made[m * rows : (m + 1) * rows]
    total = jnp.zeros((1, x_ref.shape[-1]), jnp.float32)
    for m in range(micros):
        x = x_ref[m]
        inverse = lax.rsqrt(jnp.mean(x * x, axis=-1, keepdims=True) + norm_eps)
        term, gain_grad = unit_back(x, gain_ref[0:1], inverse, grad[m])
        out_ref[m] = dx_refs[m][...] + term
        total = total + gain_grad
    stat_ref[...] = jnp.broadcast_to(total, stat_ref.shape)


def input_back(x, gains, w, dxs, parts, dkvs):
    micros, rows, width = x.shape
    kv_width = dkvs[0].shape[1]
    return call(
        input_kernel,
        (shaped(x.shape, jnp.float32), shaped((8, width), jnp.float32)),
        [in_vmem, in_vmem, in_any] + [in_vmem] * (3 * micros),
        (in_vmem,) * 2,
        [
            pltpu.VMEM((micros * rows, kv_width), low_type),
            pltpu.VMEM(x.shape, jnp.float32),
            pltpu.VMEM((width, kv_width), low_type),
            pltpu.SemaphoreType.DMA,
        ],
        2 * micros * rows * width * kv_width,
        14 * MIB,
        16,
    )(x, gains, w, *dxs, *parts, *dkvs)


def rotate_kernel(
    b_ref, g_ref, m_ref, s_ref, l_ref, r_ref, grad_ref, new_ref, moment_ref, second_ref
):
    gradient = g_ref[0].astype(jnp.float32)
    grad_ref[0] = gradient
    left = l_ref[0].astype(low_type)
    right = r_ref[0].astype(low_type)
    rotated = dot(dot(left, gradient.astype(low_type), TN).astype(low_type), right)
    moment = beta_one * m_ref[0] + (1.0 - beta_one) * rotated
    second = beta_two * s_ref[0] + (1.0 - beta_two) * rotated * rotated
    moment_ref[0] = moment
    second_ref[0] = second
    direction = (moment / (jnp.sqrt(second) + adam_eps)).astype(low_type)
    turned = dot(dot(left, direction).astype(low_type), right, NT)
    new_ref[0] = b_ref[0] - rate * turned


def rotate(weight, gradient, moment, second, left, right):
    count = weight.shape[0]
    limit = 16

    def spec(rows, cols):
        return pl.BlockSpec((1, rows, cols), lambda i: (i, 0, 0))

    block = spec(BR, BC)
    return pl.pallas_call(
        rotate_kernel,
        grid=(count,),
        out_shape=(shaped(weight.shape, jnp.float32),) * 4,
        in_specs=[block] * 4 + [spec(BR, BR), spec(BC, BC)],
        out_specs=(block,) * 4,
        compiler_params=pltpu.CompilerParams(vmem_limit_bytes=limit * MIB),
        cost_estimate=pl.CostEstimate(
            flops=4 * count * BR * BC * (BR + BC),
            bytes_accessed=count * 2 * MIB,
            transcendentals=0,
        ),
    )(weight, gradient, moment, second, left, right)


def adam(weight, gradient, moment, second, step_rate):
    moment_new = beta_one * moment + (1.0 - beta_one) * gradient
    second_new = beta_two * second + (1.0 - beta_two) * gradient * gradient
    return (
        weight - step_rate * moment_new / (jnp.sqrt(second_new) + adam_eps),
        moment_new,
        second_new,
    )


def to_partner(array, offset):
    if offset == 0:
        return array
    count = lax.axis_size("shard")
    return lax.ppermute(array, "shard", [(i, i ^ offset) for i in range(count)])


def to_ctx(array, offset):
    count = lax.axis_size("ctx")
    return lax.ppermute(array, "ctx", [(i, i ^ offset) for i in range(count)])


def to_chip(array, offset):
    count = lax.axis_size("ctx")
    return lax.ppermute(array, "ctx", [(i, (i + 2 * offset) % count) for i in range(count)])


def after(value, *others):
    return lax.optimization_barrier((value, others))[0]


def from_chips(array, chips):
    return [array] + [to_chip(array, offset) for offset in range(1, chips)]


def wide(array):
    return array.astype(jnp.float32)


def sum_to_chips(parts):
    total = wide(parts[0])
    for offset in range(1, len(parts)):
        total = total + wide(to_chip(parts[offset], -offset))
    return total


def gather_weights(blocks, chips, members):
    parts = from_chips(blocks, chips)
    pieces, arrays = [], []

    def add(array, offset, first, cut):
        pieces.append((0, offset, first, cut))
        arrays.append(array)
        pieces.append((1, offset, first, cut))
        arrays.append(to_ctx(array, 1))
        return array

    add(blocks, 0, 0, 0)
    for offset in range(1, members):
        add(to_partner(blocks, offset), offset, 0, 0)
    near = list(arrays)
    if chips > 1:
        far = after(jnp.concatenate(parts[1:], axis=0), *near)
        add(far, 0, 1, 0)
        if members == 4:
            by_one = add(to_partner(far, 1), 1, 1, 0)
            by_two = add(to_partner(far, 2), 2, 1, 0)
            half = BR // 2
            add(to_partner(by_one[:, :half], 2), 3, 1, 0)
            add(to_partner(by_two[:, half:], 1), 3, 1, half)
        else:
            for offset in range(1, members):
                add(to_partner(far, offset), offset, 1, 0)
    return near + parts[1:], pieces, arrays


def sum_slots(made, chips, members, slots):
    sums, first_got = [], []
    for offset in range(chips):
        sent, kept = made[offset]
        hops, keeps = xor_plan(members, offset)
        total = wide(kept[:slots])
        if members == 4:
            first, second = hops[0], keeps[1]
            got = to_partner(sent, first)
            total = total + wide(got[:slots])
            relay = (wide(kept[slots:]) + wide(got[slots:])).astype(low_type)
            total = total + wide(to_partner(relay, second))
        else:
            for place, hop in enumerate(hops):
                got = to_partner(sent[place * slots : (place + 1) * slots], hop)
                total = total + wide(got)
        sums.append(total if offset == 0 else total.astype(low_type))
        first_got.append(got)
    return sums, first_got


def sum_all(array):
    step = 1
    while step < lax.axis_size("ctx"):
        array = array + to_ctx(array, step)
        step *= 2
    step = 1
    while step < lax.axis_size("shard"):
        array = array + to_partner(array, step)
        step *= 2
    return array


def shards(
    tokens,
    cotangent,
    norm_gains,
    router,
    dense_weight,
    expert_weight,
    routes,
    assign,
    dense_order,
    expert_order,
    dense_moment,
    dense_second,
    dense_left,
    dense_right,
    expert_moment,
    expert_second,
    expert_left,
    expert_right,
    gains_moment,
    gains_second,
    router_moment,
    router_second,
):
    ctx_count = lax.axis_size("ctx")
    shard_count = lax.axis_size("shard")
    chips = ctx_count // 2
    micros, rows, width = tokens.shape
    slots = dense_weight.shape[0]
    span = rows // 2
    row_groups = width // BR
    ff_groups = FF // BC
    expert_blocks = 3 * row_groups * ff_groups

    expert_inverse = inverse_order(expert_order)
    ctx = lax.axis_index("ctx").astype(jnp.int32)
    me = jnp.stack([ctx, lax.axis_index("shard").astype(jnp.int32)])
    row_ids = jnp.arange(rows, dtype=jnp.int32)
    all_pos = assign[:, row_ids // span] * span + row_ids % span
    ring_ids = (ctx // 2 - jnp.arange(chips, dtype=jnp.int32)) % chips * 2
    key_ids = jnp.concatenate([ring_ids + ctx % 2, ring_ids + (1 - ctx % 2)])
    key_pos = all_pos[key_ids].reshape(1, rows * ctx_count)
    rows_pos = all_pos[ctx].reshape(rows, 1)
    router_pad = jnp.pad(router.astype(low_type), ((0, 0), (0, LANES - shard_count)))

    far, pieces, arrays = gather_weights(dense_weight.astype(low_type), chips, shard_count)
    expert_low = after(expert_weight[0].astype(low_type), *far)
    expert_all = lax.all_gather(expert_low, "ctx", axis=0, tiled=True)

    lanes = jnp.arange(LANES, dtype=jnp.int32)
    hits = jnp.sum((routes[..., None] == lanes).astype(low_type), axis=2)
    cot_rows = jnp.concatenate([cotangent.astype(low_type), hits], axis=2)
    cot_rows = cot_rows.reshape(micros * rows, width + LANES)
    cot_rows = after(cot_rows, *arrays[::2])
    cot_parts = [to_partner(cot_rows, j) for j in range(shard_count)]

    h1, kv, w_in, w_out = project(
        pieces,
        arrays,
        chips,
        shard_count,
        slots,
        dense_order,
        me,
        [tokens[m] for m in range(micros)],
        norm_gains,
    )
    q = make_queries(h1, w_in, micros)
    h1_other = to_ctx(h1, 1)
    kvs, obs, logs, x2s, h2s = [], [], [], [], []
    chip_kv = []
    for m in range(micros):
        own = kv[m] if m == 0 else after(kv[m], chip_kv[m - 1][1 % chips])
        chip_kv.append(from_chips(own, chips))
    for m in range(micros):
        query = after(q[m], *(cot_parts if m == 0 else obs[m - 1 : m]))
        parts = chip_kv[m]
        swapped = parts if m == 0 else after(parts, obs[m - 1])
        kvs.append(parts + [to_ctx(part, 1) for part in swapped])
        ob, log_total, x2, h2 = attend(
            query, kvs[m], rows_pos, key_pos, tokens[m], norm_gains, w_out
        )
        obs.append(ob)
        logs.append(log_total)
        x2s.append(x2)
        h2s.append(h2)
    ob_others = [to_ctx(ob, 1) for ob in obs]

    h_parts = []
    for m in range(micros):
        own = h2s[m] if m == 0 else after(h2s[m], *h_parts[m - 1])
        h_parts.append([own] + [to_partner(own, j) for j in range(1, shard_count)])
    sent = []
    zs, dgs, dus, cs, xs = [], [], [], [], []
    for m in range(micros):
        here = after(me, h2s[-1], h1_other, *ob_others) if m == 0 else after(me, zs[-1])
        made = run_expert(m, expert_inverse, here, router_pad, h_parts[m], cot_parts, expert_all)
        sent.append(made[:shard_count])
        z, dg, du, c, x = made[shard_count:]
        zs.append(z)
        dgs.append(dg)
        dus.append(du)
        cs.append(c)
        xs.append(x)
    backs = [[to_partner(sent[m][j], j) for j in range(shard_count)] for m in range(micros)]

    dxs, das, dqs, stats, own_grads, far_arrived = [], [], [], [], [], []
    for m in range(micros):
        here = after(me, zs[-1] if m == 0 else dqs[-1])
        dx, da, do, stat = merge(
            here, x2s[m], cotangent[m], h2s[m], norm_gains, router_pad, w_out, backs[m]
        )
        dq, dkv_own, dkv_other = attend_back(
            q[m], kvs[m], rows_pos, key_pos, obs[m], logs[m], do
        )
        got = to_ctx(dkv_other, 1)
        parts = []
        for o in range(chips):
            cut = slice(o * rows, (o + 1) * rows)
            part = wide(dkv_own[cut]) + wide(got[cut])
            parts.append(part if o == 0 else part.astype(low_type))
        own_grads.append(parts[0])
        far_arrived.append([to_chip(parts[o], -o) for o in range(1, chips)])
        dxs.append(dx)
        das.append(da)
        dqs.append(dq)
        stats.append(stat)

    dkvs = [
        sum([wide(part) for part in far_arrived[m]], own_grads[m]).astype(low_type)
        for m in range(micros)
    ]

    def other_core(parts):
        return [to_ctx(part, 1) for part in parts]

    da_others, dq_others = other_core(das), other_core(dqs)
    expert_term = outer_blocks(
        after(expert_inverse, dqs[-1]),
        lambda k: (k * row_groups * ff_groups, ff_groups),
        (width,) * 3,
        [xs, xs, cs],
        [dgs, dus, zs],
        expert_blocks,
    )
    parts_back = query_back(after(w_in, expert_term), dqs)
    expert_sum = lax.psum_scatter(
        after(expert_term, dkvs[-1]), "ctx", scatter_dimension=0, tiled=True
    )
    here = after(me, parts_back)
    made = slot_blocks(
        chips,
        shard_count,
        slots,
        dense_order,
        here,
        [h1, h1_other],
        das + da_others,
        dqs + dq_others,
        dkvs + other_core(dkvs),
        obs + ob_others,
    )
    sums, got = sum_slots(made, chips, shard_count, slots)
    dense_sum = sum_to_chips(sums)
    input_grad, gain_stat = input_back(
        after(tokens, *got[:2]), norm_gains, w_in, dxs, parts_back, dkvs
    )
    experts_up = stats[0].shape[0] - 8
    stat_rows = jnp.concatenate([sum(stats)[: experts_up + 1], gain_stat[:7]], axis=0)
    stat_rows = sum_all(stat_rows)
    router_grad = stat_rows[:shard_count].T
    gains_grad = jnp.stack([stat_rows[experts_up + 1], stat_rows[experts_up]])

    made = produce(after(expert_inverse, *got[:2]), expert_all, zs, shard_count, width)
    made = after(list(made), *sums)
    arrived = [to_partner(made[j], j) for j in range(shard_count)]
    outputs = []
    for m in range(micros):
        total = x2s[m]
        for part in arrived:
            total = total + wide(part[m * rows : (m + 1) * rows])
        outputs.append(total)

    expert_grad, expert_new, expert_moment_new, expert_second_new = rotate(
        expert_weight[0], after(expert_sum, *sums), expert_moment[0], expert_second[0], expert_left[0], expert_right[0]
    )
    dense_grad, dense_new, dense_moment_new, dense_second_new = rotate(
        dense_weight, after(dense_sum, expert_new), dense_moment, dense_second, dense_left, dense_right
    )
    gains_new, gains_moment_new, gains_second_new = adam(
        norm_gains, gains_grad, gains_moment, gains_second, gain_rate
    )
    router_new, router_moment_new, router_second_new = adam(
        router, router_grad, router_moment, router_second, rate
    )
    return (
        jnp.stack(outputs),
        input_grad,
        dense_grad,
        dense_new,
        dense_moment_new,
        dense_second_new,
        expert_grad[None],
        expert_new[None],
        expert_moment_new[None],
        expert_second_new[None],
        gains_grad,
        gains_new,
        gains_moment_new,
        gains_second_new,
        router_grad,
        router_new,
        router_moment_new,
        router_second_new,
    )


def solution(mesh):
    rows_spec = P("shard", "ctx", None)
    dense_spec = P(("ctx", "shard"), None, None)
    expert_spec = P("shard", "ctx", None, None)
    in_specs = (
        (rows_spec, rows_spec, P(), P(), dense_spec, expert_spec, rows_spec, P(), P(), P())
        + (dense_spec,) * 4
        + (expert_spec,) * 4
        + (P(),) * 4
    )
    out_specs = (rows_spec,) * 2 + (dense_spec,) * 4 + (expert_spec,) * 4 + (P(),) * 8
    return jax.shard_map(shards, mesh=mesh, in_specs=in_specs, out_specs=out_specs, check_vma=False)
```

```python
import functools

import jax
import jax.numpy as jnp
from jax import lax
from jax.experimental import pallas as pl
from jax.experimental.pallas import tpu as pltpu
from jax.sharding import PartitionSpec as P

HEADS = 24
KVH = 8
HD = 64
FF = 1024
BR = 192
BC = 256
LANES = 128

norm_eps = 1e-06
beta_one = 0.9
beta_two = 0.95
rate = 0.01
gain_rate = 0.5
adam_eps = 1e-08
masked_score = -1e30
low_type = jnp.bfloat16
MIB = 1 << 20
VMEM_LIMIT = 60 * MIB

NN = (((1,), (0,)), ((), ()))
NT = (((1,), (1,)), ((), ()))
TN = (((0,), (0,)), ((), ()))

in_vmem = pl.BlockSpec(memory_space=pltpu.VMEM)
in_smem = pl.BlockSpec(memory_space=pltpu.SMEM)
in_any = pl.BlockSpec(memory_space=pl.ANY)


def dot(left_side, right_side, dims=NN):
    return lax.dot_general(left_side, right_side, dims, preferred_element_type=jnp.float32)


def call(kernel, out_shapes, in_specs, out_specs, scratch, flops, moved):
    return pl.pallas_call(
        kernel,
        out_shape=out_shapes,
        in_specs=in_specs,
        out_specs=out_specs,
        scratch_shapes=scratch,
        compiler_params=pltpu.CompilerParams(vmem_limit_bytes=VMEM_LIMIT),
        cost_estimate=pl.CostEstimate(flops=flops, bytes_accessed=moved, transcendentals=0),
    )


def shaped(dims, kind):
    return jax.ShapeDtypeStruct(dims, kind)


def inverse_order(slot_order):
    count = slot_order.shape[0]
    numbers = jnp.arange(count, dtype=jnp.int32)
    return jnp.sum(
        jnp.where(slot_order[None, :] == numbers[:, None], numbers[None, :], 0), axis=1
    ).astype(jnp.int32)


def wait_bytes(landed, semaphore):
    pltpu.make_async_copy(landed, landed, semaphore).wait()


def unit_rows(rows, gain):
    inverse = lax.rsqrt(jnp.mean(rows * rows, axis=-1, keepdims=True) + norm_eps)
    return rows * inverse * gain, inverse


def unit_back(rows, gain, inverse, gradient):
    unit = rows * inverse
    scaled = gradient * gain
    inner = jnp.mean(scaled * unit, axis=-1, keepdims=True)
    return inverse * (scaled - unit * inner), jnp.sum(gradient * unit, axis=0, keepdims=True)


def lane_ids(dims):
    return lax.broadcasted_iota(jnp.int32, dims, len(dims) - 1)


def half_turn(tile):
    return pltpu.roll(tile, HD, 1)


def stack_heads(ref, pair, scale=None):
    base = pair * (3 * LANES)
    tiles = [
        ref[:, pl.ds(pl.multiple_of(base + LANES * t, LANES), LANES)].astype(jnp.float32)
        for t in range(3)
    ]
    if scale is not None:
        tiles = [t * scale for t in tiles]
    lower = lane_ids(tiles[0].shape) < HD
    first = [tiles[0], half_turn(tiles[0]), tiles[1]]
    second = [tiles[1], half_turn(tiles[2]), tiles[2]]
    return (
        jnp.concatenate([jnp.where(lower, t, 0.0) for t in first], axis=0),
        jnp.concatenate([jnp.where(lower, 0.0, t) for t in second], axis=0),
    )


def unstack_heads(ref, pair, first, second):
    rows = first.shape[0] // 3
    base = pair * (3 * LANES)
    lower = lane_ids((rows, LANES)) < HD
    tiles = (
        jnp.where(lower, first[:rows], half_turn(first[rows : 2 * rows])),
        jnp.where(lower, first[2 * rows :], second[:rows]),
        jnp.where(lower, half_turn(second[rows : 2 * rows]), second[2 * rows :]),
    )
    for t in range(3):
        ref[:, pl.ds(pl.multiple_of(base + LANES * t, LANES), LANES)] = tiles[t].astype(ref.dtype)


def project_kernel(
    pieces, chips, members, slots, all_groups, micros, order_ref, me_ref, *refs
):
    x_refs = refs[:micros]
    gain_ref = refs[micros]
    piece_refs = refs[micros + 1 : micros + 1 + len(pieces)]
    refs = refs[micros + 1 + len(pieces) :]
    h_ref = refs[0]
    kv_refs = refs[1 : 1 + micros]
    win_ref, wout_ref, held, held_out, sems, out_sems = refs[1 + micros :]
    groups = held.shape[1] // BC
    kv_groups = kv_refs[0].shape[-1] // BC
    rows = x_refs[0].shape[0]
    ctx, shard = me_ref[0], me_ref[1]
    chip, core = lax.div(ctx, 2), lax.rem(ctx, 2)

    for ref, (other_core, offset, first, cut) in zip(piece_refs, pieces):

        @pl.loop(0, ref.shape[0])
        def _(i):
            source = lax.rem(chip - (first + lax.div(i, slots)) + chips, chips) * 2
            source = source + jnp.bitwise_xor(core, other_core)
            source = source * members + jnp.bitwise_xor(shard, offset)
            number = order_ref[source * slots + lax.rem(i, slots)]
            a, b = lax.div(number, all_groups), lax.rem(number, all_groups)
            down = pl.ds(pl.multiple_of(a * BR + cut, 32), ref.shape[1])

            @pl.when(b < groups)
            def _():
                across = pl.ds(pl.multiple_of(b * BC, BC), BC)
                pltpu.make_async_copy(ref.at[i], held.at[down, across], sems.at[b]).start()

            @pl.when(b >= groups)
            def _():
                across = pl.ds(pl.multiple_of((b - groups) * BC, BC), BC)
                pltpu.make_async_copy(ref.at[i], held_out.at[down, across], sems.at[groups]).start()

    for m in range(micros):
        h_ref[m * rows : (m + 1) * rows, :] = unit_rows(x_refs[m][...], gain_ref[0:1])[0].astype(
            low_type
        )
    q_groups = groups - kv_groups

    @pl.loop(0, kv_groups)
    def _(b):
        across = pl.ds(pl.multiple_of((q_groups + b) * BC, BC), BC)
        wait_bytes(held.at[:, across], sems.at[q_groups + b])
        made = dot(h_ref[...], held[:, across]).astype(low_type)
        for m in range(micros):
            kv_refs[m][:, pl.ds(pl.multiple_of(b * BC, BC), BC)] = made[m * rows : (m + 1) * rows]

    @pl.loop(0, q_groups)
    def _(b):
        across = pl.ds(pl.multiple_of(b * BC, BC), BC)
        wait_bytes(held.at[:, across], sems.at[b])

    wait_bytes(held_out, sems.at[groups])
    copies = [
        pltpu.make_async_copy(held, win_ref, out_sems.at[0]),
        pltpu.make_async_copy(held_out, wout_ref, out_sems.at[1]),
    ]
    for copy in copies:
        copy.start()
    for copy in copies:
        copy.wait()


def project(pieces, arrays, chips, members, slots, order, me, xs, gains):
    micros = len(xs)
    rows, width = xs[0].shape
    in_width = (HEADS + 2 * KVH) * HD
    out_width = HEADS * HD
    kv_width = 2 * KVH * HD
    made = call(
        functools.partial(
            project_kernel, pieces, chips, members, slots, (in_width + out_width) // BC, micros
        ),
        tuple(
            [shaped((micros * rows, width), low_type)]
            + [shaped((rows, kv_width), low_type)] * micros
            + [shaped((width, in_width), low_type), shaped((width, out_width), low_type)]
        ),
        [in_smem, in_smem] + [in_vmem] * (micros + 1) + [in_any] * len(arrays),
        tuple([in_vmem] * (1 + micros) + [in_any, in_any]),
        [
            pltpu.VMEM((width, in_width), low_type),
            pltpu.VMEM((width, out_width), low_type),
            pltpu.SemaphoreType.DMA((in_width // BC + 1,)),
            pltpu.SemaphoreType.DMA((2,)),
        ],
        2 * micros * rows * width * kv_width,
        4 * width * (in_width + out_width),
    )(order, me, *xs, gains, *arrays)
    return made[0], made[1 : 1 + micros], made[1 + micros], made[2 + micros]


def query_kernel(h_ref, w_ref, *refs):
    q_refs = refs[:-2]
    held, sems = refs[-2:]
    groups = held.shape[1] // BC
    rows = q_refs[0].shape[0]

    def copy(b):
        across = pl.ds(pl.multiple_of(b * BC, BC), BC)
        return pltpu.make_async_copy(w_ref.at[:, across], held.at[:, across], sems.at[b])

    @pl.loop(0, groups)
    def _(b):
        copy(b).start()

    @pl.loop(0, groups)
    def _(b):
        copy(b).wait()
        across = pl.ds(pl.multiple_of(b * BC, BC), BC)
        made = dot(h_ref[...], held[:, across]).astype(low_type)
        for m, ref in enumerate(q_refs):
            ref[:, across] = made[m * rows : (m + 1) * rows]


def make_queries(h, w, micros):
    total, width = h.shape
    q_width = HEADS * HD
    return call(
        query_kernel,
        tuple([shaped((total // micros, q_width), low_type)] * micros),
        [in_vmem, in_any],
        tuple([in_vmem] * micros),
        [pltpu.VMEM((width, q_width), low_type), pltpu.SemaphoreType.DMA((q_width // BC,))],
        2 * total * width * q_width,
        2 * width * q_width,
    )(h, w)


def load_keys(parts, held, sem):
    start = 0
    for part in parts:
        count = part.shape[0]
        pltpu.make_async_copy(part, held.at[pl.ds(start, count)], sem).start()
        start += count


def attend_kernel(count, q_ref, rpos_ref, kpos_ref, x_ref, gain_ref, w_ref, *refs):
    parts = refs[:count]
    ob_ref, log_ref, x2_ref, h2_ref, bias, kv_ref, held, sems = refs[count:]
    rows = q_ref.shape[0]
    load_keys(parts, kv_ref, sems.at[0])
    pltpu.make_async_copy(w_ref, held, sems.at[1]).start()
    bias[...] = jnp.where(kpos_ref[...] <= rpos_ref[...], 0.0, masked_score)
    log_ref[...] = jnp.zeros_like(log_ref)
    length = kv_ref.shape[0]
    wait_bytes(kv_ref, sems.at[0])

    @pl.loop(0, KVH // 2)
    def _(pair):
        lane = pl.multiple_of(pair * LANES, LANES)
        keys = kv_ref[:, pl.ds(lane, LANES)]
        values = kv_ref[:, pl.ds(pl.multiple_of(lane + KVH * HD, LANES), LANES)]
        stacked = stack_heads(q_ref, pair, HD**-0.5)
        mixed = []
        for part in range(2):
            scores = dot(stacked[part].astype(low_type), keys, NT)
            scores = (scores.reshape(3, rows, length) + bias[...][None]).reshape(3 * rows, length)
            largest = jnp.max(scores, axis=-1, keepdims=True)
            raised = jnp.exp(scores - largest)
            summed = jnp.sum(raised, axis=-1, keepdims=True)
            mixed.append(dot(raised.astype(low_type), values) / summed)
            log_ref[...] = jnp.where(
                lane_ids(log_ref.shape) == 2 * pair + part, largest + jnp.log(summed), log_ref[...]
            )
        unstack_heads(ob_ref, pair, mixed[0], mixed[1])

    wait_bytes(held, sems.at[1])
    for n in range(held.shape[0] // BC):
        cut = slice(n * BC, (n + 1) * BC)
        x2_ref[:, cut] = x_ref[:, cut] + dot(ob_ref[...], held[cut, :], NT)
    h2_ref[...] = unit_rows(x2_ref[...], gain_ref[1:2])[0].astype(low_type)


def attend(q, kv_parts, rows_pos, key_pos, x, gains, w):
    rows, width = q.shape
    length = key_pos.shape[1]
    model = x.shape[1]
    return call(
        functools.partial(attend_kernel, len(kv_parts)),
        (
            shaped((rows, width), low_type),
            shaped((3 * rows, LANES), jnp.float32),
            shaped((rows, model), jnp.float32),
            shaped((rows, model), low_type),
        ),
        [in_vmem] * 5 + [in_any] * (1 + len(kv_parts)),
        (in_vmem,) * 4,
        [
            pltpu.VMEM((rows, length), jnp.float32),
            pltpu.VMEM((length, kv_parts[0].shape[1]), low_type),
            pltpu.VMEM((model, width), low_type),
            pltpu.SemaphoreType.DMA((2,)),
        ],
        16 * rows * length * width,
        8 * MIB,
    )(q, rows_pos, key_pos, x, gains, w, *kv_parts)


def router_parts(h2, router, experts):
    logits = dot(h2, router)
    logits = jnp.where(lane_ids(logits.shape) < experts, logits, masked_score)
    raised = jnp.exp(logits - jnp.max(logits, axis=-1, keepdims=True))
    return raised / jnp.sum(raised, axis=-1, keepdims=True)


def expert_kernel(sources, micro, order_ref, me_ref, router_ref, *refs):
    h_parts = refs[:sources]
    c_parts = refs[sources : 2 * sources]
    w_ref = refs[2 * sources]
    outs = refs[2 * sources + 1 :]
    back_refs = outs[:sources]
    z_ref, dg_ref, du_ref, cs, xs_ref = outs[sources : sources + 5]
    held, chance, load_sem, w_sems = outs[sources + 5 :]
    rows, width = h_parts[0].shape
    row_groups = width // BR
    col_groups = FF // BC
    for j in range(sources):
        pltpu.make_async_copy(h_parts[j], xs_ref.at[pl.ds(j * rows, rows)], load_sem.at[0]).start()
        pltpu.make_async_copy(
            c_parts[j].at[pl.ds(micro * rows, rows)], cs.at[pl.ds(j * rows, rows)], load_sem.at[1]
        ).start()
    for b in range(col_groups):

        @pl.loop(0, row_groups)
        def _(a):
            for k in range(3):
                pltpu.make_async_copy(
                    w_ref.at[order_ref[(k * row_groups + a) * col_groups + b]],
                    held.at[k, pl.ds(pl.multiple_of(a * BR, 64), BR), pl.ds(b * BC, BC)],
                    w_sems.at[b],
                ).start()

    wait_bytes(xs_ref, load_sem.at[0])
    wait_bytes(cs, load_sem.at[1])
    me = me_ref[1]
    probs = router_parts(xs_ref[...], router_ref[...], sources)
    hits = cs[:, width:].astype(jnp.float32)
    mine = lane_ids(hits.shape) == me
    hit = jnp.sum(jnp.where(mine, hits, 0.0), axis=-1, keepdims=True)
    weight = jnp.sum(jnp.where(mine, probs, 0.0), axis=-1, keepdims=True) * hit
    chance[...] = jnp.zeros_like(chance)

    @pl.loop(0, col_groups)
    def _(b):
        cut = pl.ds(pl.multiple_of(b * BC, BC), BC)
        wait_bytes(held.at[:, :, cut], w_sems.at[b])
        gate = dot(xs_ref[...], held[0, :, cut])
        up = dot(xs_ref[...], held[1, :, cut])
        down = dot(cs[:, :width], held[2, :, cut])
        sig = jax.nn.sigmoid(gate)
        act = gate * sig
        hidden = act * up
        chance[...] += jnp.sum(down * hidden, axis=-1, keepdims=True)
        z_ref[:, cut] = (hidden * weight).astype(low_type)
        down = down * weight
        dg_ref[:, cut] = (down * up * (sig + act * (1.0 - sig))).astype(low_type)
        du_ref[:, cut] = (down * act).astype(low_type)

    for n in range(width // BC):
        cut = slice(n * BC, (n + 1) * BC)
        back = dot(dg_ref[...], held[0, cut, :], NT) + dot(du_ref[...], held[1, cut, :], NT)
        for j in range(sources):
            back_refs[j][:, cut] = back[j * rows : (j + 1) * rows].astype(low_type)
    told = chance[...] * hit
    high_part = told.astype(low_type)
    low_part = (told - high_part.astype(jnp.float32)).astype(low_type)
    lanes = lane_ids((sources * rows, LANES))
    tail = jnp.where(lanes == 0, high_part, jnp.where(lanes == 1, low_part, jnp.zeros_like(low_part)))
    for j in range(sources):
        back_refs[j][:, width:] = tail[j * rows : (j + 1) * rows]


def run_expert(micro, order, me, router, h_parts, c_parts, w):
    sources = len(h_parts)
    rows, width = h_parts[0].shape
    total = sources * rows
    return call(
        functools.partial(expert_kernel, sources, micro),
        tuple(
            [shaped((rows, width + LANES), low_type)] * sources
            + [shaped((total, FF), low_type)] * 3
            + [shaped((total, width + LANES), low_type), shaped((total, width), low_type)]
        ),
        [in_smem, in_smem, in_vmem] + [in_any] * (2 * sources + 1),
        tuple([in_vmem] * (sources + 5)),
        [
            pltpu.VMEM((3, width, FF), low_type),
            pltpu.VMEM((total, 1), jnp.float32),
            pltpu.SemaphoreType.DMA((2,)),
            pltpu.SemaphoreType.DMA((FF // BC,)),
        ],
        10 * total * width * FF,
        20 * MIB,
    )(order, me, router, *h_parts, *c_parts, w)


def produce_kernel(sources, order_ref, w_ref, *refs):
    out_refs = refs[-3 - sources : -3]
    z_refs = refs[: -3 - sources]
    zs, held, sem = refs[-3:]
    width = held.shape[0]
    total = z_refs[0].shape[0]
    rows = total // sources
    row_groups, col_groups = width // BR, FF // BC

    @pl.loop(0, row_groups)
    def _(a):
        for b in range(col_groups):
            pltpu.make_async_copy(
                w_ref.at[order_ref[(2 * row_groups + a) * col_groups + b]],
                held.at[pl.ds(pl.multiple_of(a * BR, 64), BR), pl.ds(b * BC, BC)],
                sem,
            ).start()

    for m, z_ref in enumerate(z_refs):
        zs[m * total : (m + 1) * total] = z_ref[...]
    wait_bytes(held, sem)
    for n in range(width // BC):
        cut = slice(n * BC, (n + 1) * BC)
        made = dot(zs[...], held[cut, :], NT).astype(low_type)
        for m in range(len(z_refs)):
            for j in range(sources):
                start = m * total + j * rows
                out_refs[j][m * rows : (m + 1) * rows, cut] = made[start : start + rows]


def produce(order, w, zs, sources, width):
    micros = len(zs)
    total = zs[0].shape[0]
    return call(
        functools.partial(produce_kernel, sources),
        tuple([shaped((micros * total // sources, width), low_type)] * sources),
        [in_smem, in_any] + [in_vmem] * micros,
        tuple([in_vmem] * sources),
        [
            pltpu.VMEM((micros * total, FF), low_type),
            pltpu.VMEM((width, FF), low_type),
            pltpu.SemaphoreType.DMA,
        ],
        2 * micros * total * width * FF,
        8 * MIB,
    )(order, w, *zs)


def outer_kernel(place, widths, side, order_ref, *refs):
    count = len(widths)
    micros = len(refs[:-3]) // (2 * count)
    lefts = refs[: count * micros]
    rights = refs[count * micros : 2 * count * micros]
    out_ref, stage, sems = refs[-3:]
    span = 2 * BR
    steps = []
    for k in range(count):
        for p in range(widths[k] // span):
            steps.append((k, p))

    def wait_stage(slot, cols):
        wait_bytes(stage.at[slot, :, pl.ds(0, cols)], sems.at[slot])

    used = [None, None]
    for n, (k, p) in enumerate(steps):
        slot = n % 2
        cols = rights[k * micros].shape[-1]
        if used[slot] is not None:
            wait_stage(slot, used[slot])
        used[slot] = cols // 2
        cut = slice(p * span, (p + 1) * span)
        made = 0.0
        for m in range(micros):
            left = lefts[k * micros + m][:, cut]
            right = jnp.concatenate(
                [
                    rights[k * micros + m][:, start : start + LANES]
                    for start in range(side * LANES, cols, BC)
                ],
                axis=1,
            )
            made = made + dot(left, right, TN)
        stage[slot, :, : cols // 2] = made.astype(low_type)
        first, row_step = place(k)
        for half in range(2):
            for b in range(cols // BC):
                pltpu.make_async_copy(
                    stage.at[slot, pl.ds(half * BR, BR), pl.ds(b * LANES, LANES)],
                    out_ref.at[order_ref[first + (2 * p + half) * row_step + b]],
                    sems.at[slot],
                ).start()
    for slot in range(2):
        if used[slot] is not None:
            wait_stage(slot, used[slot])


def outer_blocks(order, place, widths, side, lefts, rights, blocks):
    widest = max(r[0].shape[-1] for r in rights)
    rows = sum(l.shape[0] for l in lefts[0])
    flat = [l for group in lefts for l in group] + [r for group in rights for r in group]
    return call(
        functools.partial(outer_kernel, place, widths, side),
        shaped((blocks, BR, LANES), low_type),
        [in_smem] + [in_vmem] * len(flat),
        in_any,
        [pltpu.VMEM((2, 2 * BR, widest // 2), low_type), pltpu.SemaphoreType.DMA((2,))],
        rows * blocks * BR * BC,
        blocks * BR * BC + sum(f.size * 2 for f in flat),
    )(order, *flat)


def xor_plan(members, offset):
    if members != 4:
        return list(range(1, members)), [0]
    first = 1 if offset % 2 else 2
    return [first, 3], [0, 3 - first]


def slots_kernel(
    counts, chips, members, slots, all_groups, in_groups, order_ref, me_ref, *refs
):
    lists = []
    for count in counts:
        lists.append(refs[:count])
        refs = refs[count:]
    outs = refs[: 2 * chips]
    lefts, turned, rights, sems = refs[2 * chips :]
    ctx, shard = me_ref[0], me_ref[1]
    chip, core = lax.div(ctx, 2), lax.rem(ctx, 2)
    h_width = lefts.shape[2]
    q_width = lists[2][0].shape[1]
    kv_width = lists[3][0].shape[1]
    total = rights.shape[0]
    targets = (
        (lefts.at[0], 0, h_width, 0),
        (lefts.at[1], 0, h_width, 1),
        (rights, 0, q_width, 2),
        (rights, q_width, kv_width, 2),
        (rights, q_width + kv_width, q_width, 2),
    )
    for group, (target, lane, lanes, sem) in zip(lists, targets):
        start = 0
        for ref in group:
            pltpu.make_async_copy(
                ref, target.at[pl.ds(start, ref.shape[0]), pl.ds(lane, lanes)], sems.at[sem]
            ).start()
            start += ref.shape[0]
    for side in range(2):
        wait_bytes(lefts.at[side], sems.at[side])
        for r in range(0, total, LANES):
            turned[side, :, r : r + LANES] = lefts[side, r : r + LANES, :].T
    wait_bytes(rights, sems.at[2])
    for offset in range(chips):
        there = lax.rem(chip - offset + chips, chips) * 2 + core
        for out, hops in zip(outs[2 * offset : 2 * offset + 2], xor_plan(members, offset)):
            for place, hop in enumerate(hops):
                base = (there * members + jnp.bitwise_xor(shard, hop)) * slots

                @pl.loop(0, slots)
                def _(i):
                    number = order_ref[base + i]
                    a, b = lax.div(number, all_groups), lax.rem(number, all_groups)
                    side = (b >= in_groups).astype(jnp.int32)
                    out[place * slots + i] = dot(
                        turned[side, pl.ds(pl.multiple_of(a * BR, 64), BR), :],
                        rights[:, pl.ds(pl.multiple_of(b * BC, BC), BC)],
                    ).astype(low_type)


def slot_blocks(chips, members, slots, order, me, h1, da, dq, dkv, ob):
    lists = (h1, da, dq, dkv, ob)
    total = sum(part.shape[0] for part in h1)
    width = h1[0].shape[1]
    in_width = dq[0].shape[1] + dkv[0].shape[1]
    all_width = in_width + ob[0].shape[1]
    outs = []
    for offset in range(chips):
        for hops in xor_plan(members, offset):
            outs.append(shaped((len(hops) * slots, BR, BC), low_type))
    made = call(
        functools.partial(
            slots_kernel,
            tuple(len(group) for group in lists),
            chips,
            members,
            slots,
            all_width // BC,
            in_width // BC,
        ),
        tuple(outs),
        [in_smem, in_smem] + [in_any] * sum(len(group) for group in lists),
        (in_vmem,) * len(outs),
        [
            pltpu.VMEM((2, total, width), low_type),
            pltpu.VMEM((2, width, total), low_type),
            pltpu.VMEM((total, all_width), low_type),
            pltpu.SemaphoreType.DMA((3,)),
        ],
        2 * total * chips * members * slots * BR * BC,
        16 * MIB,
    )(order, me, *[part for group in lists for part in group])
    return [(made[2 * offset], made[2 * offset + 1]) for offset in range(chips)]


def merge_kernel(
    sources, me_ref, x2_ref, cot_ref, h2_ref, gain_ref, router_ref, w_ref, *refs
):
    back_refs = refs[:sources]
    dx_ref, da_ref, do_ref, stat_ref, held, sem = refs[sources:]
    rows, width = x2_ref.shape
    pltpu.make_async_copy(w_ref, held, sem).start()
    lanes = lane_ids((rows, LANES))
    prob_grad = jnp.zeros((rows, LANES), jnp.float32)
    gathered = jnp.zeros((rows, width), jnp.float32)
    for j in range(sources):
        tail = back_refs[j][:, width:].astype(jnp.float32)
        told = jnp.sum(tail, axis=-1, keepdims=True)
        expert = jnp.bitwise_xor(me_ref[1], j)
        prob_grad = prob_grad + jnp.where(lanes == expert, told, 0.0)
        gathered = gathered + back_refs[j][:, :width].astype(jnp.float32)
    h2 = h2_ref[...]
    probs = router_parts(h2, router_ref[...], sources)
    logit_grad = probs * (prob_grad - jnp.sum(probs * prob_grad, axis=-1, keepdims=True))
    high_part = logit_grad.astype(low_type)
    low_part = (logit_grad - high_part.astype(jnp.float32)).astype(low_type)
    router_grad = dot(high_part, h2, TN) + dot(low_part, h2, TN)
    gathered = gathered + dot(high_part, router_ref[...], NT) + dot(low_part, router_ref[...], NT)
    x2 = x2_ref[...]
    inverse = lax.rsqrt(jnp.mean(x2 * x2, axis=-1, keepdims=True) + norm_eps)
    moe_grad, gain_grad = unit_back(x2, gain_ref[1:2], inverse, gathered)
    after = cot_ref[...] + moe_grad
    dx_ref[...] = after
    da_ref[...] = after.astype(low_type)
    experts_up = stat_ref.shape[0] - 8
    stat_ref[:experts_up] = router_grad[:experts_up]
    stat_ref[experts_up:] = jnp.broadcast_to(gain_grad, (8, width))
    wait_bytes(held, sem)
    for n in range(held.shape[1] // BC):
        cut = slice(n * BC, (n + 1) * BC)
        do_ref[:, cut] = dot(da_ref[...], held[:, cut]).astype(low_type)


def merge(me, x2, cot, h2, gains, router, w, backs):
    rows, width = x2.shape
    sources = len(backs)
    experts_up = -(-sources // 8) * 8
    return call(
        functools.partial(merge_kernel, sources),
        (
            shaped((rows, width), jnp.float32),
            shaped((rows, width), low_type),
            shaped((rows, HEADS * HD), low_type),
            shaped((experts_up + 8, width), jnp.float32),
        ),
        [in_smem] + [in_vmem] * 5 + [in_any] + [in_vmem] * sources,
        (in_vmem,) * 4,
        [pltpu.VMEM((width, HEADS * HD), low_type), pltpu.SemaphoreType.DMA],
        2 * rows * width * HEADS * HD,
        10 * MIB,
    )(me, x2, cot, h2, gains, router, w, *backs)


def attend_back_kernel(count, q_ref, rpos_ref, kpos_ref, ob_ref, log_ref, do_ref, *refs):
    parts = refs[:count]
    dq_ref, own_ref, other_ref, bias, kv_ref, sem = refs[count:]
    rows = q_ref.shape[0]
    load_keys(parts, kv_ref, sem)
    length = kv_ref.shape[0]
    bias[...] = jnp.where(kpos_ref[...] <= rpos_ref[...], 0.0, masked_score)
    wait_bytes(kv_ref, sem)

    @pl.loop(0, KVH // 2)
    def _(pair):
        lane = pl.multiple_of(pair * LANES, LANES)
        value_lane = pl.multiple_of(lane + KVH * HD, LANES)
        keys = kv_ref[:, pl.ds(lane, LANES)]
        values = kv_ref[:, pl.ds(value_lane, LANES)]
        queries = stack_heads(q_ref, pair, HD**-0.5)
        grads = stack_heads(do_ref, pair)
        mixes = stack_heads(ob_ref, pair)
        query_grads = []
        key_grad = value_grad = None
        for part in range(2):
            query = queries[part].astype(low_type)
            grad = grads[part].astype(low_type)
            log_total = jnp.sum(
                jnp.where(lane_ids(log_ref.shape) == 2 * pair + part, log_ref[...], 0.0),
                axis=-1,
                keepdims=True,
            )
            delta = jnp.sum(grads[part] * mixes[part], axis=-1, keepdims=True)
            scores = dot(query, keys, NT)
            scores = (scores.reshape(3, rows, length) + bias[...][None]).reshape(3 * rows, length)
            chance = jnp.exp(scores - log_total)
            prob_grad = dot(grad, values, NT)
            score_grad = (chance * (prob_grad - delta)).astype(low_type)
            value_term = dot(chance.astype(low_type), grad, TN)
            key_term = dot(score_grad, query, TN)
            key_grad = key_term if part == 0 else key_grad + key_term
            value_grad = value_term if part == 0 else value_grad + value_term
            query_grads.append(dot(score_grad, keys) * HD**-0.5)
        unstack_heads(dq_ref, pair, query_grads[0], query_grads[1])
        half = length // 2
        for ref, cut in ((own_ref, slice(0, half)), (other_ref, slice(half, length))):
            ref[:, pl.ds(lane, LANES)] = key_grad[cut].astype(low_type)
            ref[:, pl.ds(value_lane, LANES)] = value_grad[cut].astype(low_type)


def attend_back(q, kv_parts, rows_pos, key_pos, ob, log_total, do):
    rows, width = q.shape
    length = key_pos.shape[1]
    kv_width = kv_parts[0].shape[1]
    return call(
        functools.partial(attend_back_kernel, len(kv_parts)),
        (shaped((rows, width), low_type),) + (shaped((length // 2, kv_width), low_type),) * 2,
        [in_vmem] * 6 + [in_any] * len(kv_parts),
        (in_vmem,) * 3,
        [
            pltpu.VMEM((rows, length), jnp.float32),
            pltpu.VMEM((length, kv_width), low_type),
            pltpu.SemaphoreType.DMA,
        ],
        40 * rows * length * width,
        8 * MIB,
    )(q, rows_pos, key_pos, ob, log_total, do, *kv_parts)


def query_back_kernel(w_ref, *refs):
    micros = (len(refs) - 3) // 2
    dq_refs, out_refs = refs[:micros], refs[micros : 2 * micros]
    rows_ref, held, sem = refs[2 * micros :]
    rows = dq_refs[0].shape[0]
    copy = pltpu.make_async_copy(w_ref.at[:, pl.ds(0, held.shape[1])], held, sem)
    copy.start()
    for m in range(micros):
        rows_ref[m * rows : (m + 1) * rows] = dq_refs[m][...]
    copy.wait()
    for n in range(held.shape[0] // BC):
        cut = slice(n * BC, (n + 1) * BC)
        made = dot(rows_ref[...], held[cut, :], NT)
        for m in range(micros):
            out_refs[m][:, cut] = made[m * rows : (m + 1) * rows]


def query_back(w, dqs):
    micros = len(dqs)
    rows, q_width = dqs[0].shape
    width = w.shape[0]
    return call(
        query_back_kernel,
        tuple([shaped((rows, width), jnp.float32)] * micros),
        [in_any] + [in_vmem] * micros,
        tuple([in_vmem] * micros),
        [
            pltpu.VMEM((micros * rows, q_width), low_type),
            pltpu.VMEM((width, q_width), low_type),
            pltpu.SemaphoreType.DMA,
        ],
        2 * micros * rows * width * q_width,
        7 * MIB,
    )(w, *dqs)


def input_kernel(x_ref, gain_ref, w_ref, *refs):
    micros, rows = x_ref.shape[:2]
    dx_refs = refs[:micros]
    part_refs = refs[micros : 2 * micros]
    dkv_refs = refs[2 * micros : 3 * micros]
    out_ref, stat_ref, rows_ref, grad, held, sem = refs[3 * micros :]
    kv_width = held.shape[1]
    copy = pltpu.make_async_copy(
        w_ref.at[:, pl.ds(w_ref.shape[1] - kv_width, kv_width)], held, sem
    )
    copy.start()
    for m in range(micros):
        rows_ref[m * rows : (m + 1) * rows] = dkv_refs[m][...]
    copy.wait()
    for n in range(held.shape[0] // BC):
        cut = slice(n * BC, (n + 1) * BC)
        made = dot(rows_ref[...], held[cut, :], NT)
        for m in range(micros):
            grad[m, :, cut] = part_refs[m][:, cut] + made[m * rows : (m + 1) * rows]
    total = jnp.zeros((1, x_ref.shape[-1]), jnp.float32)
    for m in range(micros):
        x = x_ref[m]
        inverse = lax.rsqrt(jnp.mean(x * x, axis=-1, keepdims=True) + norm_eps)
        term, gain_grad = unit_back(x, gain_ref[0:1], inverse, grad[m])
        out_ref[m] = dx_refs[m][...] + term
        total = total + gain_grad
    stat_ref[...] = jnp.broadcast_to(total, stat_ref.shape)


def input_back(x, gains, w, dxs, parts, dkvs):
    micros, rows, width = x.shape
    kv_width = dkvs[0].shape[1]
    return call(
        input_kernel,
        (shaped(x.shape, jnp.float32), shaped((8, width), jnp.float32)),
        [in_vmem, in_vmem, in_any] + [in_vmem] * (3 * micros),
        (in_vmem,) * 2,
        [
            pltpu.VMEM((micros * rows, kv_width), low_type),
            pltpu.VMEM(x.shape, jnp.float32),
            pltpu.VMEM((width, kv_width), low_type),
            pltpu.SemaphoreType.DMA,
        ],
        2 * micros * rows * width * kv_width,
        14 * MIB,
    )(x, gains, w, *dxs, *parts, *dkvs)


def rotate_kernel(b_ref, m_ref, s_ref, l_ref, r_ref, *refs):
    grad_ref, new_ref, moment_ref, second_ref = refs[-4:]
    parts = [ref[0].astype(jnp.float32) for ref in refs[:-4]]
    gradient = parts[0] if len(parts) == 1 else jnp.concatenate(parts, axis=1)
    grad_ref[0] = gradient
    left = l_ref[0].astype(low_type)
    right = r_ref[0].astype(low_type)
    rotated = dot(dot(left, gradient.astype(low_type), TN).astype(low_type), right)
    moment = beta_one * m_ref[0] + (1.0 - beta_one) * rotated
    second = beta_two * s_ref[0] + (1.0 - beta_two) * rotated * rotated
    moment_ref[0] = moment
    second_ref[0] = second
    direction = (moment / (jnp.sqrt(second) + adam_eps)).astype(low_type)
    turned = dot(dot(left, direction).astype(low_type), right, NT)
    new_ref[0] = b_ref[0] - rate * turned


def rotate(weight, gradients, moment, second, left, right):
    count = weight.shape[0]

    def spec(rows, cols):
        return pl.BlockSpec((1, rows, cols), lambda i: (i, 0, 0))

    block = spec(BR, BC)
    return pl.pallas_call(
        rotate_kernel,
        grid=(count,),
        out_shape=(shaped(weight.shape, jnp.float32),) * 4,
        in_specs=[block] * 3
        + [spec(BR, BR), spec(BC, BC)]
        + [spec(BR, part.shape[2]) for part in gradients],
        out_specs=(block,) * 4,
        compiler_params=pltpu.CompilerParams(vmem_limit_bytes=VMEM_LIMIT),
        cost_estimate=pl.CostEstimate(
            flops=4 * count * BR * BC * (BR + BC),
            bytes_accessed=count * 2 * MIB,
            transcendentals=0,
        ),
    )(weight, moment, second, left, right, *gradients)


def adam(weight, gradient, moment, second, step_rate):
    moment_new = beta_one * moment + (1.0 - beta_one) * gradient
    second_new = beta_two * second + (1.0 - beta_two) * gradient * gradient
    return (
        weight - step_rate * moment_new / (jnp.sqrt(second_new) + adam_eps),
        moment_new,
        second_new,
    )


def to_partner(array, offset):
    if offset == 0:
        return array
    count = lax.axis_size("shard")
    return lax.ppermute(array, "shard", [(i, i ^ offset) for i in range(count)])


def to_ctx(array, offset):
    count = lax.axis_size("ctx")
    return lax.ppermute(array, "ctx", [(i, i ^ offset) for i in range(count)])


def to_chip(array, offset):
    count = lax.axis_size("ctx")
    return lax.ppermute(array, "ctx", [(i, (i + 2 * offset) % count) for i in range(count)])


def after(value, *others):
    return lax.optimization_barrier((value, others))[0]


def from_chips(array, chips):
    return [array] + [to_chip(array, offset) for offset in range(1, chips)]


def wide(array):
    return array.astype(jnp.float32)


def sum_to_chips(parts):
    total = wide(parts[0])
    for offset in range(1, len(parts)):
        total = total + wide(to_chip(parts[offset], -offset))
    return total


def gather_weights(blocks, chips, members):
    parts = from_chips(blocks, chips)
    pieces, arrays = [], []
    gate = []

    def add(array, offset, first, cut):
        pieces.append((0, offset, first, cut))
        arrays.append(array)
        pieces.append((1, offset, first, cut))
        arrays.append(to_ctx(after(array, *gate), 1))
        return array

    def spread(group, first):
        add(group, 0, first, 0)
        if members == 4 and first > 0:
            by_one, by_two = to_partner(group, 1), to_partner(group, 2)
            add(by_one, 1, first, 0)
            add(by_two, 2, first, 0)
            half = BR // 2
            add(to_partner(by_one[:, :half], 2), 3, first, 0)
            add(to_partner(by_two[:, half:], 1), 3, first, half)
            return [by_one, by_two]
        got = [to_partner(group, offset) for offset in range(1, members)]
        for offset in range(1, members):
            add(got[offset - 1], offset, first, 0)
        return got

    got = [to_partner(blocks, offset) for offset in range(1, members)]
    gate.append(got[0])
    add(blocks, 0, 0, 0)
    for offset in range(1, members):
        add(got[offset - 1], offset, 0, 0)
    last = list(got)
    if chips > 1:
        last = spread(after(parts[1], *last), 1)
        gate[:] = last
        got = last
    if chips > 2:
        group = after(jnp.concatenate(parts[2:], axis=0), *last)
        spread(group, 2)
    return got + parts[1:], pieces, arrays


def sum_slots(made, chips, members, slots):
    sums, first_got = [], []
    for offset in range(chips):
        sent, kept = made[offset]
        hops, keeps = xor_plan(members, offset)
        total = wide(kept[:slots])
        if members == 4:
            first, second = hops[0], keeps[1]
            got = to_partner(sent, first)
            total = total + wide(got[:slots])
            relay = (wide(kept[slots:]) + wide(got[slots:])).astype(low_type)
            total = total + wide(to_partner(relay, second))
        else:
            for place, hop in enumerate(hops):
                got = to_partner(sent[place * slots : (place + 1) * slots], hop)
                total = total + wide(got)
        sums.append(total if offset == 0 else total.astype(low_type))
        first_got.append(got)
    return sums, first_got


def sum_all(array):
    step = 1
    while step < lax.axis_size("ctx"):
        array = array + to_ctx(array, step)
        step *= 2
    step = 1
    while step < lax.axis_size("shard"):
        array = array + to_partner(array, step)
        step *= 2
    return array


def shards(
    tokens,
    cotangent,
    norm_gains,
    router,
    dense_weight,
    expert_weight,
    routes,
    assign,
    dense_order,
    expert_order,
    dense_moment,
    dense_second,
    dense_left,
    dense_right,
    expert_moment,
    expert_second,
    expert_left,
    expert_right,
    gains_moment,
    gains_second,
    router_moment,
    router_second,
):
    ctx_count = lax.axis_size("ctx")
    shard_count = lax.axis_size("shard")
    chips = ctx_count // 2
    micros, rows, width = tokens.shape
    slots = dense_weight.shape[0]
    span = rows // 2
    row_groups = width // BR
    ff_groups = FF // BC
    expert_blocks = 3 * row_groups * ff_groups

    expert_inverse = inverse_order(expert_order)
    ctx = lax.axis_index("ctx").astype(jnp.int32)
    me = jnp.stack([ctx, lax.axis_index("shard").astype(jnp.int32)])
    row_ids = jnp.arange(rows, dtype=jnp.int32)
    all_pos = assign[:, row_ids // span] * span + row_ids % span
    ring_ids = (ctx // 2 - jnp.arange(chips, dtype=jnp.int32)) % chips * 2
    key_ids = jnp.concatenate([ring_ids + ctx % 2, ring_ids + (1 - ctx % 2)])
    key_pos = all_pos[key_ids].reshape(1, rows * ctx_count)
    rows_pos = all_pos[ctx].reshape(rows, 1)
    router_pad = jnp.pad(router.astype(low_type), ((0, 0), (0, LANES - shard_count)))

    far, pieces, arrays = gather_weights(dense_weight.astype(low_type), chips, shard_count)
    expert_low = after(expert_weight[0].astype(low_type), *far)
    expert_all = lax.all_gather(expert_low, "ctx", axis=0, tiled=True)

    lanes = jnp.arange(LANES, dtype=jnp.int32)
    hits = jnp.sum((routes[..., None] == lanes).astype(low_type), axis=2)
    cot_rows = jnp.concatenate([cotangent.astype(low_type), hits], axis=2)
    cot_rows = cot_rows.reshape(micros * rows, width + LANES)
    cot_rows = after(cot_rows, *arrays[::2])
    cot_parts = [to_partner(cot_rows, j) for j in range(shard_count)]

    here, expert_inverse, router_pad, key_pos, rows_pos = lax.optimization_barrier(
        (me, expert_inverse, router_pad, key_pos, rows_pos)
    )
    h1, kv, w_in, w_out = project(
        pieces,
        arrays,
        chips,
        shard_count,
        slots,
        dense_order,
        here,
        [tokens[m] for m in range(micros)],
        norm_gains,
    )
    q = make_queries(h1, w_in, micros)
    h1_other = to_ctx(h1, 1)
    kvs, obs, logs, x2s, h2s = [], [], [], [], []
    chip_kv = []
    for m in range(micros):
        own = kv[m] if m == 0 else after(kv[m], chip_kv[m - 1][1 % chips])
        chip_kv.append(from_chips(own, chips))
    for m in range(micros):
        query = after(q[m], *(cot_parts if m == 0 else obs[m - 1 : m]))
        parts = chip_kv[m]
        swapped = after(parts, q[0] if m == 0 else obs[m - 1])
        kvs.append(parts + [to_ctx(part, 1) for part in swapped])
        ob, log_total, x2, h2 = attend(
            query, kvs[m], rows_pos, key_pos, tokens[m], norm_gains, w_out
        )
        obs.append(ob)
        logs.append(log_total)
        x2s.append(x2)
        h2s.append(h2)
    ob_others = [to_ctx(ob, 1) for ob in obs]

    h_parts = []
    for m in range(micros):
        own = h2s[m] if m == 0 else after(h2s[m], *h_parts[m - 1])
        h_parts.append([own] + [to_partner(own, j) for j in range(1, shard_count)])
    sent = []
    zs, dgs, dus, cs, xs = [], [], [], [], []
    for m in range(micros):
        here = after(me, h2s[-1], h1_other, *ob_others) if m == 0 else after(me, zs[-1])
        made = run_expert(m, expert_inverse, here, router_pad, h_parts[m], cot_parts, expert_all)
        sent.append(made[:shard_count])
        z, dg, du, c, x = made[shard_count:]
        zs.append(z)
        dgs.append(dg)
        dus.append(du)
        cs.append(c)
        xs.append(x)
    backs = [[to_partner(sent[m][j], j) for j in range(shard_count)] for m in range(micros)]

    dxs, das, dqs, stats, own_grads = [], [], [], [], []
    for m in range(micros):
        here = after(me, zs[-1] if m == 0 else dqs[-1])
        dx, da, do, stat = merge(
            here, x2s[m], cotangent[m], h2s[m], norm_gains, router_pad, w_out, backs[m]
        )
        dq, dkv_own, dkv_other = attend_back(
            q[m], kvs[m], rows_pos, key_pos, obs[m], logs[m], do
        )
        got = to_ctx(dkv_other, 1)
        parts = []
        for o in range(chips):
            cut = slice(o * rows, (o + 1) * rows)
            part = wide(dkv_own[cut]) + wide(got[cut])
            parts.append(part if o == 0 else part.astype(low_type))
        own_grads.append(parts)
        dxs.append(dx)
        das.append(da)
        dqs.append(dq)
        stats.append(stat)

    far_sums = [
        to_chip(jnp.concatenate([parts[o] for parts in own_grads], axis=0), -o)
        for o in range(1, chips)
    ]
    dkvs = []
    for m in range(micros):
        total = own_grads[m][0]
        for part in far_sums:
            total = total + wide(part[m * rows : (m + 1) * rows])
        dkvs.append(total.astype(low_type))

    def other_core(parts):
        return [to_ctx(part, 1) for part in parts]

    da_others, dq_others = other_core(das), other_core(dqs)
    expert_sums = []
    for side in range(2):
        term = outer_blocks(
            expert_inverse if side == 0 else after(expert_inverse, *backs[-1]),
            lambda k: (k * row_groups * ff_groups, ff_groups),
            (width,) * 3,
            side,
            [xs, xs, cs],
            [dgs, dus, zs],
            expert_blocks,
        )
        expert_sums.append(lax.psum_scatter(term, "ctx", scatter_dimension=0, tiled=True))
    parts_back = query_back(w_in, dqs)
    made = produce(after(expert_inverse, dqs[0]), expert_all, zs, shard_count, width)
    arrived = [to_partner(made[j], j) for j in range(shard_count)]
    here = after(me, parts_back, *arrived)
    made = slot_blocks(
        chips,
        shard_count,
        slots,
        dense_order,
        here,
        [h1, h1_other],
        das + da_others,
        dqs + dq_others,
        dkvs + other_core(dkvs),
        obs + ob_others,
    )
    sums, got = sum_slots(made, chips, shard_count, slots)
    input_grad, gain_stat = input_back(
        after(tokens, *got[:2]), norm_gains, w_in, dxs, parts_back, dkvs
    )
    experts_up = stats[0].shape[0] - 8
    stat_rows = jnp.concatenate([sum(stats)[: experts_up + 1], gain_stat[:7]], axis=0)
    stat_rows = sum_all(stat_rows)
    router_grad = stat_rows[:shard_count].T
    gains_grad = jnp.stack([stat_rows[experts_up + 1], stat_rows[experts_up]])

    outputs = []
    for m in range(micros):
        total = x2s[m]
        for part in arrived:
            total = total + wide(part[m * rows : (m + 1) * rows])
        outputs.append(total)

    expert_grad, expert_new, expert_moment_new, expert_second_new = rotate(
        expert_weight[0], after(expert_sums, *sums), expert_moment[0], expert_second[0], expert_left[0], expert_right[0]
    )
    last = [sums[0]] + [to_chip(sums[o], -o) for o in range(1, chips)]
    last = after(last, expert_new)
    dense_sum = sum([wide(part) for part in last[1:]], last[0])
    dense_grad, dense_new, dense_moment_new, dense_second_new = rotate(
        dense_weight, [dense_sum], dense_moment, dense_second, dense_left, dense_right
    )
    gains_new, gains_moment_new, gains_second_new = adam(
        norm_gains, gains_grad, gains_moment, gains_second, gain_rate
    )
    router_new, router_moment_new, router_second_new = adam(
        router, router_grad, router_moment, router_second, rate
    )
    return (
        jnp.stack(outputs),
        input_grad,
        dense_grad,
        dense_new,
        dense_moment_new,
        dense_second_new,
        expert_grad[None],
        expert_new[None],
        expert_moment_new[None],
        expert_second_new[None],
        gains_grad,
        gains_new,
        gains_moment_new,
        gains_second_new,
        router_grad,
        router_new,
        router_moment_new,
        router_second_new,
    )


def solution(mesh):
    rows_spec = P("shard", "ctx", None)
    dense_spec = P(("ctx", "shard"), None, None)
    expert_spec = P("shard", "ctx", None, None)
    in_specs = (
        (rows_spec, rows_spec, P(), P(), dense_spec, expert_spec, rows_spec, P(), P(), P())
        + (dense_spec,) * 4
        + (expert_spec,) * 4
        + (P(),) * 4
    )
    out_specs = (rows_spec,) * 2 + (dense_spec,) * 4 + (expert_spec,) * 4 + (P(),) * 8
    return jax.shard_map(shards, mesh=mesh, in_specs=in_specs, out_specs=out_specs, check_vma=False)
```

```python
import functools

import jax
import jax.numpy as jnp
from jax import lax
from jax.experimental import pallas as pl
from jax.experimental.pallas import tpu as pltpu
from jax.sharding import PartitionSpec as P

HEADS = 24
KVH = 8
HD = 64
FF = 1024
BR = 192
BC = 256
LANES = 128

norm_eps = 1e-06
beta_one = 0.9
beta_two = 0.95
rate = 0.01
gain_rate = 0.5
adam_eps = 1e-08
masked_score = -1e30
low_type = jnp.bfloat16
MIB = 1 << 20
VMEM_LIMIT = 60 * MIB

NN = (((1,), (0,)), ((), ()))
NT = (((1,), (1,)), ((), ()))
TN = (((0,), (0,)), ((), ()))

in_vmem = pl.BlockSpec(memory_space=pltpu.VMEM)
in_smem = pl.BlockSpec(memory_space=pltpu.SMEM)
in_any = pl.BlockSpec(memory_space=pl.ANY)


def dot(left_side, right_side, dims=NN):
    return lax.dot_general(left_side, right_side, dims, preferred_element_type=jnp.float32)


def call(kernel, out_shapes, in_specs, out_specs, scratch, flops, moved):
    return pl.pallas_call(
        kernel,
        out_shape=out_shapes,
        in_specs=in_specs,
        out_specs=out_specs,
        scratch_shapes=scratch,
        compiler_params=pltpu.CompilerParams(vmem_limit_bytes=VMEM_LIMIT),
        cost_estimate=pl.CostEstimate(flops=flops, bytes_accessed=moved, transcendentals=0),
    )


def shaped(dims, kind):
    return jax.ShapeDtypeStruct(dims, kind)


def inverse_order(slot_order):
    count = slot_order.shape[0]
    numbers = jnp.arange(count, dtype=jnp.int32)
    return jnp.sum(
        jnp.where(slot_order[None, :] == numbers[:, None], numbers[None, :], 0), axis=1
    ).astype(jnp.int32)


def wait_bytes(landed, semaphore):
    pltpu.make_async_copy(landed, landed, semaphore).wait()


def unit_rows(rows, gain):
    inverse = lax.rsqrt(jnp.mean(rows * rows, axis=-1, keepdims=True) + norm_eps)
    return rows * inverse * gain, inverse


def unit_back(rows, gain, inverse, gradient):
    unit = rows * inverse
    scaled = gradient * gain
    inner = jnp.mean(scaled * unit, axis=-1, keepdims=True)
    return inverse * (scaled - unit * inner), jnp.sum(gradient * unit, axis=0, keepdims=True)


def lane_ids(dims):
    return lax.broadcasted_iota(jnp.int32, dims, len(dims) - 1)


def half_turn(tile):
    return pltpu.roll(tile, HD, 1)


def stack_heads(ref, pair, scale=None):
    base = pair * (3 * LANES)
    tiles = [
        ref[:, pl.ds(pl.multiple_of(base + LANES * t, LANES), LANES)].astype(jnp.float32)
        for t in range(3)
    ]
    if scale is not None:
        tiles = [t * scale for t in tiles]
    lower = lane_ids(tiles[0].shape) < HD
    first = [tiles[0], half_turn(tiles[0]), tiles[1]]
    second = [tiles[1], half_turn(tiles[2]), tiles[2]]
    return (
        jnp.concatenate([jnp.where(lower, t, 0.0) for t in first], axis=0),
        jnp.concatenate([jnp.where(lower, 0.0, t) for t in second], axis=0),
    )


def unstack_heads(ref, pair, first, second):
    rows = first.shape[0] // 3
    base = pair * (3 * LANES)
    lower = lane_ids((rows, LANES)) < HD
    tiles = (
        jnp.where(lower, first[:rows], half_turn(first[rows : 2 * rows])),
        jnp.where(lower, first[2 * rows :], second[:rows]),
        jnp.where(lower, half_turn(second[rows : 2 * rows]), second[2 * rows :]),
    )
    for t in range(3):
        ref[:, pl.ds(pl.multiple_of(base + LANES * t, LANES), LANES)] = tiles[t].astype(ref.dtype)


def project_kernel(
    pieces, chips, members, slots, all_groups, micros, order_ref, me_ref, *refs
):
    x_refs = refs[:micros]
    gain_ref = refs[micros]
    piece_refs = refs[micros + 1 : micros + 1 + len(pieces)]
    refs = refs[micros + 1 + len(pieces) :]
    h_ref = refs[0]
    kv_refs = refs[1 : 1 + micros]
    win_ref, wout_ref, held, held_out, sems, out_sems = refs[1 + micros :]
    groups = held.shape[1] // BC
    kv_groups = kv_refs[0].shape[-1] // BC
    rows = x_refs[0].shape[0]
    ctx, shard = me_ref[0], me_ref[1]
    chip, core = lax.div(ctx, 2), lax.rem(ctx, 2)

    for ref, (other_core, offset, first, cut) in zip(piece_refs, pieces):

        @pl.loop(0, ref.shape[0])
        def _(i):
            source = lax.rem(chip - (first + lax.div(i, slots)) + chips, chips) * 2
            source = source + jnp.bitwise_xor(core, other_core)
            source = source * members + jnp.bitwise_xor(shard, offset)
            number = order_ref[source * slots + lax.rem(i, slots)]
            a, b = lax.div(number, all_groups), lax.rem(number, all_groups)
            down = pl.ds(pl.multiple_of(a * BR + cut, 32), ref.shape[1])

            @pl.when(b < groups)
            def _():
                across = pl.ds(pl.multiple_of(b * BC, BC), BC)
                pltpu.make_async_copy(ref.at[i], held.at[down, across], sems.at[b]).start()

            @pl.when(b >= groups)
            def _():
                across = pl.ds(pl.multiple_of((b - groups) * BC, BC), BC)
                pltpu.make_async_copy(ref.at[i], held_out.at[down, across], sems.at[groups]).start()

    for m in range(micros):
        h_ref[m * rows : (m + 1) * rows, :] = unit_rows(x_refs[m][...], gain_ref[0:1])[0].astype(
            low_type
        )
    q_groups = groups - kv_groups

    @pl.loop(0, kv_groups)
    def _(b):
        across = pl.ds(pl.multiple_of((q_groups + b) * BC, BC), BC)
        wait_bytes(held.at[:, across], sems.at[q_groups + b])
        made = dot(h_ref[...], held[:, across]).astype(low_type)
        for m in range(micros):
            kv_refs[m][:, pl.ds(pl.multiple_of(b * BC, BC), BC)] = made[m * rows : (m + 1) * rows]

    @pl.loop(0, q_groups)
    def _(b):
        across = pl.ds(pl.multiple_of(b * BC, BC), BC)
        wait_bytes(held.at[:, across], sems.at[b])

    wait_bytes(held_out, sems.at[groups])
    copies = [
        pltpu.make_async_copy(held, win_ref, out_sems.at[0]),
        pltpu.make_async_copy(held_out, wout_ref, out_sems.at[1]),
    ]
    for copy in copies:
        copy.start()
    for copy in copies:
        copy.wait()


def project(pieces, arrays, chips, members, slots, order, me, xs, gains):
    micros = len(xs)
    rows, width = xs[0].shape
    in_width = (HEADS + 2 * KVH) * HD
    out_width = HEADS * HD
    kv_width = 2 * KVH * HD
    made = call(
        functools.partial(
            project_kernel, pieces, chips, members, slots, (in_width + out_width) // BC, micros
        ),
        tuple(
            [shaped((micros * rows, width), low_type)]
            + [shaped((rows, kv_width), low_type)] * micros
            + [shaped((width, in_width), low_type), shaped((width, out_width), low_type)]
        ),
        [in_smem, in_smem] + [in_vmem] * (micros + 1) + [in_any] * len(arrays),
        tuple([in_vmem] * (1 + micros) + [in_any, in_any]),
        [
            pltpu.VMEM((width, in_width), low_type),
            pltpu.VMEM((width, out_width), low_type),
            pltpu.SemaphoreType.DMA((in_width // BC + 1,)),
            pltpu.SemaphoreType.DMA((2,)),
        ],
        2 * micros * rows * width * kv_width,
        4 * width * (in_width + out_width),
    )(order, me, *xs, gains, *arrays)
    return made[0], made[1 : 1 + micros], made[1 + micros], made[2 + micros]


def query_kernel(h_ref, w_ref, *refs):
    q_refs = refs[:-2]
    held, sems = refs[-2:]
    groups = held.shape[1] // BC
    rows = q_refs[0].shape[0]

    def copy(b):
        across = pl.ds(pl.multiple_of(b * BC, BC), BC)
        return pltpu.make_async_copy(w_ref.at[:, across], held.at[:, across], sems.at[b])

    @pl.loop(0, groups)
    def _(b):
        copy(b).start()

    @pl.loop(0, groups)
    def _(b):
        copy(b).wait()
        across = pl.ds(pl.multiple_of(b * BC, BC), BC)
        made = dot(h_ref[...], held[:, across]).astype(low_type)
        for m, ref in enumerate(q_refs):
            ref[:, across] = made[m * rows : (m + 1) * rows]


def make_queries(h, w, micros):
    total, width = h.shape
    q_width = HEADS * HD
    return call(
        query_kernel,
        tuple([shaped((total // micros, q_width), low_type)] * micros),
        [in_vmem, in_any],
        tuple([in_vmem] * micros),
        [pltpu.VMEM((width, q_width), low_type), pltpu.SemaphoreType.DMA((q_width // BC,))],
        2 * total * width * q_width,
        2 * width * q_width,
    )(h, w)


def load_keys(parts, held, sem):
    start = 0
    for part in parts:
        count = part.shape[0]
        pltpu.make_async_copy(part, held.at[pl.ds(start, count)], sem).start()
        start += count


def attend_kernel(count, q_ref, rpos_ref, kpos_ref, x_ref, gain_ref, w_ref, *refs):
    parts = refs[:count]
    ob_ref, log_ref, x2_ref, h2_ref, bias, kv_ref, held, sems = refs[count:]
    rows = q_ref.shape[0]
    load_keys(parts, kv_ref, sems.at[0])
    pltpu.make_async_copy(w_ref, held, sems.at[1]).start()
    bias[...] = jnp.where(kpos_ref[...] <= rpos_ref[...], 0.0, masked_score)
    log_ref[...] = jnp.zeros_like(log_ref)
    length = kv_ref.shape[0]
    wait_bytes(kv_ref, sems.at[0])

    @pl.loop(0, KVH // 2)
    def _(pair):
        lane = pl.multiple_of(pair * LANES, LANES)
        keys = kv_ref[:, pl.ds(lane, LANES)]
        values = kv_ref[:, pl.ds(pl.multiple_of(lane + KVH * HD, LANES), LANES)]
        stacked = stack_heads(q_ref, pair, HD**-0.5)
        mixed = []
        for part in range(2):
            scores = dot(stacked[part].astype(low_type), keys, NT)
            scores = (scores.reshape(3, rows, length) + bias[...][None]).reshape(3 * rows, length)
            largest = jnp.max(scores, axis=-1, keepdims=True)
            raised = jnp.exp(scores - largest)
            summed = jnp.sum(raised, axis=-1, keepdims=True)
            mixed.append(dot(raised.astype(low_type), values) / summed)
            log_ref[...] = jnp.where(
                lane_ids(log_ref.shape) == 2 * pair + part, largest + jnp.log(summed), log_ref[...]
            )
        unstack_heads(ob_ref, pair, mixed[0], mixed[1])

    wait_bytes(held, sems.at[1])
    for n in range(held.shape[0] // BC):
        cut = slice(n * BC, (n + 1) * BC)
        x2_ref[:, cut] = x_ref[:, cut] + dot(ob_ref[...], held[cut, :], NT)
    h2_ref[...] = unit_rows(x2_ref[...], gain_ref[1:2])[0].astype(low_type)


def attend(q, kv_parts, rows_pos, key_pos, x, gains, w):
    rows, width = q.shape
    length = key_pos.shape[1]
    model = x.shape[1]
    return call(
        functools.partial(attend_kernel, len(kv_parts)),
        (
            shaped((rows, width), low_type),
            shaped((3 * rows, LANES), jnp.float32),
            shaped((rows, model), jnp.float32),
            shaped((rows, model), low_type),
        ),
        [in_vmem] * 5 + [in_any] * (1 + len(kv_parts)),
        (in_vmem,) * 4,
        [
            pltpu.VMEM((rows, length), jnp.float32),
            pltpu.VMEM((length, kv_parts[0].shape[1]), low_type),
            pltpu.VMEM((model, width), low_type),
            pltpu.SemaphoreType.DMA((2,)),
        ],
        16 * rows * length * width,
        8 * MIB,
    )(q, rows_pos, key_pos, x, gains, w, *kv_parts)


def router_parts(h2, router, experts):
    logits = dot(h2, router)
    logits = jnp.where(lane_ids(logits.shape) < experts, logits, masked_score)
    raised = jnp.exp(logits - jnp.max(logits, axis=-1, keepdims=True))
    return raised / jnp.sum(raised, axis=-1, keepdims=True)


def expert_kernel(sources, micro, order_ref, me_ref, router_ref, *refs):
    h_parts = refs[:sources]
    c_parts = refs[sources : 2 * sources]
    w_ref = refs[2 * sources]
    outs = refs[2 * sources + 1 :]
    back_refs = outs[:sources]
    z_ref, dg_ref, du_ref, cs, xs_ref = outs[sources : sources + 5]
    held, chance, load_sem, w_sems = outs[sources + 5 :]
    rows, width = h_parts[0].shape
    row_groups = width // BR
    col_groups = FF // BC
    for j in range(sources):
        pltpu.make_async_copy(h_parts[j], xs_ref.at[pl.ds(j * rows, rows)], load_sem.at[0]).start()
        pltpu.make_async_copy(
            c_parts[j].at[pl.ds(micro * rows, rows)], cs.at[pl.ds(j * rows, rows)], load_sem.at[1]
        ).start()
    for b in range(col_groups):

        @pl.loop(0, row_groups)
        def _(a):
            for k in range(3):
                pltpu.make_async_copy(
                    w_ref.at[order_ref[(k * row_groups + a) * col_groups + b]],
                    held.at[k, pl.ds(pl.multiple_of(a * BR, 64), BR), pl.ds(b * BC, BC)],
                    w_sems.at[b],
                ).start()

    wait_bytes(xs_ref, load_sem.at[0])
    wait_bytes(cs, load_sem.at[1])
    me = me_ref[1]
    probs = router_parts(xs_ref[...], router_ref[...], sources)
    hits = cs[:, width:].astype(jnp.float32)
    mine = lane_ids(hits.shape) == me
    hit = jnp.sum(jnp.where(mine, hits, 0.0), axis=-1, keepdims=True)
    weight = jnp.sum(jnp.where(mine, probs, 0.0), axis=-1, keepdims=True) * hit
    chance[...] = jnp.zeros_like(chance)

    @pl.loop(0, col_groups)
    def _(b):
        cut = pl.ds(pl.multiple_of(b * BC, BC), BC)
        wait_bytes(held.at[:, :, cut], w_sems.at[b])
        gate = dot(xs_ref[...], held[0, :, cut])
        up = dot(xs_ref[...], held[1, :, cut])
        down = dot(cs[:, :width], held[2, :, cut])
        sig = jax.nn.sigmoid(gate)
        act = gate * sig
        hidden = act * up
        chance[...] += jnp.sum(down * hidden, axis=-1, keepdims=True)
        z_ref[:, cut] = (hidden * weight).astype(low_type)
        down = down * weight
        dg_ref[:, cut] = (down * up * (sig + act * (1.0 - sig))).astype(low_type)
        du_ref[:, cut] = (down * act).astype(low_type)

    for n in range(width // BC):
        cut = slice(n * BC, (n + 1) * BC)
        back = dot(dg_ref[...], held[0, cut, :], NT) + dot(du_ref[...], held[1, cut, :], NT)
        for j in range(sources):
            back_refs[j][:, cut] = back[j * rows : (j + 1) * rows].astype(low_type)
    told = chance[...] * hit
    high_part = told.astype(low_type)
    low_part = (told - high_part.astype(jnp.float32)).astype(low_type)
    lanes = lane_ids((sources * rows, LANES))
    tail = jnp.where(lanes == 0, high_part, jnp.where(lanes == 1, low_part, jnp.zeros_like(low_part)))
    for j in range(sources):
        back_refs[j][:, width:] = tail[j * rows : (j + 1) * rows]


def run_expert(micro, order, me, router, h_parts, c_parts, w):
    sources = len(h_parts)
    rows, width = h_parts[0].shape
    total = sources * rows
    return call(
        functools.partial(expert_kernel, sources, micro),
        tuple(
            [shaped((rows, width + LANES), low_type)] * sources
            + [shaped((total, FF), low_type)] * 3
            + [shaped((total, width + LANES), low_type), shaped((total, width), low_type)]
        ),
        [in_smem, in_smem, in_vmem] + [in_any] * (2 * sources + 1),
        tuple([in_vmem] * (sources + 5)),
        [
            pltpu.VMEM((3, width, FF), low_type),
            pltpu.VMEM((total, 1), jnp.float32),
            pltpu.SemaphoreType.DMA((2,)),
            pltpu.SemaphoreType.DMA((FF // BC,)),
        ],
        10 * total * width * FF,
        20 * MIB,
    )(order, me, router, *h_parts, *c_parts, w)


def produce_kernel(sources, order_ref, w_ref, *refs):
    out_refs = refs[-3 - sources : -3]
    z_refs = refs[: -3 - sources]
    zs, held, sem = refs[-3:]
    width = held.shape[0]
    total = z_refs[0].shape[0]
    rows = total // sources
    row_groups, col_groups = width // BR, FF // BC

    @pl.loop(0, row_groups)
    def _(a):
        for b in range(col_groups):
            pltpu.make_async_copy(
                w_ref.at[order_ref[(2 * row_groups + a) * col_groups + b]],
                held.at[pl.ds(pl.multiple_of(a * BR, 64), BR), pl.ds(b * BC, BC)],
                sem,
            ).start()

    for m, z_ref in enumerate(z_refs):
        zs[m * total : (m + 1) * total] = z_ref[...]
    wait_bytes(held, sem)
    for n in range(width // BC):
        cut = slice(n * BC, (n + 1) * BC)
        made = dot(zs[...], held[cut, :], NT).astype(low_type)
        for m in range(len(z_refs)):
            for j in range(sources):
                start = m * total + j * rows
                out_refs[j][m * rows : (m + 1) * rows, cut] = made[start : start + rows]


def produce(order, w, zs, sources, width):
    micros = len(zs)
    total = zs[0].shape[0]
    return call(
        functools.partial(produce_kernel, sources),
        tuple([shaped((micros * total // sources, width), low_type)] * sources),
        [in_smem, in_any] + [in_vmem] * micros,
        tuple([in_vmem] * sources),
        [
            pltpu.VMEM((micros * total, FF), low_type),
            pltpu.VMEM((width, FF), low_type),
            pltpu.SemaphoreType.DMA,
        ],
        2 * micros * total * width * FF,
        8 * MIB,
    )(order, w, *zs)


def outer_kernel(groups, col_groups, order_ref, *refs):
    micros = len(refs[:-4]) // (len(groups) + 2)
    lefts = [refs[i * micros : (i + 1) * micros] for i in range(2)]
    rights = [refs[(2 + i) * micros : (3 + i) * micros] for i in range(len(groups))]
    out_ref, turned, stage, sems = refs[-4:]
    rows = rights[0][0].shape[0]
    width = turned.shape[1]
    span = 2 * BR
    for side in range(2):
        for m in range(micros):
            for r in range(0, rows, LANES):
                part = lefts[side][m][r : r + LANES, :width]
                turned[side, :, m * rows + r : m * rows + r + LANES] = part.T
    row_groups = width // BR
    steps = [(k, p) for k in range(len(groups)) for p in range(width // span)]
    for n, (k, p) in enumerate(steps):
        slot = n % 2
        if n >= 2:
            wait_bytes(stage.at[slot], sems.at[slot])
        cut = slice(p * span, (p + 1) * span)
        made = 0.0
        for m in range(micros):
            left = turned[groups[k], cut, m * rows : (m + 1) * rows]
            made = made + dot(left, rights[k][m][...])
        stage[slot] = made.astype(low_type)
        for half in range(2):
            for b in range(col_groups):
                number = (k * row_groups + 2 * p + half) * col_groups + b
                pltpu.make_async_copy(
                    stage.at[slot, pl.ds(half * BR, BR), pl.ds(b * BC, BC)],
                    out_ref.at[order_ref[number]],
                    sems.at[slot],
                ).start()
    for slot in range(2):
        wait_bytes(stage.at[slot], sems.at[slot])


def outer_blocks(order, width, groups, lefts, rights):
    flat = [part for group in lefts + rights for part in group]
    rows = sum(part.shape[0] for part in rights[0])
    cols = rights[0][0].shape[1]
    blocks = len(groups) * width * cols // (BR * BC)
    return call(
        functools.partial(outer_kernel, groups, cols // BC),
        shaped((blocks, BR, BC), low_type),
        [in_smem] + [in_vmem] * len(flat),
        in_any,
        [
            pltpu.VMEM((2, width, rows), low_type),
            pltpu.VMEM((2, 2 * BR, cols), low_type),
            pltpu.SemaphoreType.DMA((2,)),
        ],
        2 * rows * blocks * BR * BC,
        blocks * BR * BC * 2 + sum(f.size * 2 for f in flat),
    )(order, *flat)


def xor_plan(members, offset):
    if members != 4:
        return list(range(1, members)), [0]
    first = 1 if offset % 2 else 2
    return [first, 3], [0, 3 - first]


def slots_kernel(
    counts, chips, members, slots, all_groups, in_groups, order_ref, me_ref, *refs
):
    lists = []
    for count in counts:
        lists.append(refs[:count])
        refs = refs[count:]
    outs = refs[: 2 * chips]
    lefts, turned, rights, sems = refs[2 * chips :]
    ctx, shard = me_ref[0], me_ref[1]
    chip, core = lax.div(ctx, 2), lax.rem(ctx, 2)
    h_width = lefts.shape[2]
    q_width = lists[2][0].shape[1]
    kv_width = lists[3][0].shape[1]
    total = rights.shape[0]
    targets = (
        (lefts.at[0], 0, h_width, 0),
        (lefts.at[1], 0, h_width, 1),
        (rights, 0, q_width, 2),
        (rights, q_width, kv_width, 2),
        (rights, q_width + kv_width, q_width, 2),
    )
    for group, (target, lane, lanes, sem) in zip(lists, targets):
        start = 0
        for ref in group:
            pltpu.make_async_copy(
                ref, target.at[pl.ds(start, ref.shape[0]), pl.ds(lane, lanes)], sems.at[sem]
            ).start()
            start += ref.shape[0]
    for side in range(2):
        wait_bytes(lefts.at[side], sems.at[side])
        for r in range(0, total, LANES):
            turned[side, :, r : r + LANES] = lefts[side, r : r + LANES, :].T
    wait_bytes(rights, sems.at[2])
    for offset in range(chips):
        there = lax.rem(chip - offset + chips, chips) * 2 + core
        for out, hops in zip(outs[2 * offset : 2 * offset + 2], xor_plan(members, offset)):
            for place, hop in enumerate(hops):
                base = (there * members + jnp.bitwise_xor(shard, hop)) * slots

                @pl.loop(0, slots)
                def _(i):
                    number = order_ref[base + i]
                    a, b = lax.div(number, all_groups), lax.rem(number, all_groups)
                    side = (b >= in_groups).astype(jnp.int32)
                    out[place * slots + i] = dot(
                        turned[side, pl.ds(pl.multiple_of(a * BR, 64), BR), :],
                        rights[:, pl.ds(pl.multiple_of(b * BC, BC), BC)],
                    ).astype(low_type)


def slot_blocks(chips, members, slots, order, me, h1, da, dq, dkv, ob):
    lists = (h1, da, dq, dkv, ob)
    total = sum(part.shape[0] for part in h1)
    width = h1[0].shape[1]
    in_width = dq[0].shape[1] + dkv[0].shape[1]
    all_width = in_width + ob[0].shape[1]
    outs = []
    for offset in range(chips):
        for hops in xor_plan(members, offset):
            outs.append(shaped((len(hops) * slots, BR, BC), low_type))
    made = call(
        functools.partial(
            slots_kernel,
            tuple(len(group) for group in lists),
            chips,
            members,
            slots,
            all_width // BC,
            in_width // BC,
        ),
        tuple(outs),
        [in_smem, in_smem] + [in_any] * sum(len(group) for group in lists),
        (in_vmem,) * len(outs),
        [
            pltpu.VMEM((2, total, width), low_type),
            pltpu.VMEM((2, width, total), low_type),
            pltpu.VMEM((total, all_width), low_type),
            pltpu.SemaphoreType.DMA((3,)),
        ],
        2 * total * chips * members * slots * BR * BC,
        16 * MIB,
    )(order, me, *[part for group in lists for part in group])
    return [(made[2 * offset], made[2 * offset + 1]) for offset in range(chips)]


def merge_kernel(
    sources, me_ref, x2_ref, cot_ref, h2_ref, gain_ref, router_ref, w_ref, *refs
):
    back_refs = refs[:sources]
    dx_ref, da_ref, do_ref, stat_ref, held, sem = refs[sources:]
    rows, width = x2_ref.shape
    pltpu.make_async_copy(w_ref, held, sem).start()
    lanes = lane_ids((rows, LANES))
    prob_grad = jnp.zeros((rows, LANES), jnp.float32)
    gathered = jnp.zeros((rows, width), jnp.float32)
    for j in range(sources):
        tail = back_refs[j][:, width:].astype(jnp.float32)
        told = jnp.sum(tail, axis=-1, keepdims=True)
        expert = jnp.bitwise_xor(me_ref[1], j)
        prob_grad = prob_grad + jnp.where(lanes == expert, told, 0.0)
        gathered = gathered + back_refs[j][:, :width].astype(jnp.float32)
    h2 = h2_ref[...]
    probs = router_parts(h2, router_ref[...], sources)
    logit_grad = probs * (prob_grad - jnp.sum(probs * prob_grad, axis=-1, keepdims=True))
    high_part = logit_grad.astype(low_type)
    low_part = (logit_grad - high_part.astype(jnp.float32)).astype(low_type)
    router_grad = dot(high_part, h2, TN) + dot(low_part, h2, TN)
    gathered = gathered + dot(high_part, router_ref[...], NT) + dot(low_part, router_ref[...], NT)
    x2 = x2_ref[...]
    inverse = lax.rsqrt(jnp.mean(x2 * x2, axis=-1, keepdims=True) + norm_eps)
    moe_grad, gain_grad = unit_back(x2, gain_ref[1:2], inverse, gathered)
    after = cot_ref[...] + moe_grad
    dx_ref[...] = after
    da_ref[...] = after.astype(low_type)
    experts_up = stat_ref.shape[0] - 8
    stat_ref[:experts_up] = router_grad[:experts_up]
    stat_ref[experts_up:] = jnp.broadcast_to(gain_grad, (8, width))
    wait_bytes(held, sem)
    for n in range(held.shape[1] // BC):
        cut = slice(n * BC, (n + 1) * BC)
        do_ref[:, cut] = dot(da_ref[...], held[:, cut]).astype(low_type)


def merge(me, x2, cot, h2, gains, router, w, backs):
    rows, width = x2.shape
    sources = len(backs)
    experts_up = -(-sources // 8) * 8
    return call(
        functools.partial(merge_kernel, sources),
        (
            shaped((rows, width), jnp.float32),
            shaped((rows, width), low_type),
            shaped((rows, HEADS * HD), low_type),
            shaped((experts_up + 8, width), jnp.float32),
        ),
        [in_smem] + [in_vmem] * 5 + [in_any] + [in_vmem] * sources,
        (in_vmem,) * 4,
        [pltpu.VMEM((width, HEADS * HD), low_type), pltpu.SemaphoreType.DMA],
        2 * rows * width * HEADS * HD,
        10 * MIB,
    )(me, x2, cot, h2, gains, router, w, *backs)


def attend_back_kernel(count, q_ref, rpos_ref, kpos_ref, ob_ref, log_ref, do_ref, *refs):
    parts = refs[:count]
    dq_ref, own_ref, other_ref, bias, kv_ref, sem = refs[count:]
    rows = q_ref.shape[0]
    load_keys(parts, kv_ref, sem)
    length = kv_ref.shape[0]
    bias[...] = jnp.where(kpos_ref[...] <= rpos_ref[...], 0.0, masked_score)
    wait_bytes(kv_ref, sem)

    @pl.loop(0, KVH // 2)
    def _(pair):
        lane = pl.multiple_of(pair * LANES, LANES)
        value_lane = pl.multiple_of(lane + KVH * HD, LANES)
        keys = kv_ref[:, pl.ds(lane, LANES)]
        values = kv_ref[:, pl.ds(value_lane, LANES)]
        queries = stack_heads(q_ref, pair, HD**-0.5)
        grads = stack_heads(do_ref, pair)
        mixes = stack_heads(ob_ref, pair)
        query_grads = []
        key_grad = value_grad = None
        for part in range(2):
            query = queries[part].astype(low_type)
            grad = grads[part].astype(low_type)
            log_total = jnp.sum(
                jnp.where(lane_ids(log_ref.shape) == 2 * pair + part, log_ref[...], 0.0),
                axis=-1,
                keepdims=True,
            )
            delta = jnp.sum(grads[part] * mixes[part], axis=-1, keepdims=True)
            scores = dot(query, keys, NT)
            scores = (scores.reshape(3, rows, length) + bias[...][None]).reshape(3 * rows, length)
            chance = jnp.exp(scores - log_total)
            prob_grad = dot(grad, values, NT)
            score_grad = (chance * (prob_grad - delta)).astype(low_type)
            value_term = dot(chance.astype(low_type), grad, TN)
            key_term = dot(score_grad, query, TN)
            key_grad = key_term if part == 0 else key_grad + key_term
            value_grad = value_term if part == 0 else value_grad + value_term
            query_grads.append(dot(score_grad, keys) * HD**-0.5)
        unstack_heads(dq_ref, pair, query_grads[0], query_grads[1])
        half = length // 2
        for ref, cut in ((own_ref, slice(0, half)), (other_ref, slice(half, length))):
            ref[:, pl.ds(lane, LANES)] = key_grad[cut].astype(low_type)
            ref[:, pl.ds(value_lane, LANES)] = value_grad[cut].astype(low_type)


def attend_back(q, kv_parts, rows_pos, key_pos, ob, log_total, do):
    rows, width = q.shape
    length = key_pos.shape[1]
    kv_width = kv_parts[0].shape[1]
    return call(
        functools.partial(attend_back_kernel, len(kv_parts)),
        (shaped((rows, width), low_type),) + (shaped((length // 2, kv_width), low_type),) * 2,
        [in_vmem] * 6 + [in_any] * len(kv_parts),
        (in_vmem,) * 3,
        [
            pltpu.VMEM((rows, length), jnp.float32),
            pltpu.VMEM((length, kv_width), low_type),
            pltpu.SemaphoreType.DMA,
        ],
        40 * rows * length * width,
        8 * MIB,
    )(q, rows_pos, key_pos, ob, log_total, do, *kv_parts)


def query_back_kernel(w_ref, *refs):
    micros = (len(refs) - 3) // 2
    dq_refs, out_refs = refs[:micros], refs[micros : 2 * micros]
    rows_ref, held, sem = refs[2 * micros :]
    rows = dq_refs[0].shape[0]
    copy = pltpu.make_async_copy(w_ref.at[:, pl.ds(0, held.shape[1])], held, sem)
    copy.start()
    for m in range(micros):
        rows_ref[m * rows : (m + 1) * rows] = dq_refs[m][...]
    copy.wait()
    for n in range(held.shape[0] // BC):
        cut = slice(n * BC, (n + 1) * BC)
        made = dot(rows_ref[...], held[cut, :], NT)
        for m in range(micros):
            out_refs[m][:, cut] = made[m * rows : (m + 1) * rows]


def query_back(w, dqs):
    micros = len(dqs)
    rows, q_width = dqs[0].shape
    width = w.shape[0]
    return call(
        query_back_kernel,
        tuple([shaped((rows, width), jnp.float32)] * micros),
        [in_any] + [in_vmem] * micros,
        tuple([in_vmem] * micros),
        [
            pltpu.VMEM((micros * rows, q_width), low_type),
            pltpu.VMEM((width, q_width), low_type),
            pltpu.SemaphoreType.DMA,
        ],
        2 * micros * rows * width * q_width,
        7 * MIB,
    )(w, *dqs)


def input_kernel(x_ref, gain_ref, w_ref, *refs):
    micros, rows = x_ref.shape[:2]
    dx_refs = refs[:micros]
    part_refs = refs[micros : 2 * micros]
    dkv_refs = refs[2 * micros : 3 * micros]
    out_ref, stat_ref, rows_ref, grad, held, sem = refs[3 * micros :]
    kv_width = held.shape[1]
    copy = pltpu.make_async_copy(
        w_ref.at[:, pl.ds(w_ref.shape[1] - kv_width, kv_width)], held, sem
    )
    copy.start()
    for m in range(micros):
        rows_ref[m * rows : (m + 1) * rows] = dkv_refs[m][...]
    copy.wait()
    for n in range(held.shape[0] // BC):
        cut = slice(n * BC, (n + 1) * BC)
        made = dot(rows_ref[...], held[cut, :], NT)
        for m in range(micros):
            grad[m, :, cut] = part_refs[m][:, cut] + made[m * rows : (m + 1) * rows]
    total = jnp.zeros((1, x_ref.shape[-1]), jnp.float32)
    for m in range(micros):
        x = x_ref[m]
        inverse = lax.rsqrt(jnp.mean(x * x, axis=-1, keepdims=True) + norm_eps)
        term, gain_grad = unit_back(x, gain_ref[0:1], inverse, grad[m])
        out_ref[m] = dx_refs[m][...] + term
        total = total + gain_grad
    stat_ref[...] = jnp.broadcast_to(total, stat_ref.shape)


def input_back(x, gains, w, dxs, parts, dkvs):
    micros, rows, width = x.shape
    kv_width = dkvs[0].shape[1]
    return call(
        input_kernel,
        (shaped(x.shape, jnp.float32), shaped((8, width), jnp.float32)),
        [in_vmem, in_vmem, in_any] + [in_vmem] * (3 * micros),
        (in_vmem,) * 2,
        [
            pltpu.VMEM((micros * rows, kv_width), low_type),
            pltpu.VMEM(x.shape, jnp.float32),
            pltpu.VMEM((width, kv_width), low_type),
            pltpu.SemaphoreType.DMA,
        ],
        2 * micros * rows * width * kv_width,
        14 * MIB,
    )(x, gains, w, *dxs, *parts, *dkvs)


def rotate_kernel(b_ref, m_ref, s_ref, l_ref, r_ref, *refs):
    grad_ref, new_ref, moment_ref, second_ref = refs[-4:]
    parts = [ref[0].astype(jnp.float32) for ref in refs[:-4]]
    gradient = parts[0] if len(parts) == 1 else jnp.concatenate(parts, axis=1)
    grad_ref[0] = gradient
    left = l_ref[0].astype(low_type)
    right = r_ref[0].astype(low_type)
    rotated = dot(dot(left, gradient.astype(low_type), TN).astype(low_type), right)
    moment = beta_one * m_ref[0] + (1.0 - beta_one) * rotated
    second = beta_two * s_ref[0] + (1.0 - beta_two) * rotated * rotated
    moment_ref[0] = moment
    second_ref[0] = second
    direction = (moment / (jnp.sqrt(second) + adam_eps)).astype(low_type)
    turned = dot(dot(left, direction).astype(low_type), right, NT)
    new_ref[0] = b_ref[0] - rate * turned


def rotate(weight, gradients, moment, second, left, right):
    count = weight.shape[0]

    def spec(rows, cols):
        return pl.BlockSpec((1, rows, cols), lambda i: (i, 0, 0))

    block = spec(BR, BC)
    return pl.pallas_call(
        rotate_kernel,
        grid=(count,),
        out_shape=(shaped(weight.shape, jnp.float32),) * 4,
        in_specs=[block] * 3
        + [spec(BR, BR), spec(BC, BC)]
        + [spec(BR, part.shape[2]) for part in gradients],
        out_specs=(block,) * 4,
        compiler_params=pltpu.CompilerParams(vmem_limit_bytes=VMEM_LIMIT),
        cost_estimate=pl.CostEstimate(
            flops=4 * count * BR * BC * (BR + BC),
            bytes_accessed=count * 2 * MIB,
            transcendentals=0,
        ),
    )(weight, moment, second, left, right, *gradients)


def adam(weight, gradient, moment, second, step_rate):
    moment_new = beta_one * moment + (1.0 - beta_one) * gradient
    second_new = beta_two * second + (1.0 - beta_two) * gradient * gradient
    return (
        weight - step_rate * moment_new / (jnp.sqrt(second_new) + adam_eps),
        moment_new,
        second_new,
    )


def to_partner(array, offset):
    if offset == 0:
        return array
    count = lax.axis_size("shard")
    return lax.ppermute(array, "shard", [(i, i ^ offset) for i in range(count)])


def to_ctx(array, offset):
    count = lax.axis_size("ctx")
    return lax.ppermute(array, "ctx", [(i, i ^ offset) for i in range(count)])


def to_chip(array, offset):
    count = lax.axis_size("ctx")
    return lax.ppermute(array, "ctx", [(i, (i + 2 * offset) % count) for i in range(count)])


def after(value, *others):
    return lax.optimization_barrier((value, others))[0]


def from_chips(array, chips):
    return [array] + [to_chip(array, offset) for offset in range(1, chips)]


def wide(array):
    return array.astype(jnp.float32)


def sum_to_chips(parts):
    total = wide(parts[0])
    for offset in range(1, len(parts)):
        total = total + wide(to_chip(parts[offset], -offset))
    return total


def gather_weights(blocks, chips, members):
    parts = from_chips(blocks, chips)
    pieces, arrays = [], []
    gate = []

    def add(array, offset, first, cut):
        pieces.append((0, offset, first, cut))
        arrays.append(array)
        pieces.append((1, offset, first, cut))
        arrays.append(to_ctx(after(array, *gate), 1))
        return array

    def spread(group, first):
        add(group, 0, first, 0)
        if members == 4 and first > 0:
            by_one, by_two = to_partner(group, 1), to_partner(group, 2)
            add(by_one, 1, first, 0)
            add(by_two, 2, first, 0)
            half = BR // 2
            add(to_partner(by_one[:, :half], 2), 3, first, 0)
            add(to_partner(by_two[:, half:], 1), 3, first, half)
            return [by_one, by_two]
        got = [to_partner(group, offset) for offset in range(1, members)]
        for offset in range(1, members):
            add(got[offset - 1], offset, first, 0)
        return got

    got = [to_partner(blocks, offset) for offset in range(1, members)]
    gate.append(got[0])
    add(blocks, 0, 0, 0)
    for offset in range(1, members):
        add(got[offset - 1], offset, 0, 0)
    last = list(got)
    if chips > 1:
        last = spread(after(parts[1], *last), 1)
        gate[:] = last
        got = last
    if chips > 2:
        group = after(jnp.concatenate(parts[2:], axis=0), *last)
        spread(group, 2)
    return got + parts[1:], pieces, arrays


def sum_slots(made, ready, chips, members, slots):
    sums, first_got = [], []
    for offset in range(chips):
        sent, kept = made[offset]
        hops, keeps = xor_plan(members, offset)
        total = wide(kept[:slots])
        if members == 4:
            first, second = hops[0], keeps[1]
            got = after(to_partner(sent, first), ready)
            total = total + wide(got[:slots])
            relay = (wide(kept[slots:]) + wide(got[slots:])).astype(low_type)
            total = total + wide(to_partner(relay, second))
        else:
            for place, hop in enumerate(hops):
                got = to_partner(sent[place * slots : (place + 1) * slots], hop)
                total = total + wide(got)
        sums.append(total if offset == 0 else total.astype(low_type))
        first_got.append(got)
    return sums, first_got


def sum_all(array):
    step = 1
    while step < lax.axis_size("ctx"):
        array = array + to_ctx(array, step)
        step *= 2
    step = 1
    while step < lax.axis_size("shard"):
        array = array + to_partner(array, step)
        step *= 2
    return array


def shards(
    tokens,
    cotangent,
    norm_gains,
    router,
    dense_weight,
    expert_weight,
    routes,
    assign,
    dense_order,
    expert_order,
    dense_moment,
    dense_second,
    dense_left,
    dense_right,
    expert_moment,
    expert_second,
    expert_left,
    expert_right,
    gains_moment,
    gains_second,
    router_moment,
    router_second,
):
    ctx_count = lax.axis_size("ctx")
    shard_count = lax.axis_size("shard")
    chips = ctx_count // 2
    micros, rows, width = tokens.shape
    slots = dense_weight.shape[0]
    span = rows // 2
    row_groups = width // BR
    ff_groups = FF // BC
    expert_blocks = 3 * row_groups * ff_groups

    expert_inverse = inverse_order(expert_order)
    ctx = lax.axis_index("ctx").astype(jnp.int32)
    me = jnp.stack([ctx, lax.axis_index("shard").astype(jnp.int32)])
    row_ids = jnp.arange(rows, dtype=jnp.int32)
    all_pos = assign[:, row_ids // span] * span + row_ids % span
    ring_ids = (ctx // 2 - jnp.arange(chips, dtype=jnp.int32)) % chips * 2
    key_ids = jnp.concatenate([ring_ids + ctx % 2, ring_ids + (1 - ctx % 2)])
    key_pos = all_pos[key_ids].reshape(1, rows * ctx_count)
    rows_pos = all_pos[ctx].reshape(rows, 1)
    router_pad = jnp.pad(router.astype(low_type), ((0, 0), (0, LANES - shard_count)))

    far, pieces, arrays = gather_weights(dense_weight.astype(low_type), chips, shard_count)
    expert_low = after(expert_weight[0].astype(low_type), *far)
    expert_all = lax.all_gather(expert_low, "ctx", axis=0, tiled=True)

    lanes = jnp.arange(LANES, dtype=jnp.int32)
    hits = jnp.sum((routes[..., None] == lanes).astype(low_type), axis=2)
    cot_rows = jnp.concatenate([cotangent.astype(low_type), hits], axis=2)
    cot_rows = cot_rows.reshape(micros * rows, width + LANES)
    cot_rows = after(cot_rows, *arrays[::2])
    cot_parts = [to_partner(cot_rows, j) for j in range(min(3, shard_count))]

    here, expert_inverse, router_pad, key_pos, rows_pos = lax.optimization_barrier(
        (me, expert_inverse, router_pad, key_pos, rows_pos)
    )
    h1, kv, w_in, w_out = project(
        pieces,
        arrays,
        chips,
        shard_count,
        slots,
        dense_order,
        here,
        [tokens[m] for m in range(micros)],
        norm_gains,
    )
    q = make_queries(h1, w_in, micros)
    h1_other = to_ctx(h1, 1)
    kvs, obs, logs, x2s, h2s = [], [], [], [], []
    chip_kv = []
    for m in range(micros):
        own = kv[m] if m == 0 else after(kv[m], chip_kv[m - 1][1 % chips])
        chip_kv.append(from_chips(own, chips))
    late_rows = after(cot_rows, *chip_kv[0])
    cot_parts = cot_parts + [to_partner(late_rows, j) for j in range(3, shard_count)]
    for m in range(micros):
        query = after(q[m], *(cot_parts[:3] if m == 0 else obs[m - 1 : m]))
        parts = chip_kv[m]
        swapped = after(parts, q[0] if m == 0 else obs[m - 1])
        kvs.append(parts + [to_ctx(part, 1) for part in swapped])
        ob, log_total, x2, h2 = attend(
            query, kvs[m], rows_pos, key_pos, tokens[m], norm_gains, w_out
        )
        obs.append(ob)
        logs.append(log_total)
        x2s.append(x2)
        h2s.append(h2)
    ob_others = [to_ctx(ob, 1) for ob in obs]

    h_parts = []
    for m in range(micros):
        own = h2s[m] if m == 0 else after(h2s[m], *h_parts[m - 1])
        h_parts.append([own] + [to_partner(own, j) for j in range(1, shard_count)])
    sent = []
    zs, dgs, dus, cs, xs = [], [], [], [], []
    for m in range(micros):
        here = after(me, h2s[-1], h1_other, *ob_others) if m == 0 else after(me, zs[-1])
        made = run_expert(m, expert_inverse, here, router_pad, h_parts[m], cot_parts, expert_all)
        sent.append(made[:shard_count])
        z, dg, du, c, x = made[shard_count:]
        zs.append(z)
        dgs.append(dg)
        dus.append(du)
        cs.append(c)
        xs.append(x)
    backs = [[to_partner(sent[m][j], j) for j in range(shard_count)] for m in range(micros)]

    dxs, das, dqs, stats, own_grads = [], [], [], [], []
    for m in range(micros):
        here = after(me, zs[-1] if m == 0 else dqs[-1])
        dx, da, do, stat = merge(
            here, x2s[m], cotangent[m], h2s[m], norm_gains, router_pad, w_out, backs[m]
        )
        dq, dkv_own, dkv_other = attend_back(
            q[m], kvs[m], rows_pos, key_pos, obs[m], logs[m], do
        )
        got = to_ctx(dkv_other, 1)
        parts = []
        for o in range(chips):
            cut = slice(o * rows, (o + 1) * rows)
            part = wide(dkv_own[cut]) + wide(got[cut])
            parts.append(part if o == 0 else part.astype(low_type))
        own_grads.append(parts)
        dxs.append(dx)
        das.append(da)
        dqs.append(dq)
        stats.append(stat)

    far_sums = [
        to_chip(jnp.concatenate([parts[o] for parts in own_grads], axis=0), -o)
        for o in range(1, chips)
    ]
    dkvs = []
    for m in range(micros):
        total = own_grads[m][0]
        for part in far_sums:
            total = total + wide(part[m * rows : (m + 1) * rows])
        dkvs.append(total.astype(low_type))

    def other_core(parts):
        return [to_ctx(part, 1) for part in parts]

    da_others, dq_others = other_core(das), other_core(dqs)
    expert_term = outer_blocks(
        after(expert_inverse, *backs[0]), width, (0, 0, 1), [xs, cs], [dgs, dus, zs]
    )
    expert_sum = lax.psum_scatter(expert_term, "ctx", scatter_dimension=0, tiled=True)
    parts_back = query_back(w_in, dqs)
    made = produce(after(expert_inverse, own_grads[-1][1 % chips]), expert_all, zs, shard_count, width)
    arrived = [to_partner(made[j], j) for j in range(shard_count)]
    here = after(me, parts_back, *arrived)
    made = slot_blocks(
        chips,
        shard_count,
        slots,
        dense_order,
        here,
        [h1, h1_other],
        das + da_others,
        dqs + dq_others,
        dkvs + other_core(dkvs),
        obs + ob_others,
    )
    input_grad, gain_stat = input_back(
        after(tokens, made[0][0]), norm_gains, w_in, dxs, parts_back, dkvs
    )
    sums, got = sum_slots(made, input_grad, chips, shard_count, slots)
    experts_up = stats[0].shape[0] - 8
    stat_rows = jnp.concatenate([sum(stats)[: experts_up + 1], gain_stat[:7]], axis=0)
    stat_rows = sum_all(after(stat_rows, *sums))
    router_grad = stat_rows[:shard_count].T
    gains_grad = jnp.stack([stat_rows[experts_up + 1], stat_rows[experts_up]])

    outputs = []
    for m in range(micros):
        total = x2s[m]
        for part in arrived:
            total = total + wide(part[m * rows : (m + 1) * rows])
        outputs.append(total)

    expert_grad, expert_new, expert_moment_new, expert_second_new = rotate(
        expert_weight[0], [after(expert_sum, *sums)], expert_moment[0], expert_second[0], expert_left[0], expert_right[0]
    )
    last = [sums[0]] + [to_chip(sums[o], -o) for o in range(1, chips)]
    last = after(last, expert_new)
    dense_sum = sum([wide(part) for part in last[1:]], last[0])
    dense_grad, dense_new, dense_moment_new, dense_second_new = rotate(
        dense_weight, [dense_sum], dense_moment, dense_second, dense_left, dense_right
    )
    gains_new, gains_moment_new, gains_second_new = adam(
        norm_gains, gains_grad, gains_moment, gains_second, gain_rate
    )
    router_new, router_moment_new, router_second_new = adam(
        router, router_grad, router_moment, router_second, rate
    )
    return (
        jnp.stack(outputs),
        input_grad,
        dense_grad,
        dense_new,
        dense_moment_new,
        dense_second_new,
        expert_grad[None],
        expert_new[None],
        expert_moment_new[None],
        expert_second_new[None],
        gains_grad,
        gains_new,
        gains_moment_new,
        gains_second_new,
        router_grad,
        router_new,
        router_moment_new,
        router_second_new,
    )


def solution(mesh):
    rows_spec = P("shard", "ctx", None)
    dense_spec = P(("ctx", "shard"), None, None)
    expert_spec = P("shard", "ctx", None, None)
    in_specs = (
        (rows_spec, rows_spec, P(), P(), dense_spec, expert_spec, rows_spec, P(), P(), P())
        + (dense_spec,) * 4
        + (expert_spec,) * 4
        + (P(),) * 4
    )
    out_specs = (rows_spec,) * 2 + (dense_spec,) * 4 + (expert_spec,) * 4 + (P(),) * 8
    return jax.shard_map(shards, mesh=mesh, in_specs=in_specs, out_specs=out_specs, check_vma=False)
```

```python
import functools

import jax
import jax.numpy as jnp
from jax import lax
from jax.experimental import pallas as pl
from jax.experimental.pallas import tpu as pltpu
from jax.sharding import PartitionSpec as P

HEADS = 24
KVH = 8
HD = 64
FF = 1024
BR = 192
BC = 256
LANES = 128

norm_eps = 1e-06
beta_one = 0.9
beta_two = 0.95
rate = 0.01
gain_rate = 0.5
adam_eps = 1e-08
masked_score = -1e30
low_type = jnp.bfloat16
MIB = 1 << 20
VMEM_LIMIT = 60 * MIB

NN = (((1,), (0,)), ((), ()))
NT = (((1,), (1,)), ((), ()))
TN = (((0,), (0,)), ((), ()))

in_vmem = pl.BlockSpec(memory_space=pltpu.VMEM)
in_smem = pl.BlockSpec(memory_space=pltpu.SMEM)
in_any = pl.BlockSpec(memory_space=pl.ANY)


def dot(left_side, right_side, dims=NN):
    return lax.dot_general(left_side, right_side, dims, preferred_element_type=jnp.float32)


def call(kernel, out_shapes, in_specs, out_specs, scratch, flops, moved):
    return pl.pallas_call(
        kernel,
        out_shape=out_shapes,
        in_specs=in_specs,
        out_specs=out_specs,
        scratch_shapes=scratch,
        compiler_params=pltpu.CompilerParams(vmem_limit_bytes=VMEM_LIMIT),
        cost_estimate=pl.CostEstimate(flops=flops, bytes_accessed=moved, transcendentals=0),
    )


def shaped(dims, kind):
    return jax.ShapeDtypeStruct(dims, kind)


def inverse_order(slot_order):
    count = slot_order.shape[0]
    numbers = jnp.arange(count, dtype=jnp.int32)
    return jnp.sum(
        jnp.where(slot_order[None, :] == numbers[:, None], numbers[None, :], 0), axis=1
    ).astype(jnp.int32)


def wait_bytes(landed, semaphore):
    pltpu.make_async_copy(landed, landed, semaphore).wait()


def unit_rows(rows, gain):
    inverse = lax.rsqrt(jnp.mean(rows * rows, axis=-1, keepdims=True) + norm_eps)
    return rows * inverse * gain, inverse


def unit_back(rows, gain, inverse, gradient):
    unit = rows * inverse
    scaled = gradient * gain
    inner = jnp.mean(scaled * unit, axis=-1, keepdims=True)
    return inverse * (scaled - unit * inner), jnp.sum(gradient * unit, axis=0, keepdims=True)


def lane_ids(dims):
    return lax.broadcasted_iota(jnp.int32, dims, len(dims) - 1)


def half_turn(tile):
    return pltpu.roll(tile, HD, 1)


def stack_heads(ref, pair, scale=None):
    base = pair * (3 * LANES)
    tiles = [
        ref[:, pl.ds(pl.multiple_of(base + LANES * t, LANES), LANES)].astype(jnp.float32)
        for t in range(3)
    ]
    if scale is not None:
        tiles = [t * scale for t in tiles]
    lower = lane_ids(tiles[0].shape) < HD
    first = [tiles[0], half_turn(tiles[0]), tiles[1]]
    second = [tiles[1], half_turn(tiles[2]), tiles[2]]
    return (
        jnp.concatenate([jnp.where(lower, t, 0.0) for t in first], axis=0),
        jnp.concatenate([jnp.where(lower, 0.0, t) for t in second], axis=0),
    )


def unstack_heads(ref, pair, first, second):
    rows = first.shape[0] // 3
    base = pair * (3 * LANES)
    lower = lane_ids((rows, LANES)) < HD
    tiles = (
        jnp.where(lower, first[:rows], half_turn(first[rows : 2 * rows])),
        jnp.where(lower, first[2 * rows :], second[:rows]),
        jnp.where(lower, half_turn(second[rows : 2 * rows]), second[2 * rows :]),
    )
    for t in range(3):
        ref[:, pl.ds(pl.multiple_of(base + LANES * t, LANES), LANES)] = tiles[t].astype(ref.dtype)


def project_kernel(
    pieces, chips, members, slots, all_groups, micros, order_ref, me_ref, *refs
):
    x_refs = refs[:micros]
    gain_ref = refs[micros]
    piece_refs = refs[micros + 1 : micros + 1 + len(pieces)]
    refs = refs[micros + 1 + len(pieces) :]
    h_ref = refs[0]
    kv_refs = refs[1 : 1 + micros]
    win_ref, wout_ref, held, held_out, sems, out_sems = refs[1 + micros :]
    groups = held.shape[1] // BC
    kv_groups = kv_refs[0].shape[-1] // BC
    rows = x_refs[0].shape[0]
    ctx, shard = me_ref[0], me_ref[1]
    chip, core = lax.div(ctx, 2), lax.rem(ctx, 2)

    for ref, (other_core, offset, first, cut) in zip(piece_refs, pieces):

        @pl.loop(0, ref.shape[0])
        def _(i):
            source = lax.rem(chip - (first + lax.div(i, slots)) + chips, chips) * 2
            source = source + jnp.bitwise_xor(core, other_core)
            source = source * members + jnp.bitwise_xor(shard, offset)
            number = order_ref[source * slots + lax.rem(i, slots)]
            a, b = lax.div(number, all_groups), lax.rem(number, all_groups)
            down = pl.ds(pl.multiple_of(a * BR + cut, 32), ref.shape[1])

            @pl.when(b < groups)
            def _():
                across = pl.ds(pl.multiple_of(b * BC, BC), BC)
                pltpu.make_async_copy(ref.at[i], held.at[down, across], sems.at[b]).start()

            @pl.when(b >= groups)
            def _():
                across = pl.ds(pl.multiple_of((b - groups) * BC, BC), BC)
                pltpu.make_async_copy(ref.at[i], held_out.at[down, across], sems.at[groups]).start()

    for m in range(micros):
        h_ref[m * rows : (m + 1) * rows, :] = unit_rows(x_refs[m][...], gain_ref[0:1])[0].astype(
            low_type
        )
    q_groups = groups - kv_groups

    @pl.loop(0, groups)
    def _(b):
        across = pl.ds(pl.multiple_of(b * BC, BC), BC)
        wait_bytes(held.at[:, across], sems.at[b])

    wait_bytes(held_out, sems.at[groups])
    copies = [
        pltpu.make_async_copy(held, win_ref, out_sems.at[0]),
        pltpu.make_async_copy(held_out, wout_ref, out_sems.at[1]),
    ]
    for copy in copies:
        copy.start()

    @pl.loop(0, kv_groups)
    def _(b):
        across = pl.ds(pl.multiple_of((q_groups + b) * BC, BC), BC)
        made = dot(h_ref[...], held[:, across]).astype(low_type)
        for m in range(micros):
            kv_refs[m][:, pl.ds(pl.multiple_of(b * BC, BC), BC)] = made[m * rows : (m + 1) * rows]

    for copy in copies:
        copy.wait()


def project(pieces, arrays, chips, members, slots, order, me, xs, gains):
    micros = len(xs)
    rows, width = xs[0].shape
    in_width = (HEADS + 2 * KVH) * HD
    out_width = HEADS * HD
    kv_width = 2 * KVH * HD
    made = call(
        functools.partial(
            project_kernel, pieces, chips, members, slots, (in_width + out_width) // BC, micros
        ),
        tuple(
            [shaped((micros * rows, width), low_type)]
            + [shaped((rows, kv_width), low_type)] * micros
            + [shaped((width, in_width), low_type), shaped((width, out_width), low_type)]
        ),
        [in_smem, in_smem] + [in_vmem] * (micros + 1) + [in_any] * len(arrays),
        tuple([in_vmem] * (1 + micros) + [in_any, in_any]),
        [
            pltpu.VMEM((width, in_width), low_type),
            pltpu.VMEM((width, out_width), low_type),
            pltpu.SemaphoreType.DMA((in_width // BC + 1,)),
            pltpu.SemaphoreType.DMA((2,)),
        ],
        2 * micros * rows * width * kv_width,
        4 * width * (in_width + out_width),
    )(order, me, *xs, gains, *arrays)
    return made[0], made[1 : 1 + micros], made[1 + micros], made[2 + micros]


def query_kernel(h_ref, w_ref, *refs):
    q_refs = refs[:-2]
    held, sems = refs[-2:]
    groups = held.shape[1] // BC
    rows = q_refs[0].shape[0]

    def copy(b):
        across = pl.ds(pl.multiple_of(b * BC, BC), BC)
        return pltpu.make_async_copy(w_ref.at[:, across], held.at[:, across], sems.at[b])

    @pl.loop(0, groups)
    def _(b):
        copy(b).start()

    @pl.loop(0, groups)
    def _(b):
        copy(b).wait()
        across = pl.ds(pl.multiple_of(b * BC, BC), BC)
        made = dot(h_ref[...], held[:, across]).astype(low_type)
        for m, ref in enumerate(q_refs):
            ref[:, across] = made[m * rows : (m + 1) * rows]


def make_queries(h, w, micros):
    total, width = h.shape
    q_width = HEADS * HD
    return call(
        query_kernel,
        tuple([shaped((total // micros, q_width), low_type)] * micros),
        [in_vmem, in_any],
        tuple([in_vmem] * micros),
        [pltpu.VMEM((width, q_width), low_type), pltpu.SemaphoreType.DMA((q_width // BC,))],
        2 * total * width * q_width,
        2 * width * q_width,
    )(h, w)


def load_keys(parts, held, sem):
    start = 0
    for part in parts:
        count = part.shape[0]
        pltpu.make_async_copy(part, held.at[pl.ds(start, count)], sem).start()
        start += count


def attend_kernel(count, q_ref, rpos_ref, kpos_ref, x_ref, gain_ref, w_ref, *refs):
    parts = refs[:count]
    ob_ref, log_ref, x2_ref, h2_ref, bias, kv_ref, held, sems = refs[count:]
    rows = q_ref.shape[0]
    load_keys(parts, kv_ref, sems.at[0])
    pltpu.make_async_copy(w_ref, held, sems.at[1]).start()
    bias[...] = jnp.where(kpos_ref[...] <= rpos_ref[...], 0.0, masked_score)
    log_ref[...] = jnp.zeros_like(log_ref)
    length = kv_ref.shape[0]
    wait_bytes(kv_ref, sems.at[0])

    @pl.loop(0, KVH // 2)
    def _(pair):
        lane = pl.multiple_of(pair * LANES, LANES)
        keys = kv_ref[:, pl.ds(lane, LANES)]
        values = kv_ref[:, pl.ds(pl.multiple_of(lane + KVH * HD, LANES), LANES)]
        stacked = stack_heads(q_ref, pair, HD**-0.5)
        mixed = []
        for part in range(2):
            scores = dot(stacked[part].astype(low_type), keys, NT)
            scores = (scores.reshape(3, rows, length) + bias[...][None]).reshape(3 * rows, length)
            largest = jnp.max(scores, axis=-1, keepdims=True)
            raised = jnp.exp(scores - largest)
            summed = jnp.sum(raised, axis=-1, keepdims=True)
            mixed.append(dot(raised.astype(low_type), values) / summed)
            log_ref[...] = jnp.where(
                lane_ids(log_ref.shape) == 2 * pair + part, largest + jnp.log(summed), log_ref[...]
            )
        unstack_heads(ob_ref, pair, mixed[0], mixed[1])

    wait_bytes(held, sems.at[1])
    for n in range(held.shape[0] // BC):
        cut = slice(n * BC, (n + 1) * BC)
        x2_ref[:, cut] = x_ref[:, cut] + dot(ob_ref[...], held[cut, :], NT)
    h2_ref[...] = unit_rows(x2_ref[...], gain_ref[1:2])[0].astype(low_type)


def attend(q, kv_parts, rows_pos, key_pos, x, gains, w):
    rows, width = q.shape
    length = key_pos.shape[1]
    model = x.shape[1]
    return call(
        functools.partial(attend_kernel, len(kv_parts)),
        (
            shaped((rows, width), low_type),
            shaped((3 * rows, LANES), jnp.float32),
            shaped((rows, model), jnp.float32),
            shaped((rows, model), low_type),
        ),
        [in_vmem] * 5 + [in_any] * (1 + len(kv_parts)),
        (in_vmem,) * 4,
        [
            pltpu.VMEM((rows, length), jnp.float32),
            pltpu.VMEM((length, kv_parts[0].shape[1]), low_type),
            pltpu.VMEM((model, width), low_type),
            pltpu.SemaphoreType.DMA((2,)),
        ],
        16 * rows * length * width,
        8 * MIB,
    )(q, rows_pos, key_pos, x, gains, w, *kv_parts)


def router_parts(h2, router, experts):
    logits = dot(h2, router)
    logits = jnp.where(lane_ids(logits.shape) < experts, logits, masked_score)
    raised = jnp.exp(logits - jnp.max(logits, axis=-1, keepdims=True))
    return raised / jnp.sum(raised, axis=-1, keepdims=True)


def expert_kernel(sources, micro, order_ref, me_ref, router_ref, *refs):
    h_parts = refs[:sources]
    c_parts = refs[sources : 2 * sources]
    w_ref = refs[2 * sources]
    outs = refs[2 * sources + 1 :]
    back_refs = outs[:sources]
    z_ref, dg_ref, du_ref, cs, xs_ref = outs[sources : sources + 5]
    held, chance, load_sem, w_sems = outs[sources + 5 :]
    rows, width = h_parts[0].shape
    row_groups = width // BR
    col_groups = FF // BC
    for j in range(sources):
        pltpu.make_async_copy(h_parts[j], xs_ref.at[pl.ds(j * rows, rows)], load_sem.at[0]).start()
        pltpu.make_async_copy(
            c_parts[j].at[pl.ds(micro * rows, rows)], cs.at[pl.ds(j * rows, rows)], load_sem.at[1]
        ).start()
    for b in range(col_groups):

        @pl.loop(0, row_groups)
        def _(a):
            for k in range(3):
                pltpu.make_async_copy(
                    w_ref.at[order_ref[(k * row_groups + a) * col_groups + b]],
                    held.at[k, pl.ds(pl.multiple_of(a * BR, 64), BR), pl.ds(b * BC, BC)],
                    w_sems.at[b],
                ).start()

    wait_bytes(xs_ref, load_sem.at[0])
    wait_bytes(cs, load_sem.at[1])
    me = me_ref[1]
    probs = router_parts(xs_ref[...], router_ref[...], sources)
    hits = cs[:, width:].astype(jnp.float32)
    mine = lane_ids(hits.shape) == me
    hit = jnp.sum(jnp.where(mine, hits, 0.0), axis=-1, keepdims=True)
    weight = jnp.sum(jnp.where(mine, probs, 0.0), axis=-1, keepdims=True) * hit
    chance[...] = jnp.zeros_like(chance)

    @pl.loop(0, col_groups)
    def _(b):
        cut = pl.ds(pl.multiple_of(b * BC, BC), BC)
        wait_bytes(held.at[:, :, cut], w_sems.at[b])
        gate = dot(xs_ref[...], held[0, :, cut])
        up = dot(xs_ref[...], held[1, :, cut])
        down = dot(cs[:, :width], held[2, :, cut])
        sig = jax.nn.sigmoid(gate)
        act = gate * sig
        hidden = act * up
        chance[...] += jnp.sum(down * hidden, axis=-1, keepdims=True)
        z_ref[:, cut] = (hidden * weight).astype(low_type)
        down = down * weight
        dg_ref[:, cut] = (down * up * (sig + act * (1.0 - sig))).astype(low_type)
        du_ref[:, cut] = (down * act).astype(low_type)

    for n in range(width // BC):
        cut = slice(n * BC, (n + 1) * BC)
        back = dot(dg_ref[...], held[0, cut, :], NT) + dot(du_ref[...], held[1, cut, :], NT)
        for j in range(sources):
            back_refs[j][:, cut] = back[j * rows : (j + 1) * rows].astype(low_type)
    told = chance[...] * hit
    high_part = told.astype(low_type)
    low_part = (told - high_part.astype(jnp.float32)).astype(low_type)
    lanes = lane_ids((sources * rows, LANES))
    tail = jnp.where(lanes == 0, high_part, jnp.where(lanes == 1, low_part, jnp.zeros_like(low_part)))
    for j in range(sources):
        back_refs[j][:, width:] = tail[j * rows : (j + 1) * rows]


def run_expert(micro, order, me, router, h_parts, c_parts, w):
    sources = len(h_parts)
    rows, width = h_parts[0].shape
    total = sources * rows
    return call(
        functools.partial(expert_kernel, sources, micro),
        tuple(
            [shaped((rows, width + LANES), low_type)] * sources
            + [shaped((total, FF), low_type)] * 3
            + [shaped((total, width + LANES), low_type), shaped((total, width), low_type)]
        ),
        [in_smem, in_smem, in_vmem] + [in_any] * (2 * sources + 1),
        tuple([in_vmem] * (sources + 5)),
        [
            pltpu.VMEM((3, width, FF), low_type),
            pltpu.VMEM((total, 1), jnp.float32),
            pltpu.SemaphoreType.DMA((2,)),
            pltpu.SemaphoreType.DMA((FF // BC,)),
        ],
        10 * total * width * FF,
        20 * MIB,
    )(order, me, router, *h_parts, *c_parts, w)


def produce_kernel(sources, order_ref, w_ref, *refs):
    out_refs = refs[-3 - sources : -3]
    z_refs = refs[: -3 - sources]
    zs, held, sem = refs[-3:]
    width = held.shape[0]
    total = z_refs[0].shape[0]
    rows = total // sources
    row_groups, col_groups = width // BR, FF // BC

    @pl.loop(0, row_groups)
    def _(a):
        for b in range(col_groups):
            pltpu.make_async_copy(
                w_ref.at[order_ref[(2 * row_groups + a) * col_groups + b]],
                held.at[pl.ds(pl.multiple_of(a * BR, 64), BR), pl.ds(b * BC, BC)],
                sem,
            ).start()

    for m, z_ref in enumerate(z_refs):
        zs[m * total : (m + 1) * total] = z_ref[...]
    wait_bytes(held, sem)
    for n in range(width // BC):
        cut = slice(n * BC, (n + 1) * BC)
        made = dot(zs[...], held[cut, :], NT).astype(low_type)
        for m in range(len(z_refs)):
            for j in range(sources):
                start = m * total + j * rows
                out_refs[j][m * rows : (m + 1) * rows, cut] = made[start : start + rows]


def produce(order, w, zs, sources, width):
    micros = len(zs)
    total = zs[0].shape[0]
    return call(
        functools.partial(produce_kernel, sources),
        tuple([shaped((micros * total // sources, width), low_type)] * sources),
        [in_smem, in_any] + [in_vmem] * micros,
        tuple([in_vmem] * sources),
        [
            pltpu.VMEM((micros * total, FF), low_type),
            pltpu.VMEM((width, FF), low_type),
            pltpu.SemaphoreType.DMA,
        ],
        2 * micros * total * width * FF,
        8 * MIB,
    )(order, w, *zs)


def outer_kernel(groups, col_groups, order_ref, *refs):
    micros = len(refs[:-5]) // (len(groups) + 2)
    lefts = [refs[i * micros : (i + 1) * micros] for i in range(2)]
    rights = [refs[(2 + i) * micros : (3 + i) * micros] for i in range(len(groups))]
    out_refs, (turned, stage, sems) = refs[-5:-3], refs[-3:]
    rows = rights[0][0].shape[0]
    width = turned.shape[1]
    span = 2 * BR
    for side in range(2):
        for m in range(micros):
            for r in range(0, rows, LANES):
                part = lefts[side][m][r : r + LANES, :width]
                turned[side, :, m * rows + r : m * rows + r + LANES] = part.T
    row_groups = width // BR
    steps = [(k, p) for k in range(len(groups)) for p in range(width // span)]
    for n, (k, p) in enumerate(steps):
        slot = n % 2
        if n >= 2:
            wait_bytes(stage.at[slot], sems.at[slot])
        cut = slice(p * span, (p + 1) * span)
        made = 0.0
        for m in range(micros):
            left = turned[groups[k], cut, m * rows : (m + 1) * rows]
            made = made + dot(left, rights[k][m][...])
        stage[slot] = made.astype(low_type)
        for half in range(2):
            for b in range(col_groups):
                number = (k * row_groups + 2 * p + half) * col_groups + b
                place = order_ref[number]
                for side in range(2):
                    pltpu.make_async_copy(
                        stage.at[
                            slot, pl.ds(half * BR, BR), pl.ds(b * BC + side * LANES, LANES)
                        ],
                        out_refs[side].at[place],
                        sems.at[slot],
                    ).start()
    for slot in range(2):
        wait_bytes(stage.at[slot], sems.at[slot])


def outer_blocks(order, width, groups, lefts, rights):
    flat = [part for group in lefts + rights for part in group]
    rows = sum(part.shape[0] for part in rights[0])
    cols = rights[0][0].shape[1]
    blocks = len(groups) * width * cols // (BR * BC)
    return call(
        functools.partial(outer_kernel, groups, cols // BC),
        (shaped((blocks, BR, LANES), low_type),) * 2,
        [in_smem] + [in_vmem] * len(flat),
        (in_any,) * 2,
        [
            pltpu.VMEM((2, width, rows), low_type),
            pltpu.VMEM((2, 2 * BR, cols), low_type),
            pltpu.SemaphoreType.DMA((2,)),
        ],
        2 * rows * blocks * BR * BC,
        blocks * BR * BC * 2 + sum(f.size * 2 for f in flat),
    )(order, *flat)


def xor_plan(members, offset):
    if members != 4:
        return list(range(1, members)), [0]
    first = 1 if offset % 2 else 2
    return [first, 3], [0, 3 - first]


def pieces_kernel(members, counts, cols, turned_first, me_ref, *refs):
    row_groups = 8
    lists = []
    for left_count, right_count in counts:
        lists.append((refs[:left_count], refs[left_count : left_count + right_count]))
        refs = refs[left_count + right_count :]
    outs, refs = refs[:4], refs[4:]
    extra = refs[0] if not turned_first else None
    turned, rights, stage, sems = refs[0 if turned_first else 1 :]
    ctx, shard = me_ref[0], me_ref[1]
    core = lax.rem(ctx, 2)
    total = turned.shape[2]
    row_groups = turned.shape[1] // BR
    base = 0
    for g, (_, parts) in enumerate(lists):
        start = 0
        for part in parts:
            count = part.shape[0]
            for b in range(cols[g]):
                lane = pl.multiple_of(b * BC + core * LANES, LANES)
                pltpu.make_async_copy(
                    part.at[:, pl.ds(lane, LANES)],
                    rights.at[pl.ds(start, count), pl.ds((base + b) * LANES, LANES)],
                    sems.at[g],
                ).start()
            start += count
        base += cols[g]
    for g, (parts, _) in enumerate(lists):
        if g == 0 and turned_first:
            turned[0] = parts[0][...]
            continue
        start = 0
        for part in parts:
            for r in range(0, part.shape[0], LANES):
                turned[g, :, start : start + LANES] = part[r : r + LANES, :].T
                start += LANES
    if extra is not None:
        extra[...] = turned[0]
    all_cols = sum(cols)
    half_blocks = row_groups // 2 * all_cols
    span = BR // members
    base = 0
    for g in range(len(lists)):
        wide_cols = cols[g] * LANES
        wait_bytes(rights.at[:, pl.ds(base * LANES, wide_cols)], sems.at[g])
        for a in range(row_groups):
            made = dot(
                turned[g, a * BR : (a + 1) * BR, :],
                rights[:, base * LANES : base * LANES + wide_cols],
            )
            stage[a % 2, :, :wide_cols] = made.astype(stage.dtype)
            half = a // (row_groups // 2)
            first = (a % (row_groups // 2)) * all_cols + base
            for out, hops in zip(outs[2 * half : 2 * half + 2], xor_plan(members, 1 - half)):
                for place, hop in enumerate(hops):
                    down = pl.multiple_of(jnp.bitwise_xor(shard, hop) * span, 16 if span % 16 == 0 else 8)
                    for b in range(cols[g]):
                        out[place * half_blocks + first + b] = stage[
                            a % 2, pl.ds(down, span), b * LANES : (b + 1) * LANES
                        ].astype(low_type)
        base += cols[g]


def gradient_pieces(members, me, groups, cols, turned_first):
    counts = tuple((len(left), len(right)) for left, right in groups)
    flat = [part for left, right in groups for part in left + right]
    total = sum(part.shape[0] for part in groups[0][1])
    width = groups[0][0][0].shape[0 if turned_first else 1]
    row_groups = width // BR
    half_blocks = row_groups // 2 * sum(cols)
    span = BR // members
    stage_type = jnp.float32 if span % 16 else low_type
    outs = []
    for half in range(2):
        for hops in xor_plan(members, 1 - half):
            outs.append(shaped((len(hops) * half_blocks, span, LANES), low_type))
    out_specs = [in_vmem] * 4
    if not turned_first:
        outs.append(shaped((width, total), low_type))
        out_specs.append(in_vmem)
    in_specs = [in_smem]
    for left, right in groups:
        in_specs += [in_vmem] * len(left) + [in_any] * len(right)
    return call(
        functools.partial(pieces_kernel, members, counts, tuple(cols), turned_first),
        tuple(outs),
        in_specs,
        tuple(out_specs),
        [
            pltpu.VMEM((len(groups), width, total), low_type),
            pltpu.VMEM((total, sum(cols) * LANES), low_type),
            pltpu.VMEM((2, BR, max(cols) * LANES), stage_type),
            pltpu.SemaphoreType.DMA((len(groups),)),
        ],
        2 * total * width * sum(cols) * LANES,
        16 * MIB,
    )(me, *flat)


def merge_kernel(
    sources, me_ref, x2_ref, cot_ref, h2_ref, gain_ref, router_ref, w_ref, *refs
):
    back_refs = refs[:sources]
    dx_ref, da_ref, do_ref, stat_ref, held, sem = refs[sources:]
    rows, width = x2_ref.shape
    pltpu.make_async_copy(w_ref, held, sem).start()
    lanes = lane_ids((rows, LANES))
    prob_grad = jnp.zeros((rows, LANES), jnp.float32)
    gathered = jnp.zeros((rows, width), jnp.float32)
    for j in range(sources):
        tail = back_refs[j][:, width:].astype(jnp.float32)
        told = jnp.sum(tail, axis=-1, keepdims=True)
        expert = jnp.bitwise_xor(me_ref[1], j)
        prob_grad = prob_grad + jnp.where(lanes == expert, told, 0.0)
        gathered = gathered + back_refs[j][:, :width].astype(jnp.float32)
    h2 = h2_ref[...]
    probs = router_parts(h2, router_ref[...], sources)
    logit_grad = probs * (prob_grad - jnp.sum(probs * prob_grad, axis=-1, keepdims=True))
    high_part = logit_grad.astype(low_type)
    low_part = (logit_grad - high_part.astype(jnp.float32)).astype(low_type)
    router_grad = dot(high_part, h2, TN) + dot(low_part, h2, TN)
    gathered = gathered + dot(high_part, router_ref[...], NT) + dot(low_part, router_ref[...], NT)
    x2 = x2_ref[...]
    inverse = lax.rsqrt(jnp.mean(x2 * x2, axis=-1, keepdims=True) + norm_eps)
    moe_grad, gain_grad = unit_back(x2, gain_ref[1:2], inverse, gathered)
    after = cot_ref[...] + moe_grad
    dx_ref[...] = after
    da_ref[...] = after.astype(low_type)
    experts_up = stat_ref.shape[0] - 8
    stat_ref[:experts_up] = router_grad[:experts_up]
    stat_ref[experts_up:] = jnp.broadcast_to(gain_grad, (8, width))
    wait_bytes(held, sem)
    for n in range(held.shape[1] // BC):
        cut = slice(n * BC, (n + 1) * BC)
        do_ref[:, cut] = dot(da_ref[...], held[:, cut]).astype(low_type)


def merge(me, x2, cot, h2, gains, router, w, backs):
    rows, width = x2.shape
    sources = len(backs)
    experts_up = -(-sources // 8) * 8
    return call(
        functools.partial(merge_kernel, sources),
        (
            shaped((rows, width), jnp.float32),
            shaped((rows, width), low_type),
            shaped((rows, HEADS * HD), low_type),
            shaped((experts_up + 8, width), jnp.float32),
        ),
        [in_smem] + [in_vmem] * 5 + [in_any] + [in_vmem] * sources,
        (in_vmem,) * 4,
        [pltpu.VMEM((width, HEADS * HD), low_type), pltpu.SemaphoreType.DMA],
        2 * rows * width * HEADS * HD,
        10 * MIB,
    )(me, x2, cot, h2, gains, router, w, *backs)


def attend_back_kernel(count, q_ref, rpos_ref, kpos_ref, ob_ref, log_ref, do_ref, *refs):
    parts = refs[:count]
    dq_ref, own_ref, other_ref, bias, kv_ref, sem = refs[count:]
    rows = q_ref.shape[0]
    load_keys(parts, kv_ref, sem)
    length = kv_ref.shape[0]
    bias[...] = jnp.where(kpos_ref[...] <= rpos_ref[...], 0.0, masked_score)
    wait_bytes(kv_ref, sem)

    @pl.loop(0, KVH // 2)
    def _(pair):
        lane = pl.multiple_of(pair * LANES, LANES)
        value_lane = pl.multiple_of(lane + KVH * HD, LANES)
        keys = kv_ref[:, pl.ds(lane, LANES)]
        values = kv_ref[:, pl.ds(value_lane, LANES)]
        queries = stack_heads(q_ref, pair, HD**-0.5)
        grads = stack_heads(do_ref, pair)
        mixes = stack_heads(ob_ref, pair)
        query_grads = []
        key_grad = value_grad = None
        for part in range(2):
            query = queries[part].astype(low_type)
            grad = grads[part].astype(low_type)
            log_total = jnp.sum(
                jnp.where(lane_ids(log_ref.shape) == 2 * pair + part, log_ref[...], 0.0),
                axis=-1,
                keepdims=True,
            )
            delta = jnp.sum(grads[part] * mixes[part], axis=-1, keepdims=True)
            scores = dot(query, keys, NT)
            scores = (scores.reshape(3, rows, length) + bias[...][None]).reshape(3 * rows, length)
            chance = jnp.exp(scores - log_total)
            prob_grad = dot(grad, values, NT)
            score_grad = (chance * (prob_grad - delta)).astype(low_type)
            value_term = dot(chance.astype(low_type), grad, TN)
            key_term = dot(score_grad, query, TN)
            key_grad = key_term if part == 0 else key_grad + key_term
            value_grad = value_term if part == 0 else value_grad + value_term
            query_grads.append(dot(score_grad, keys) * HD**-0.5)
        unstack_heads(dq_ref, pair, query_grads[0], query_grads[1])
        half = length // 2
        for ref, cut in ((own_ref, slice(0, half)), (other_ref, slice(half, length))):
            ref[:, pl.ds(lane, LANES)] = key_grad[cut].astype(low_type)
            ref[:, pl.ds(value_lane, LANES)] = value_grad[cut].astype(low_type)


def attend_back(q, kv_parts, rows_pos, key_pos, ob, log_total, do):
    rows, width = q.shape
    length = key_pos.shape[1]
    kv_width = kv_parts[0].shape[1]
    return call(
        functools.partial(attend_back_kernel, len(kv_parts)),
        (shaped((rows, width), low_type),) + (shaped((length // 2, kv_width), low_type),) * 2,
        [in_vmem] * 6 + [in_any] * len(kv_parts),
        (in_vmem,) * 3,
        [
            pltpu.VMEM((rows, length), jnp.float32),
            pltpu.VMEM((length, kv_width), low_type),
            pltpu.SemaphoreType.DMA,
        ],
        40 * rows * length * width,
        8 * MIB,
    )(q, rows_pos, key_pos, ob, log_total, do, *kv_parts)


def query_back_kernel(w_ref, *refs):
    micros = (len(refs) - 3) // 2
    dq_refs, out_refs = refs[:micros], refs[micros : 2 * micros]
    rows_ref, held, sem = refs[2 * micros :]
    rows = dq_refs[0].shape[0]
    copy = pltpu.make_async_copy(w_ref.at[:, pl.ds(0, held.shape[1])], held, sem)
    copy.start()
    for m in range(micros):
        rows_ref[m * rows : (m + 1) * rows] = dq_refs[m][...]
    copy.wait()
    for n in range(held.shape[0] // BC):
        cut = slice(n * BC, (n + 1) * BC)
        made = dot(rows_ref[...], held[cut, :], NT)
        for m in range(micros):
            out_refs[m][:, cut] = made[m * rows : (m + 1) * rows]


def query_back(w, dqs):
    micros = len(dqs)
    rows, q_width = dqs[0].shape
    width = w.shape[0]
    return call(
        query_back_kernel,
        tuple([shaped((rows, width), jnp.float32)] * micros),
        [in_any] + [in_vmem] * micros,
        tuple([in_vmem] * micros),
        [
            pltpu.VMEM((micros * rows, q_width), low_type),
            pltpu.VMEM((width, q_width), low_type),
            pltpu.SemaphoreType.DMA,
        ],
        2 * micros * rows * width * q_width,
        7 * MIB,
    )(w, *dqs)


def input_kernel(x_ref, gain_ref, w_ref, *refs):
    micros, rows = x_ref.shape[:2]
    dx_refs = refs[:micros]
    part_refs = refs[micros : 2 * micros]
    dkv_refs = refs[2 * micros : 3 * micros]
    out_ref, stat_ref, rows_ref, grad, held, sem = refs[3 * micros :]
    kv_width = held.shape[1]
    copy = pltpu.make_async_copy(
        w_ref.at[:, pl.ds(w_ref.shape[1] - kv_width, kv_width)], held, sem
    )
    copy.start()
    for m in range(micros):
        rows_ref[m * rows : (m + 1) * rows] = dkv_refs[m][...]
    copy.wait()
    for n in range(held.shape[0] // BC):
        cut = slice(n * BC, (n + 1) * BC)
        made = dot(rows_ref[...], held[cut, :], NT)
        for m in range(micros):
            grad[m, :, cut] = part_refs[m][:, cut] + made[m * rows : (m + 1) * rows]
    total = jnp.zeros((1, x_ref.shape[-1]), jnp.float32)
    for m in range(micros):
        x = x_ref[m]
        inverse = lax.rsqrt(jnp.mean(x * x, axis=-1, keepdims=True) + norm_eps)
        term, gain_grad = unit_back(x, gain_ref[0:1], inverse, grad[m])
        out_ref[m] = dx_refs[m][...] + term
        total = total + gain_grad
    stat_ref[...] = jnp.broadcast_to(total, stat_ref.shape)


def input_back(x, gains, w, dxs, parts, dkvs):
    micros, rows, width = x.shape
    kv_width = dkvs[0].shape[1]
    return call(
        input_kernel,
        (shaped(x.shape, jnp.float32), shaped((8, width), jnp.float32)),
        [in_vmem, in_vmem, in_any] + [in_vmem] * (3 * micros),
        (in_vmem,) * 2,
        [
            pltpu.VMEM((micros * rows, kv_width), low_type),
            pltpu.VMEM(x.shape, jnp.float32),
            pltpu.VMEM((width, kv_width), low_type),
            pltpu.SemaphoreType.DMA,
        ],
        2 * micros * rows * width * kv_width,
        14 * MIB,
    )(x, gains, w, *dxs, *parts, *dkvs)


def rotate_kernel(b_ref, m_ref, s_ref, l_ref, r_ref, *refs):
    grad_ref, new_ref, moment_ref, second_ref = refs[-4:]
    parts = [ref[0].astype(jnp.float32) for ref in refs[:-4]]
    gradient = parts[0] if len(parts) == 1 else jnp.concatenate(parts, axis=1)
    grad_ref[0] = gradient
    left = l_ref[0].astype(low_type)
    right = r_ref[0].astype(low_type)
    rotated = dot(dot(left, gradient.astype(low_type), TN).astype(low_type), right)
    moment = beta_one * m_ref[0] + (1.0 - beta_one) * rotated
    second = beta_two * s_ref[0] + (1.0 - beta_two) * rotated * rotated
    moment_ref[0] = moment
    second_ref[0] = second
    direction = (moment / (jnp.sqrt(second) + adam_eps)).astype(low_type)
    turned = dot(dot(left, direction).astype(low_type), right, NT)
    new_ref[0] = b_ref[0] - rate * turned


def rotate(weight, gradients, moment, second, left, right):
    count = weight.shape[0]

    def spec(rows, cols):
        return pl.BlockSpec((1, rows, cols), lambda i: (i, 0, 0))

    block = spec(BR, BC)
    return pl.pallas_call(
        rotate_kernel,
        grid=(count,),
        out_shape=(shaped(weight.shape, jnp.float32),) * 4,
        in_specs=[block] * 3
        + [spec(BR, BR), spec(BC, BC)]
        + [spec(BR, part.shape[2]) for part in gradients],
        out_specs=(block,) * 4,
        compiler_params=pltpu.CompilerParams(vmem_limit_bytes=VMEM_LIMIT),
        cost_estimate=pl.CostEstimate(
            flops=4 * count * BR * BC * (BR + BC),
            bytes_accessed=count * 2 * MIB,
            transcendentals=0,
        ),
    )(weight, moment, second, left, right, *gradients)


def adam(weight, gradient, moment, second, step_rate):
    moment_new = beta_one * moment + (1.0 - beta_one) * gradient
    second_new = beta_two * second + (1.0 - beta_two) * gradient * gradient
    return (
        weight - step_rate * moment_new / (jnp.sqrt(second_new) + adam_eps),
        moment_new,
        second_new,
    )


def piece_places(row_groups, q_groups, kv_groups):
    all_groups = 2 * q_groups + kv_groups
    out_groups = list(range(q_groups)) + list(range(q_groups + kv_groups, all_groups))
    numbers = [a * all_groups + b for a in range(row_groups) for b in out_groups]
    numbers += [a * all_groups + q_groups + b for a in range(row_groups) for b in range(kv_groups)]
    places = [0] * len(numbers)
    for place, number in enumerate(numbers):
        places[number] = place
    return places


def to_partner(array, offset):
    if offset == 0:
        return array
    count = lax.axis_size("shard")
    return lax.ppermute(array, "shard", [(i, i ^ offset) for i in range(count)])


def to_ctx(array, offset):
    count = lax.axis_size("ctx")
    return lax.ppermute(array, "ctx", [(i, i ^ offset) for i in range(count)])


def to_chip(array, offset):
    count = lax.axis_size("ctx")
    return lax.ppermute(array, "ctx", [(i, (i + 2 * offset) % count) for i in range(count)])


def after(value, *others):
    return lax.optimization_barrier((value, others))[0]


def from_chips(array, chips):
    return [array] + [to_chip(array, offset) for offset in range(1, chips)]


def wide(array):
    return array.astype(jnp.float32)


def sum_to_chips(parts):
    total = wide(parts[0])
    for offset in range(1, len(parts)):
        total = total + wide(to_chip(parts[offset], -offset))
    return total


def gather_weights(blocks, chips, members):
    parts = [blocks]
    for _ in range(chips - 1):
        parts.append(to_chip(parts[-1], 1))
    pieces, arrays = [], []
    gate = []

    def add(array, offset, first, cut):
        pieces.append((0, offset, first, cut))
        arrays.append(array)
        pieces.append((1, offset, first, cut))
        arrays.append(to_ctx(after(array, *gate), 1))
        return array

    def spread(group, first):
        add(group, 0, first, 0)
        if members == 4 and first > 0:
            by_one, by_two = to_partner(group, 1), to_partner(group, 2)
            add(by_one, 1, first, 0)
            add(by_two, 2, first, 0)
            half = BR // 2
            add(to_partner(by_one[:, :half], 2), 3, first, 0)
            add(to_partner(by_two[:, half:], 1), 3, first, half)
            return [by_one, by_two]
        got = [to_partner(group, offset) for offset in range(1, members)]
        for offset in range(1, members):
            add(got[offset - 1], offset, first, 0)
        return got

    got = [to_partner(blocks, offset) for offset in range(1, members)]
    gate.append(got[0])
    add(blocks, 0, 0, 0)
    for offset in range(1, members):
        add(got[offset - 1], offset, 0, 0)
    last = list(got)
    if chips > 1:
        last = spread(after(parts[1], *last), 1)
        gate[:] = last
        got = last
    if chips > 2:
        group = after(jnp.concatenate(parts[2:], axis=0), *last)
        spread(group, 2)
    return got + parts[1:], pieces, arrays


def add_wide(parts):
    total = wide(parts[0])
    for part in parts[1:]:
        total = total + wide(part)
    return total


def sum_members(made, ready, members):
    sums, seen = [], []
    for half in range(2):
        sent, kept = made[2 * half : 2 * half + 2]
        hops, keeps = xor_plan(members, 1 - half)
        count = kept.shape[0] // len(keeps)
        total = wide(kept[:count])
        if members == 4:
            got = to_partner(sent, hops[0])
            got = got if ready is None else after(got, ready)
            total = total + wide(got[:count])
            relay = (wide(kept[count:]) + wide(got[count:])).astype(low_type)
            second = to_partner(relay, keeps[1])
            seen.append(second)
            total = total + wide(second)
        else:
            for place, hop in enumerate(hops):
                total = total + wide(to_partner(sent[place * count : (place + 1) * count], hop))
        sums.append(total.astype(low_type).reshape(count, -1))
    return jnp.concatenate(sums, axis=0), seen


def sum_chips(rows, chip, chips):
    count = rows.shape[1] // chips

    def piece(offset):
        start = lax.rem(chip - offset + chips, chips) * count
        return lax.dynamic_slice_in_dim(rows, start, count, axis=1)

    return [piece(0)] + [to_chip(piece(offset), -offset) for offset in range(1, chips)]


def shards(
    tokens,
    cotangent,
    norm_gains,
    router,
    dense_weight,
    expert_weight,
    routes,
    assign,
    dense_order,
    expert_order,
    dense_moment,
    dense_second,
    dense_left,
    dense_right,
    expert_moment,
    expert_second,
    expert_left,
    expert_right,
    gains_moment,
    gains_second,
    router_moment,
    router_second,
):
    ctx_count = lax.axis_size("ctx")
    shard_count = lax.axis_size("shard")
    chips = ctx_count // 2
    micros, rows, width = tokens.shape
    slots = dense_weight.shape[0]
    span = rows // 2
    row_groups = width // BR
    q_groups = HEADS * HD // BC
    kv_groups = 2 * KVH * HD // BC

    expert_inverse = inverse_order(expert_order)
    ctx = lax.axis_index("ctx").astype(jnp.int32)
    me = jnp.stack([ctx, lax.axis_index("shard").astype(jnp.int32)])
    row_ids = jnp.arange(rows, dtype=jnp.int32)
    all_pos = assign[:, row_ids // span] * span + row_ids % span
    ring_ids = (ctx // 2 - jnp.arange(chips, dtype=jnp.int32)) % chips * 2
    key_ids = jnp.concatenate([ring_ids + ctx % 2, ring_ids + (1 - ctx % 2)])
    key_pos = all_pos[key_ids].reshape(1, rows * ctx_count)
    rows_pos = all_pos[ctx].reshape(rows, 1)
    router_pad = jnp.pad(router.astype(low_type), ((0, 0), (0, LANES - shard_count)))

    far, pieces, arrays = gather_weights(dense_weight.astype(low_type), chips, shard_count)
    expert_low = after(expert_weight[0].astype(low_type), *far)
    expert_all = lax.all_gather(expert_low, "ctx", axis=0, tiled=True)

    lanes = jnp.arange(LANES, dtype=jnp.int32)
    hits = jnp.sum((routes[..., None] == lanes).astype(low_type), axis=2)
    cot_rows = jnp.concatenate([cotangent.astype(low_type), hits], axis=2)
    cot_rows = cot_rows.reshape(micros * rows, width + LANES)
    cot_rows = after(cot_rows, *arrays[::2])
    cot_parts = [to_partner(cot_rows, j) for j in range(shard_count)]

    here, expert_inverse, router_pad, key_pos, rows_pos = lax.optimization_barrier(
        (me, expert_inverse, router_pad, key_pos, rows_pos)
    )
    h1, kv, w_in, w_out = project(
        pieces,
        arrays,
        chips,
        shard_count,
        slots,
        dense_order,
        here,
        [tokens[m] for m in range(micros)],
        norm_gains,
    )
    q = make_queries(h1, w_in, micros)
    h1_other = to_ctx(h1, 1)
    kvs, obs, logs, x2s, h2s = [], [], [], [], []
    chip_kv = []
    for m in range(micros):
        own = kv[m] if m == 0 else after(kv[m], chip_kv[m - 1][1 % chips])
        chip_kv.append(from_chips(own, chips))
    for m in range(micros):
        query = after(q[m], *(cot_parts if m == 0 else obs[m - 1 : m]))
        parts = chip_kv[m]
        swapped = after(parts, q[0] if m == 0 else obs[m - 1])
        kvs.append(parts + [to_ctx(part, 1) for part in swapped])
        ob, log_total, x2, h2 = attend(
            query, kvs[m], rows_pos, key_pos, tokens[m], norm_gains, w_out
        )
        obs.append(ob)
        logs.append(log_total)
        x2s.append(x2)
        h2s.append(h2)
    ob_others = [to_ctx(ob, 1) for ob in obs]

    h_parts = []
    for m in range(micros):
        own = h2s[m] if m == 0 else after(h2s[m], *h_parts[m - 1])
        h_parts.append([own] + [to_partner(own, j) for j in range(1, shard_count)])
    sent = []
    zs, dgs, dus, cs, xs = [], [], [], [], []
    for m in range(micros):
        here = after(me, h2s[-1], h1_other, *ob_others) if m == 0 else after(me, zs[-1])
        made = run_expert(m, expert_inverse, here, router_pad, h_parts[m], cot_parts, expert_all)
        sent.append(made[:shard_count])
        z, dg, du, c, x = made[shard_count:]
        zs.append(z)
        dgs.append(dg)
        dus.append(du)
        cs.append(c)
        xs.append(x)
    backs = [[to_partner(sent[m][j], j) for j in range(shard_count)] for m in range(micros)]

    expert_terms = outer_blocks(
        after(expert_inverse, *backs[0]), width, (0, 0, 1), [xs, cs], [dgs, dus, zs]
    )
    dxs, das, dqs, stats, own_grads, far_grads = [], [], [], [], [], []
    outs = None
    for m in range(micros):
        here = after(me, expert_terms, backs[-1]) if m == 0 else after(me, dqs[-1])
        dx, da, do, stat = merge(
            here, x2s[m], cotangent[m], h2s[m], norm_gains, router_pad, w_out, backs[m]
        )
        if m == micros - 1:
            ready = own_grads[-1][1 % chips] if m else da
            outs = produce(after(expert_inverse, da, ready), expert_all, zs, shard_count, width)
            do = after(do, outs[0], *(far_grads[-1][:1] + far_grads[-1][-1:] if m else []))
        dq, dkv_own, dkv_other = attend_back(
            q[m], kvs[m], rows_pos, key_pos, obs[m], logs[m], do
        )
        got = to_ctx(dkv_other, 1)
        parts = []
        for o in range(chips):
            cut = slice(o * rows, (o + 1) * rows)
            part = wide(dkv_own[cut]) + wide(got[cut])
            parts.append(part if o == 0 else part.astype(low_type))
        own_grads.append(parts)
        far_grads.append([to_chip(part, -o) for o, part in enumerate(parts[1:], 1)])
        dxs.append(dx)
        das.append(da)
        dqs.append(dq)
        stats.append(stat)

    dkvs = [add_wide([own_grads[m][0]] + far_grads[m]).astype(low_type) for m in range(micros)]

    def other_core(parts):
        return [to_ctx(part, 1) for part in parts]

    da_others, dq_others = other_core(das), other_core(dqs)
    first_term = after(expert_terms[0], *backs[-1])
    expert_sums = [lax.psum_scatter(first_term, "ctx", scatter_dimension=0, tiled=True)]
    late_term = after(expert_terms[1], *dkvs)
    expert_sums.append(lax.psum_scatter(late_term, "ctx", scatter_dimension=0, tiled=True))
    early = gradient_pieces(
        shard_count,
        after(me, own_grads[-1][1 % chips]),
        [([h1, h1_other], dqs + dq_others), (das + da_others, obs + ob_others)],
        [q_groups, q_groups],
        False,
    )
    h1_turned = early[4]
    early_rows, early_seen = sum_members(early[:4], None, shard_count)
    parts_back = query_back(after(w_in, early[0]), dqs)
    dkv_others = other_core(after(dkvs, parts_back))
    late = gradient_pieces(
        shard_count,
        after(me, *early_seen),
        [([h1_turned], dkvs + dkv_others)],
        [kv_groups],
        True,
    )
    input_grad, gain_stat = input_back(
        after(tokens, late[0]), norm_gains, w_in, dxs, parts_back, dkvs
    )
    late_rows, late_seen = sum_members(late[:4], input_grad, shard_count)
    arrived = [to_partner(part, j) for j, part in enumerate(after(list(outs), *late_seen))]
    chip = ctx // 2
    early_sum = add_wide(sum_chips(early_rows, chip, chips)).astype(low_type)
    late_sum = add_wide(sum_chips(late_rows, chip, chips)).astype(low_type)
    all_sums = jnp.concatenate([early_sum, late_sum], axis=0)
    places = jnp.asarray(piece_places(row_groups, q_groups, kv_groups), jnp.int32)[dense_order]
    chosen = (places[:, None] == jnp.arange(all_sums.shape[0])[None, :]).astype(low_type)
    ordered = jnp.dot(chosen, all_sums, preferred_element_type=jnp.float32).astype(low_type)
    devices = ctx_count * shard_count
    piece_width = ordered.shape[1]
    experts_up = stats[0].shape[0] - 8
    stat_rows = add_wide(stats)
    stat_rows = jnp.concatenate(
        [stat_rows[:shard_count], gain_stat[:1], stat_rows[experts_up : experts_up + 1]], axis=0
    )
    stat_parts = stat_rows.astype(low_type).reshape(-1, piece_width)
    extra = stat_parts.shape[0]
    ordered = jnp.concatenate(
        [
            ordered.reshape(devices, slots, piece_width),
            jnp.broadcast_to(stat_parts, (devices, extra, piece_width)),
        ],
        axis=1,
    ).reshape(devices * (slots + extra), piece_width)
    ordered = lax.all_to_all(ordered, ("ctx", "shard"), split_axis=0, concat_axis=0, tiled=True)
    ordered = ordered.reshape(devices, slots + extra, piece_width)
    stat_rows = jnp.sum(wide(ordered[:, slots:]), axis=0).reshape(shard_count + 2, width)
    ordered = ordered[:, :slots].reshape(
        chips, 2, shard_count, slots, BR // (shard_count * chips), LANES
    )
    dense_sum = ordered.transpose(3, 2, 0, 4, 1, 5).reshape(slots, BR, BC)
    router_grad = stat_rows[:shard_count].T
    gains_grad = stat_rows[shard_count:]

    expert_grad, expert_new, expert_moment_new, expert_second_new = rotate(
        expert_weight[0], expert_sums, expert_moment[0], expert_second[0], expert_left[0], expert_right[0]
    )
    dense_grad, dense_new, dense_moment_new, dense_second_new = rotate(
        dense_weight, [dense_sum], dense_moment, dense_second, dense_left, dense_right
    )
    outputs = []
    for m in range(micros):
        total = x2s[m]
        for part in after(arrived, dense_new, expert_new):
            total = total + wide(part[m * rows : (m + 1) * rows])
        outputs.append(total)

    gains_new, gains_moment_new, gains_second_new = adam(
        norm_gains, gains_grad, gains_moment, gains_second, gain_rate
    )
    router_new, router_moment_new, router_second_new = adam(
        router, router_grad, router_moment, router_second, rate
    )
    return (
        jnp.stack(outputs),
        input_grad,
        dense_grad,
        dense_new,
        dense_moment_new,
        dense_second_new,
        expert_grad[None],
        expert_new[None],
        expert_moment_new[None],
        expert_second_new[None],
        gains_grad,
        gains_new,
        gains_moment_new,
        gains_second_new,
        router_grad,
        router_new,
        router_moment_new,
        router_second_new,
    )


def solution(mesh):
    rows_spec = P("shard", "ctx", None)
    dense_spec = P(("ctx", "shard"), None, None)
    expert_spec = P("shard", "ctx", None, None)
    in_specs = (
        (rows_spec, rows_spec, P(), P(), dense_spec, expert_spec, rows_spec, P(), P(), P())
        + (dense_spec,) * 4
        + (expert_spec,) * 4
        + (P(),) * 4
    )
    out_specs = (rows_spec,) * 2 + (dense_spec,) * 4 + (expert_spec,) * 4 + (P(),) * 8
    return jax.shard_map(shards, mesh=mesh, in_specs=in_specs, out_specs=out_specs, check_vma=False)
```

```python
import functools

import jax
import jax.numpy as jnp
from jax import lax
from jax.experimental import pallas as pl
from jax.experimental.pallas import tpu as pltpu
from jax.sharding import PartitionSpec as P

HEADS = 24
KVH = 8
HD = 64
FF = 1024
BR = 192
BC = 256
LANES = 128
UPPER = 128

norm_eps = 1e-06
beta_one = 0.9
beta_two = 0.95
rate = 0.01
gain_rate = 0.5
adam_eps = 1e-08
masked_score = -1e30
low_type = jnp.bfloat16
MIB = 1 << 20
VMEM_LIMIT = 60 * MIB

NN = (((1,), (0,)), ((), ()))
NT = (((1,), (1,)), ((), ()))
TN = (((0,), (0,)), ((), ()))

in_vmem = pl.BlockSpec(memory_space=pltpu.VMEM)
in_smem = pl.BlockSpec(memory_space=pltpu.SMEM)
in_any = pl.BlockSpec(memory_space=pl.ANY)


def dot(left_side, right_side, dims=NN):
    return lax.dot_general(left_side, right_side, dims, preferred_element_type=jnp.float32)


def call(kernel, out_shapes, in_specs, out_specs, scratch, flops, moved):
    return pl.pallas_call(
        kernel,
        out_shape=out_shapes,
        in_specs=in_specs,
        out_specs=out_specs,
        scratch_shapes=scratch,
        compiler_params=pltpu.CompilerParams(vmem_limit_bytes=VMEM_LIMIT),
        cost_estimate=pl.CostEstimate(flops=flops, bytes_accessed=moved, transcendentals=0),
    )


def shaped(dims, kind):
    return jax.ShapeDtypeStruct(dims, kind)


def inverse_order(slot_order):
    count = slot_order.shape[0]
    numbers = jnp.arange(count, dtype=jnp.int32)
    return jnp.sum(
        jnp.where(slot_order[None, :] == numbers[:, None], numbers[None, :], 0), axis=1
    ).astype(jnp.int32)


def wait_bytes(landed, semaphore):
    pltpu.make_async_copy(landed, landed, semaphore).wait()


def unit_rows(rows, gain):
    inverse = lax.rsqrt(jnp.mean(rows * rows, axis=-1, keepdims=True) + norm_eps)
    return rows * inverse * gain, inverse


def unit_back(rows, gain, inverse, gradient):
    unit = rows * inverse
    scaled = gradient * gain
    inner = jnp.mean(scaled * unit, axis=-1, keepdims=True)
    return inverse * (scaled - unit * inner), jnp.sum(gradient * unit, axis=0, keepdims=True)


def lane_ids(dims):
    return lax.broadcasted_iota(jnp.int32, dims, len(dims) - 1)


def half_turn(tile):
    return pltpu.roll(tile, HD, 1)


def stack_heads(ref, pair, scale=None):
    base = pair * (3 * LANES)
    tiles = [
        ref[:, pl.ds(pl.multiple_of(base + LANES * t, LANES), LANES)].astype(jnp.float32)
        for t in range(3)
    ]
    if scale is not None:
        tiles = [t * scale for t in tiles]
    lower = lane_ids(tiles[0].shape) < HD
    first = [tiles[0], half_turn(tiles[0]), tiles[1]]
    second = [tiles[1], half_turn(tiles[2]), tiles[2]]
    return (
        jnp.concatenate([jnp.where(lower, t, 0.0) for t in first], axis=0),
        jnp.concatenate([jnp.where(lower, 0.0, t) for t in second], axis=0),
    )


def unstack_heads(ref, pair, first, second):
    rows = first.shape[0] // 3
    base = pair * (3 * LANES)
    lower = lane_ids((rows, LANES)) < HD
    tiles = (
        jnp.where(lower, first[:rows], half_turn(first[rows : 2 * rows])),
        jnp.where(lower, first[2 * rows :], second[:rows]),
        jnp.where(lower, half_turn(second[rows : 2 * rows]), second[2 * rows :]),
    )
    for t in range(3):
        ref[:, pl.ds(pl.multiple_of(base + LANES * t, LANES), LANES)] = tiles[t].astype(ref.dtype)


def project_kernel(
    pieces, chips, members, slots, all_groups, micros, order_ref, me_ref, *refs
):
    x_refs = refs[:micros]
    gain_ref = refs[micros]
    piece_refs = refs[micros + 1 : micros + 1 + len(pieces)]
    refs = refs[micros + 1 + len(pieces) :]
    h_ref = refs[0]
    kv_ref, win_ref, wout_ref, held, held_out, sems, out_sems = refs[1:]
    groups = held.shape[1] // BC
    kv_groups = kv_ref.shape[-1] // BC
    rows = x_refs[0].shape[0]
    ctx, shard = me_ref[0], me_ref[1]
    chip, core = lax.div(ctx, 2), lax.rem(ctx, 2)

    for ref, (other_core, offset, first, cut) in zip(piece_refs, pieces):

        @pl.loop(0, ref.shape[0])
        def _(i):
            source = lax.rem(chip - (first + lax.div(i, slots)) + chips, chips) * 2
            source = source + jnp.bitwise_xor(core, other_core)
            source = source * members + jnp.bitwise_xor(shard, offset)
            number = order_ref[source * slots + lax.rem(i, slots)]
            a, b = lax.div(number, all_groups), lax.rem(number, all_groups)
            down = pl.ds(pl.multiple_of(a * BR + cut, 32), ref.shape[1])

            @pl.when(b < groups)
            def _():
                across = pl.ds(pl.multiple_of(b * BC, BC), BC)
                pltpu.make_async_copy(ref.at[i], held.at[down, across], sems.at[b]).start()

            @pl.when(b >= groups)
            def _():
                across = pl.ds(pl.multiple_of((b - groups) * BC, BC), BC)
                pltpu.make_async_copy(ref.at[i], held_out.at[down, across], sems.at[groups]).start()

    for m in range(micros):
        h_ref[m * rows : (m + 1) * rows, :] = unit_rows(x_refs[m][...], gain_ref[0:1])[0].astype(
            low_type
        )
    q_groups = groups - kv_groups

    @pl.loop(0, groups)
    def _(b):
        across = pl.ds(pl.multiple_of(b * BC, BC), BC)
        wait_bytes(held.at[:, across], sems.at[b])

    wait_bytes(held_out, sems.at[groups])
    copies = [
        pltpu.make_async_copy(held, win_ref, out_sems.at[0]),
        pltpu.make_async_copy(held_out, wout_ref, out_sems.at[1]),
    ]
    for copy in copies:
        copy.start()

    @pl.loop(0, kv_groups)
    def _(b):
        across = pl.ds(pl.multiple_of((q_groups + b) * BC, BC), BC)
        made = dot(h_ref[...], held[:, across]).astype(low_type)
        kv_ref[:, pl.ds(pl.multiple_of(b * BC, BC), BC)] = made

    for copy in copies:
        copy.wait()


def project(pieces, arrays, chips, members, slots, order, me, xs, gains):
    micros = len(xs)
    rows, width = xs[0].shape
    in_width = (HEADS + 2 * KVH) * HD
    out_width = HEADS * HD
    kv_width = 2 * KVH * HD
    return call(
        functools.partial(
            project_kernel, pieces, chips, members, slots, (in_width + out_width) // BC, micros
        ),
        tuple(
            [shaped((micros * rows, width), low_type)]
            + [shaped((micros * rows, kv_width), low_type)]
            + [shaped((width, in_width), low_type), shaped((width, out_width), low_type)]
        ),
        [in_smem, in_smem] + [in_vmem] * (micros + 1) + [in_any] * len(arrays),
        (in_vmem, in_vmem, in_any, in_any),
        [
            pltpu.VMEM((width, in_width), low_type),
            pltpu.VMEM((width, out_width), low_type),
            pltpu.SemaphoreType.DMA((in_width // BC + 1,)),
            pltpu.SemaphoreType.DMA((2,)),
        ],
        2 * micros * rows * width * kv_width,
        4 * width * (in_width + out_width),
    )(order, me, *xs, gains, *arrays)


def query_kernel(h_ref, w_ref, *refs):
    q_refs = refs[:-2]
    held, sems = refs[-2:]
    groups = held.shape[1] // BC
    rows = q_refs[0].shape[0]

    def copy(b):
        across = pl.ds(pl.multiple_of(b * BC, BC), BC)
        return pltpu.make_async_copy(w_ref.at[:, across], held.at[:, across], sems.at[b])

    @pl.loop(0, groups)
    def _(b):
        copy(b).start()

    @pl.loop(0, groups)
    def _(b):
        copy(b).wait()
        across = pl.ds(pl.multiple_of(b * BC, BC), BC)
        made = dot(h_ref[...], held[:, across]).astype(low_type)
        for m, ref in enumerate(q_refs):
            ref[:, across] = made[m * rows : (m + 1) * rows]


def make_queries(h, w, micros):
    total, width = h.shape
    q_width = HEADS * HD
    return call(
        query_kernel,
        tuple([shaped((total // micros, q_width), low_type)] * micros),
        [in_vmem, in_any],
        tuple([in_vmem] * micros),
        [pltpu.VMEM((width, q_width), low_type), pltpu.SemaphoreType.DMA((q_width // BC,))],
        2 * total * width * q_width,
        2 * width * q_width,
    )(h, w)


def load_keys(kv_ref, micro, rows, held, sem):
    count = held.shape[0] // rows
    span = kv_ref.shape[0] // count

    @pl.loop(0, count)
    def _(i):
        pltpu.make_async_copy(
            kv_ref.at[pl.ds(pl.multiple_of(i * span + micro * rows, 16), rows)],
            held.at[pl.ds(pl.multiple_of(i * rows, 16), rows)],
            sem,
        ).start()


def attend_kernel(
    micro, q_ref, rpos_ref, kpos_ref, x_ref, gain_ref, w_ref, all_ref,
    ob_ref, log_ref, x2_ref, h2_ref, bias, kv_ref, held, sems,
):
    rows = q_ref.shape[0]
    load_keys(all_ref, micro, rows, kv_ref, sems.at[0])
    pltpu.make_async_copy(w_ref, held, sems.at[1]).start()
    bias[...] = jnp.where(kpos_ref[...] <= rpos_ref[...], 0.0, masked_score)
    log_ref[...] = jnp.zeros_like(log_ref)
    length = kv_ref.shape[0]
    wait_bytes(kv_ref, sems.at[0])

    @pl.loop(0, KVH // 2)
    def _(pair):
        lane = pl.multiple_of(pair * LANES, LANES)
        keys = kv_ref[:, pl.ds(lane, LANES)]
        values = kv_ref[:, pl.ds(pl.multiple_of(lane + KVH * HD, LANES), LANES)]
        stacked = stack_heads(q_ref, pair, HD**-0.5)
        mixed = []
        for part in range(2):
            scores = dot(stacked[part].astype(low_type), keys, NT)
            scores = (scores.reshape(3, rows, length) + bias[...][None]).reshape(3 * rows, length)
            largest = jnp.max(scores, axis=-1, keepdims=True)
            raised = jnp.exp(scores - largest)
            summed = jnp.sum(raised, axis=-1, keepdims=True)
            mixed.append(dot(raised.astype(low_type), values) / summed)
            log_ref[...] = jnp.where(
                lane_ids(log_ref.shape) == 2 * pair + part, largest + jnp.log(summed), log_ref[...]
            )
        unstack_heads(ob_ref, pair, mixed[0], mixed[1])

    wait_bytes(held, sems.at[1])
    for n in range(held.shape[0] // BC):
        cut = slice(n * BC, (n + 1) * BC)
        x2_ref[:, cut] = x_ref[:, cut] + dot(ob_ref[...], held[cut, :], NT)
    h2_ref[...] = unit_rows(x2_ref[...], gain_ref[1:2])[0].astype(low_type)


def attend(micro, q, kv, rows_pos, key_pos, x, gains, w):
    rows, width = q.shape
    length = key_pos.shape[1]
    model = x.shape[1]
    return call(
        functools.partial(attend_kernel, micro),
        (
            shaped((rows, width), low_type),
            shaped((3 * rows, LANES), jnp.float32),
            shaped((rows, model), jnp.float32),
            shaped((rows, model), low_type),
        ),
        [in_vmem] * 5 + [in_any] * 2,
        (in_vmem,) * 4,
        [
            pltpu.VMEM((rows, length), jnp.float32),
            pltpu.VMEM((length, kv.shape[1]), low_type),
            pltpu.VMEM((model, width), low_type),
            pltpu.SemaphoreType.DMA((2,)),
        ],
        16 * rows * length * width,
        8 * MIB,
    )(q, rows_pos, key_pos, x, gains, w, kv)


def router_parts(h2, router, experts):
    logits = dot(h2, router)
    logits = jnp.where(lane_ids(logits.shape) < experts, logits, masked_score)
    raised = jnp.exp(logits - jnp.max(logits, axis=-1, keepdims=True))
    return raised / jnp.sum(raised, axis=-1, keepdims=True)


def expert_kernel(sources, micro, order_ref, me_ref, router_ref, *refs):
    h_parts = refs[:sources]
    c_parts = refs[sources : 2 * sources]
    w_refs = refs[2 * sources : 2 * sources + 2]
    outs = refs[2 * sources + 2 :]
    back_refs = outs[:sources]
    z_ref, dg_ref, du_ref, cs, xs_ref = outs[sources : sources + 5]
    held, chance, load_sem, w_sems = outs[sources + 5 :]
    rows, width = h_parts[0].shape
    row_groups = width // BR
    col_groups = FF // BC
    for j in range(sources):
        pltpu.make_async_copy(h_parts[j], xs_ref.at[pl.ds(j * rows, rows)], load_sem.at[0]).start()
        pltpu.make_async_copy(
            c_parts[j].at[pl.ds(micro * rows, rows)], cs.at[pl.ds(j * rows, rows)], load_sem.at[1]
        ).start()
    for b in range(col_groups):

        @pl.loop(0, row_groups)
        def _(a):
            for k in range(3):
                slot = order_ref[(k * row_groups + a) * col_groups + b]
                for start, ref in zip((0, UPPER), w_refs):
                    down = pl.ds(pl.multiple_of(a * BR + start, 64), ref.shape[1])
                    pltpu.make_async_copy(
                        ref.at[slot], held.at[k, down, pl.ds(b * BC, BC)], w_sems.at[b]
                    ).start()

    wait_bytes(xs_ref, load_sem.at[0])
    wait_bytes(cs, load_sem.at[1])
    me = me_ref[1]
    probs = router_parts(xs_ref[...], router_ref[...], sources)
    hits = cs[:, width:].astype(jnp.float32)
    mine = lane_ids(hits.shape) == me
    hit = jnp.sum(jnp.where(mine, hits, 0.0), axis=-1, keepdims=True)
    weight = jnp.sum(jnp.where(mine, probs, 0.0), axis=-1, keepdims=True) * hit
    chance[...] = jnp.zeros_like(chance)

    @pl.loop(0, col_groups)
    def _(b):
        cut = pl.ds(pl.multiple_of(b * BC, BC), BC)
        wait_bytes(held.at[:, :, cut], w_sems.at[b])
        gate = dot(xs_ref[...], held[0, :, cut])
        up = dot(xs_ref[...], held[1, :, cut])
        down = dot(cs[:, :width], held[2, :, cut])
        sig = jax.nn.sigmoid(gate)
        act = gate * sig
        hidden = act * up
        chance[...] += jnp.sum(down * hidden, axis=-1, keepdims=True)
        z_ref[:, cut] = (hidden * weight).astype(low_type)
        down = down * weight
        dg_ref[:, cut] = (down * up * (sig + act * (1.0 - sig))).astype(low_type)
        du_ref[:, cut] = (down * act).astype(low_type)

    for n in range(width // BC):
        cut = slice(n * BC, (n + 1) * BC)
        back = dot(dg_ref[...], held[0, cut, :], NT) + dot(du_ref[...], held[1, cut, :], NT)
        for j in range(sources):
            back_refs[j][:, cut] = back[j * rows : (j + 1) * rows].astype(low_type)
    told = chance[...] * hit
    high_part = told.astype(low_type)
    low_part = (told - high_part.astype(jnp.float32)).astype(low_type)
    lanes = lane_ids((sources * rows, LANES))
    tail = jnp.where(lanes == 0, high_part, jnp.where(lanes == 1, low_part, jnp.zeros_like(low_part)))
    for j in range(sources):
        back_refs[j][:, width:] = tail[j * rows : (j + 1) * rows]


def run_expert(micro, order, me, router, h_parts, c_parts, ws):
    sources = len(h_parts)
    rows, width = h_parts[0].shape
    total = sources * rows
    return call(
        functools.partial(expert_kernel, sources, micro),
        tuple(
            [shaped((rows, width + LANES), low_type)] * sources
            + [shaped((total, FF), low_type)] * 3
            + [shaped((total, width + LANES), low_type), shaped((total, width), low_type)]
        ),
        [in_smem, in_smem, in_vmem] + [in_any] * (2 * sources + 2),
        tuple([in_vmem] * (sources + 5)),
        [
            pltpu.VMEM((3, width, FF), low_type),
            pltpu.VMEM((total, 1), jnp.float32),
            pltpu.SemaphoreType.DMA((2,)),
            pltpu.SemaphoreType.DMA((FF // BC,)),
        ],
        10 * total * width * FF,
        20 * MIB,
    )(order, me, router, *h_parts, *c_parts, *ws)


def produce_kernel(sources, order_ref, upper_ref, lower_ref, *refs):
    out_refs = refs[-3 - sources : -3]
    z_refs = refs[: -3 - sources]
    zs, held, sem = refs[-3:]
    width = held.shape[0]
    total = z_refs[0].shape[0]
    rows = total // sources
    row_groups, col_groups = width // BR, FF // BC

    @pl.loop(0, row_groups)
    def _(a):
        for b in range(col_groups):
            slot = order_ref[(2 * row_groups + a) * col_groups + b]
            for start, ref in zip((0, UPPER), (upper_ref, lower_ref)):
                down = pl.ds(pl.multiple_of(a * BR + start, 64), ref.shape[1])
                pltpu.make_async_copy(
                    ref.at[slot], held.at[down, pl.ds(b * BC, BC)], sem
                ).start()

    for m, z_ref in enumerate(z_refs):
        zs[m * total : (m + 1) * total] = z_ref[...]
    wait_bytes(held, sem)
    for n in range(width // BC):
        cut = slice(n * BC, (n + 1) * BC)
        made = dot(zs[...], held[cut, :], NT).astype(low_type)
        for m in range(len(z_refs)):
            for j in range(sources):
                start = m * total + j * rows
                out_refs[j][m * rows : (m + 1) * rows, cut] = made[start : start + rows]


def produce(order, ws, zs, sources, width):
    micros = len(zs)
    total = zs[0].shape[0]
    return call(
        functools.partial(produce_kernel, sources),
        tuple([shaped((micros * total // sources, width), low_type)] * sources),
        [in_smem, in_any, in_any] + [in_vmem] * micros,
        tuple([in_vmem] * sources),
        [
            pltpu.VMEM((micros * total, FF), low_type),
            pltpu.VMEM((width, FF), low_type),
            pltpu.SemaphoreType.DMA,
        ],
        2 * micros * total * width * FF,
        8 * MIB,
    )(order, *ws, *zs)


def outer_kernel(groups, col_groups, order_ref, *refs):
    micros = len(refs[:-5]) // (len(groups) + 2)
    lefts = [refs[i * micros : (i + 1) * micros] for i in range(2)]
    rights = [refs[(2 + i) * micros : (3 + i) * micros] for i in range(len(groups))]
    out_refs, (turned, stage, sems) = refs[-5:-3], refs[-3:]
    rows = rights[0][0].shape[0]
    width = turned.shape[1]
    span = 2 * BR
    for side in range(2):
        for m in range(micros):
            for r in range(0, rows, LANES):
                part = lefts[side][m][r : r + LANES, :width]
                turned[side, :, m * rows + r : m * rows + r + LANES] = part.T
    row_groups = width // BR
    steps = [(k, p) for k in range(len(groups)) for p in range(width // span)]
    for n, (k, p) in enumerate(steps):
        slot = n % 2
        if n >= 2:
            wait_bytes(stage.at[slot], sems.at[slot])
        cut = slice(p * span, (p + 1) * span)
        made = 0.0
        for m in range(micros):
            left = turned[groups[k], cut, m * rows : (m + 1) * rows]
            made = made + dot(left, rights[k][m][...])
        stage[slot] = made.astype(low_type)
        for half in range(2):
            for b in range(col_groups):
                number = (k * row_groups + 2 * p + half) * col_groups + b
                place = order_ref[number]
                for side in range(2):
                    pltpu.make_async_copy(
                        stage.at[
                            slot, pl.ds(half * BR, BR), pl.ds(b * BC + side * LANES, LANES)
                        ],
                        out_refs[side].at[place],
                        sems.at[slot],
                    ).start()
    for slot in range(2):
        wait_bytes(stage.at[slot], sems.at[slot])


def outer_blocks(order, width, groups, lefts, rights):
    flat = [part for group in lefts + rights for part in group]
    rows = sum(part.shape[0] for part in rights[0])
    cols = rights[0][0].shape[1]
    blocks = len(groups) * width * cols // (BR * BC)
    return call(
        functools.partial(outer_kernel, groups, cols // BC),
        (shaped((blocks, BR, LANES), low_type),) * 2,
        [in_smem] + [in_vmem] * len(flat),
        (in_any,) * 2,
        [
            pltpu.VMEM((2, width, rows), low_type),
            pltpu.VMEM((2, 2 * BR, cols), low_type),
            pltpu.SemaphoreType.DMA((2,)),
        ],
        2 * rows * blocks * BR * BC,
        blocks * BR * BC * 2 + sum(f.size * 2 for f in flat),
    )(order, *flat)


def xor_plan(members, offset):
    if members != 4:
        return list(range(1, members)), [0]
    first = 1 if offset % 2 else 2
    return [first, 3], [0, 3 - first]


def pieces_kernel(members, counts, cols, turned_first, me_ref, *refs):
    row_groups = 8
    lists = []
    for left_count, right_count in counts:
        lists.append((refs[:left_count], refs[left_count : left_count + right_count]))
        refs = refs[left_count + right_count :]
    outs, refs = refs[:4], refs[4:]
    extra = refs[0] if not turned_first else None
    turned, rights, stage, sems = refs[0 if turned_first else 1 :]
    ctx, shard = me_ref[0], me_ref[1]
    core = lax.rem(ctx, 2)
    total = turned.shape[2]
    row_groups = turned.shape[1] // BR
    base = 0
    for g, (_, parts) in enumerate(lists):
        start = 0
        for part in parts:
            count = part.shape[0]
            for b in range(cols[g]):
                lane = pl.multiple_of(b * BC + core * LANES, LANES)
                pltpu.make_async_copy(
                    part.at[:, pl.ds(lane, LANES)],
                    rights.at[pl.ds(start, count), pl.ds((base + b) * LANES, LANES)],
                    sems.at[g],
                ).start()
            start += count
        base += cols[g]
    for g, (parts, _) in enumerate(lists):
        if g == 0 and turned_first:
            turned[0] = parts[0][...]
            continue
        start = 0
        for part in parts:
            for r in range(0, part.shape[0], LANES):
                turned[g, :, start : start + LANES] = part[r : r + LANES, :].T
                start += LANES
    if extra is not None:
        extra[...] = turned[0]
    all_cols = sum(cols)
    half_blocks = row_groups // 2 * all_cols
    span = BR // members
    base = 0
    for g in range(len(lists)):
        wide_cols = cols[g] * LANES
        wait_bytes(rights.at[:, pl.ds(base * LANES, wide_cols)], sems.at[g])
        for a in range(row_groups):
            made = dot(
                turned[g, a * BR : (a + 1) * BR, :],
                rights[:, base * LANES : base * LANES + wide_cols],
            )
            stage[a % 2, :, :wide_cols] = made.astype(stage.dtype)
            half = a // (row_groups // 2)
            first = (a % (row_groups // 2)) * all_cols + base
            for out, hops in zip(outs[2 * half : 2 * half + 2], xor_plan(members, 1 - half)):
                for place, hop in enumerate(hops):
                    down = pl.multiple_of(jnp.bitwise_xor(shard, hop) * span, 16 if span % 16 == 0 else 8)
                    for b in range(cols[g]):
                        out[place * half_blocks + first + b] = stage[
                            a % 2, pl.ds(down, span), b * LANES : (b + 1) * LANES
                        ].astype(low_type)
        base += cols[g]


def gradient_pieces(members, me, groups, cols, turned_first):
    counts = tuple((len(left), len(right)) for left, right in groups)
    flat = [part for left, right in groups for part in left + right]
    total = sum(part.shape[0] for part in groups[0][1])
    width = groups[0][0][0].shape[0 if turned_first else 1]
    row_groups = width // BR
    half_blocks = row_groups // 2 * sum(cols)
    span = BR // members
    stage_type = jnp.float32 if span % 16 else low_type
    outs = []
    for half in range(2):
        for hops in xor_plan(members, 1 - half):
            outs.append(shaped((len(hops) * half_blocks, span, LANES), low_type))
    out_specs = [in_vmem] * 4
    if not turned_first:
        outs.append(shaped((width, total), low_type))
        out_specs.append(in_vmem)
    in_specs = [in_smem]
    for left, right in groups:
        in_specs += [in_vmem] * len(left) + [in_any] * len(right)
    return call(
        functools.partial(pieces_kernel, members, counts, tuple(cols), turned_first),
        tuple(outs),
        in_specs,
        tuple(out_specs),
        [
            pltpu.VMEM((len(groups), width, total), low_type),
            pltpu.VMEM((total, sum(cols) * LANES), low_type),
            pltpu.VMEM((2, BR, max(cols) * LANES), stage_type),
            pltpu.SemaphoreType.DMA((len(groups),)),
        ],
        2 * total * width * sum(cols) * LANES,
        16 * MIB,
    )(me, *flat)


def merge_kernel(
    sources, me_ref, x2_ref, cot_ref, h2_ref, gain_ref, router_ref, w_ref, *refs
):
    back_refs = refs[:sources]
    dx_ref, da_ref, do_ref, stat_ref, held, sem = refs[sources:]
    rows, width = x2_ref.shape
    pltpu.make_async_copy(w_ref, held, sem).start()
    lanes = lane_ids((rows, LANES))
    prob_grad = jnp.zeros((rows, LANES), jnp.float32)
    gathered = jnp.zeros((rows, width), jnp.float32)
    for j in range(sources):
        tail = back_refs[j][:, width:].astype(jnp.float32)
        told = jnp.sum(tail, axis=-1, keepdims=True)
        expert = jnp.bitwise_xor(me_ref[1], j)
        prob_grad = prob_grad + jnp.where(lanes == expert, told, 0.0)
        gathered = gathered + back_refs[j][:, :width].astype(jnp.float32)
    h2 = h2_ref[...]
    probs = router_parts(h2, router_ref[...], sources)
    logit_grad = probs * (prob_grad - jnp.sum(probs * prob_grad, axis=-1, keepdims=True))
    high_part = logit_grad.astype(low_type)
    low_part = (logit_grad - high_part.astype(jnp.float32)).astype(low_type)
    router_grad = dot(high_part, h2, TN) + dot(low_part, h2, TN)
    gathered = gathered + dot(high_part, router_ref[...], NT) + dot(low_part, router_ref[...], NT)
    x2 = x2_ref[...]
    inverse = lax.rsqrt(jnp.mean(x2 * x2, axis=-1, keepdims=True) + norm_eps)
    moe_grad, gain_grad = unit_back(x2, gain_ref[1:2], inverse, gathered)
    after = cot_ref[...] + moe_grad
    dx_ref[...] = after
    da_ref[...] = after.astype(low_type)
    experts_up = stat_ref.shape[0] - 8
    stat_ref[:experts_up] = router_grad[:experts_up]
    stat_ref[experts_up:] = jnp.broadcast_to(gain_grad, (8, width))
    wait_bytes(held, sem)
    for n in range(held.shape[1] // BC):
        cut = slice(n * BC, (n + 1) * BC)
        do_ref[:, cut] = dot(da_ref[...], held[:, cut]).astype(low_type)


def merge(me, x2, cot, h2, gains, router, w, backs):
    rows, width = x2.shape
    sources = len(backs)
    experts_up = -(-sources // 8) * 8
    return call(
        functools.partial(merge_kernel, sources),
        (
            shaped((rows, width), jnp.float32),
            shaped((rows, width), low_type),
            shaped((rows, HEADS * HD), low_type),
            shaped((experts_up + 8, width), jnp.float32),
        ),
        [in_smem] + [in_vmem] * 5 + [in_any] + [in_vmem] * sources,
        (in_vmem,) * 4,
        [pltpu.VMEM((width, HEADS * HD), low_type), pltpu.SemaphoreType.DMA],
        2 * rows * width * HEADS * HD,
        10 * MIB,
    )(me, x2, cot, h2, gains, router, w, *backs)


def attend_back_kernel(
    micro, q_ref, rpos_ref, kpos_ref, ob_ref, log_ref, do_ref, all_ref, *refs
):
    dq_ref, out_ref, bias, kv_ref, grad_ref, sems = refs[-6:]
    rows = q_ref.shape[0]
    load_keys(all_ref, micro, rows, kv_ref, sems.at[0])
    length = kv_ref.shape[0]
    bias[...] = jnp.where(kpos_ref[...] <= rpos_ref[...], 0.0, masked_score)
    wait_bytes(kv_ref, sems.at[0])

    @pl.loop(0, KVH // 2)
    def _(pair):
        lane = pl.multiple_of(pair * LANES, LANES)
        value_lane = pl.multiple_of(lane + KVH * HD, LANES)
        keys = kv_ref[:, pl.ds(lane, LANES)]
        values = kv_ref[:, pl.ds(value_lane, LANES)]
        queries = stack_heads(q_ref, pair, HD**-0.5)
        grads = stack_heads(do_ref, pair)
        mixes = stack_heads(ob_ref, pair)
        query_grads = []
        key_grad = value_grad = None
        for part in range(2):
            query = queries[part].astype(low_type)
            grad = grads[part].astype(low_type)
            log_total = jnp.sum(
                jnp.where(lane_ids(log_ref.shape) == 2 * pair + part, log_ref[...], 0.0),
                axis=-1,
                keepdims=True,
            )
            delta = jnp.sum(grads[part] * mixes[part], axis=-1, keepdims=True)
            scores = dot(query, keys, NT)
            scores = (scores.reshape(3, rows, length) + bias[...][None]).reshape(3 * rows, length)
            chance = jnp.exp(scores - log_total)
            prob_grad = dot(grad, values, NT)
            score_grad = (chance * (prob_grad - delta)).astype(low_type)
            value_term = dot(chance.astype(low_type), grad, TN)
            key_term = dot(score_grad, query, TN)
            key_grad = key_term if part == 0 else key_grad + key_term
            value_grad = value_term if part == 0 else value_grad + value_term
            query_grads.append(dot(score_grad, keys) * HD**-0.5)
        unstack_heads(dq_ref, pair, query_grads[0], query_grads[1])
        grad_ref[:, pl.ds(lane, LANES)] = key_grad.astype(low_type)
        grad_ref[:, pl.ds(value_lane, LANES)] = value_grad.astype(low_type)

    count = length // rows
    span = out_ref.shape[0] // count

    @pl.loop(0, count)
    def _(i):
        pltpu.make_async_copy(
            grad_ref.at[pl.ds(pl.multiple_of(i * rows, 16), rows)],
            out_ref.at[pl.ds(pl.multiple_of(i * span + micro * rows, 16), rows)],
            sems.at[1],
        ).start()

    wait_bytes(grad_ref, sems.at[1])


def attend_back(micro, q, kv, rows_pos, key_pos, ob, log_total, do, shared):
    rows, width = q.shape
    length = key_pos.shape[1]
    operands = [q, rows_pos, key_pos, ob, log_total, do, kv]
    in_specs = [in_vmem] * 6 + [in_any]
    aliases = {}
    if shared is not None:
        aliases = {len(operands): 1}
        operands.append(shared)
        in_specs.append(in_any)
    return pl.pallas_call(
        functools.partial(attend_back_kernel, micro),
        out_shape=(shaped((rows, width), low_type), shaped(kv.shape, low_type)),
        in_specs=in_specs,
        out_specs=(in_vmem, in_any),
        scratch_shapes=[
            pltpu.VMEM((rows, length), jnp.float32),
            pltpu.VMEM((length, kv.shape[1]), low_type),
            pltpu.VMEM((length, kv.shape[1]), low_type),
            pltpu.SemaphoreType.DMA((2,)),
        ],
        input_output_aliases=aliases,
        compiler_params=pltpu.CompilerParams(vmem_limit_bytes=VMEM_LIMIT),
        cost_estimate=pl.CostEstimate(
            flops=40 * rows * length * width, bytes_accessed=8 * MIB, transcendentals=0
        ),
    )(*operands)


def query_back_kernel(w_ref, *refs):
    micros = (len(refs) - 3) // 2
    dq_refs, out_refs = refs[:micros], refs[micros : 2 * micros]
    rows_ref, held, sem = refs[2 * micros :]
    rows = dq_refs[0].shape[0]
    copy = pltpu.make_async_copy(w_ref.at[:, pl.ds(0, held.shape[1])], held, sem)
    copy.start()
    for m in range(micros):
        rows_ref[m * rows : (m + 1) * rows] = dq_refs[m][...]
    copy.wait()
    for n in range(held.shape[0] // BC):
        cut = slice(n * BC, (n + 1) * BC)
        made = dot(rows_ref[...], held[cut, :], NT)
        for m in range(micros):
            out_refs[m][:, cut] = made[m * rows : (m + 1) * rows]


def query_back(w, dqs):
    micros = len(dqs)
    rows, q_width = dqs[0].shape
    width = w.shape[0]
    return call(
        query_back_kernel,
        tuple([shaped((rows, width), jnp.float32)] * micros),
        [in_any] + [in_vmem] * micros,
        tuple([in_vmem] * micros),
        [
            pltpu.VMEM((micros * rows, q_width), low_type),
            pltpu.VMEM((width, q_width), low_type),
            pltpu.SemaphoreType.DMA,
        ],
        2 * micros * rows * width * q_width,
        7 * MIB,
    )(w, *dqs)


def input_kernel(x_ref, gain_ref, w_ref, *refs):
    micros, rows = x_ref.shape[:2]
    dx_refs = refs[:micros]
    part_refs = refs[micros : 2 * micros]
    dkv_ref, out_ref, stat_ref, grad, held, sem = refs[2 * micros :]
    kv_width = held.shape[1]
    copy = pltpu.make_async_copy(
        w_ref.at[:, pl.ds(w_ref.shape[1] - kv_width, kv_width)], held, sem
    )
    copy.start()
    copy.wait()
    for n in range(held.shape[0] // BC):
        cut = slice(n * BC, (n + 1) * BC)
        made = dot(dkv_ref[...], held[cut, :], NT)
        for m in range(micros):
            grad[m, :, cut] = part_refs[m][:, cut] + made[m * rows : (m + 1) * rows]
    total = jnp.zeros((1, x_ref.shape[-1]), jnp.float32)
    for m in range(micros):
        x = x_ref[m]
        inverse = lax.rsqrt(jnp.mean(x * x, axis=-1, keepdims=True) + norm_eps)
        term, gain_grad = unit_back(x, gain_ref[0:1], inverse, grad[m])
        out_ref[m] = dx_refs[m][...] + term
        total = total + gain_grad
    stat_ref[...] = jnp.broadcast_to(total, stat_ref.shape)


def input_back(x, gains, w, dxs, parts, dkv):
    micros, rows, width = x.shape
    kv_width = dkv.shape[1]
    return call(
        input_kernel,
        (shaped(x.shape, jnp.float32), shaped((8, width), jnp.float32)),
        [in_vmem, in_vmem, in_any] + [in_vmem] * (2 * micros + 1),
        (in_vmem,) * 2,
        [
            pltpu.VMEM(x.shape, jnp.float32),
            pltpu.VMEM((width, kv_width), low_type),
            pltpu.SemaphoreType.DMA,
        ],
        2 * micros * rows * width * kv_width,
        14 * MIB,
    )(x, gains, w, *dxs, *parts, dkv)


def rotate_kernel(b_ref, m_ref, s_ref, l_ref, r_ref, *refs):
    grad_ref, new_ref, moment_ref, second_ref = refs[-4:]
    parts = [ref[0].astype(jnp.float32) for ref in refs[:-4]]
    gradient = parts[0] if len(parts) == 1 else jnp.concatenate(parts, axis=1)
    grad_ref[0] = gradient
    left = l_ref[0].astype(low_type)
    right = r_ref[0].astype(low_type)
    rotated = dot(dot(left, gradient.astype(low_type), TN).astype(low_type), right)
    moment = beta_one * m_ref[0] + (1.0 - beta_one) * rotated
    second = beta_two * s_ref[0] + (1.0 - beta_two) * rotated * rotated
    moment_ref[0] = moment
    second_ref[0] = second
    direction = (moment / (jnp.sqrt(second) + adam_eps)).astype(low_type)
    turned = dot(dot(left, direction).astype(low_type), right, NT)
    new_ref[0] = b_ref[0] - rate * turned


def rotate(weight, gradients, moment, second, left, right):
    count = weight.shape[0]

    def spec(rows, cols):
        return pl.BlockSpec((1, rows, cols), lambda i: (i, 0, 0))

    block = spec(BR, BC)
    return pl.pallas_call(
        rotate_kernel,
        grid=(count,),
        out_shape=(shaped(weight.shape, jnp.float32),) * 4,
        in_specs=[block] * 3
        + [spec(BR, BR), spec(BC, BC)]
        + [spec(BR, part.shape[2]) for part in gradients],
        out_specs=(block,) * 4,
        compiler_params=pltpu.CompilerParams(vmem_limit_bytes=VMEM_LIMIT),
        cost_estimate=pl.CostEstimate(
            flops=4 * count * BR * BC * (BR + BC),
            bytes_accessed=count * 2 * MIB,
            transcendentals=0,
        ),
    )(weight, moment, second, left, right, *gradients)


def adam(weight, gradient, moment, second, step_rate):
    moment_new = beta_one * moment + (1.0 - beta_one) * gradient
    second_new = beta_two * second + (1.0 - beta_two) * gradient * gradient
    return (
        weight - step_rate * moment_new / (jnp.sqrt(second_new) + adam_eps),
        moment_new,
        second_new,
    )


def piece_places(row_groups, q_groups, kv_groups):
    all_groups = 2 * q_groups + kv_groups
    out_groups = list(range(q_groups)) + list(range(q_groups + kv_groups, all_groups))
    numbers = [a * all_groups + b for a in range(row_groups) for b in out_groups]
    numbers += [a * all_groups + q_groups + b for a in range(row_groups) for b in range(kv_groups)]
    places = [0] * len(numbers)
    for place, number in enumerate(numbers):
        places[number] = place
    return places


def to_partner(array, offset):
    if offset == 0:
        return array
    count = lax.axis_size("shard")
    return lax.ppermute(array, "shard", [(i, i ^ offset) for i in range(count)])


def to_ctx(array, offset):
    count = lax.axis_size("ctx")
    return lax.ppermute(array, "ctx", [(i, i ^ offset) for i in range(count)])


def to_chip(array, offset):
    count = lax.axis_size("ctx")
    return lax.ppermute(array, "ctx", [(i, (i + 2 * offset) % count) for i in range(count)])


def after(value, *others):
    return lax.optimization_barrier((value, others))[0]


def from_chips(array, chips):
    return [array] + [to_chip(array, offset) for offset in range(1, chips)]


def wide(array):
    return array.astype(jnp.float32)


def sum_to_chips(parts):
    total = wide(parts[0])
    for offset in range(1, len(parts)):
        total = total + wide(to_chip(parts[offset], -offset))
    return total


def gather_weights(blocks, chips, members):
    parts = [blocks]
    for _ in range(chips - 1):
        parts.append(to_chip(parts[-1], 1))
    pieces, arrays = [], []
    gate = []

    def add(array, offset, first, cut):
        pieces.append((0, offset, first, cut))
        arrays.append(array)
        pieces.append((1, offset, first, cut))
        arrays.append(to_ctx(after(array, *gate), 1))
        return array

    def spread(group, first):
        add(group, 0, first, 0)
        if members == 4 and first > 0:
            by_one, by_two = to_partner(group, 1), to_partner(group, 2)
            add(by_one, 1, first, 0)
            add(by_two, 2, first, 0)
            half = BR // 2
            add(to_partner(by_one[:, :half], 2), 3, first, 0)
            add(to_partner(by_two[:, half:], 1), 3, first, half)
            return [by_one, by_two]
        got = [to_partner(group, offset) for offset in range(1, members)]
        for offset in range(1, members):
            add(got[offset - 1], offset, first, 0)
        return got

    got = [to_partner(blocks, offset) for offset in range(1, members)]
    gate.append(got[0])
    add(blocks, 0, 0, 0)
    for offset in range(1, members):
        add(got[offset - 1], offset, 0, 0)
    last = list(got)
    if chips > 1:
        last = spread(after(parts[1], *last), 1)
        gate[:] = last
        got = last
    if chips > 2:
        group = after(jnp.concatenate(parts[2:], axis=0), *last)
        spread(group, 2)
    return got + parts[1:], pieces, arrays


def add_wide(parts):
    total = wide(parts[0])
    for part in parts[1:]:
        total = total + wide(part)
    return total


def sum_members(made, ready, members):
    sums, seen = [], []
    for half in range(2):
        sent, kept = made[2 * half : 2 * half + 2]
        hops, keeps = xor_plan(members, 1 - half)
        count = kept.shape[0] // len(keeps)
        total = wide(kept[:count])
        if members == 4:
            got = to_partner(sent, hops[0])
            got = got if ready is None else after(got, ready)
            total = total + wide(got[:count])
            relay = (wide(kept[count:]) + wide(got[count:])).astype(low_type)
            second = to_partner(relay, keeps[1])
            seen.append(second)
            total = total + wide(second)
        else:
            for place, hop in enumerate(hops):
                total = total + wide(to_partner(sent[place * count : (place + 1) * count], hop))
        sums.append(total.astype(low_type).reshape(count, -1))
    return jnp.concatenate(sums, axis=0), seen


def sum_chips(rows, chip, chips):
    count = rows.shape[1] // chips

    def piece(offset):
        start = lax.rem(chip - offset + chips, chips) * count
        return lax.dynamic_slice_in_dim(rows, start, count, axis=1)

    return [piece(0)] + [to_chip(piece(offset), -offset) for offset in range(1, chips)]


def shards(
    tokens,
    cotangent,
    norm_gains,
    router,
    dense_weight,
    expert_weight,
    routes,
    assign,
    dense_order,
    expert_order,
    dense_moment,
    dense_second,
    dense_left,
    dense_right,
    expert_moment,
    expert_second,
    expert_left,
    expert_right,
    gains_moment,
    gains_second,
    router_moment,
    router_second,
):
    ctx_count = lax.axis_size("ctx")
    shard_count = lax.axis_size("shard")
    chips = ctx_count // 2
    micros, rows, width = tokens.shape
    slots = dense_weight.shape[0]
    span = rows // 2
    row_groups = width // BR
    q_groups = HEADS * HD // BC
    kv_groups = 2 * KVH * HD // BC

    expert_inverse = inverse_order(expert_order)
    ctx = lax.axis_index("ctx").astype(jnp.int32)
    me = jnp.stack([ctx, lax.axis_index("shard").astype(jnp.int32)])
    row_ids = jnp.arange(rows, dtype=jnp.int32)
    all_pos = assign[:, row_ids // span] * span + row_ids % span
    key_pos = all_pos.reshape(1, rows * ctx_count)
    rows_pos = all_pos[ctx].reshape(rows, 1)
    router_pad = jnp.pad(router.astype(low_type), ((0, 0), (0, LANES - shard_count)))

    far, pieces, arrays = gather_weights(dense_weight.astype(low_type), chips, shard_count)
    expert_low = after(expert_weight[0].astype(low_type), *far)
    expert_all = [lax.all_gather(expert_low[:, :UPPER], "ctx", axis=0, tiled=True)]

    lanes = jnp.arange(LANES, dtype=jnp.int32)
    hits = jnp.sum((routes[..., None] == lanes).astype(low_type), axis=2)
    cot_rows = jnp.concatenate([cotangent.astype(low_type), hits], axis=2)
    cot_rows = cot_rows.reshape(micros * rows, width + LANES)
    cot_rows = after(cot_rows, *arrays[::2])
    cot_parts = [to_partner(cot_rows, j) for j in range(shard_count)]

    here, expert_inverse, router_pad, key_pos, rows_pos = lax.optimization_barrier(
        (me, expert_inverse, router_pad, key_pos, rows_pos)
    )
    h1, kv, w_in, w_out = project(
        pieces,
        arrays,
        chips,
        shard_count,
        slots,
        dense_order,
        here,
        [tokens[m] for m in range(micros)],
        norm_gains,
    )
    q = make_queries(h1, w_in, micros)
    h1_other = to_ctx(h1, 1)
    obs, logs, x2s, h2s = [], [], [], []
    kv_all = lax.all_gather(after(kv, expert_all[0]), "ctx", axis=0, tiled=True)
    lower = after(expert_low[:, UPPER:], kv_all, q, cot_parts)
    expert_all.append(lax.all_gather(lower, "ctx", axis=0, tiled=True))
    for m in range(micros):
        query = after(q[m], *(cot_parts if m == 0 else obs[m - 1 : m]))
        ob, log_total, x2, h2 = attend(
            m, query, kv_all, rows_pos, key_pos, tokens[m], norm_gains, w_out
        )
        obs.append(ob)
        logs.append(log_total)
        x2s.append(x2)
        h2s.append(h2)
    ob_others = [to_ctx(ob, 1) for ob in obs]

    h_parts = []
    for m in range(micros):
        own = h2s[m] if m == 0 else after(h2s[m], *h_parts[m - 1])
        h_parts.append([own] + [to_partner(own, j) for j in range(1, shard_count)])
    sent = []
    zs, dgs, dus, cs, xs = [], [], [], [], []
    for m in range(micros):
        here = after(me, h2s[-1], h1_other, *ob_others) if m == 0 else after(me, zs[-1])
        made = run_expert(m, expert_inverse, here, router_pad, h_parts[m], cot_parts, expert_all)
        sent.append(made[:shard_count])
        z, dg, du, c, x = made[shard_count:]
        zs.append(z)
        dgs.append(dg)
        dus.append(du)
        cs.append(c)
        xs.append(x)
    backs = [[to_partner(sent[m][j], j) for j in range(shard_count)] for m in range(micros)]

    expert_terms = outer_blocks(
        after(expert_inverse, *backs[0]), width, (0, 0, 1), [xs, cs], [dgs, dus, zs]
    )
    dxs, das, dqs, stats = [], [], [], []
    dkv_terms = None
    for m in range(micros):
        here = after(me, expert_terms, backs[-1]) if m == 0 else after(me, dqs[-1])
        dx, da, do, stat = merge(
            here, x2s[m], cotangent[m], h2s[m], norm_gains, router_pad, w_out, backs[m]
        )
        dq, dkv_terms = attend_back(
            m, q[m], kv_all, rows_pos, key_pos, obs[m], logs[m], do, dkv_terms
        )
        dxs.append(dx)
        das.append(da)
        dqs.append(dq)
        stats.append(stat)

    def other_core(parts):
        return [to_ctx(part, 1) for part in parts]

    da_others, dq_others = other_core(das), other_core(dqs)
    first_term = after(expert_terms[0], *backs[-1])
    expert_sums = [lax.psum_scatter(first_term, "ctx", scatter_dimension=0, tiled=True)]
    dkv = lax.psum_scatter(
        after(dkv_terms, expert_sums[0]), "ctx", scatter_dimension=0, tiled=True
    )
    early = gradient_pieces(
        shard_count,
        after(me, dkv_terms),
        [([h1, h1_other], dqs + dq_others), (das + da_others, obs + ob_others)],
        [q_groups, q_groups],
        False,
    )
    h1_turned = early[4]
    outs = produce(after(expert_inverse, early[0]), expert_all, zs, shard_count, width)
    parts_back = query_back(after(w_in, early[0]), dqs)
    early_rows, early_seen = sum_members(early[:4], (outs, parts_back), shard_count)
    chip = ctx // 2
    early_parts = sum_chips(early_rows, chip, chips)
    late = gradient_pieces(
        shard_count,
        after(me, *early_seen),
        [([h1_turned], [dkv, to_ctx(dkv, 1)])],
        [kv_groups],
        True,
    )
    input_grad, gain_stat = input_back(
        after(tokens, late[0]), norm_gains, w_in, dxs, parts_back, dkv
    )
    late_rows, late_seen = sum_members(late[:4], (input_grad, early_parts), shard_count)
    late_term = after(expert_terms[1], *late_seen)
    expert_sums.append(lax.psum_scatter(late_term, "ctx", scatter_dimension=0, tiled=True))
    arrived = [to_partner(part, j) for j, part in enumerate(after(list(outs), *late_seen))]
    early_sum = add_wide(early_parts).astype(low_type)
    late_sum = add_wide(sum_chips(late_rows, chip, chips)).astype(low_type)
    all_sums = jnp.concatenate([early_sum, late_sum], axis=0)
    places = jnp.asarray(piece_places(row_groups, q_groups, kv_groups), jnp.int32)[dense_order]
    chosen = (places[:, None] == jnp.arange(all_sums.shape[0])[None, :]).astype(low_type)
    ordered = jnp.dot(chosen, all_sums, preferred_element_type=jnp.float32).astype(low_type)
    devices = ctx_count * shard_count
    piece_width = ordered.shape[1]
    experts_up = stats[0].shape[0] - 8
    stat_rows = add_wide(stats)
    stat_rows = jnp.concatenate(
        [stat_rows[:shard_count], gain_stat[:1], stat_rows[experts_up : experts_up + 1]], axis=0
    )
    stat_parts = stat_rows.astype(low_type).reshape(-1, piece_width)
    extra = stat_parts.shape[0]
    ordered = jnp.concatenate(
        [
            ordered.reshape(devices, slots, piece_width),
            jnp.broadcast_to(stat_parts, (devices, extra, piece_width)),
        ],
        axis=1,
    ).reshape(devices * 2, (slots + extra) * piece_width // 2)
    ordered = lax.all_to_all(ordered, ("ctx", "shard"), split_axis=0, concat_axis=0, tiled=True)
    ordered = ordered.reshape(devices, slots + extra, piece_width)
    stat_rows = jnp.sum(wide(ordered[:, slots:]), axis=0).reshape(shard_count + 2, width)
    ordered = ordered[:, :slots].reshape(
        chips, 2, shard_count, slots, BR // (shard_count * chips), LANES
    )
    dense_sum = ordered.transpose(3, 2, 0, 4, 1, 5).reshape(slots, BR, BC)
    router_grad = stat_rows[:shard_count].T
    gains_grad = stat_rows[shard_count:]

    expert_grad, expert_new, expert_moment_new, expert_second_new = rotate(
        expert_weight[0], expert_sums, expert_moment[0], expert_second[0], expert_left[0], expert_right[0]
    )
    dense_grad, dense_new, dense_moment_new, dense_second_new = rotate(
        dense_weight, [dense_sum], dense_moment, dense_second, dense_left, dense_right
    )
    outputs = []
    for m in range(micros):
        total = x2s[m]
        for part in after(arrived, dense_new, expert_new):
            total = total + wide(part[m * rows : (m + 1) * rows])
        outputs.append(total)

    gains_new, gains_moment_new, gains_second_new = adam(
        norm_gains, gains_grad, gains_moment, gains_second, gain_rate
    )
    router_new, router_moment_new, router_second_new = adam(
        router, router_grad, router_moment, router_second, rate
    )
    return (
        jnp.stack(outputs),
        input_grad,
        dense_grad,
        dense_new,
        dense_moment_new,
        dense_second_new,
        expert_grad[None],
        expert_new[None],
        expert_moment_new[None],
        expert_second_new[None],
        gains_grad,
        gains_new,
        gains_moment_new,
        gains_second_new,
        router_grad,
        router_new,
        router_moment_new,
        router_second_new,
    )


def solution(mesh):
    rows_spec = P("shard", "ctx", None)
    dense_spec = P(("ctx", "shard"), None, None)
    expert_spec = P("shard", "ctx", None, None)
    in_specs = (
        (rows_spec, rows_spec, P(), P(), dense_spec, expert_spec, rows_spec, P(), P(), P())
        + (dense_spec,) * 4
        + (expert_spec,) * 4
        + (P(),) * 4
    )
    out_specs = (rows_spec,) * 2 + (dense_spec,) * 4 + (expert_spec,) * 4 + (P(),) * 8
    return jax.shard_map(shards, mesh=mesh, in_specs=in_specs, out_specs=out_specs, check_vma=False)
```

```python
import functools

import jax
import jax.numpy as jnp
from jax import lax
from jax.experimental import pallas as pl
from jax.experimental.pallas import tpu as pltpu
from jax.sharding import PartitionSpec as P

HEADS = 24
KVH = 8
HD = 64
FF = 1024
BR = 192
BC = 256
LANES = 128
UPPER = 144

norm_eps = 1e-06
beta_one = 0.9
beta_two = 0.95
rate = 0.01
gain_rate = 0.5
adam_eps = 1e-08
masked_score = -1e30
low_type = jnp.bfloat16
MIB = 1 << 20
VMEM_LIMIT = 60 * MIB

NN = (((1,), (0,)), ((), ()))
NT = (((1,), (1,)), ((), ()))
TN = (((0,), (0,)), ((), ()))

in_vmem = pl.BlockSpec(memory_space=pltpu.VMEM)
in_smem = pl.BlockSpec(memory_space=pltpu.SMEM)
in_any = pl.BlockSpec(memory_space=pl.ANY)


def dot(left_side, right_side, dims=NN):
    return lax.dot_general(left_side, right_side, dims, preferred_element_type=jnp.float32)


def call(kernel, out_shapes, in_specs, out_specs, scratch, flops, moved):
    return pl.pallas_call(
        kernel,
        out_shape=out_shapes,
        in_specs=in_specs,
        out_specs=out_specs,
        scratch_shapes=scratch,
        compiler_params=pltpu.CompilerParams(vmem_limit_bytes=VMEM_LIMIT),
        cost_estimate=pl.CostEstimate(flops=flops, bytes_accessed=moved, transcendentals=0),
    )


def shaped(dims, kind):
    return jax.ShapeDtypeStruct(dims, kind)


def inverse_order(slot_order):
    count = slot_order.shape[0]
    numbers = jnp.arange(count, dtype=jnp.int32)
    return jnp.sum(
        jnp.where(slot_order[None, :] == numbers[:, None], numbers[None, :], 0), axis=1
    ).astype(jnp.int32)


def wait_bytes(landed, semaphore):
    pltpu.make_async_copy(landed, landed, semaphore).wait()


def unit_rows(rows, gain):
    inverse = lax.rsqrt(jnp.mean(rows * rows, axis=-1, keepdims=True) + norm_eps)
    return rows * inverse * gain, inverse


def unit_back(rows, gain, inverse, gradient):
    unit = rows * inverse
    scaled = gradient * gain
    inner = jnp.mean(scaled * unit, axis=-1, keepdims=True)
    return inverse * (scaled - unit * inner), jnp.sum(gradient * unit, axis=0, keepdims=True)


def lane_ids(dims):
    return lax.broadcasted_iota(jnp.int32, dims, len(dims) - 1)


def half_turn(tile):
    return pltpu.roll(tile, HD, 1)


def stack_heads(ref, pair, scale=None):
    base = pair * (3 * LANES)
    tiles = [
        ref[:, pl.ds(pl.multiple_of(base + LANES * t, LANES), LANES)].astype(jnp.float32)
        for t in range(3)
    ]
    if scale is not None:
        tiles = [t * scale for t in tiles]
    lower = lane_ids(tiles[0].shape) < HD
    first = [tiles[0], half_turn(tiles[0]), tiles[1]]
    second = [tiles[1], half_turn(tiles[2]), tiles[2]]
    return (
        jnp.concatenate([jnp.where(lower, t, 0.0) for t in first], axis=0),
        jnp.concatenate([jnp.where(lower, 0.0, t) for t in second], axis=0),
    )


def unstack_heads(ref, pair, first, second):
    rows = first.shape[0] // 3
    base = pair * (3 * LANES)
    lower = lane_ids((rows, LANES)) < HD
    tiles = (
        jnp.where(lower, first[:rows], half_turn(first[rows : 2 * rows])),
        jnp.where(lower, first[2 * rows :], second[:rows]),
        jnp.where(lower, half_turn(second[rows : 2 * rows]), second[2 * rows :]),
    )
    for t in range(3):
        ref[:, pl.ds(pl.multiple_of(base + LANES * t, LANES), LANES)] = tiles[t].astype(ref.dtype)


def project_kernel(
    pieces, chips, members, slots, all_groups, micros, order_ref, me_ref, *refs
):
    x_refs = refs[:micros]
    gain_ref = refs[micros]
    piece_refs = refs[micros + 1 : micros + 1 + len(pieces)]
    refs = refs[micros + 1 + len(pieces) :]
    h_ref = refs[0]
    kv_refs = refs[1 : 1 + micros]
    win_ref, wout_ref, held, held_out, sems, out_sems = refs[1 + micros :]
    groups = held.shape[1] // BC
    kv_groups = kv_refs[0].shape[-1] // BC
    rows = x_refs[0].shape[0]
    ctx, shard = me_ref[0], me_ref[1]
    chip, core = lax.div(ctx, 2), lax.rem(ctx, 2)

    for ref, (other_core, offset, first, cut) in zip(piece_refs, pieces):

        @pl.loop(0, ref.shape[0])
        def _(i):
            source = lax.rem(chip - (first + lax.div(i, slots)) + chips, chips) * 2
            source = source + jnp.bitwise_xor(core, other_core)
            source = source * members + jnp.bitwise_xor(shard, offset)
            number = order_ref[source * slots + lax.rem(i, slots)]
            a, b = lax.div(number, all_groups), lax.rem(number, all_groups)
            down = pl.ds(pl.multiple_of(a * BR + cut, 32), ref.shape[1])

            @pl.when(b < groups)
            def _():
                across = pl.ds(pl.multiple_of(b * BC, BC), BC)
                pltpu.make_async_copy(ref.at[i], held.at[down, across], sems.at[b]).start()

            @pl.when(b >= groups)
            def _():
                across = pl.ds(pl.multiple_of((b - groups) * BC, BC), BC)
                pltpu.make_async_copy(ref.at[i], held_out.at[down, across], sems.at[groups]).start()

    for m in range(micros):
        h_ref[m * rows : (m + 1) * rows, :] = unit_rows(x_refs[m][...], gain_ref[0:1])[0].astype(
            low_type
        )
    q_groups = groups - kv_groups

    @pl.loop(0, groups)
    def _(b):
        across = pl.ds(pl.multiple_of(b * BC, BC), BC)
        wait_bytes(held.at[:, across], sems.at[b])

    wait_bytes(held_out, sems.at[groups])
    copies = [
        pltpu.make_async_copy(held, win_ref, out_sems.at[0]),
        pltpu.make_async_copy(held_out, wout_ref, out_sems.at[1]),
    ]
    for copy in copies:
        copy.start()

    @pl.loop(0, kv_groups)
    def _(b):
        across = pl.ds(pl.multiple_of((q_groups + b) * BC, BC), BC)
        made = dot(h_ref[...], held[:, across]).astype(low_type)
        for m in range(micros):
            kv_refs[m][:, pl.ds(pl.multiple_of(b * BC, BC), BC)] = made[m * rows : (m + 1) * rows]

    for copy in copies:
        copy.wait()


def project(pieces, arrays, chips, members, slots, order, me, xs, gains):
    micros = len(xs)
    rows, width = xs[0].shape
    in_width = (HEADS + 2 * KVH) * HD
    out_width = HEADS * HD
    kv_width = 2 * KVH * HD
    return call(
        functools.partial(
            project_kernel, pieces, chips, members, slots, (in_width + out_width) // BC, micros
        ),
        tuple(
            [shaped((micros * rows, width), low_type)]
            + [shaped((rows, kv_width), low_type)] * micros
            + [shaped((width, in_width), low_type), shaped((width, out_width), low_type)]
        ),
        [in_smem, in_smem] + [in_vmem] * (micros + 1) + [in_any] * len(arrays),
        tuple([in_vmem] * (1 + micros) + [in_any, in_any]),
        [
            pltpu.VMEM((width, in_width), low_type),
            pltpu.VMEM((width, out_width), low_type),
            pltpu.SemaphoreType.DMA((in_width // BC + 1,)),
            pltpu.SemaphoreType.DMA((2,)),
        ],
        2 * micros * rows * width * kv_width,
        4 * width * (in_width + out_width),
    )(order, me, *xs, gains, *arrays)


def query_kernel(h_ref, w_ref, *refs):
    q_refs = refs[:-2]
    held, sems = refs[-2:]
    groups = held.shape[1] // BC
    rows = q_refs[0].shape[0]

    def copy(b):
        across = pl.ds(pl.multiple_of(b * BC, BC), BC)
        return pltpu.make_async_copy(w_ref.at[:, across], held.at[:, across], sems.at[b])

    @pl.loop(0, groups)
    def _(b):
        copy(b).start()

    @pl.loop(0, groups)
    def _(b):
        copy(b).wait()
        across = pl.ds(pl.multiple_of(b * BC, BC), BC)
        made = dot(h_ref[...], held[:, across]).astype(low_type)
        for m, ref in enumerate(q_refs):
            ref[:, across] = made[m * rows : (m + 1) * rows]


def make_queries(h, w, micros):
    total, width = h.shape
    q_width = HEADS * HD
    return call(
        query_kernel,
        tuple([shaped((total // micros, q_width), low_type)] * micros),
        [in_vmem, in_any],
        tuple([in_vmem] * micros),
        [pltpu.VMEM((width, q_width), low_type), pltpu.SemaphoreType.DMA((q_width // BC,))],
        2 * total * width * q_width,
        2 * width * q_width,
    )(h, w)


def attend_kernel(
    q_ref, rpos_ref, kpos_ref, x_ref, gain_ref, w_ref, all_ref,
    ob_ref, log_ref, x2_ref, h2_ref, bias, kv_ref, held, sems,
):
    rows = q_ref.shape[0]
    pltpu.make_async_copy(all_ref, kv_ref, sems.at[0]).start()
    pltpu.make_async_copy(w_ref, held, sems.at[1]).start()
    bias[...] = jnp.where(kpos_ref[...] <= rpos_ref[...], 0.0, masked_score)
    log_ref[...] = jnp.zeros_like(log_ref)
    length = kv_ref.shape[0]
    wait_bytes(kv_ref, sems.at[0])

    @pl.loop(0, KVH // 2)
    def _(pair):
        lane = pl.multiple_of(pair * LANES, LANES)
        keys = kv_ref[:, pl.ds(lane, LANES)]
        values = kv_ref[:, pl.ds(pl.multiple_of(lane + KVH * HD, LANES), LANES)]
        stacked = stack_heads(q_ref, pair, HD**-0.5)
        mixed = []
        for part in range(2):
            scores = dot(stacked[part].astype(low_type), keys, NT)
            scores = (scores.reshape(3, rows, length) + bias[...][None]).reshape(3 * rows, length)
            largest = jnp.max(scores, axis=-1, keepdims=True)
            raised = jnp.exp(scores - largest)
            summed = jnp.sum(raised, axis=-1, keepdims=True)
            mixed.append(dot(raised.astype(low_type), values) / summed)
            log_ref[...] = jnp.where(
                lane_ids(log_ref.shape) == 2 * pair + part, largest + jnp.log(summed), log_ref[...]
            )
        unstack_heads(ob_ref, pair, mixed[0], mixed[1])

    wait_bytes(held, sems.at[1])
    for n in range(held.shape[0] // BC):
        cut = slice(n * BC, (n + 1) * BC)
        x2_ref[:, cut] = x_ref[:, cut] + dot(ob_ref[...], held[cut, :], NT)
    h2_ref[...] = unit_rows(x2_ref[...], gain_ref[1:2])[0].astype(low_type)


def attend(q, kv, rows_pos, key_pos, x, gains, w):
    rows, width = q.shape
    length = key_pos.shape[1]
    model = x.shape[1]
    return call(
        attend_kernel,
        (
            shaped((rows, width), low_type),
            shaped((3 * rows, LANES), jnp.float32),
            shaped((rows, model), jnp.float32),
            shaped((rows, model), low_type),
        ),
        [in_vmem] * 5 + [in_any] * 2,
        (in_vmem,) * 4,
        [
            pltpu.VMEM((rows, length), jnp.float32),
            pltpu.VMEM((length, kv.shape[1]), low_type),
            pltpu.VMEM((model, width), low_type),
            pltpu.SemaphoreType.DMA((2,)),
        ],
        16 * rows * length * width,
        8 * MIB,
    )(q, rows_pos, key_pos, x, gains, w, kv)


def router_parts(h2, router, experts):
    logits = dot(h2, router)
    logits = jnp.where(lane_ids(logits.shape) < experts, logits, masked_score)
    raised = jnp.exp(logits - jnp.max(logits, axis=-1, keepdims=True))
    return raised / jnp.sum(raised, axis=-1, keepdims=True)


def expert_kernel(sources, micro, order_ref, me_ref, router_ref, *refs):
    h_parts = refs[:sources]
    c_parts = refs[sources : 2 * sources]
    w_refs = refs[2 * sources : 2 * sources + 2]
    outs = refs[2 * sources + 2 :]
    back_refs = outs[:sources]
    z_ref, dg_ref, du_ref, cs, xs_ref = outs[sources : sources + 5]
    held, chance, load_sem, w_sems = outs[sources + 5 :]
    rows, width = h_parts[0].shape
    row_groups = width // BR
    col_groups = FF // BC
    for j in range(sources):
        pltpu.make_async_copy(h_parts[j], xs_ref.at[pl.ds(j * rows, rows)], load_sem.at[0]).start()
        pltpu.make_async_copy(
            c_parts[j].at[pl.ds(micro * rows, rows)], cs.at[pl.ds(j * rows, rows)], load_sem.at[1]
        ).start()
    for b in range(col_groups):

        @pl.loop(0, row_groups)
        def _(a):
            for k in range(3):
                slot = order_ref[(k * row_groups + a) * col_groups + b]
                for start, ref in zip((0, UPPER), w_refs):
                    down = pl.ds(pl.multiple_of(a * BR + start, 64), ref.shape[1])
                    pltpu.make_async_copy(
                        ref.at[slot], held.at[k, down, pl.ds(b * BC, BC)], w_sems.at[b]
                    ).start()

    wait_bytes(xs_ref, load_sem.at[0])
    wait_bytes(cs, load_sem.at[1])
    me = me_ref[1]
    probs = router_parts(xs_ref[...], router_ref[...], sources)
    hits = cs[:, width:].astype(jnp.float32)
    mine = lane_ids(hits.shape) == me
    hit = jnp.sum(jnp.where(mine, hits, 0.0), axis=-1, keepdims=True)
    weight = jnp.sum(jnp.where(mine, probs, 0.0), axis=-1, keepdims=True) * hit
    chance[...] = jnp.zeros_like(chance)

    @pl.loop(0, col_groups)
    def _(b):
        cut = pl.ds(pl.multiple_of(b * BC, BC), BC)
        wait_bytes(held.at[:, :, cut], w_sems.at[b])
        gate = dot(xs_ref[...], held[0, :, cut])
        up = dot(xs_ref[...], held[1, :, cut])
        down = dot(cs[:, :width], held[2, :, cut])
        sig = jax.nn.sigmoid(gate)
        act = gate * sig
        hidden = act * up
        chance[...] += jnp.sum(down * hidden, axis=-1, keepdims=True)
        z_ref[:, cut] = (hidden * weight).astype(low_type)
        down = down * weight
        dg_ref[:, cut] = (down * up * (sig + act * (1.0 - sig))).astype(low_type)
        du_ref[:, cut] = (down * act).astype(low_type)

    for n in range(width // BC):
        cut = slice(n * BC, (n + 1) * BC)
        back = dot(dg_ref[...], held[0, cut, :], NT) + dot(du_ref[...], held[1, cut, :], NT)
        for j in range(sources):
            back_refs[j][:, cut] = back[j * rows : (j + 1) * rows].astype(low_type)
    told = chance[...] * hit
    high_part = told.astype(low_type)
    low_part = (told - high_part.astype(jnp.float32)).astype(low_type)
    lanes = lane_ids((sources * rows, LANES))
    tail = jnp.where(lanes == 0, high_part, jnp.where(lanes == 1, low_part, jnp.zeros_like(low_part)))
    for j in range(sources):
        back_refs[j][:, width:] = tail[j * rows : (j + 1) * rows]


def run_expert(micro, order, me, router, h_parts, c_parts, ws):
    sources = len(h_parts)
    rows, width = h_parts[0].shape
    total = sources * rows
    return call(
        functools.partial(expert_kernel, sources, micro),
        tuple(
            [shaped((rows, width + LANES), low_type)] * sources
            + [shaped((total, FF), low_type)] * 3
            + [shaped((total, width + LANES), low_type), shaped((total, width), low_type)]
        ),
        [in_smem, in_smem, in_vmem] + [in_any] * (2 * sources + 2),
        tuple([in_vmem] * (sources + 5)),
        [
            pltpu.VMEM((3, width, FF), low_type),
            pltpu.VMEM((total, 1), jnp.float32),
            pltpu.SemaphoreType.DMA((2,)),
            pltpu.SemaphoreType.DMA((FF // BC,)),
        ],
        10 * total * width * FF,
        20 * MIB,
    )(order, me, router, *h_parts, *c_parts, *ws)


def produce_kernel(sources, order_ref, upper_ref, lower_ref, *refs):
    out_refs = refs[-3 - sources : -3]
    z_refs = refs[: -3 - sources]
    zs, held, sem = refs[-3:]
    width = held.shape[0]
    total = z_refs[0].shape[0]
    rows = total // sources
    row_groups, col_groups = width // BR, FF // BC

    @pl.loop(0, row_groups)
    def _(a):
        for b in range(col_groups):
            slot = order_ref[(2 * row_groups + a) * col_groups + b]
            for start, ref in zip((0, UPPER), (upper_ref, lower_ref)):
                down = pl.ds(pl.multiple_of(a * BR + start, 64), ref.shape[1])
                pltpu.make_async_copy(
                    ref.at[slot], held.at[down, pl.ds(b * BC, BC)], sem
                ).start()

    for m, z_ref in enumerate(z_refs):
        zs[m * total : (m + 1) * total] = z_ref[...]
    wait_bytes(held, sem)
    for n in range(width // BC):
        cut = slice(n * BC, (n + 1) * BC)
        made = dot(zs[...], held[cut, :], NT).astype(low_type)
        for m in range(len(z_refs)):
            for j in range(sources):
                start = m * total + j * rows
                out_refs[j][m * rows : (m + 1) * rows, cut] = made[start : start + rows]


def produce(order, ws, zs, sources, width):
    micros = len(zs)
    total = zs[0].shape[0]
    return call(
        functools.partial(produce_kernel, sources),
        tuple([shaped((micros * total // sources, width), low_type)] * sources),
        [in_smem, in_any, in_any] + [in_vmem] * micros,
        tuple([in_vmem] * sources),
        [
            pltpu.VMEM((micros * total, FF), low_type),
            pltpu.VMEM((width, FF), low_type),
            pltpu.SemaphoreType.DMA,
        ],
        2 * micros * total * width * FF,
        8 * MIB,
    )(order, *ws, *zs)


def outer_kernel(groups, col_groups, order_ref, *refs):
    micros = len(refs[:-5]) // (len(groups) + 2)
    lefts = [refs[i * micros : (i + 1) * micros] for i in range(2)]
    rights = [refs[(2 + i) * micros : (3 + i) * micros] for i in range(len(groups))]
    out_refs, (turned, stage, sems) = refs[-5:-3], refs[-3:]
    rows = rights[0][0].shape[0]
    width = turned.shape[1]
    span = 2 * BR
    for side in range(2):
        for m in range(micros):
            for r in range(0, rows, LANES):
                part = lefts[side][m][r : r + LANES, :width]
                turned[side, :, m * rows + r : m * rows + r + LANES] = part.T
    row_groups = width // BR
    steps = [(k, p) for k in range(len(groups)) for p in range(width // span)]
    for n, (k, p) in enumerate(steps):
        slot = n % 2
        if n >= 2:
            wait_bytes(stage.at[slot], sems.at[slot])
        cut = slice(p * span, (p + 1) * span)
        made = 0.0
        for m in range(micros):
            left = turned[groups[k], cut, m * rows : (m + 1) * rows]
            made = made + dot(left, rights[k][m][...])
        stage[slot] = made.astype(low_type)
        for half in range(2):
            for b in range(col_groups):
                number = (k * row_groups + 2 * p + half) * col_groups + b
                place = order_ref[number]
                for side in range(2):
                    pltpu.make_async_copy(
                        stage.at[
                            slot, pl.ds(half * BR, BR), pl.ds(b * BC + side * LANES, LANES)
                        ],
                        out_refs[side].at[place],
                        sems.at[slot],
                    ).start()
    for slot in range(2):
        wait_bytes(stage.at[slot], sems.at[slot])


def outer_blocks(order, width, groups, lefts, rights):
    flat = [part for group in lefts + rights for part in group]
    rows = sum(part.shape[0] for part in rights[0])
    cols = rights[0][0].shape[1]
    blocks = len(groups) * width * cols // (BR * BC)
    return call(
        functools.partial(outer_kernel, groups, cols // BC),
        (shaped((blocks, BR, LANES), low_type),) * 2,
        [in_smem] + [in_vmem] * len(flat),
        (in_any,) * 2,
        [
            pltpu.VMEM((2, width, rows), low_type),
            pltpu.VMEM((2, 2 * BR, cols), low_type),
            pltpu.SemaphoreType.DMA((2,)),
        ],
        2 * rows * blocks * BR * BC,
        blocks * BR * BC * 2 + sum(f.size * 2 for f in flat),
    )(order, *flat)


def xor_plan(members, offset):
    if members != 4:
        return list(range(1, members)), [0]
    first = 1 if offset % 2 else 2
    return [first, 3], [0, 3 - first]


def pieces_kernel(members, counts, cols, turned_first, me_ref, *refs):
    row_groups = 8
    lists = []
    for left_count, right_count in counts:
        lists.append((refs[:left_count], refs[left_count : left_count + right_count]))
        refs = refs[left_count + right_count :]
    outs, refs = refs[:4], refs[4:]
    extra = refs[0] if not turned_first else None
    turned, rights, stage, sems = refs[0 if turned_first else 1 :]
    ctx, shard = me_ref[0], me_ref[1]
    core = lax.rem(ctx, 2)
    total = turned.shape[2]
    row_groups = turned.shape[1] // BR
    base = 0
    for g, (_, parts) in enumerate(lists):
        start = 0
        for part in parts:
            count = part.shape[0]
            for b in range(cols[g]):
                lane = pl.multiple_of(b * BC + core * LANES, LANES)
                pltpu.make_async_copy(
                    part.at[:, pl.ds(lane, LANES)],
                    rights.at[pl.ds(start, count), pl.ds((base + b) * LANES, LANES)],
                    sems.at[g],
                ).start()
            start += count
        base += cols[g]
    for g, (parts, _) in enumerate(lists):
        if g == 0 and turned_first:
            turned[0] = parts[0][...]
            continue
        start = 0
        for part in parts:
            for r in range(0, part.shape[0], LANES):
                turned[g, :, start : start + LANES] = part[r : r + LANES, :].T
                start += LANES
    if extra is not None:
        extra[...] = turned[0]
    all_cols = sum(cols)
    half_blocks = row_groups // 2 * all_cols
    span = BR // members
    base = 0
    for g in range(len(lists)):
        wide_cols = cols[g] * LANES
        wait_bytes(rights.at[:, pl.ds(base * LANES, wide_cols)], sems.at[g])
        for a in range(row_groups):
            made = dot(
                turned[g, a * BR : (a + 1) * BR, :],
                rights[:, base * LANES : base * LANES + wide_cols],
            )
            stage[a % 2, :, :wide_cols] = made.astype(stage.dtype)
            half = a // (row_groups // 2)
            first = (a % (row_groups // 2)) * all_cols + base
            for out, hops in zip(outs[2 * half : 2 * half + 2], xor_plan(members, 1 - half)):
                for place, hop in enumerate(hops):
                    down = pl.multiple_of(jnp.bitwise_xor(shard, hop) * span, 16 if span % 16 == 0 else 8)
                    for b in range(cols[g]):
                        out[place * half_blocks + first + b] = stage[
                            a % 2, pl.ds(down, span), b * LANES : (b + 1) * LANES
                        ].astype(low_type)
        base += cols[g]


def gradient_pieces(members, me, groups, cols, turned_first):
    counts = tuple((len(left), len(right)) for left, right in groups)
    flat = [part for left, right in groups for part in left + right]
    total = sum(part.shape[0] for part in groups[0][1])
    width = groups[0][0][0].shape[0 if turned_first else 1]
    row_groups = width // BR
    half_blocks = row_groups // 2 * sum(cols)
    span = BR // members
    stage_type = jnp.float32 if span % 16 else low_type
    outs = []
    for half in range(2):
        for hops in xor_plan(members, 1 - half):
            outs.append(shaped((len(hops) * half_blocks, span, LANES), low_type))
    out_specs = [in_vmem] * 4
    if not turned_first:
        outs.append(shaped((width, total), low_type))
        out_specs.append(in_vmem)
    in_specs = [in_smem]
    for left, right in groups:
        in_specs += [in_vmem] * len(left) + [in_any] * len(right)
    return call(
        functools.partial(pieces_kernel, members, counts, tuple(cols), turned_first),
        tuple(outs),
        in_specs,
        tuple(out_specs),
        [
            pltpu.VMEM((len(groups), width, total), low_type),
            pltpu.VMEM((total, sum(cols) * LANES), low_type),
            pltpu.VMEM((2, BR, max(cols) * LANES), stage_type),
            pltpu.SemaphoreType.DMA((len(groups),)),
        ],
        2 * total * width * sum(cols) * LANES,
        16 * MIB,
    )(me, *flat)


def merge_kernel(
    sources, me_ref, x2_ref, cot_ref, h2_ref, gain_ref, router_ref, w_ref, *refs
):
    back_refs = refs[:sources]
    dx_ref, da_ref, do_ref, stat_ref, held, sem = refs[sources:]
    rows, width = x2_ref.shape
    pltpu.make_async_copy(w_ref, held, sem).start()
    lanes = lane_ids((rows, LANES))
    prob_grad = jnp.zeros((rows, LANES), jnp.float32)
    gathered = jnp.zeros((rows, width), jnp.float32)
    for j in range(sources):
        tail = back_refs[j][:, width:].astype(jnp.float32)
        told = jnp.sum(tail, axis=-1, keepdims=True)
        expert = jnp.bitwise_xor(me_ref[1], j)
        prob_grad = prob_grad + jnp.where(lanes == expert, told, 0.0)
        gathered = gathered + back_refs[j][:, :width].astype(jnp.float32)
    h2 = h2_ref[...]
    probs = router_parts(h2, router_ref[...], sources)
    logit_grad = probs * (prob_grad - jnp.sum(probs * prob_grad, axis=-1, keepdims=True))
    high_part = logit_grad.astype(low_type)
    low_part = (logit_grad - high_part.astype(jnp.float32)).astype(low_type)
    router_grad = dot(high_part, h2, TN) + dot(low_part, h2, TN)
    gathered = gathered + dot(high_part, router_ref[...], NT) + dot(low_part, router_ref[...], NT)
    x2 = x2_ref[...]
    inverse = lax.rsqrt(jnp.mean(x2 * x2, axis=-1, keepdims=True) + norm_eps)
    moe_grad, gain_grad = unit_back(x2, gain_ref[1:2], inverse, gathered)
    after = cot_ref[...] + moe_grad
    dx_ref[...] = after
    da_ref[...] = after.astype(low_type)
    experts_up = stat_ref.shape[0] - 8
    stat_ref[:experts_up] = router_grad[:experts_up]
    stat_ref[experts_up:] = jnp.broadcast_to(gain_grad, (8, width))
    wait_bytes(held, sem)
    for n in range(held.shape[1] // BC):
        cut = slice(n * BC, (n + 1) * BC)
        do_ref[:, cut] = dot(da_ref[...], held[:, cut]).astype(low_type)


def merge(me, x2, cot, h2, gains, router, w, backs):
    rows, width = x2.shape
    sources = len(backs)
    experts_up = -(-sources // 8) * 8
    return call(
        functools.partial(merge_kernel, sources),
        (
            shaped((rows, width), jnp.float32),
            shaped((rows, width), low_type),
            shaped((rows, HEADS * HD), low_type),
            shaped((experts_up + 8, width), jnp.float32),
        ),
        [in_smem] + [in_vmem] * 5 + [in_any] + [in_vmem] * sources,
        (in_vmem,) * 4,
        [pltpu.VMEM((width, HEADS * HD), low_type), pltpu.SemaphoreType.DMA],
        2 * rows * width * HEADS * HD,
        10 * MIB,
    )(me, x2, cot, h2, gains, router, w, *backs)


def attend_back_kernel(
    micro, q_ref, rpos_ref, kpos_ref, ob_ref, log_ref, do_ref, all_ref, *refs
):
    dq_ref, out_ref, bias, kv_ref, grad_ref, sems = refs[-6:]
    rows = q_ref.shape[0]
    pltpu.make_async_copy(all_ref, kv_ref, sems.at[0]).start()
    length = kv_ref.shape[0]
    bias[...] = jnp.where(kpos_ref[...] <= rpos_ref[...], 0.0, masked_score)
    wait_bytes(kv_ref, sems.at[0])

    @pl.loop(0, KVH // 2)
    def _(pair):
        lane = pl.multiple_of(pair * LANES, LANES)
        value_lane = pl.multiple_of(lane + KVH * HD, LANES)
        keys = kv_ref[:, pl.ds(lane, LANES)]
        values = kv_ref[:, pl.ds(value_lane, LANES)]
        queries = stack_heads(q_ref, pair, HD**-0.5)
        grads = stack_heads(do_ref, pair)
        mixes = stack_heads(ob_ref, pair)
        query_grads = []
        key_grad = value_grad = None
        for part in range(2):
            query = queries[part].astype(low_type)
            grad = grads[part].astype(low_type)
            log_total = jnp.sum(
                jnp.where(lane_ids(log_ref.shape) == 2 * pair + part, log_ref[...], 0.0),
                axis=-1,
                keepdims=True,
            )
            delta = jnp.sum(grads[part] * mixes[part], axis=-1, keepdims=True)
            scores = dot(query, keys, NT)
            scores = (scores.reshape(3, rows, length) + bias[...][None]).reshape(3 * rows, length)
            chance = jnp.exp(scores - log_total)
            prob_grad = dot(grad, values, NT)
            score_grad = (chance * (prob_grad - delta)).astype(low_type)
            value_term = dot(chance.astype(low_type), grad, TN)
            key_term = dot(score_grad, query, TN)
            key_grad = key_term if part == 0 else key_grad + key_term
            value_grad = value_term if part == 0 else value_grad + value_term
            query_grads.append(dot(score_grad, keys) * HD**-0.5)
        unstack_heads(dq_ref, pair, query_grads[0], query_grads[1])
        grad_ref[:, pl.ds(lane, LANES)] = key_grad.astype(low_type)
        grad_ref[:, pl.ds(value_lane, LANES)] = value_grad.astype(low_type)

    count = length // rows
    span = out_ref.shape[0] // count

    @pl.loop(0, count)
    def _(i):
        pltpu.make_async_copy(
            grad_ref.at[pl.ds(pl.multiple_of(i * rows, 16), rows)],
            out_ref.at[pl.ds(pl.multiple_of(i * span + micro * rows, 16), rows)],
            sems.at[1],
        ).start()

    wait_bytes(grad_ref, sems.at[1])


def attend_back(micro, micros, q, kv, rows_pos, key_pos, ob, log_total, do, shared):
    rows, width = q.shape
    length = key_pos.shape[1]
    operands = [q, rows_pos, key_pos, ob, log_total, do, kv]
    in_specs = [in_vmem] * 6 + [in_any]
    aliases = {}
    if shared is not None:
        aliases = {len(operands): 1}
        operands.append(shared)
        in_specs.append(in_any)
    return pl.pallas_call(
        functools.partial(attend_back_kernel, micro),
        out_shape=(
            shaped((rows, width), low_type),
            shaped((micros * length, kv.shape[1]), low_type),
        ),
        in_specs=in_specs,
        out_specs=(in_vmem, in_any),
        scratch_shapes=[
            pltpu.VMEM((rows, length), jnp.float32),
            pltpu.VMEM((length, kv.shape[1]), low_type),
            pltpu.VMEM((length, kv.shape[1]), low_type),
            pltpu.SemaphoreType.DMA((2,)),
        ],
        input_output_aliases=aliases,
        compiler_params=pltpu.CompilerParams(vmem_limit_bytes=VMEM_LIMIT),
        cost_estimate=pl.CostEstimate(
            flops=40 * rows * length * width, bytes_accessed=8 * MIB, transcendentals=0
        ),
    )(*operands)


def query_back_kernel(w_ref, *refs):
    micros = (len(refs) - 3) // 2
    dq_refs, out_refs = refs[:micros], refs[micros : 2 * micros]
    rows_ref, held, sem = refs[2 * micros :]
    rows = dq_refs[0].shape[0]
    copy = pltpu.make_async_copy(w_ref.at[:, pl.ds(0, held.shape[1])], held, sem)
    copy.start()
    for m in range(micros):
        rows_ref[m * rows : (m + 1) * rows] = dq_refs[m][...]
    copy.wait()
    for n in range(held.shape[0] // BC):
        cut = slice(n * BC, (n + 1) * BC)
        made = dot(rows_ref[...], held[cut, :], NT)
        for m in range(micros):
            out_refs[m][:, cut] = made[m * rows : (m + 1) * rows]


def query_back(w, dqs):
    micros = len(dqs)
    rows, q_width = dqs[0].shape
    width = w.shape[0]
    return call(
        query_back_kernel,
        tuple([shaped((rows, width), jnp.float32)] * micros),
        [in_any] + [in_vmem] * micros,
        tuple([in_vmem] * micros),
        [
            pltpu.VMEM((micros * rows, q_width), low_type),
            pltpu.VMEM((width, q_width), low_type),
            pltpu.SemaphoreType.DMA,
        ],
        2 * micros * rows * width * q_width,
        7 * MIB,
    )(w, *dqs)


def input_kernel(x_ref, gain_ref, w_ref, *refs):
    micros, rows = x_ref.shape[:2]
    dx_refs = refs[:micros]
    part_refs = refs[micros : 2 * micros]
    dkv_ref, out_ref, stat_ref, grad, held, sem = refs[2 * micros :]
    kv_width = held.shape[1]
    copy = pltpu.make_async_copy(
        w_ref.at[:, pl.ds(w_ref.shape[1] - kv_width, kv_width)], held, sem
    )
    copy.start()
    copy.wait()
    for n in range(held.shape[0] // BC):
        cut = slice(n * BC, (n + 1) * BC)
        made = dot(dkv_ref[...], held[cut, :], NT)
        for m in range(micros):
            grad[m, :, cut] = part_refs[m][:, cut] + made[m * rows : (m + 1) * rows]
    total = jnp.zeros((1, x_ref.shape[-1]), jnp.float32)
    for m in range(micros):
        x = x_ref[m]
        inverse = lax.rsqrt(jnp.mean(x * x, axis=-1, keepdims=True) + norm_eps)
        term, gain_grad = unit_back(x, gain_ref[0:1], inverse, grad[m])
        out_ref[m] = dx_refs[m][...] + term
        total = total + gain_grad
    stat_ref[...] = jnp.broadcast_to(total, stat_ref.shape)


def input_back(x, gains, w, dxs, parts, dkv):
    micros, rows, width = x.shape
    kv_width = dkv.shape[1]
    return call(
        input_kernel,
        (shaped(x.shape, jnp.float32), shaped((8, width), jnp.float32)),
        [in_vmem, in_vmem, in_any] + [in_vmem] * (2 * micros + 1),
        (in_vmem,) * 2,
        [
            pltpu.VMEM(x.shape, jnp.float32),
            pltpu.VMEM((width, kv_width), low_type),
            pltpu.SemaphoreType.DMA,
        ],
        2 * micros * rows * width * kv_width,
        14 * MIB,
    )(x, gains, w, *dxs, *parts, dkv)


def rotate_kernel(b_ref, m_ref, s_ref, l_ref, r_ref, *refs):
    grad_ref, new_ref, moment_ref, second_ref = refs[-4:]
    parts = [ref[0].astype(jnp.float32) for ref in refs[:-4]]
    gradient = parts[0] if len(parts) == 1 else jnp.concatenate(parts, axis=1)
    grad_ref[0] = gradient
    left = l_ref[0].astype(low_type)
    right = r_ref[0].astype(low_type)
    rotated = dot(dot(left, gradient.astype(low_type), TN).astype(low_type), right)
    moment = beta_one * m_ref[0] + (1.0 - beta_one) * rotated
    second = beta_two * s_ref[0] + (1.0 - beta_two) * rotated * rotated
    moment_ref[0] = moment
    second_ref[0] = second
    direction = (moment / (jnp.sqrt(second) + adam_eps)).astype(low_type)
    turned = dot(dot(left, direction).astype(low_type), right, NT)
    new_ref[0] = b_ref[0] - rate * turned


def rotate(weight, gradients, moment, second, left, right):
    count = weight.shape[0]

    def spec(rows, cols):
        return pl.BlockSpec((1, rows, cols), lambda i: (i, 0, 0))

    block = spec(BR, BC)
    return pl.pallas_call(
        rotate_kernel,
        grid=(count,),
        out_shape=(shaped(weight.shape, jnp.float32),) * 4,
        in_specs=[block] * 3
        + [spec(BR, BR), spec(BC, BC)]
        + [spec(BR, part.shape[2]) for part in gradients],
        out_specs=(block,) * 4,
        compiler_params=pltpu.CompilerParams(vmem_limit_bytes=VMEM_LIMIT),
        cost_estimate=pl.CostEstimate(
            flops=4 * count * BR * BC * (BR + BC),
            bytes_accessed=count * 2 * MIB,
            transcendentals=0,
        ),
    )(weight, moment, second, left, right, *gradients)


def adam(weight, gradient, moment, second, step_rate):
    moment_new = beta_one * moment + (1.0 - beta_one) * gradient
    second_new = beta_two * second + (1.0 - beta_two) * gradient * gradient
    return (
        weight - step_rate * moment_new / (jnp.sqrt(second_new) + adam_eps),
        moment_new,
        second_new,
    )


def piece_places(row_groups, q_groups, kv_groups):
    all_groups = 2 * q_groups + kv_groups
    out_groups = list(range(q_groups)) + list(range(q_groups + kv_groups, all_groups))
    numbers = [a * all_groups + b for a in range(row_groups) for b in out_groups]
    numbers += [a * all_groups + q_groups + b for a in range(row_groups) for b in range(kv_groups)]
    places = [0] * len(numbers)
    for place, number in enumerate(numbers):
        places[number] = place
    return places


def to_partner(array, offset):
    if offset == 0:
        return array
    count = lax.axis_size("shard")
    return lax.ppermute(array, "shard", [(i, i ^ offset) for i in range(count)])


def to_ctx(array, offset):
    count = lax.axis_size("ctx")
    return lax.ppermute(array, "ctx", [(i, i ^ offset) for i in range(count)])


def to_chip(array, offset):
    count = lax.axis_size("ctx")
    return lax.ppermute(array, "ctx", [(i, (i + 2 * offset) % count) for i in range(count)])


def after(value, *others):
    return lax.optimization_barrier((value, others))[0]


def from_chips(array, chips):
    return [array] + [to_chip(array, offset) for offset in range(1, chips)]


def wide(array):
    return array.astype(jnp.float32)


def sum_to_chips(parts):
    total = wide(parts[0])
    for offset in range(1, len(parts)):
        total = total + wide(to_chip(parts[offset], -offset))
    return total


def gather_weights(blocks, chips, members):
    parts = [blocks]
    for _ in range(chips - 1):
        parts.append(to_chip(parts[-1], 1))
    pieces, arrays = [], []
    gate = []

    def add(array, offset, first, cut):
        pieces.append((0, offset, first, cut))
        arrays.append(array)
        pieces.append((1, offset, first, cut))
        arrays.append(to_ctx(after(array, *gate), 1))
        return array

    def spread(group, first):
        add(group, 0, first, 0)
        if members == 4 and first > 0:
            by_one, by_two = to_partner(group, 1), to_partner(group, 2)
            add(by_one, 1, first, 0)
            add(by_two, 2, first, 0)
            half = BR // 2
            add(to_partner(by_one[:, :half], 2), 3, first, 0)
            add(to_partner(by_two[:, half:], 1), 3, first, half)
            return [by_one, by_two]
        got = [to_partner(group, offset) for offset in range(1, members)]
        for offset in range(1, members):
            add(got[offset - 1], offset, first, 0)
        return got

    got = [to_partner(blocks, offset) for offset in range(1, members)]
    first = got + parts[1:3]
    gate.append(got[0])
    add(blocks, 0, 0, 0)
    for offset in range(1, members):
        add(got[offset - 1], offset, 0, 0)
    last = list(got)
    if chips > 1:
        last = spread(after(parts[1], *last), 1)
        gate[:] = last
    if chips > 2:
        group = after(jnp.concatenate(parts[2:], axis=0), *last)
        spread(group, 2)
    return first, pieces, arrays


def add_wide(parts):
    total = wide(parts[0])
    for part in parts[1:]:
        total = total + wide(part)
    return total


def sum_members(made, ready, members):
    sums, seen = [], []
    for half in range(2):
        sent, kept = made[2 * half : 2 * half + 2]
        hops, keeps = xor_plan(members, 1 - half)
        count = kept.shape[0] // len(keeps)
        total = wide(kept[:count])
        if members == 4:
            got = to_partner(sent, hops[0])
            got = got if ready is None else after(got, ready)
            total = total + wide(got[:count])
            relay = (wide(kept[count:]) + wide(got[count:])).astype(low_type)
            second = to_partner(relay, keeps[1])
            seen.append(second)
            total = total + wide(second)
        else:
            for place, hop in enumerate(hops):
                total = total + wide(to_partner(sent[place * count : (place + 1) * count], hop))
        sums.append(total.astype(low_type).reshape(count, -1))
    return jnp.concatenate(sums, axis=0), seen


def sum_chips(rows, chip, chips):
    count = rows.shape[1] // chips

    def piece(offset):
        start = lax.rem(chip - offset + chips, chips) * count
        return lax.dynamic_slice_in_dim(rows, start, count, axis=1)

    return [piece(0)] + [to_chip(piece(offset), -offset) for offset in range(1, chips)]


def shards(
    tokens,
    cotangent,
    norm_gains,
    router,
    dense_weight,
    expert_weight,
    routes,
    assign,
    dense_order,
    expert_order,
    dense_moment,
    dense_second,
    dense_left,
    dense_right,
    expert_moment,
    expert_second,
    expert_left,
    expert_right,
    gains_moment,
    gains_second,
    router_moment,
    router_second,
):
    ctx_count = lax.axis_size("ctx")
    shard_count = lax.axis_size("shard")
    chips = ctx_count // 2
    micros, rows, width = tokens.shape
    slots = dense_weight.shape[0]
    span = rows // 2
    row_groups = width // BR
    q_groups = HEADS * HD // BC
    kv_groups = 2 * KVH * HD // BC

    expert_inverse = inverse_order(expert_order)
    ctx = lax.axis_index("ctx").astype(jnp.int32)
    me = jnp.stack([ctx, lax.axis_index("shard").astype(jnp.int32)])
    row_ids = jnp.arange(rows, dtype=jnp.int32)
    all_pos = assign[:, row_ids // span] * span + row_ids % span
    key_pos = all_pos.reshape(1, rows * ctx_count)
    rows_pos = all_pos[ctx].reshape(rows, 1)
    router_pad = jnp.pad(router.astype(low_type), ((0, 0), (0, LANES - shard_count)))

    far, pieces, arrays = gather_weights(dense_weight.astype(low_type), chips, shard_count)
    expert_low = after(expert_weight[0].astype(low_type), *far)
    expert_all = [lax.all_gather(expert_low[:, :UPPER], "ctx", axis=0, tiled=True)]

    lanes = jnp.arange(LANES, dtype=jnp.int32)
    hits = jnp.sum((routes[..., None] == lanes).astype(low_type), axis=2)
    cot_rows = jnp.concatenate([cotangent.astype(low_type), hits], axis=2)
    cot_rows = cot_rows.reshape(micros * rows, width + LANES)
    cot_rows = after(cot_rows, *arrays[::2])
    cot_parts = [to_partner(cot_rows, j) for j in range(shard_count)]

    here, expert_inverse, router_pad, key_pos, rows_pos = lax.optimization_barrier(
        (me, expert_inverse, router_pad, key_pos, rows_pos)
    )
    h1, *kv, w_in, w_out = project(
        pieces,
        arrays,
        chips,
        shard_count,
        slots,
        dense_order,
        here,
        [tokens[m] for m in range(micros)],
        norm_gains,
    )
    q = make_queries(h1, w_in, micros)
    h1_other = to_ctx(h1, 1)
    obs, logs, x2s, h2s = [], [], [], []
    kv = after(kv, expert_all[0])
    kv_all = []
    for m in range(micros):
        own = after(kv[m], kv_all, q, cot_parts[1:3]) if m else kv[m]
        kv_all.append(lax.all_gather(own, "ctx", axis=0, tiled=True))
    for m in range(micros):
        if m == micros - 1:
            lower = after(expert_low[:, UPPER:], kv_all[m], obs, cot_parts)
            expert_all.append(lax.all_gather(lower, "ctx", axis=0, tiled=True))
        query = after(q[m], *(cot_parts[1:3] if m == 0 else obs[m - 1 : m]))
        ob, log_total, x2, h2 = attend(
            query, kv_all[m], rows_pos, key_pos, tokens[m], norm_gains, w_out
        )
        obs.append(ob)
        logs.append(log_total)
        x2s.append(x2)
        h2s.append(h2)
    ob_others = [to_ctx(ob, 1) for ob in obs]

    h_parts = []
    for m in range(micros):
        own = h2s[m] if m == 0 else after(h2s[m], *h_parts[m - 1])
        h_parts.append([own] + [to_partner(own, j) for j in range(1, shard_count)])
    sent = []
    zs, dgs, dus, cs, xs = [], [], [], [], []
    for m in range(micros):
        here = after(me, h2s[-1], h1_other, *ob_others) if m == 0 else after(me, zs[-1])
        made = run_expert(m, expert_inverse, here, router_pad, h_parts[m], cot_parts, expert_all)
        sent.append(made[:shard_count])
        z, dg, du, c, x = made[shard_count:]
        zs.append(z)
        dgs.append(dg)
        dus.append(du)
        cs.append(c)
        xs.append(x)
    backs = [[to_partner(sent[m][j], j) for j in range(shard_count)] for m in range(micros)]

    expert_terms = outer_blocks(
        after(expert_inverse, *backs[0]), width, (0, 0, 1), [xs, cs], [dgs, dus, zs]
    )
    outs = produce(after(expert_inverse, *expert_terms), expert_all, zs, shard_count, width)
    arrived = [to_partner(outs[j], j) for j in range(min(3, shard_count))]
    dxs, das, dqs, stats = [], [], [], []
    dkv_terms = None
    for m in range(micros):
        here = after(me, outs, backs[-1]) if m == 0 else after(me, dqs[-1], arrived[1:])
        dx, da, do, stat = merge(
            here, x2s[m], cotangent[m], h2s[m], norm_gains, router_pad, w_out, backs[m]
        )
        dq, dkv_terms = attend_back(
            m, micros, q[m], kv_all[m], rows_pos, key_pos, obs[m], logs[m], do, dkv_terms
        )
        dxs.append(dx)
        das.append(da)
        dqs.append(dq)
        stats.append(stat)

    def other_core(parts):
        return [to_ctx(part, 1) for part in parts]

    da_others, dq_others = other_core(das), other_core(dqs)
    first_term = after(expert_terms[0], *backs[-1])
    expert_sums = [lax.psum_scatter(first_term, "ctx", scatter_dimension=0, tiled=True)]
    dkv = lax.psum_scatter(
        after(dkv_terms, expert_sums[0]), "ctx", scatter_dimension=0, tiled=True
    )
    early = gradient_pieces(
        shard_count,
        after(me, dkv_terms),
        [([h1, h1_other], dqs + dq_others), (das + da_others, obs + ob_others)],
        [q_groups, q_groups],
        False,
    )
    h1_turned = early[4]
    parts_back = query_back(after(w_in, early[0]), dqs)
    early_rows, early_seen = sum_members(early[:4], parts_back, shard_count)
    chip = ctx // 2
    early_parts = sum_chips(early_rows, chip, chips)
    late = gradient_pieces(
        shard_count,
        after(me, *early_seen),
        [([h1_turned], [dkv, to_ctx(dkv, 1)])],
        [kv_groups],
        True,
    )
    input_grad, gain_stat = input_back(
        after(tokens, late[0]), norm_gains, w_in, dxs, parts_back, dkv
    )
    late_rows, late_seen = sum_members(late[:4], (input_grad, early_parts), shard_count)
    late_term = after(expert_terms[1], dkv)
    expert_sums.append(lax.psum_scatter(late_term, "ctx", scatter_dimension=0, tiled=True))
    last_outs = after(list(outs), *late_seen)
    arrived += [to_partner(last_outs[j], j) for j in range(3, shard_count)]
    early_sum = add_wide(early_parts).astype(low_type)
    late_sum = add_wide(sum_chips(late_rows, chip, chips)).astype(low_type)
    all_sums = jnp.concatenate([early_sum, late_sum], axis=0)
    places = jnp.asarray(piece_places(row_groups, q_groups, kv_groups), jnp.int32)[dense_order]
    chosen = (places[:, None] == jnp.arange(all_sums.shape[0])[None, :]).astype(low_type)
    ordered = jnp.dot(chosen, all_sums, preferred_element_type=jnp.float32).astype(low_type)
    devices = ctx_count * shard_count
    piece_width = ordered.shape[1]
    experts_up = stats[0].shape[0] - 8
    stat_rows = add_wide(stats)
    stat_rows = jnp.concatenate(
        [stat_rows[:shard_count], gain_stat[:1], stat_rows[experts_up : experts_up + 1]], axis=0
    )
    stat_parts = stat_rows.astype(low_type).reshape(-1, piece_width)
    extra = stat_parts.shape[0]
    ordered = jnp.concatenate(
        [
            ordered.reshape(devices, slots, piece_width),
            jnp.broadcast_to(stat_parts, (devices, extra, piece_width)),
        ],
        axis=1,
    ).reshape(devices * 2, (slots + extra) * piece_width // 2)
    ordered = lax.all_to_all(ordered, ("ctx", "shard"), split_axis=0, concat_axis=0, tiled=True)
    ordered = ordered.reshape(devices, slots + extra, piece_width)
    stat_rows = jnp.sum(wide(ordered[:, slots:]), axis=0).reshape(shard_count + 2, width)
    ordered = ordered[:, :slots].reshape(
        chips, 2, shard_count, slots, BR // (shard_count * chips), LANES
    )
    dense_sum = ordered.transpose(3, 2, 0, 4, 1, 5).reshape(slots, BR, BC)
    router_grad = stat_rows[:shard_count].T
    gains_grad = stat_rows[shard_count:]

    expert_grad, expert_new, expert_moment_new, expert_second_new = rotate(
        expert_weight[0], expert_sums, expert_moment[0], expert_second[0], expert_left[0], expert_right[0]
    )
    dense_grad, dense_new, dense_moment_new, dense_second_new = rotate(
        dense_weight, [dense_sum], dense_moment, dense_second, dense_left, dense_right
    )
    outputs = []
    for m in range(micros):
        total = x2s[m]
        for part in after(arrived, dense_new, expert_new):
            total = total + wide(part[m * rows : (m + 1) * rows])
        outputs.append(total)

    gains_new, gains_moment_new, gains_second_new = adam(
        norm_gains, gains_grad, gains_moment, gains_second, gain_rate
    )
    router_new, router_moment_new, router_second_new = adam(
        router, router_grad, router_moment, router_second, rate
    )
    return (
        jnp.stack(outputs),
        input_grad,
        dense_grad,
        dense_new,
        dense_moment_new,
        dense_second_new,
        expert_grad[None],
        expert_new[None],
        expert_moment_new[None],
        expert_second_new[None],
        gains_grad,
        gains_new,
        gains_moment_new,
        gains_second_new,
        router_grad,
        router_new,
        router_moment_new,
        router_second_new,
    )


def solution(mesh):
    rows_spec = P("shard", "ctx", None)
    dense_spec = P(("ctx", "shard"), None, None)
    expert_spec = P("shard", "ctx", None, None)
    in_specs = (
        (rows_spec, rows_spec, P(), P(), dense_spec, expert_spec, rows_spec, P(), P(), P())
        + (dense_spec,) * 4
        + (expert_spec,) * 4
        + (P(),) * 4
    )
    out_specs = (rows_spec,) * 2 + (dense_spec,) * 4 + (expert_spec,) * 4 + (P(),) * 8
    return jax.shard_map(shards, mesh=mesh, in_specs=in_specs, out_specs=out_specs, check_vma=False)
```

```python
import functools

import jax
import jax.numpy as jnp
from jax import lax
from jax.experimental import pallas as pl
from jax.experimental.pallas import tpu as pltpu
from jax.sharding import PartitionSpec as P

HEADS = 24
KVH = 8
HD = 64
FF = 1024
BR = 192
BC = 256
LANES = 128
UPPER = 144

norm_eps = 1e-06
beta_one = 0.9
beta_two = 0.95
rate = 0.01
gain_rate = 0.5
adam_eps = 1e-08
masked_score = -1e30
low_type = jnp.bfloat16
MIB = 1 << 20
VMEM_LIMIT = 60 * MIB

NN = (((1,), (0,)), ((), ()))
NT = (((1,), (1,)), ((), ()))
TN = (((0,), (0,)), ((), ()))

in_vmem = pl.BlockSpec(memory_space=pltpu.VMEM)
in_smem = pl.BlockSpec(memory_space=pltpu.SMEM)
in_any = pl.BlockSpec(memory_space=pl.ANY)


def dot(left_side, right_side, dims=NN):
    return lax.dot_general(left_side, right_side, dims, preferred_element_type=jnp.float32)


def call(kernel, out_shapes, in_specs, out_specs, scratch, flops, moved):
    return pl.pallas_call(
        kernel,
        out_shape=out_shapes,
        in_specs=in_specs,
        out_specs=out_specs,
        scratch_shapes=scratch,
        compiler_params=pltpu.CompilerParams(vmem_limit_bytes=VMEM_LIMIT),
        cost_estimate=pl.CostEstimate(flops=flops, bytes_accessed=moved, transcendentals=0),
    )


def shaped(dims, kind):
    return jax.ShapeDtypeStruct(dims, kind)


def inverse_order(slot_order):
    count = slot_order.shape[0]
    numbers = jnp.arange(count, dtype=jnp.int32)
    return jnp.sum(
        jnp.where(slot_order[None, :] == numbers[:, None], numbers[None, :], 0), axis=1
    ).astype(jnp.int32)


def wait_bytes(landed, semaphore):
    pltpu.make_async_copy(landed, landed, semaphore).wait()


def unit_rows(rows, gain):
    inverse = lax.rsqrt(jnp.mean(rows * rows, axis=-1, keepdims=True) + norm_eps)
    return rows * inverse * gain, inverse


def unit_back(rows, gain, inverse, gradient):
    unit = rows * inverse
    scaled = gradient * gain
    inner = jnp.mean(scaled * unit, axis=-1, keepdims=True)
    return inverse * (scaled - unit * inner), jnp.sum(gradient * unit, axis=0, keepdims=True)


def lane_ids(dims):
    return lax.broadcasted_iota(jnp.int32, dims, len(dims) - 1)


def half_turn(tile):
    return pltpu.roll(tile, HD, 1)


def stack_heads(ref, pair, scale=None):
    base = pair * (3 * LANES)
    tiles = [
        ref[:, pl.ds(pl.multiple_of(base + LANES * t, LANES), LANES)].astype(jnp.float32)
        for t in range(3)
    ]
    if scale is not None:
        tiles = [t * scale for t in tiles]
    lower = lane_ids(tiles[0].shape) < HD
    first = [tiles[0], half_turn(tiles[0]), tiles[1]]
    second = [tiles[1], half_turn(tiles[2]), tiles[2]]
    return (
        jnp.concatenate([jnp.where(lower, t, 0.0) for t in first], axis=0),
        jnp.concatenate([jnp.where(lower, 0.0, t) for t in second], axis=0),
    )


def unstack_heads(ref, pair, first, second):
    rows = first.shape[0] // 3
    base = pair * (3 * LANES)
    lower = lane_ids((rows, LANES)) < HD
    tiles = (
        jnp.where(lower, first[:rows], half_turn(first[rows : 2 * rows])),
        jnp.where(lower, first[2 * rows :], second[:rows]),
        jnp.where(lower, half_turn(second[rows : 2 * rows]), second[2 * rows :]),
    )
    for t in range(3):
        ref[:, pl.ds(pl.multiple_of(base + LANES * t, LANES), LANES)] = tiles[t].astype(ref.dtype)


def project_kernel(
    pieces, chips, members, slots, all_groups, micros, order_ref, me_ref, *refs
):
    x_refs = refs[:micros]
    gain_ref = refs[micros]
    piece_refs = refs[micros + 1 : micros + 1 + len(pieces)]
    refs = refs[micros + 1 + len(pieces) :]
    h_ref = refs[0]
    kv_ref, win_ref, wout_ref, held, held_out, sems, out_sems = refs[1:]
    groups = held.shape[1] // BC
    kv_groups = kv_ref.shape[-1] // BC
    rows = x_refs[0].shape[0]
    ctx, shard = me_ref[0], me_ref[1]
    chip, core = lax.div(ctx, 2), lax.rem(ctx, 2)

    for ref, (other_core, offset, first, cut) in zip(piece_refs, pieces):

        @pl.loop(0, ref.shape[0])
        def _(i):
            source = lax.rem(chip - (first + lax.div(i, slots)) + chips, chips) * 2
            source = source + jnp.bitwise_xor(core, other_core)
            source = source * members + jnp.bitwise_xor(shard, offset)
            number = order_ref[source * slots + lax.rem(i, slots)]
            a, b = lax.div(number, all_groups), lax.rem(number, all_groups)
            down = pl.ds(pl.multiple_of(a * BR + cut, 32), ref.shape[1])

            @pl.when(b < groups)
            def _():
                across = pl.ds(pl.multiple_of(b * BC, BC), BC)
                pltpu.make_async_copy(ref.at[i], held.at[down, across], sems.at[b]).start()

            @pl.when(b >= groups)
            def _():
                across = pl.ds(pl.multiple_of((b - groups) * BC, BC), BC)
                pltpu.make_async_copy(ref.at[i], held_out.at[down, across], sems.at[groups]).start()

    for m in range(micros):
        h_ref[m * rows : (m + 1) * rows, :] = unit_rows(x_refs[m][...], gain_ref[0:1])[0].astype(
            low_type
        )
    q_groups = groups - kv_groups

    @pl.loop(0, groups)
    def _(b):
        across = pl.ds(pl.multiple_of(b * BC, BC), BC)
        wait_bytes(held.at[:, across], sems.at[b])

    wait_bytes(held_out, sems.at[groups])
    copies = [
        pltpu.make_async_copy(held, win_ref, out_sems.at[0]),
        pltpu.make_async_copy(held_out, wout_ref, out_sems.at[1]),
    ]
    for copy in copies:
        copy.start()

    @pl.loop(0, kv_groups)
    def _(b):
        across = pl.ds(pl.multiple_of((q_groups + b) * BC, BC), BC)
        made = dot(h_ref[...], held[:, across]).astype(low_type)
        kv_ref[:, pl.ds(pl.multiple_of(b * BC, BC), BC)] = made

    for copy in copies:
        copy.wait()


def project(pieces, arrays, chips, members, slots, order, me, xs, gains):
    micros = len(xs)
    rows, width = xs[0].shape
    in_width = (HEADS + 2 * KVH) * HD
    out_width = HEADS * HD
    kv_width = 2 * KVH * HD
    return call(
        functools.partial(
            project_kernel, pieces, chips, members, slots, (in_width + out_width) // BC, micros
        ),
        tuple(
            [shaped((micros * rows, width), low_type)]
            + [shaped((micros * rows, kv_width), low_type)]
            + [shaped((width, in_width), low_type), shaped((width, out_width), low_type)]
        ),
        [in_smem, in_smem] + [in_vmem] * (micros + 1) + [in_any] * len(arrays),
        (in_vmem, in_vmem, in_any, in_any),
        [
            pltpu.VMEM((width, in_width), low_type),
            pltpu.VMEM((width, out_width), low_type),
            pltpu.SemaphoreType.DMA((in_width // BC + 1,)),
            pltpu.SemaphoreType.DMA((2,)),
        ],
        2 * micros * rows * width * kv_width,
        4 * width * (in_width + out_width),
    )(order, me, *xs, gains, *arrays)


def query_kernel(h_ref, w_ref, *refs):
    q_refs = refs[:-2]
    held, sems = refs[-2:]
    groups = held.shape[1] // BC
    rows = q_refs[0].shape[0]

    def copy(b):
        across = pl.ds(pl.multiple_of(b * BC, BC), BC)
        return pltpu.make_async_copy(w_ref.at[:, across], held.at[:, across], sems.at[b])

    @pl.loop(0, groups)
    def _(b):
        copy(b).start()

    @pl.loop(0, groups)
    def _(b):
        copy(b).wait()
        across = pl.ds(pl.multiple_of(b * BC, BC), BC)
        made = dot(h_ref[...], held[:, across]).astype(low_type)
        for m, ref in enumerate(q_refs):
            ref[:, across] = made[m * rows : (m + 1) * rows]


def make_queries(h, w, micros):
    total, width = h.shape
    q_width = HEADS * HD
    return call(
        query_kernel,
        tuple([shaped((total // micros, q_width), low_type)] * micros),
        [in_vmem, in_any],
        tuple([in_vmem] * micros),
        [pltpu.VMEM((width, q_width), low_type), pltpu.SemaphoreType.DMA((q_width // BC,))],
        2 * total * width * q_width,
        2 * width * q_width,
    )(h, w)


def load_keys(kv_ref, micro, rows, held, sem):
    count = held.shape[0] // rows
    span = kv_ref.shape[0] // count

    @pl.loop(0, count)
    def _(i):
        pltpu.make_async_copy(
            kv_ref.at[pl.ds(pl.multiple_of(i * span + micro * rows, 16), rows)],
            held.at[pl.ds(pl.multiple_of(i * rows, 16), rows)],
            sem,
        ).start()


def attend_kernel(
    micro, q_ref, rpos_ref, kpos_ref, x_ref, gain_ref, w_ref, all_ref,
    ob_ref, log_ref, x2_ref, h2_ref, bias, kv_ref, held, sems,
):
    rows = q_ref.shape[0]
    load_keys(all_ref, micro, rows, kv_ref, sems.at[0])
    pltpu.make_async_copy(w_ref, held, sems.at[1]).start()
    bias[...] = jnp.where(kpos_ref[...] <= rpos_ref[...], 0.0, masked_score)
    log_ref[...] = jnp.zeros_like(log_ref)
    length = kv_ref.shape[0]
    wait_bytes(kv_ref, sems.at[0])

    @pl.loop(0, KVH // 2)
    def _(pair):
        lane = pl.multiple_of(pair * LANES, LANES)
        keys = kv_ref[:, pl.ds(lane, LANES)]
        values = kv_ref[:, pl.ds(pl.multiple_of(lane + KVH * HD, LANES), LANES)]
        stacked = stack_heads(q_ref, pair, HD**-0.5)
        mixed = []
        for part in range(2):
            scores = dot(stacked[part].astype(low_type), keys, NT)
            scores = (scores.reshape(3, rows, length) + bias[...][None]).reshape(3 * rows, length)
            largest = jnp.max(scores, axis=-1, keepdims=True)
            raised = jnp.exp(scores - largest)
            summed = jnp.sum(raised, axis=-1, keepdims=True)
            mixed.append(dot(raised.astype(low_type), values) / summed)
            log_ref[...] = jnp.where(
                lane_ids(log_ref.shape) == 2 * pair + part, largest + jnp.log(summed), log_ref[...]
            )
        unstack_heads(ob_ref, pair, mixed[0], mixed[1])

    wait_bytes(held, sems.at[1])
    for n in range(held.shape[0] // BC):
        cut = slice(n * BC, (n + 1) * BC)
        x2_ref[:, cut] = x_ref[:, cut] + dot(ob_ref[...], held[cut, :], NT)
    h2_ref[...] = unit_rows(x2_ref[...], gain_ref[1:2])[0].astype(low_type)


def attend(micro, q, kv, rows_pos, key_pos, x, gains, w):
    rows, width = q.shape
    length = key_pos.shape[1]
    model = x.shape[1]
    return call(
        functools.partial(attend_kernel, micro),
        (
            shaped((rows, width), low_type),
            shaped((3 * rows, LANES), jnp.float32),
            shaped((rows, model), jnp.float32),
            shaped((rows, model), low_type),
        ),
        [in_vmem] * 5 + [in_any] * 2,
        (in_vmem,) * 4,
        [
            pltpu.VMEM((rows, length), jnp.float32),
            pltpu.VMEM((length, kv.shape[1]), low_type),
            pltpu.VMEM((model, width), low_type),
            pltpu.SemaphoreType.DMA((2,)),
        ],
        16 * rows * length * width,
        8 * MIB,
    )(q, rows_pos, key_pos, x, gains, w, kv)


def router_parts(h2, router, experts):
    logits = dot(h2, router)
    logits = jnp.where(lane_ids(logits.shape) < experts, logits, masked_score)
    raised = jnp.exp(logits - jnp.max(logits, axis=-1, keepdims=True))
    return raised / jnp.sum(raised, axis=-1, keepdims=True)


def expert_kernel(sources, micro, order_ref, me_ref, router_ref, *refs):
    h_parts = refs[:sources]
    c_parts = refs[sources : 2 * sources]
    w_refs = refs[2 * sources : 2 * sources + 2]
    outs = refs[2 * sources + 2 :]
    back_refs = outs[:sources]
    z_ref, dg_ref, du_ref, cs, xs_ref = outs[sources : sources + 5]
    held, chance, load_sem, w_sems = outs[sources + 5 :]
    rows, width = h_parts[0].shape
    row_groups = width // BR
    col_groups = FF // BC
    for j in range(sources):
        pltpu.make_async_copy(h_parts[j], xs_ref.at[pl.ds(j * rows, rows)], load_sem.at[0]).start()
        pltpu.make_async_copy(
            c_parts[j].at[pl.ds(micro * rows, rows)], cs.at[pl.ds(j * rows, rows)], load_sem.at[1]
        ).start()
    for b in range(col_groups):

        @pl.loop(0, row_groups)
        def _(a):
            for k in range(3):
                slot = order_ref[(k * row_groups + a) * col_groups + b]
                for start, ref in zip((0, UPPER), w_refs):
                    down = pl.ds(pl.multiple_of(a * BR + start, 64), ref.shape[1])
                    pltpu.make_async_copy(
                        ref.at[slot], held.at[k, down, pl.ds(b * BC, BC)], w_sems.at[b]
                    ).start()

    wait_bytes(xs_ref, load_sem.at[0])
    wait_bytes(cs, load_sem.at[1])
    me = me_ref[1]
    probs = router_parts(xs_ref[...], router_ref[...], sources)
    hits = cs[:, width:].astype(jnp.float32)
    mine = lane_ids(hits.shape) == me
    hit = jnp.sum(jnp.where(mine, hits, 0.0), axis=-1, keepdims=True)
    weight = jnp.sum(jnp.where(mine, probs, 0.0), axis=-1, keepdims=True) * hit
    chance[...] = jnp.zeros_like(chance)

    @pl.loop(0, col_groups)
    def _(b):
        cut = pl.ds(pl.multiple_of(b * BC, BC), BC)
        wait_bytes(held.at[:, :, cut], w_sems.at[b])
        gate = dot(xs_ref[...], held[0, :, cut])
        up = dot(xs_ref[...], held[1, :, cut])
        down = dot(cs[:, :width], held[2, :, cut])
        sig = jax.nn.sigmoid(gate)
        act = gate * sig
        hidden = act * up
        chance[...] += jnp.sum(down * hidden, axis=-1, keepdims=True)
        z_ref[:, cut] = (hidden * weight).astype(low_type)
        down = down * weight
        dg_ref[:, cut] = (down * up * (sig + act * (1.0 - sig))).astype(low_type)
        du_ref[:, cut] = (down * act).astype(low_type)

    for n in range(width // BC):
        cut = slice(n * BC, (n + 1) * BC)
        back = dot(dg_ref[...], held[0, cut, :], NT) + dot(du_ref[...], held[1, cut, :], NT)
        for j in range(sources):
            back_refs[j][:, cut] = back[j * rows : (j + 1) * rows].astype(low_type)
    told = chance[...] * hit
    high_part = told.astype(low_type)
    low_part = (told - high_part.astype(jnp.float32)).astype(low_type)
    lanes = lane_ids((sources * rows, LANES))
    tail = jnp.where(lanes == 0, high_part, jnp.where(lanes == 1, low_part, jnp.zeros_like(low_part)))
    for j in range(sources):
        back_refs[j][:, width:] = tail[j * rows : (j + 1) * rows]


def run_expert(micro, order, me, router, h_parts, c_parts, ws):
    sources = len(h_parts)
    rows, width = h_parts[0].shape
    total = sources * rows
    return call(
        functools.partial(expert_kernel, sources, micro),
        tuple(
            [shaped((rows, width + LANES), low_type)] * sources
            + [shaped((total, FF), low_type)] * 3
            + [shaped((total, width + LANES), low_type), shaped((total, width), low_type)]
        ),
        [in_smem, in_smem, in_vmem] + [in_any] * (2 * sources + 2),
        tuple([in_vmem] * (sources + 5)),
        [
            pltpu.VMEM((3, width, FF), low_type),
            pltpu.VMEM((total, 1), jnp.float32),
            pltpu.SemaphoreType.DMA((2,)),
            pltpu.SemaphoreType.DMA((FF // BC,)),
        ],
        10 * total * width * FF,
        20 * MIB,
    )(order, me, router, *h_parts, *c_parts, *ws)


def produce_kernel(sources, order_ref, upper_ref, lower_ref, *refs):
    out_refs = refs[-3 - sources : -3]
    z_refs = refs[: -3 - sources]
    zs, held, sem = refs[-3:]
    width = held.shape[0]
    total = z_refs[0].shape[0]
    rows = total // sources
    row_groups, col_groups = width // BR, FF // BC

    @pl.loop(0, row_groups)
    def _(a):
        for b in range(col_groups):
            slot = order_ref[(2 * row_groups + a) * col_groups + b]
            for start, ref in zip((0, UPPER), (upper_ref, lower_ref)):
                down = pl.ds(pl.multiple_of(a * BR + start, 64), ref.shape[1])
                pltpu.make_async_copy(
                    ref.at[slot], held.at[down, pl.ds(b * BC, BC)], sem
                ).start()

    for m, z_ref in enumerate(z_refs):
        zs[m * total : (m + 1) * total] = z_ref[...]
    wait_bytes(held, sem)
    for n in range(width // BC):
        cut = slice(n * BC, (n + 1) * BC)
        made = dot(zs[...], held[cut, :], NT).astype(low_type)
        for m in range(len(z_refs)):
            for j in range(sources):
                start = m * total + j * rows
                out_refs[j][m * rows : (m + 1) * rows, cut] = made[start : start + rows]


def produce(order, ws, zs, sources, width):
    micros = len(zs)
    total = zs[0].shape[0]
    return call(
        functools.partial(produce_kernel, sources),
        tuple([shaped((micros * total // sources, width), low_type)] * sources),
        [in_smem, in_any, in_any] + [in_vmem] * micros,
        tuple([in_vmem] * sources),
        [
            pltpu.VMEM((micros * total, FF), low_type),
            pltpu.VMEM((width, FF), low_type),
            pltpu.SemaphoreType.DMA,
        ],
        2 * micros * total * width * FF,
        8 * MIB,
    )(order, *ws, *zs)


def outer_kernel(groups, col_groups, order_ref, *refs):
    micros = len(refs[:-5]) // (len(groups) + 2)
    lefts = [refs[i * micros : (i + 1) * micros] for i in range(2)]
    rights = [refs[(2 + i) * micros : (3 + i) * micros] for i in range(len(groups))]
    out_refs, (turned, stage, sems) = refs[-5:-3], refs[-3:]
    rows = rights[0][0].shape[0]
    width = turned.shape[1]
    span = 2 * BR
    for side in range(2):
        for m in range(micros):
            for r in range(0, rows, LANES):
                part = lefts[side][m][r : r + LANES, :width]
                turned[side, :, m * rows + r : m * rows + r + LANES] = part.T
    row_groups = width // BR
    steps = [(k, p) for k in range(len(groups)) for p in range(width // span)]
    for n, (k, p) in enumerate(steps):
        slot = n % 2
        if n >= 2:
            wait_bytes(stage.at[slot], sems.at[slot])
        cut = slice(p * span, (p + 1) * span)
        made = 0.0
        for m in range(micros):
            left = turned[groups[k], cut, m * rows : (m + 1) * rows]
            made = made + dot(left, rights[k][m][...])
        stage[slot] = made.astype(low_type)
        for half in range(2):
            for b in range(col_groups):
                number = (k * row_groups + 2 * p + half) * col_groups + b
                place = order_ref[number]
                for side in range(2):
                    pltpu.make_async_copy(
                        stage.at[
                            slot, pl.ds(half * BR, BR), pl.ds(b * BC + side * LANES, LANES)
                        ],
                        out_refs[side].at[place],
                        sems.at[slot],
                    ).start()
    for slot in range(2):
        wait_bytes(stage.at[slot], sems.at[slot])


def outer_blocks(order, width, groups, lefts, rights):
    flat = [part for group in lefts + rights for part in group]
    rows = sum(part.shape[0] for part in rights[0])
    cols = rights[0][0].shape[1]
    blocks = len(groups) * width * cols // (BR * BC)
    return call(
        functools.partial(outer_kernel, groups, cols // BC),
        (shaped((blocks, BR, LANES), low_type),) * 2,
        [in_smem] + [in_vmem] * len(flat),
        (in_any,) * 2,
        [
            pltpu.VMEM((2, width, rows), low_type),
            pltpu.VMEM((2, 2 * BR, cols), low_type),
            pltpu.SemaphoreType.DMA((2,)),
        ],
        2 * rows * blocks * BR * BC,
        blocks * BR * BC * 2 + sum(f.size * 2 for f in flat),
    )(order, *flat)


def xor_plan(members, offset):
    if members != 4:
        return list(range(1, members)), [0]
    first = 1 if offset % 2 else 2
    return [first, 3], [0, 3 - first]


def pieces_kernel(members, counts, cols, turned_first, me_ref, *refs):
    row_groups = 8
    lists = []
    for left_count, right_count in counts:
        lists.append((refs[:left_count], refs[left_count : left_count + right_count]))
        refs = refs[left_count + right_count :]
    outs, refs = refs[:4], refs[4:]
    extra = refs[0] if not turned_first else None
    turned, rights, stage, sems = refs[0 if turned_first else 1 :]
    ctx, shard = me_ref[0], me_ref[1]
    core = lax.rem(ctx, 2)
    total = turned.shape[2]
    row_groups = turned.shape[1] // BR
    base = 0
    for g, (_, parts) in enumerate(lists):
        start = 0
        for part in parts:
            count = part.shape[0]
            for b in range(cols[g]):
                lane = pl.multiple_of(b * BC + core * LANES, LANES)
                pltpu.make_async_copy(
                    part.at[:, pl.ds(lane, LANES)],
                    rights.at[pl.ds(start, count), pl.ds((base + b) * LANES, LANES)],
                    sems.at[g],
                ).start()
            start += count
        base += cols[g]
    for g, (parts, _) in enumerate(lists):
        if g == 0 and turned_first:
            turned[0] = parts[0][...]
            continue
        start = 0
        for part in parts:
            for r in range(0, part.shape[0], LANES):
                turned[g, :, start : start + LANES] = part[r : r + LANES, :].T
                start += LANES
    if extra is not None:
        extra[...] = turned[0]
    all_cols = sum(cols)
    half_blocks = row_groups // 2 * all_cols
    span = BR // members
    base = 0
    for g in range(len(lists)):
        wide_cols = cols[g] * LANES
        wait_bytes(rights.at[:, pl.ds(base * LANES, wide_cols)], sems.at[g])
        for a in range(row_groups):
            made = dot(
                turned[g, a * BR : (a + 1) * BR, :],
                rights[:, base * LANES : base * LANES + wide_cols],
            )
            stage[a % 2, :, :wide_cols] = made.astype(stage.dtype)
            half = a // (row_groups // 2)
            first = (a % (row_groups // 2)) * all_cols + base
            for out, hops in zip(outs[2 * half : 2 * half + 2], xor_plan(members, 1 - half)):
                for place, hop in enumerate(hops):
                    down = pl.multiple_of(jnp.bitwise_xor(shard, hop) * span, 16 if span % 16 == 0 else 8)
                    for b in range(cols[g]):
                        out[place * half_blocks + first + b] = stage[
                            a % 2, pl.ds(down, span), b * LANES : (b + 1) * LANES
                        ].astype(low_type)
        base += cols[g]


def gradient_pieces(members, me, groups, cols, turned_first):
    counts = tuple((len(left), len(right)) for left, right in groups)
    flat = [part for left, right in groups for part in left + right]
    total = sum(part.shape[0] for part in groups[0][1])
    width = groups[0][0][0].shape[0 if turned_first else 1]
    row_groups = width // BR
    half_blocks = row_groups // 2 * sum(cols)
    span = BR // members
    stage_type = jnp.float32 if span % 16 else low_type
    outs = []
    for half in range(2):
        for hops in xor_plan(members, 1 - half):
            outs.append(shaped((len(hops) * half_blocks, span, LANES), low_type))
    out_specs = [in_vmem] * 4
    if not turned_first:
        outs.append(shaped((width, total), low_type))
        out_specs.append(in_vmem)
    in_specs = [in_smem]
    for left, right in groups:
        in_specs += [in_vmem] * len(left) + [in_any] * len(right)
    return call(
        functools.partial(pieces_kernel, members, counts, tuple(cols), turned_first),
        tuple(outs),
        in_specs,
        tuple(out_specs),
        [
            pltpu.VMEM((len(groups), width, total), low_type),
            pltpu.VMEM((total, sum(cols) * LANES), low_type),
            pltpu.VMEM((2, BR, max(cols) * LANES), stage_type),
            pltpu.SemaphoreType.DMA((len(groups),)),
        ],
        2 * total * width * sum(cols) * LANES,
        16 * MIB,
    )(me, *flat)


def merge_kernel(
    sources, me_ref, x2_ref, cot_ref, h2_ref, gain_ref, router_ref, w_ref, *refs
):
    back_refs = refs[:sources]
    dx_ref, da_ref, do_ref, stat_ref, held, sem = refs[sources:]
    rows, width = x2_ref.shape
    pltpu.make_async_copy(w_ref, held, sem).start()
    lanes = lane_ids((rows, LANES))
    prob_grad = jnp.zeros((rows, LANES), jnp.float32)
    gathered = jnp.zeros((rows, width), jnp.float32)
    for j in range(sources):
        tail = back_refs[j][:, width:].astype(jnp.float32)
        told = jnp.sum(tail, axis=-1, keepdims=True)
        expert = jnp.bitwise_xor(me_ref[1], j)
        prob_grad = prob_grad + jnp.where(lanes == expert, told, 0.0)
        gathered = gathered + back_refs[j][:, :width].astype(jnp.float32)
    h2 = h2_ref[...]
    probs = router_parts(h2, router_ref[...], sources)
    logit_grad = probs * (prob_grad - jnp.sum(probs * prob_grad, axis=-1, keepdims=True))
    high_part = logit_grad.astype(low_type)
    low_part = (logit_grad - high_part.astype(jnp.float32)).astype(low_type)
    router_grad = dot(high_part, h2, TN) + dot(low_part, h2, TN)
    gathered = gathered + dot(high_part, router_ref[...], NT) + dot(low_part, router_ref[...], NT)
    x2 = x2_ref[...]
    inverse = lax.rsqrt(jnp.mean(x2 * x2, axis=-1, keepdims=True) + norm_eps)
    moe_grad, gain_grad = unit_back(x2, gain_ref[1:2], inverse, gathered)
    after = cot_ref[...] + moe_grad
    dx_ref[...] = after
    da_ref[...] = after.astype(low_type)
    experts_up = stat_ref.shape[0] - 8
    stat_ref[:experts_up] = router_grad[:experts_up]
    stat_ref[experts_up:] = jnp.broadcast_to(gain_grad, (8, width))
    wait_bytes(held, sem)
    for n in range(held.shape[1] // BC):
        cut = slice(n * BC, (n + 1) * BC)
        do_ref[:, cut] = dot(da_ref[...], held[:, cut]).astype(low_type)


def merge(me, x2, cot, h2, gains, router, w, backs):
    rows, width = x2.shape
    sources = len(backs)
    experts_up = -(-sources // 8) * 8
    return call(
        functools.partial(merge_kernel, sources),
        (
            shaped((rows, width), jnp.float32),
            shaped((rows, width), low_type),
            shaped((rows, HEADS * HD), low_type),
            shaped((experts_up + 8, width), jnp.float32),
        ),
        [in_smem] + [in_vmem] * 5 + [in_any] + [in_vmem] * sources,
        (in_vmem,) * 4,
        [pltpu.VMEM((width, HEADS * HD), low_type), pltpu.SemaphoreType.DMA],
        2 * rows * width * HEADS * HD,
        10 * MIB,
    )(me, x2, cot, h2, gains, router, w, *backs)


def attend_back_kernel(
    micro, q_ref, rpos_ref, kpos_ref, ob_ref, log_ref, do_ref, all_ref, *refs
):
    dq_ref, out_ref, bias, kv_ref, grad_ref, sems = refs[-6:]
    rows = q_ref.shape[0]
    load_keys(all_ref, micro, rows, kv_ref, sems.at[0])
    length = kv_ref.shape[0]
    bias[...] = jnp.where(kpos_ref[...] <= rpos_ref[...], 0.0, masked_score)
    wait_bytes(kv_ref, sems.at[0])

    @pl.loop(0, KVH // 2)
    def _(pair):
        lane = pl.multiple_of(pair * LANES, LANES)
        value_lane = pl.multiple_of(lane + KVH * HD, LANES)
        keys = kv_ref[:, pl.ds(lane, LANES)]
        values = kv_ref[:, pl.ds(value_lane, LANES)]
        queries = stack_heads(q_ref, pair, HD**-0.5)
        grads = stack_heads(do_ref, pair)
        mixes = stack_heads(ob_ref, pair)
        query_grads = []
        key_grad = value_grad = None
        for part in range(2):
            query = queries[part].astype(low_type)
            grad = grads[part].astype(low_type)
            log_total = jnp.sum(
                jnp.where(lane_ids(log_ref.shape) == 2 * pair + part, log_ref[...], 0.0),
                axis=-1,
                keepdims=True,
            )
            delta = jnp.sum(grads[part] * mixes[part], axis=-1, keepdims=True)
            scores = dot(query, keys, NT)
            scores = (scores.reshape(3, rows, length) + bias[...][None]).reshape(3 * rows, length)
            chance = jnp.exp(scores - log_total)
            prob_grad = dot(grad, values, NT)
            score_grad = (chance * (prob_grad - delta)).astype(low_type)
            value_term = dot(chance.astype(low_type), grad, TN)
            key_term = dot(score_grad, query, TN)
            key_grad = key_term if part == 0 else key_grad + key_term
            value_grad = value_term if part == 0 else value_grad + value_term
            query_grads.append(dot(score_grad, keys) * HD**-0.5)
        unstack_heads(dq_ref, pair, query_grads[0], query_grads[1])
        grad_ref[:, pl.ds(lane, LANES)] = key_grad.astype(low_type)
        grad_ref[:, pl.ds(value_lane, LANES)] = value_grad.astype(low_type)

    count = length // rows
    span = out_ref.shape[0] // count

    @pl.loop(0, count)
    def _(i):
        pltpu.make_async_copy(
            grad_ref.at[pl.ds(pl.multiple_of(i * rows, 16), rows)],
            out_ref.at[pl.ds(pl.multiple_of(i * span + micro * rows, 16), rows)],
            sems.at[1],
        ).start()

    wait_bytes(grad_ref, sems.at[1])


def attend_back(micro, q, kv, rows_pos, key_pos, ob, log_total, do, shared):
    rows, width = q.shape
    length = key_pos.shape[1]
    operands = [q, rows_pos, key_pos, ob, log_total, do, kv]
    in_specs = [in_vmem] * 6 + [in_any]
    aliases = {}
    if shared is not None:
        aliases = {len(operands): 1}
        operands.append(shared)
        in_specs.append(in_any)
    return pl.pallas_call(
        functools.partial(attend_back_kernel, micro),
        out_shape=(shaped((rows, width), low_type), shaped(kv.shape, low_type)),
        in_specs=in_specs,
        out_specs=(in_vmem, in_any),
        scratch_shapes=[
            pltpu.VMEM((rows, length), jnp.float32),
            pltpu.VMEM((length, kv.shape[1]), low_type),
            pltpu.VMEM((length, kv.shape[1]), low_type),
            pltpu.SemaphoreType.DMA((2,)),
        ],
        input_output_aliases=aliases,
        compiler_params=pltpu.CompilerParams(vmem_limit_bytes=VMEM_LIMIT),
        cost_estimate=pl.CostEstimate(
            flops=40 * rows * length * width, bytes_accessed=8 * MIB, transcendentals=0
        ),
    )(*operands)


def query_back_kernel(w_ref, *refs):
    micros = (len(refs) - 3) // 2
    dq_refs, out_refs = refs[:micros], refs[micros : 2 * micros]
    rows_ref, held, sem = refs[2 * micros :]
    rows = dq_refs[0].shape[0]
    copy = pltpu.make_async_copy(w_ref.at[:, pl.ds(0, held.shape[1])], held, sem)
    copy.start()
    for m in range(micros):
        rows_ref[m * rows : (m + 1) * rows] = dq_refs[m][...]
    copy.wait()
    for n in range(held.shape[0] // BC):
        cut = slice(n * BC, (n + 1) * BC)
        made = dot(rows_ref[...], held[cut, :], NT)
        for m in range(micros):
            out_refs[m][:, cut] = made[m * rows : (m + 1) * rows]


def query_back(w, dqs):
    micros = len(dqs)
    rows, q_width = dqs[0].shape
    width = w.shape[0]
    return call(
        query_back_kernel,
        tuple([shaped((rows, width), jnp.float32)] * micros),
        [in_any] + [in_vmem] * micros,
        tuple([in_vmem] * micros),
        [
            pltpu.VMEM((micros * rows, q_width), low_type),
            pltpu.VMEM((width, q_width), low_type),
            pltpu.SemaphoreType.DMA,
        ],
        2 * micros * rows * width * q_width,
        7 * MIB,
    )(w, *dqs)


def input_kernel(x_ref, gain_ref, w_ref, *refs):
    micros, rows = x_ref.shape[:2]
    dx_refs = refs[:micros]
    part_refs = refs[micros : 2 * micros]
    dkv_ref, out_ref, stat_ref, grad, held, sem = refs[2 * micros :]
    kv_width = held.shape[1]
    copy = pltpu.make_async_copy(
        w_ref.at[:, pl.ds(w_ref.shape[1] - kv_width, kv_width)], held, sem
    )
    copy.start()
    copy.wait()
    for n in range(held.shape[0] // BC):
        cut = slice(n * BC, (n + 1) * BC)
        made = dot(dkv_ref[...], held[cut, :], NT)
        for m in range(micros):
            grad[m, :, cut] = part_refs[m][:, cut] + made[m * rows : (m + 1) * rows]
    total = jnp.zeros((1, x_ref.shape[-1]), jnp.float32)
    for m in range(micros):
        x = x_ref[m]
        inverse = lax.rsqrt(jnp.mean(x * x, axis=-1, keepdims=True) + norm_eps)
        term, gain_grad = unit_back(x, gain_ref[0:1], inverse, grad[m])
        out_ref[m] = dx_refs[m][...] + term
        total = total + gain_grad
    stat_ref[...] = jnp.broadcast_to(total, stat_ref.shape)


def input_back(x, gains, w, dxs, parts, dkv):
    micros, rows, width = x.shape
    kv_width = dkv.shape[1]
    return call(
        input_kernel,
        (shaped(x.shape, jnp.float32), shaped((8, width), jnp.float32)),
        [in_vmem, in_vmem, in_any] + [in_vmem] * (2 * micros + 1),
        (in_vmem,) * 2,
        [
            pltpu.VMEM(x.shape, jnp.float32),
            pltpu.VMEM((width, kv_width), low_type),
            pltpu.SemaphoreType.DMA,
        ],
        2 * micros * rows * width * kv_width,
        14 * MIB,
    )(x, gains, w, *dxs, *parts, dkv)


def rotate_kernel(b_ref, m_ref, s_ref, l_ref, r_ref, *refs):
    grad_ref, new_ref, moment_ref, second_ref = refs[-4:]
    parts = [ref[0].astype(jnp.float32) for ref in refs[:-4]]
    gradient = parts[0] if len(parts) == 1 else jnp.concatenate(parts, axis=1)
    grad_ref[0] = gradient
    left = l_ref[0].astype(low_type)
    right = r_ref[0].astype(low_type)
    rotated = dot(dot(left, gradient.astype(low_type), TN).astype(low_type), right)
    moment = beta_one * m_ref[0] + (1.0 - beta_one) * rotated
    second = beta_two * s_ref[0] + (1.0 - beta_two) * rotated * rotated
    moment_ref[0] = moment
    second_ref[0] = second
    direction = (moment / (jnp.sqrt(second) + adam_eps)).astype(low_type)
    turned = dot(dot(left, direction).astype(low_type), right, NT)
    new_ref[0] = b_ref[0] - rate * turned


def rotate(weight, gradients, moment, second, left, right):
    count = weight.shape[0]

    def spec(rows, cols):
        return pl.BlockSpec((1, rows, cols), lambda i: (i, 0, 0))

    block = spec(BR, BC)
    return pl.pallas_call(
        rotate_kernel,
        grid=(count,),
        out_shape=(shaped(weight.shape, jnp.float32),) * 4,
        in_specs=[block] * 3
        + [spec(BR, BR), spec(BC, BC)]
        + [spec(BR, part.shape[2]) for part in gradients],
        out_specs=(block,) * 4,
        compiler_params=pltpu.CompilerParams(vmem_limit_bytes=VMEM_LIMIT),
        cost_estimate=pl.CostEstimate(
            flops=4 * count * BR * BC * (BR + BC),
            bytes_accessed=count * 2 * MIB,
            transcendentals=0,
        ),
    )(weight, moment, second, left, right, *gradients)


def adam(weight, gradient, moment, second, step_rate):
    moment_new = beta_one * moment + (1.0 - beta_one) * gradient
    second_new = beta_two * second + (1.0 - beta_two) * gradient * gradient
    return (
        weight - step_rate * moment_new / (jnp.sqrt(second_new) + adam_eps),
        moment_new,
        second_new,
    )


def piece_places(row_groups, q_groups, kv_groups):
    all_groups = 2 * q_groups + kv_groups
    out_groups = list(range(q_groups)) + list(range(q_groups + kv_groups, all_groups))
    numbers = [a * all_groups + b for a in range(row_groups) for b in out_groups]
    numbers += [a * all_groups + q_groups + b for a in range(row_groups) for b in range(kv_groups)]
    places = [0] * len(numbers)
    for place, number in enumerate(numbers):
        places[number] = place
    return places


def to_partner(array, offset):
    if offset == 0:
        return array
    count = lax.axis_size("shard")
    return lax.ppermute(array, "shard", [(i, i ^ offset) for i in range(count)])


def to_ctx(array, offset):
    count = lax.axis_size("ctx")
    return lax.ppermute(array, "ctx", [(i, i ^ offset) for i in range(count)])


def to_chip(array, offset):
    count = lax.axis_size("ctx")
    return lax.ppermute(array, "ctx", [(i, (i + 2 * offset) % count) for i in range(count)])


def after(value, *others):
    return lax.optimization_barrier((value, others))[0]


def from_chips(array, chips):
    return [array] + [to_chip(array, offset) for offset in range(1, chips)]


def wide(array):
    return array.astype(jnp.float32)


def sum_to_chips(parts):
    total = wide(parts[0])
    for offset in range(1, len(parts)):
        total = total + wide(to_chip(parts[offset], -offset))
    return total


def gather_weights(blocks, chips, members, small):
    parts = [blocks]
    for _ in range(chips - 1):
        parts.append(to_chip(parts[-1], 1))
    pieces, arrays = [], []
    gate = []

    def add(array, offset, first, cut):
        pieces.append((0, offset, first, cut))
        arrays.append(array)
        pieces.append((1, offset, first, cut))
        arrays.append(to_ctx(after(array, *gate), 1))
        return array

    def spread(group, first):
        add(group, 0, first, 0)
        if members == 4 and first > 0:
            by_one, by_two = to_partner(group, 1), to_partner(group, 2)
            add(by_one, 1, first, 0)
            add(by_two, 2, first, 0)
            half = BR // 2
            add(to_partner(by_one[:, :half], 2), 3, first, 0)
            add(to_partner(by_two[:, half:], 1), 3, first, half)
            return [by_one, by_two]
        got = [to_partner(group, offset) for offset in range(1, members)]
        for offset in range(1, members):
            add(got[offset - 1], offset, first, 0)
        return got

    got = [to_partner(blocks, offset) for offset in range(1, members)]
    first = got + parts[1:3]
    gate.append(got[0])
    add(blocks, 0, 0, 0)
    for offset in range(1, members):
        add(got[offset - 1], offset, 0, 0)
    last = list(got)
    if chips > 1:
        last = spread(after(parts[1], *last), 1)
        gate[:] = last
    if chips > 2:
        group = after(jnp.concatenate(parts[2:], axis=0), *last, *small)
        spread(group, 2)
    return first, pieces, arrays


def add_wide(parts):
    total = wide(parts[0])
    for part in parts[1:]:
        total = total + wide(part)
    return total


def sum_members(made, ready, members):
    sums, seen = [], []
    for half in range(2):
        sent, kept = made[2 * half : 2 * half + 2]
        hops, keeps = xor_plan(members, 1 - half)
        count = kept.shape[0] // len(keeps)
        total = wide(kept[:count])
        if members == 4:
            got = to_partner(sent, hops[0])
            got = got if ready is None else after(got, ready)
            total = total + wide(got[:count])
            relay = (wide(kept[count:]) + wide(got[count:])).astype(low_type)
            second = to_partner(relay, keeps[1])
            seen.append(second)
            total = total + wide(second)
        else:
            for place, hop in enumerate(hops):
                total = total + wide(to_partner(sent[place * count : (place + 1) * count], hop))
        sums.append(total.astype(low_type).reshape(count, -1))
    return jnp.concatenate(sums, axis=0), seen


def sum_chips(rows, chip, chips):
    count = rows.shape[1] // chips

    def piece(offset):
        start = lax.rem(chip - offset + chips, chips) * count
        return lax.dynamic_slice_in_dim(rows, start, count, axis=1)

    return [piece(0)] + [to_chip(piece(offset), -offset) for offset in range(1, chips)]


def shards(
    tokens,
    cotangent,
    norm_gains,
    router,
    dense_weight,
    expert_weight,
    routes,
    assign,
    dense_order,
    expert_order,
    dense_moment,
    dense_second,
    dense_left,
    dense_right,
    expert_moment,
    expert_second,
    expert_left,
    expert_right,
    gains_moment,
    gains_second,
    router_moment,
    router_second,
):
    ctx_count = lax.axis_size("ctx")
    shard_count = lax.axis_size("shard")
    chips = ctx_count // 2
    micros, rows, width = tokens.shape
    slots = dense_weight.shape[0]
    span = rows // 2
    row_groups = width // BR
    q_groups = HEADS * HD // BC
    kv_groups = 2 * KVH * HD // BC

    expert_inverse = inverse_order(expert_order)
    ctx = lax.axis_index("ctx").astype(jnp.int32)
    me = jnp.stack([ctx, lax.axis_index("shard").astype(jnp.int32)])
    row_ids = jnp.arange(rows, dtype=jnp.int32)
    all_pos = assign[:, row_ids // span] * span + row_ids % span
    key_pos = all_pos.reshape(1, rows * ctx_count)
    rows_pos = all_pos[ctx].reshape(rows, 1)
    router_pad = jnp.pad(router.astype(low_type), ((0, 0), (0, LANES - shard_count)))

    small = (me, expert_inverse, router_pad, key_pos, rows_pos)
    far, pieces, arrays = gather_weights(
        dense_weight.astype(low_type), chips, shard_count, small
    )
    expert_low = after(expert_weight[0].astype(low_type), *far)
    expert_all = [lax.all_gather(expert_low[:, :UPPER], "ctx", axis=0, tiled=True)]

    lanes = jnp.arange(LANES, dtype=jnp.int32)
    hits = jnp.sum((routes[..., None] == lanes).astype(low_type), axis=2)
    cot_rows = jnp.concatenate([cotangent.astype(low_type), hits], axis=2)
    cot_rows = cot_rows.reshape(micros * rows, width + LANES)
    cot_rows = after(cot_rows, *arrays[::2])
    cot_parts = [to_partner(cot_rows, j) for j in range(shard_count)]

    h1, kv, w_in, w_out = project(
        pieces,
        arrays,
        chips,
        shard_count,
        slots,
        dense_order,
        me,
        [tokens[m] for m in range(micros)],
        norm_gains,
    )
    q = make_queries(h1, w_in, micros)
    h1_other = to_ctx(h1, 1)
    obs, logs, x2s, h2s = [], [], [], []
    kv_all = lax.all_gather(after(kv, expert_all[0]), "ctx", axis=0, tiled=True)
    lower = after(expert_low[:, UPPER:], kv_all, q, cot_parts)
    expert_all.append(lax.all_gather(lower, "ctx", axis=0, tiled=True))
    for m in range(micros):
        query = after(q[m], *(cot_parts if m == 0 else obs[m - 1 : m]))
        ob, log_total, x2, h2 = attend(
            m, query, kv_all, rows_pos, key_pos, tokens[m], norm_gains, w_out
        )
        obs.append(ob)
        logs.append(log_total)
        x2s.append(x2)
        h2s.append(h2)
    ob_others = [to_ctx(ob, 1) for ob in obs]

    h_parts = []
    for m in range(micros):
        own = h2s[m] if m == 0 else after(h2s[m], *h_parts[m - 1])
        h_parts.append([own] + [to_partner(own, j) for j in range(1, shard_count)])
    sent = []
    zs, dgs, dus, cs, xs = [], [], [], [], []
    for m in range(micros):
        here = after(me, h2s[-1], h1_other, *ob_others) if m == 0 else after(me, zs[-1])
        made = run_expert(m, expert_inverse, here, router_pad, h_parts[m], cot_parts, expert_all)
        sent.append(made[:shard_count])
        z, dg, du, c, x = made[shard_count:]
        zs.append(z)
        dgs.append(dg)
        dus.append(du)
        cs.append(c)
        xs.append(x)
    backs = [[to_partner(sent[m][j], j) for j in range(shard_count)] for m in range(micros)]

    expert_terms = outer_blocks(
        after(expert_inverse, *backs[0]), width, (0, 0, 1), [xs, cs], [dgs, dus, zs]
    )
    outs = produce(after(expert_inverse, *expert_terms), expert_all, zs, shard_count, width)
    arrived = [to_partner(outs[j], j) for j in range(min(3, shard_count))]
    dxs, das, dqs, stats = [], [], [], []
    dkv_terms = None
    for m in range(micros):
        here = after(me, outs, backs[-1]) if m == 0 else after(me, dqs[-1], arrived[1:])
        dx, da, do, stat = merge(
            here, x2s[m], cotangent[m], h2s[m], norm_gains, router_pad, w_out, backs[m]
        )
        dq, dkv_terms = attend_back(
            m, q[m], kv_all, rows_pos, key_pos, obs[m], logs[m], do, dkv_terms
        )
        dxs.append(dx)
        das.append(da)
        dqs.append(dq)
        stats.append(stat)

    def other_core(parts):
        return [to_ctx(part, 1) for part in parts]

    da_others, dq_others = other_core(das), other_core(dqs)
    first_term = after(expert_terms[0], *backs[-1])
    expert_sums = [lax.psum_scatter(first_term, "ctx", scatter_dimension=0, tiled=True)]
    dkv = lax.psum_scatter(
        after(dkv_terms, expert_sums[0]), "ctx", scatter_dimension=0, tiled=True
    )
    early = gradient_pieces(
        shard_count,
        after(me, dkv_terms),
        [([h1, h1_other], dqs + dq_others), (das + da_others, obs + ob_others)],
        [q_groups, q_groups],
        False,
    )
    h1_turned = early[4]
    parts_back = query_back(after(w_in, early[0]), dqs)
    early_rows, early_seen = sum_members(early[:4], parts_back, shard_count)
    chip = ctx // 2
    early_parts = sum_chips(early_rows, chip, chips)
    late = gradient_pieces(
        shard_count,
        after(me, *early_seen),
        [([h1_turned], [dkv, to_ctx(dkv, 1)])],
        [kv_groups],
        True,
    )
    input_grad, gain_stat = input_back(
        after(tokens, late[0]), norm_gains, w_in, dxs, parts_back, dkv
    )
    late_rows, late_seen = sum_members(late[:4], (input_grad, early_parts), shard_count)
    late_term = after(expert_terms[1], dkv)
    expert_sums.append(lax.psum_scatter(late_term, "ctx", scatter_dimension=0, tiled=True))
    last_outs = after(list(outs), *late_seen)
    arrived += [to_partner(last_outs[j], j) for j in range(3, shard_count)]
    early_sum = add_wide(early_parts).astype(low_type)
    late_sum = add_wide(sum_chips(late_rows, chip, chips)).astype(low_type)
    all_sums = jnp.concatenate([early_sum, late_sum], axis=0)
    places = jnp.asarray(piece_places(row_groups, q_groups, kv_groups), jnp.int32)[dense_order]
    chosen = (places[:, None] == jnp.arange(all_sums.shape[0])[None, :]).astype(low_type)
    ordered = jnp.dot(chosen, all_sums, preferred_element_type=jnp.float32).astype(low_type)
    devices = ctx_count * shard_count
    piece_width = ordered.shape[1]
    experts_up = stats[0].shape[0] - 8
    stat_rows = add_wide(stats)
    stat_rows = jnp.concatenate(
        [stat_rows[:shard_count], gain_stat[:1], stat_rows[experts_up : experts_up + 1]], axis=0
    )
    stat_parts = stat_rows.astype(low_type).reshape(-1, piece_width)
    extra = stat_parts.shape[0]
    ordered = jnp.concatenate(
        [
            ordered.reshape(devices, slots, piece_width),
            jnp.broadcast_to(stat_parts, (devices, extra, piece_width)),
        ],
        axis=1,
    ).reshape(devices * 2, (slots + extra) * piece_width // 2)
    ordered = lax.all_to_all(ordered, ("ctx", "shard"), split_axis=0, concat_axis=0, tiled=True)
    expert_grad, expert_new, expert_moment_new, expert_second_new = rotate(
        expert_weight[0], expert_sums, expert_moment[0], expert_second[0], expert_left[0], expert_right[0]
    )
    ordered = after(ordered, expert_new).reshape(devices, slots + extra, piece_width)
    stat_rows = jnp.sum(wide(ordered[:, slots:]), axis=0).reshape(shard_count + 2, width)
    ordered = ordered[:, :slots].reshape(
        chips, 2, shard_count, slots, BR // (shard_count * chips), LANES
    )
    dense_sum = ordered.transpose(3, 2, 0, 4, 1, 5).reshape(slots, BR, BC)
    router_grad = stat_rows[:shard_count].T
    gains_grad = stat_rows[shard_count:]

    dense_grad, dense_new, dense_moment_new, dense_second_new = rotate(
        dense_weight, [dense_sum], dense_moment, dense_second, dense_left, dense_right
    )
    outputs = []
    for m in range(micros):
        total = x2s[m]
        for part in after(arrived, dense_new, expert_new):
            total = total + wide(part[m * rows : (m + 1) * rows])
        outputs.append(total)

    gains_new, gains_moment_new, gains_second_new = adam(
        norm_gains, gains_grad, gains_moment, gains_second, gain_rate
    )
    router_new, router_moment_new, router_second_new = adam(
        router, router_grad, router_moment, router_second, rate
    )
    return (
        jnp.stack(outputs),
        input_grad,
        dense_grad,
        dense_new,
        dense_moment_new,
        dense_second_new,
        expert_grad[None],
        expert_new[None],
        expert_moment_new[None],
        expert_second_new[None],
        gains_grad,
        gains_new,
        gains_moment_new,
        gains_second_new,
        router_grad,
        router_new,
        router_moment_new,
        router_second_new,
    )


def solution(mesh):
    rows_spec = P("shard", "ctx", None)
    dense_spec = P(("ctx", "shard"), None, None)
    expert_spec = P("shard", "ctx", None, None)
    in_specs = (
        (rows_spec, rows_spec, P(), P(), dense_spec, expert_spec, rows_spec, P(), P(), P())
        + (dense_spec,) * 4
        + (expert_spec,) * 4
        + (P(),) * 4
    )
    out_specs = (rows_spec,) * 2 + (dense_spec,) * 4 + (expert_spec,) * 4 + (P(),) * 8
    return jax.shard_map(shards, mesh=mesh, in_specs=in_specs, out_specs=out_specs, check_vma=False)
```

```python
import functools

import jax
import jax.numpy as jnp
from jax import lax
from jax.experimental import pallas as pl
from jax.experimental.pallas import tpu as pltpu
from jax.sharding import PartitionSpec as P

HEADS = 24
KVH = 8
HD = 64
FF = 1024
BR = 192
BC = 256
LANES = 128
UPPER = 128

norm_eps = 1e-06
beta_one = 0.9
beta_two = 0.95
rate = 0.01
gain_rate = 0.5
adam_eps = 1e-08
masked_score = -1e30
low_type = jnp.bfloat16
MIB = 1 << 20
VMEM_LIMIT = 60 * MIB

NN = (((1,), (0,)), ((), ()))
NT = (((1,), (1,)), ((), ()))
TN = (((0,), (0,)), ((), ()))

in_vmem = pl.BlockSpec(memory_space=pltpu.VMEM)
in_smem = pl.BlockSpec(memory_space=pltpu.SMEM)
in_any = pl.BlockSpec(memory_space=pl.ANY)


def dot(left_side, right_side, dims=NN):
    return lax.dot_general(left_side, right_side, dims, preferred_element_type=jnp.float32)


def call(kernel, out_shapes, in_specs, out_specs, scratch, flops, moved):
    return pl.pallas_call(
        kernel,
        out_shape=out_shapes,
        in_specs=in_specs,
        out_specs=out_specs,
        scratch_shapes=scratch,
        compiler_params=pltpu.CompilerParams(vmem_limit_bytes=VMEM_LIMIT),
        cost_estimate=pl.CostEstimate(flops=flops, bytes_accessed=moved, transcendentals=0),
    )


def shaped(dims, kind):
    return jax.ShapeDtypeStruct(dims, kind)


def inverse_order(slot_order):
    count = slot_order.shape[0]
    numbers = jnp.arange(count, dtype=jnp.int32)
    return jnp.sum(
        jnp.where(slot_order[None, :] == numbers[:, None], numbers[None, :], 0), axis=1
    ).astype(jnp.int32)


def wait_bytes(landed, semaphore):
    pltpu.make_async_copy(landed, landed, semaphore).wait()


def unit_rows(rows, gain):
    inverse = lax.rsqrt(jnp.mean(rows * rows, axis=-1, keepdims=True) + norm_eps)
    return rows * inverse * gain, inverse


def unit_back(rows, gain, inverse, gradient):
    unit = rows * inverse
    scaled = gradient * gain
    inner = jnp.mean(scaled * unit, axis=-1, keepdims=True)
    return inverse * (scaled - unit * inner), jnp.sum(gradient * unit, axis=0, keepdims=True)


def lane_ids(dims):
    return lax.broadcasted_iota(jnp.int32, dims, len(dims) - 1)


def half_turn(tile):
    return pltpu.roll(tile, HD, 1)


def stack_heads(ref, pair, scale=None):
    base = pair * (3 * LANES)
    tiles = [
        ref[:, pl.ds(pl.multiple_of(base + LANES * t, LANES), LANES)].astype(jnp.float32)
        for t in range(3)
    ]
    if scale is not None:
        tiles = [t * scale for t in tiles]
    lower = lane_ids(tiles[0].shape) < HD
    first = [tiles[0], half_turn(tiles[0]), tiles[1]]
    second = [tiles[1], half_turn(tiles[2]), tiles[2]]
    return (
        jnp.concatenate([jnp.where(lower, t, 0.0) for t in first], axis=0),
        jnp.concatenate([jnp.where(lower, 0.0, t) for t in second], axis=0),
    )


def unstack_heads(ref, pair, first, second):
    rows = first.shape[0] // 3
    base = pair * (3 * LANES)
    lower = lane_ids((rows, LANES)) < HD
    tiles = (
        jnp.where(lower, first[:rows], half_turn(first[rows : 2 * rows])),
        jnp.where(lower, first[2 * rows :], second[:rows]),
        jnp.where(lower, half_turn(second[rows : 2 * rows]), second[2 * rows :]),
    )
    for t in range(3):
        ref[:, pl.ds(pl.multiple_of(base + LANES * t, LANES), LANES)] = tiles[t].astype(ref.dtype)


def project_kernel(
    pieces, chips, members, slots, all_groups, micros, order_ref, me_ref, *refs
):
    x_refs = refs[:micros]
    gain_ref = refs[micros]
    piece_refs = refs[micros + 1 : micros + 1 + len(pieces)]
    refs = refs[micros + 1 + len(pieces) :]
    h_ref = refs[0]
    kv_ref, win_ref, wout_ref, held, held_out, sems, out_sems = refs[1:]
    groups = held.shape[1] // BC
    kv_groups = kv_ref.shape[-1] // BC
    rows = x_refs[0].shape[0]
    ctx, shard = me_ref[0], me_ref[1]
    chip, core = lax.div(ctx, 2), lax.rem(ctx, 2)

    for ref, (other_core, offset, first, cut) in zip(piece_refs, pieces):

        @pl.loop(0, ref.shape[0])
        def _(i):
            source = lax.rem(chip - (first + lax.div(i, slots)) + chips, chips) * 2
            source = source + jnp.bitwise_xor(core, other_core)
            source = source * members + jnp.bitwise_xor(shard, offset)
            number = order_ref[source * slots + lax.rem(i, slots)]
            a, b = lax.div(number, all_groups), lax.rem(number, all_groups)
            down = pl.ds(pl.multiple_of(a * BR + cut, 32), ref.shape[1])

            @pl.when(b < groups)
            def _():
                across = pl.ds(pl.multiple_of(b * BC, BC), BC)
                pltpu.make_async_copy(ref.at[i], held.at[down, across], sems.at[b]).start()

            @pl.when(b >= groups)
            def _():
                across = pl.ds(pl.multiple_of((b - groups) * BC, BC), BC)
                pltpu.make_async_copy(ref.at[i], held_out.at[down, across], sems.at[groups]).start()

    for m in range(micros):
        h_ref[m * rows : (m + 1) * rows, :] = unit_rows(x_refs[m][...], gain_ref[0:1])[0].astype(
            low_type
        )
    q_groups = groups - kv_groups

    @pl.loop(0, groups)
    def _(b):
        across = pl.ds(pl.multiple_of(b * BC, BC), BC)
        wait_bytes(held.at[:, across], sems.at[b])

    wait_bytes(held_out, sems.at[groups])
    copies = [
        pltpu.make_async_copy(held, win_ref, out_sems.at[0]),
        pltpu.make_async_copy(held_out, wout_ref, out_sems.at[1]),
    ]
    for copy in copies:
        copy.start()

    @pl.loop(0, kv_groups)
    def _(b):
        across = pl.ds(pl.multiple_of((q_groups + b) * BC, BC), BC)
        made = dot(h_ref[...], held[:, across]).astype(low_type)
        kv_ref[:, pl.ds(pl.multiple_of(b * BC, BC), BC)] = made

    for copy in copies:
        copy.wait()


def project(pieces, arrays, chips, members, slots, order, me, xs, gains):
    micros = len(xs)
    rows, width = xs[0].shape
    in_width = (HEADS + 2 * KVH) * HD
    out_width = HEADS * HD
    kv_width = 2 * KVH * HD
    return call(
        functools.partial(
            project_kernel, pieces, chips, members, slots, (in_width + out_width) // BC, micros
        ),
        tuple(
            [shaped((micros * rows, width), low_type)]
            + [shaped((micros * rows, kv_width), low_type)]
            + [shaped((width, in_width), low_type), shaped((width, out_width), low_type)]
        ),
        [in_smem, in_smem] + [in_vmem] * (micros + 1) + [in_any] * len(arrays),
        (in_vmem, in_vmem, in_any, in_any),
        [
            pltpu.VMEM((width, in_width), low_type),
            pltpu.VMEM((width, out_width), low_type),
            pltpu.SemaphoreType.DMA((in_width // BC + 1,)),
            pltpu.SemaphoreType.DMA((2,)),
        ],
        2 * micros * rows * width * kv_width,
        4 * width * (in_width + out_width),
    )(order, me, *xs, gains, *arrays)


def query_kernel(h_ref, w_ref, *refs):
    q_refs = refs[:-2]
    held, sems = refs[-2:]
    groups = held.shape[1] // BC
    rows = q_refs[0].shape[0]

    def copy(b):
        across = pl.ds(pl.multiple_of(b * BC, BC), BC)
        return pltpu.make_async_copy(w_ref.at[:, across], held.at[:, across], sems.at[b])

    @pl.loop(0, groups)
    def _(b):
        copy(b).start()

    @pl.loop(0, groups)
    def _(b):
        copy(b).wait()
        across = pl.ds(pl.multiple_of(b * BC, BC), BC)
        made = dot(h_ref[...], held[:, across]).astype(low_type)
        for m, ref in enumerate(q_refs):
            ref[:, across] = made[m * rows : (m + 1) * rows]


def make_queries(h, w, micros):
    total, width = h.shape
    q_width = HEADS * HD
    return call(
        query_kernel,
        tuple([shaped((total // micros, q_width), low_type)] * micros),
        [in_vmem, in_any],
        tuple([in_vmem] * micros),
        [pltpu.VMEM((width, q_width), low_type), pltpu.SemaphoreType.DMA((q_width // BC,))],
        2 * total * width * q_width,
        2 * width * q_width,
    )(h, w)


def load_keys(kv_ref, micro, rows, held, sem):
    count = held.shape[0] // rows
    span = kv_ref.shape[0] // count

    @pl.loop(0, count)
    def _(i):
        pltpu.make_async_copy(
            kv_ref.at[pl.ds(pl.multiple_of(i * span + micro * rows, 16), rows)],
            held.at[pl.ds(pl.multiple_of(i * rows, 16), rows)],
            sem,
        ).start()


def attend_kernel(
    micro, q_ref, rpos_ref, kpos_ref, x_ref, gain_ref, w_ref, all_ref,
    ob_ref, log_ref, x2_ref, h2_ref, bias, kv_ref, held, sems,
):
    rows = q_ref.shape[0]
    load_keys(all_ref, micro, rows, kv_ref, sems.at[0])
    pltpu.make_async_copy(w_ref, held, sems.at[1]).start()
    bias[...] = jnp.where(kpos_ref[...] <= rpos_ref[...], 0.0, masked_score)
    log_ref[...] = jnp.zeros_like(log_ref)
    length = kv_ref.shape[0]
    wait_bytes(kv_ref, sems.at[0])

    @pl.loop(0, KVH // 2)
    def _(pair):
        lane = pl.multiple_of(pair * LANES, LANES)
        keys = kv_ref[:, pl.ds(lane, LANES)]
        values = kv_ref[:, pl.ds(pl.multiple_of(lane + KVH * HD, LANES), LANES)]
        stacked = stack_heads(q_ref, pair, HD**-0.5)
        mixed = []
        for part in range(2):
            scores = dot(stacked[part].astype(low_type), keys, NT)
            scores = (scores.reshape(3, rows, length) + bias[...][None]).reshape(3 * rows, length)
            largest = jnp.max(scores, axis=-1, keepdims=True)
            raised = jnp.exp(scores - largest)
            summed = jnp.sum(raised, axis=-1, keepdims=True)
            mixed.append(dot(raised.astype(low_type), values) / summed)
            log_ref[...] = jnp.where(
                lane_ids(log_ref.shape) == 2 * pair + part, largest + jnp.log(summed), log_ref[...]
            )
        unstack_heads(ob_ref, pair, mixed[0], mixed[1])

    wait_bytes(held, sems.at[1])
    for n in range(held.shape[0] // BC):
        cut = slice(n * BC, (n + 1) * BC)
        x2_ref[:, cut] = x_ref[:, cut] + dot(ob_ref[...], held[cut, :], NT)
    h2_ref[...] = unit_rows(x2_ref[...], gain_ref[1:2])[0].astype(low_type)


def attend(micro, q, kv, rows_pos, key_pos, x, gains, w):
    rows, width = q.shape
    length = key_pos.shape[1]
    model = x.shape[1]
    return call(
        functools.partial(attend_kernel, micro),
        (
            shaped((rows, width), low_type),
            shaped((3 * rows, LANES), jnp.float32),
            shaped((rows, model), jnp.float32),
            shaped((rows, model), low_type),
        ),
        [in_vmem] * 5 + [in_any] * 2,
        (in_vmem,) * 4,
        [
            pltpu.VMEM((rows, length), jnp.float32),
            pltpu.VMEM((length, kv.shape[1]), low_type),
            pltpu.VMEM((model, width), low_type),
            pltpu.SemaphoreType.DMA((2,)),
        ],
        16 * rows * length * width,
        8 * MIB,
    )(q, rows_pos, key_pos, x, gains, w, kv)


def router_parts(h2, router, experts):
    logits = dot(h2, router)
    logits = jnp.where(lane_ids(logits.shape) < experts, logits, masked_score)
    raised = jnp.exp(logits - jnp.max(logits, axis=-1, keepdims=True))
    return raised / jnp.sum(raised, axis=-1, keepdims=True)


def expert_kernel(sources, micro, order_ref, me_ref, router_ref, *refs):
    h_parts = refs[:sources]
    c_parts = refs[sources : 2 * sources]
    w_refs = refs[2 * sources : 2 * sources + 2]
    outs = refs[2 * sources + 2 :]
    back_refs = outs[:sources]
    z_ref, dg_ref, du_ref, cs, xs_ref = outs[sources : sources + 5]
    held, chance, load_sem, w_sems = outs[sources + 5 :]
    rows, width = h_parts[0].shape
    row_groups = width // BR
    col_groups = FF // BC
    for j in range(sources):
        pltpu.make_async_copy(h_parts[j], xs_ref.at[pl.ds(j * rows, rows)], load_sem.at[0]).start()
        pltpu.make_async_copy(
            c_parts[j].at[pl.ds(micro * rows, rows)], cs.at[pl.ds(j * rows, rows)], load_sem.at[1]
        ).start()
    for b in range(col_groups):

        @pl.loop(0, row_groups)
        def _(a):
            for k in range(3):
                slot = order_ref[(k * row_groups + a) * col_groups + b]
                for start, ref in zip((0, UPPER), w_refs):
                    down = pl.ds(pl.multiple_of(a * BR + start, 64), ref.shape[1])
                    pltpu.make_async_copy(
                        ref.at[slot], held.at[k, down, pl.ds(b * BC, BC)], w_sems.at[b]
                    ).start()

    wait_bytes(xs_ref, load_sem.at[0])
    wait_bytes(cs, load_sem.at[1])
    me = me_ref[1]
    probs = router_parts(xs_ref[...], router_ref[...], sources)
    hits = cs[:, width:].astype(jnp.float32)
    mine = lane_ids(hits.shape) == me
    hit = jnp.sum(jnp.where(mine, hits, 0.0), axis=-1, keepdims=True)
    weight = jnp.sum(jnp.where(mine, probs, 0.0), axis=-1, keepdims=True) * hit
    chance[...] = jnp.zeros_like(chance)

    @pl.loop(0, col_groups)
    def _(b):
        cut = pl.ds(pl.multiple_of(b * BC, BC), BC)
        wait_bytes(held.at[:, :, cut], w_sems.at[b])
        gate = dot(xs_ref[...], held[0, :, cut])
        up = dot(xs_ref[...], held[1, :, cut])
        down = dot(cs[:, :width], held[2, :, cut])
        sig = jax.nn.sigmoid(gate)
        act = gate * sig
        hidden = act * up
        chance[...] += jnp.sum(down * hidden, axis=-1, keepdims=True)
        z_ref[:, cut] = (hidden * weight).astype(low_type)
        down = down * weight
        dg_ref[:, cut] = (down * up * (sig + act * (1.0 - sig))).astype(low_type)
        du_ref[:, cut] = (down * act).astype(low_type)

    for n in range(width // BC):
        cut = slice(n * BC, (n + 1) * BC)
        back = dot(dg_ref[...], held[0, cut, :], NT) + dot(du_ref[...], held[1, cut, :], NT)
        for j in range(sources):
            back_refs[j][:, cut] = back[j * rows : (j + 1) * rows].astype(low_type)
    told = chance[...] * hit
    high_part = told.astype(low_type)
    low_part = (told - high_part.astype(jnp.float32)).astype(low_type)
    lanes = lane_ids((sources * rows, LANES))
    tail = jnp.where(lanes == 0, high_part, jnp.where(lanes == 1, low_part, jnp.zeros_like(low_part)))
    for j in range(sources):
        back_refs[j][:, width:] = tail[j * rows : (j + 1) * rows]


def run_expert(micro, order, me, router, h_parts, c_parts, ws):
    sources = len(h_parts)
    rows, width = h_parts[0].shape
    total = sources * rows
    return call(
        functools.partial(expert_kernel, sources, micro),
        tuple(
            [shaped((rows, width + LANES), low_type)] * sources
            + [shaped((total, FF), low_type)] * 3
            + [shaped((total, width + LANES), low_type), shaped((total, width), low_type)]
        ),
        [in_smem, in_smem, in_vmem] + [in_any] * (2 * sources + 2),
        tuple([in_vmem] * (sources + 5)),
        [
            pltpu.VMEM((3, width, FF), low_type),
            pltpu.VMEM((total, 1), jnp.float32),
            pltpu.SemaphoreType.DMA((2,)),
            pltpu.SemaphoreType.DMA((FF // BC,)),
        ],
        10 * total * width * FF,
        20 * MIB,
    )(order, me, router, *h_parts, *c_parts, *ws)


def produce_kernel(sources, order_ref, upper_ref, lower_ref, *refs):
    out_refs = refs[-3 - sources : -3]
    z_refs = refs[: -3 - sources]
    zs, held, sem = refs[-3:]
    width = held.shape[0]
    total = z_refs[0].shape[0]
    rows = total // sources
    row_groups, col_groups = width // BR, FF // BC

    @pl.loop(0, row_groups)
    def _(a):
        for b in range(col_groups):
            slot = order_ref[(2 * row_groups + a) * col_groups + b]
            for start, ref in zip((0, UPPER), (upper_ref, lower_ref)):
                down = pl.ds(pl.multiple_of(a * BR + start, 64), ref.shape[1])
                pltpu.make_async_copy(
                    ref.at[slot], held.at[down, pl.ds(b * BC, BC)], sem
                ).start()

    for m, z_ref in enumerate(z_refs):
        zs[m * total : (m + 1) * total] = z_ref[...]
    wait_bytes(held, sem)
    for n in range(width // BC):
        cut = slice(n * BC, (n + 1) * BC)
        made = dot(zs[...], held[cut, :], NT).astype(low_type)
        for m in range(len(z_refs)):
            for j in range(sources):
                start = m * total + j * rows
                out_refs[j][m * rows : (m + 1) * rows, cut] = made[start : start + rows]


def produce(order, ws, zs, sources, width):
    micros = len(zs)
    total = zs[0].shape[0]
    return call(
        functools.partial(produce_kernel, sources),
        tuple([shaped((micros * total // sources, width), low_type)] * sources),
        [in_smem, in_any, in_any] + [in_vmem] * micros,
        tuple([in_vmem] * sources),
        [
            pltpu.VMEM((micros * total, FF), low_type),
            pltpu.VMEM((width, FF), low_type),
            pltpu.SemaphoreType.DMA,
        ],
        2 * micros * total * width * FF,
        8 * MIB,
    )(order, *ws, *zs)


def outer_kernel(groups, col_groups, order_ref, *refs):
    micros = len(refs[:-5]) // (len(groups) + 2)
    lefts = [refs[i * micros : (i + 1) * micros] for i in range(2)]
    rights = [refs[(2 + i) * micros : (3 + i) * micros] for i in range(len(groups))]
    out_refs, (turned, stage, sems) = refs[-5:-3], refs[-3:]
    rows = rights[0][0].shape[0]
    width = turned.shape[1]
    span = 2 * BR
    for side in range(2):
        for m in range(micros):
            for r in range(0, rows, LANES):
                part = lefts[side][m][r : r + LANES, :width]
                turned[side, :, m * rows + r : m * rows + r + LANES] = part.T
    row_groups = width // BR
    steps = [(k, p) for k in range(len(groups)) for p in range(width // span)]
    for n, (k, p) in enumerate(steps):
        slot = n % 2
        if n >= 2:
            wait_bytes(stage.at[slot], sems.at[slot])
        cut = slice(p * span, (p + 1) * span)
        made = 0.0
        for m in range(micros):
            left = turned[groups[k], cut, m * rows : (m + 1) * rows]
            made = made + dot(left, rights[k][m][...])
        stage[slot] = made.astype(low_type)
        for half in range(2):
            for b in range(col_groups):
                number = (k * row_groups + 2 * p + half) * col_groups + b
                place = order_ref[number]
                for side in range(2):
                    pltpu.make_async_copy(
                        stage.at[
                            slot, pl.ds(half * BR, BR), pl.ds(b * BC + side * LANES, LANES)
                        ],
                        out_refs[side].at[place],
                        sems.at[slot],
                    ).start()
    for slot in range(2):
        wait_bytes(stage.at[slot], sems.at[slot])


def outer_blocks(order, width, groups, lefts, rights):
    flat = [part for group in lefts + rights for part in group]
    rows = sum(part.shape[0] for part in rights[0])
    cols = rights[0][0].shape[1]
    blocks = len(groups) * width * cols // (BR * BC)
    return call(
        functools.partial(outer_kernel, groups, cols // BC),
        (shaped((blocks, BR, LANES), low_type),) * 2,
        [in_smem] + [in_vmem] * len(flat),
        (in_any,) * 2,
        [
            pltpu.VMEM((2, width, rows), low_type),
            pltpu.VMEM((2, 2 * BR, cols), low_type),
            pltpu.SemaphoreType.DMA((2,)),
        ],
        2 * rows * blocks * BR * BC,
        blocks * BR * BC * 2 + sum(f.size * 2 for f in flat),
    )(order, *flat)


def xor_plan(members, offset):
    if members != 4:
        return list(range(1, members)), [0]
    first = 1 if offset % 2 else 2
    return [first, 3], [0, 3 - first]


def pieces_kernel(members, counts, cols, turned_first, me_ref, *refs):
    lists = []
    for left_count, right_count in counts:
        lists.append((refs[:left_count], refs[left_count : left_count + right_count]))
        refs = refs[left_count + right_count :]
    stat_refs = refs[: len(refs) - 8] if turned_first else refs[: len(refs) - 10]
    refs = refs[len(stat_refs) :]
    outs, refs = refs[:4], refs[4:]
    extra = refs[0] if not turned_first else None
    turned, rights, stage, sems = refs[0 if turned_first else 1 :][:4]
    ctx, shard = me_ref[0], me_ref[1]
    core = lax.rem(ctx, 2)
    total = turned.shape[2]
    row_groups = turned.shape[1] // BR
    base = 0
    for g, (_, parts) in enumerate(lists):
        start = 0
        for part in parts:
            count = part.shape[0]
            for b in range(cols[g]):
                lane = pl.multiple_of(b * BC + core * LANES, LANES)
                pltpu.make_async_copy(
                    part.at[:, pl.ds(lane, LANES)],
                    rights.at[pl.ds(start, count), pl.ds((base + b) * LANES, LANES)],
                    sems.at[g],
                ).start()
            start += count
        base += cols[g]
    for g, (parts, _) in enumerate(lists):
        if g == 0 and turned_first:
            turned[0] = parts[0][...]
            continue
        start = 0
        for part in parts:
            for r in range(0, part.shape[0], LANES):
                turned[g, :, start : start + LANES] = part[r : r + LANES, :].T
                start += LANES
    if extra is not None:
        extra[...] = turned[0]
    all_cols = sum(cols)
    half_blocks = row_groups // 2 * all_cols
    counts = [half_blocks + (1 if stat_refs else 0), half_blocks]
    span = BR // members
    if stat_refs:
        block = refs[-1]
        block[...] = jnp.zeros_like(block)
        up = stat_refs[0].shape[0] - 8
        for r, row in enumerate(list(range(members)) + [up]):
            total_row = sum(ref[row : row + 1, :] for ref in stat_refs)
            for t in range(total_row.shape[1] // BC):
                place = r * (total_row.shape[1] // BC) + t
                block[place : place + 1, :] = total_row[:, t * BC : (t + 1) * BC]
        lane = pl.multiple_of(core * LANES, LANES)
        for out, hops in zip(outs[:2], xor_plan(members, 1)):
            for place, hop in enumerate(hops):
                down = pl.multiple_of(jnp.bitwise_xor(shard, hop) * span, 8)
                out[place * counts[0] + half_blocks] = block[
                    pl.ds(down, span), pl.ds(lane, LANES)
                ].astype(low_type)
    base = 0
    for g in range(len(lists)):
        wide_cols = cols[g] * LANES
        wait_bytes(rights.at[:, pl.ds(base * LANES, wide_cols)], sems.at[g])
        for a in range(row_groups):
            made = dot(
                turned[g, a * BR : (a + 1) * BR, :],
                rights[:, base * LANES : base * LANES + wide_cols],
            )
            stage[a % 2, :, :wide_cols] = made.astype(stage.dtype)
            half = a // (row_groups // 2)
            first = (a % (row_groups // 2)) * all_cols + base
            for out, hops in zip(outs[2 * half : 2 * half + 2], xor_plan(members, 1 - half)):
                for place, hop in enumerate(hops):
                    down = pl.multiple_of(jnp.bitwise_xor(shard, hop) * span, 16 if span % 16 == 0 else 8)
                    for b in range(cols[g]):
                        out[place * counts[half] + first + b] = stage[
                            a % 2, pl.ds(down, span), b * LANES : (b + 1) * LANES
                        ].astype(low_type)
        base += cols[g]


def gradient_pieces(members, me, groups, cols, turned_first, stats):
    counts = tuple((len(left), len(right)) for left, right in groups)
    flat = [part for left, right in groups for part in left + right]
    total = sum(part.shape[0] for part in groups[0][1])
    width = groups[0][0][0].shape[0 if turned_first else 1]
    row_groups = width // BR
    half_blocks = row_groups // 2 * sum(cols)
    span = BR // members
    stage_type = jnp.float32 if span % 16 else low_type
    outs = []
    for half in range(2):
        count = half_blocks + (1 if stats and half == 0 else 0)
        for hops in xor_plan(members, 1 - half):
            outs.append(shaped((len(hops) * count, span, LANES), low_type))
    out_specs = [in_vmem] * 4
    if not turned_first:
        outs.append(shaped((width, total), low_type))
        out_specs.append(in_vmem)
    in_specs = [in_smem]
    for left, right in groups:
        in_specs += [in_vmem] * len(left) + [in_any] * len(right)
    in_specs += [in_vmem] * len(stats)
    return call(
        functools.partial(pieces_kernel, members, counts, tuple(cols), turned_first),
        tuple(outs),
        in_specs,
        tuple(out_specs),
        [
            pltpu.VMEM((len(groups), width, total), low_type),
            pltpu.VMEM((total, sum(cols) * LANES), low_type),
            pltpu.VMEM((2, BR, max(cols) * LANES), stage_type),
            pltpu.SemaphoreType.DMA((len(groups),)),
        ]
        + ([pltpu.VMEM((BR, BC), jnp.float32)] if stats else []),
        2 * total * width * sum(cols) * LANES,
        16 * MIB,
    )(me, *flat, *stats)


def merge_kernel(
    sources, me_ref, x2_ref, cot_ref, h2_ref, gain_ref, router_ref, w_ref, *refs
):
    back_refs = refs[:sources]
    dx_ref, da_ref, do_ref, stat_ref, held, sem = refs[sources:]
    rows, width = x2_ref.shape
    pltpu.make_async_copy(w_ref, held, sem).start()
    lanes = lane_ids((rows, LANES))
    prob_grad = jnp.zeros((rows, LANES), jnp.float32)
    gathered = jnp.zeros((rows, width), jnp.float32)
    for j in range(sources):
        tail = back_refs[j][:, width:].astype(jnp.float32)
        told = jnp.sum(tail, axis=-1, keepdims=True)
        expert = jnp.bitwise_xor(me_ref[1], j)
        prob_grad = prob_grad + jnp.where(lanes == expert, told, 0.0)
        gathered = gathered + back_refs[j][:, :width].astype(jnp.float32)
    h2 = h2_ref[...]
    probs = router_parts(h2, router_ref[...], sources)
    logit_grad = probs * (prob_grad - jnp.sum(probs * prob_grad, axis=-1, keepdims=True))
    high_part = logit_grad.astype(low_type)
    low_part = (logit_grad - high_part.astype(jnp.float32)).astype(low_type)
    router_grad = dot(high_part, h2, TN) + dot(low_part, h2, TN)
    gathered = gathered + dot(high_part, router_ref[...], NT) + dot(low_part, router_ref[...], NT)
    x2 = x2_ref[...]
    inverse = lax.rsqrt(jnp.mean(x2 * x2, axis=-1, keepdims=True) + norm_eps)
    moe_grad, gain_grad = unit_back(x2, gain_ref[1:2], inverse, gathered)
    after = cot_ref[...] + moe_grad
    dx_ref[...] = after
    da_ref[...] = after.astype(low_type)
    experts_up = stat_ref.shape[0] - 8
    stat_ref[:experts_up] = router_grad[:experts_up]
    stat_ref[experts_up:] = jnp.broadcast_to(gain_grad, (8, width))
    wait_bytes(held, sem)
    for n in range(held.shape[1] // BC):
        cut = slice(n * BC, (n + 1) * BC)
        do_ref[:, cut] = dot(da_ref[...], held[:, cut]).astype(low_type)


def merge(me, x2, cot, h2, gains, router, w, backs):
    rows, width = x2.shape
    sources = len(backs)
    experts_up = -(-sources // 8) * 8
    return call(
        functools.partial(merge_kernel, sources),
        (
            shaped((rows, width), jnp.float32),
            shaped((rows, width), low_type),
            shaped((rows, HEADS * HD), low_type),
            shaped((experts_up + 8, width), jnp.float32),
        ),
        [in_smem] + [in_vmem] * 5 + [in_any] + [in_vmem] * sources,
        (in_vmem,) * 4,
        [pltpu.VMEM((width, HEADS * HD), low_type), pltpu.SemaphoreType.DMA],
        2 * rows * width * HEADS * HD,
        10 * MIB,
    )(me, x2, cot, h2, gains, router, w, *backs)


def attend_back_kernel(
    micro, q_ref, rpos_ref, kpos_ref, ob_ref, log_ref, do_ref, all_ref, *refs
):
    dq_ref, out_ref, bias, kv_ref, grad_ref, sems = refs[-6:]
    rows = q_ref.shape[0]
    load_keys(all_ref, micro, rows, kv_ref, sems.at[0])
    length = kv_ref.shape[0]
    bias[...] = jnp.where(kpos_ref[...] <= rpos_ref[...], 0.0, masked_score)
    wait_bytes(kv_ref, sems.at[0])

    @pl.loop(0, KVH // 2)
    def _(pair):
        lane = pl.multiple_of(pair * LANES, LANES)
        value_lane = pl.multiple_of(lane + KVH * HD, LANES)
        keys = kv_ref[:, pl.ds(lane, LANES)]
        values = kv_ref[:, pl.ds(value_lane, LANES)]
        queries = stack_heads(q_ref, pair, HD**-0.5)
        grads = stack_heads(do_ref, pair)
        mixes = stack_heads(ob_ref, pair)
        query_grads = []
        key_grad = value_grad = None
        for part in range(2):
            query = queries[part].astype(low_type)
            grad = grads[part].astype(low_type)
            log_total = jnp.sum(
                jnp.where(lane_ids(log_ref.shape) == 2 * pair + part, log_ref[...], 0.0),
                axis=-1,
                keepdims=True,
            )
            delta = jnp.sum(grads[part] * mixes[part], axis=-1, keepdims=True)
            scores = dot(query, keys, NT)
            scores = (scores.reshape(3, rows, length) + bias[...][None]).reshape(3 * rows, length)
            chance = jnp.exp(scores - log_total)
            prob_grad = dot(grad, values, NT)
            score_grad = (chance * (prob_grad - delta)).astype(low_type)
            value_term = dot(chance.astype(low_type), grad, TN)
            key_term = dot(score_grad, query, TN)
            key_grad = key_term if part == 0 else key_grad + key_term
            value_grad = value_term if part == 0 else value_grad + value_term
            query_grads.append(dot(score_grad, keys) * HD**-0.5)
        unstack_heads(dq_ref, pair, query_grads[0], query_grads[1])
        grad_ref[:, pl.ds(lane, LANES)] = key_grad.astype(low_type)
        grad_ref[:, pl.ds(value_lane, LANES)] = value_grad.astype(low_type)

    count = length // rows
    span = out_ref.shape[0] // count

    @pl.loop(0, count)
    def _(i):
        pltpu.make_async_copy(
            grad_ref.at[pl.ds(pl.multiple_of(i * rows, 16), rows)],
            out_ref.at[pl.ds(pl.multiple_of(i * span + micro * rows, 16), rows)],
            sems.at[1],
        ).start()

    wait_bytes(grad_ref, sems.at[1])


def attend_back(micro, q, kv, rows_pos, key_pos, ob, log_total, do, shared):
    rows, width = q.shape
    length = key_pos.shape[1]
    operands = [q, rows_pos, key_pos, ob, log_total, do, kv]
    in_specs = [in_vmem] * 6 + [in_any]
    aliases = {}
    if shared is not None:
        aliases = {len(operands): 1}
        operands.append(shared)
        in_specs.append(in_any)
    return pl.pallas_call(
        functools.partial(attend_back_kernel, micro),
        out_shape=(shaped((rows, width), low_type), shaped(kv.shape, low_type)),
        in_specs=in_specs,
        out_specs=(in_vmem, in_any),
        scratch_shapes=[
            pltpu.VMEM((rows, length), jnp.float32),
            pltpu.VMEM((length, kv.shape[1]), low_type),
            pltpu.VMEM((length, kv.shape[1]), low_type),
            pltpu.SemaphoreType.DMA((2,)),
        ],
        input_output_aliases=aliases,
        compiler_params=pltpu.CompilerParams(vmem_limit_bytes=VMEM_LIMIT),
        cost_estimate=pl.CostEstimate(
            flops=40 * rows * length * width, bytes_accessed=8 * MIB, transcendentals=0
        ),
    )(*operands)


def query_back_kernel(w_ref, *refs):
    micros = (len(refs) - 3) // 2
    dq_refs, out_refs = refs[:micros], refs[micros : 2 * micros]
    rows_ref, held, sem = refs[2 * micros :]
    rows = dq_refs[0].shape[0]
    copy = pltpu.make_async_copy(w_ref.at[:, pl.ds(0, held.shape[1])], held, sem)
    copy.start()
    for m in range(micros):
        rows_ref[m * rows : (m + 1) * rows] = dq_refs[m][...]
    copy.wait()
    for n in range(held.shape[0] // BC):
        cut = slice(n * BC, (n + 1) * BC)
        made = dot(rows_ref[...], held[cut, :], NT)
        for m in range(micros):
            out_refs[m][:, cut] = made[m * rows : (m + 1) * rows]


def query_back(w, dqs):
    micros = len(dqs)
    rows, q_width = dqs[0].shape
    width = w.shape[0]
    return call(
        query_back_kernel,
        tuple([shaped((rows, width), jnp.float32)] * micros),
        [in_any] + [in_vmem] * micros,
        tuple([in_vmem] * micros),
        [
            pltpu.VMEM((micros * rows, q_width), low_type),
            pltpu.VMEM((width, q_width), low_type),
            pltpu.SemaphoreType.DMA,
        ],
        2 * micros * rows * width * q_width,
        7 * MIB,
    )(w, *dqs)


def input_kernel(x_ref, gain_ref, w_ref, *refs):
    micros, rows = x_ref.shape[:2]
    dx_refs = refs[:micros]
    part_refs = refs[micros : 2 * micros]
    dkv_ref, out_ref, stat_ref, grad, held, sem = refs[2 * micros :]
    kv_width = held.shape[1]
    copy = pltpu.make_async_copy(
        w_ref.at[:, pl.ds(w_ref.shape[1] - kv_width, kv_width)], held, sem
    )
    copy.start()
    copy.wait()
    for n in range(held.shape[0] // BC):
        cut = slice(n * BC, (n + 1) * BC)
        made = dot(dkv_ref[...], held[cut, :], NT)
        for m in range(micros):
            grad[m, :, cut] = part_refs[m][:, cut] + made[m * rows : (m + 1) * rows]
    total = jnp.zeros((1, x_ref.shape[-1]), jnp.float32)
    for m in range(micros):
        x = x_ref[m]
        inverse = lax.rsqrt(jnp.mean(x * x, axis=-1, keepdims=True) + norm_eps)
        term, gain_grad = unit_back(x, gain_ref[0:1], inverse, grad[m])
        out_ref[m] = dx_refs[m][...] + term
        total = total + gain_grad
    stat_ref[...] = jnp.broadcast_to(total, stat_ref.shape)


def input_back(x, gains, w, dxs, parts, dkv):
    micros, rows, width = x.shape
    kv_width = dkv.shape[1]
    return call(
        input_kernel,
        (shaped(x.shape, jnp.float32), shaped((8, width), jnp.float32)),
        [in_vmem, in_vmem, in_any] + [in_vmem] * (2 * micros + 1),
        (in_vmem,) * 2,
        [
            pltpu.VMEM(x.shape, jnp.float32),
            pltpu.VMEM((width, kv_width), low_type),
            pltpu.SemaphoreType.DMA,
        ],
        2 * micros * rows * width * kv_width,
        14 * MIB,
    )(x, gains, w, *dxs, *parts, dkv)


def rotate_kernel(b_ref, m_ref, s_ref, l_ref, r_ref, *refs):
    grad_ref, new_ref, moment_ref, second_ref = refs[-4:]
    parts = [ref[0].astype(jnp.float32) for ref in refs[:-4]]
    gradient = parts[0] if len(parts) == 1 else jnp.concatenate(parts, axis=1)
    grad_ref[0] = gradient
    left = l_ref[0].astype(low_type)
    right = r_ref[0].astype(low_type)
    rotated = dot(dot(left, gradient.astype(low_type), TN).astype(low_type), right)
    moment = beta_one * m_ref[0] + (1.0 - beta_one) * rotated
    second = beta_two * s_ref[0] + (1.0 - beta_two) * rotated * rotated
    moment_ref[0] = moment
    second_ref[0] = second
    direction = (moment / (jnp.sqrt(second) + adam_eps)).astype(low_type)
    turned = dot(dot(left, direction).astype(low_type), right, NT)
    new_ref[0] = b_ref[0] - rate * turned


def rotate(weight, gradients, moment, second, left, right):
    count = weight.shape[0]

    def spec(rows, cols):
        return pl.BlockSpec((1, rows, cols), lambda i: (i, 0, 0))

    block = spec(BR, BC)
    return pl.pallas_call(
        rotate_kernel,
        grid=(count,),
        out_shape=(shaped(weight.shape, jnp.float32),) * 4,
        in_specs=[block] * 3
        + [spec(BR, BR), spec(BC, BC)]
        + [spec(BR, part.shape[2]) for part in gradients],
        out_specs=(block,) * 4,
        compiler_params=pltpu.CompilerParams(vmem_limit_bytes=VMEM_LIMIT),
        cost_estimate=pl.CostEstimate(
            flops=4 * count * BR * BC * (BR + BC),
            bytes_accessed=count * 2 * MIB,
            transcendentals=0,
        ),
    )(weight, moment, second, left, right, *gradients)


def adam(weight, gradient, moment, second, step_rate):
    moment_new = beta_one * moment + (1.0 - beta_one) * gradient
    second_new = beta_two * second + (1.0 - beta_two) * gradient * gradient
    return (
        weight - step_rate * moment_new / (jnp.sqrt(second_new) + adam_eps),
        moment_new,
        second_new,
    )


def piece_places(row_groups, q_groups, kv_groups):
    all_groups = 2 * q_groups + kv_groups
    out_groups = list(range(q_groups)) + list(range(q_groups + kv_groups, all_groups))
    half = row_groups // 2
    numbers = [a * all_groups + b for a in range(half) for b in out_groups] + [None]
    numbers += [a * all_groups + b for a in range(half, row_groups) for b in out_groups]
    numbers += [a * all_groups + q_groups + b for a in range(row_groups) for b in range(kv_groups)]
    places = [0] * (len(numbers) - 1)
    for place, number in enumerate(numbers):
        if number is not None:
            places[number] = place
    return places


def to_partner(array, offset):
    if offset == 0:
        return array
    count = lax.axis_size("shard")
    return lax.ppermute(array, "shard", [(i, i ^ offset) for i in range(count)])


def to_ctx(array, offset):
    count = lax.axis_size("ctx")
    return lax.ppermute(array, "ctx", [(i, i ^ offset) for i in range(count)])


def to_chip(array, offset):
    count = lax.axis_size("ctx")
    return lax.ppermute(array, "ctx", [(i, (i + 2 * offset) % count) for i in range(count)])


def after(value, *others):
    return lax.optimization_barrier((value, others))[0]


def from_chips(array, chips):
    return [array] + [to_chip(array, offset) for offset in range(1, chips)]


def wide(array):
    return array.astype(jnp.float32)


def sum_to_chips(parts):
    total = wide(parts[0])
    for offset in range(1, len(parts)):
        total = total + wide(to_chip(parts[offset], -offset))
    return total


def gather_weights(blocks, chips, members, small):
    parts = [blocks]
    for _ in range(chips - 1):
        parts.append(to_chip(parts[-1], 1))
    pieces, arrays = [], []
    gate = []

    def add(array, offset, first, cut):
        pieces.append((0, offset, first, cut))
        arrays.append(array)
        pieces.append((1, offset, first, cut))
        arrays.append(to_ctx(after(array, *gate), 1))
        return array

    def spread(group, first):
        add(group, 0, first, 0)
        if members == 4 and first > 0:
            by_one, by_two = to_partner(group, 1), to_partner(group, 2)
            add(by_one, 1, first, 0)
            add(by_two, 2, first, 0)
            half = BR // 2
            add(to_partner(by_one[:, :half], 2), 3, first, 0)
            add(to_partner(by_two[:, half:], 1), 3, first, half)
            return [by_one, by_two]
        got = [to_partner(group, offset) for offset in range(1, members)]
        for offset in range(1, members):
            add(got[offset - 1], offset, first, 0)
        return got

    got = [to_partner(blocks, offset) for offset in range(1, members)]
    first = got + parts[1:3]
    gate.append(got[0])
    add(blocks, 0, 0, 0)
    for offset in range(1, members):
        add(got[offset - 1], offset, 0, 0)
    last = list(got)
    if chips > 1:
        last = spread(after(parts[1], *last), 1)
        gate[:] = last
    if chips > 2:
        group = after(jnp.concatenate(parts[2:], axis=0), *last, *small)
        spread(group, 2)
    return first, pieces, arrays


def add_wide(parts):
    total = wide(parts[0])
    for part in parts[1:]:
        total = total + wide(part)
    return total


def sum_members(made, ready, members):
    sums, seen = [], []
    for half in range(2):
        sent, kept = made[2 * half : 2 * half + 2]
        hops, keeps = xor_plan(members, 1 - half)
        count = kept.shape[0] // len(keeps)
        total = wide(kept[:count])
        if members == 4:
            got = to_partner(sent, hops[0])
            got = got if ready is None else after(got, ready)
            total = total + wide(got[:count])
            relay = (wide(kept[count:]) + wide(got[count:])).astype(low_type)
            second = to_partner(relay, keeps[1])
            seen.append(second)
            total = total + wide(second)
        else:
            for place, hop in enumerate(hops):
                total = total + wide(to_partner(sent[place * count : (place + 1) * count], hop))
        sums.append(total.astype(low_type).reshape(count, -1))
    return jnp.concatenate(sums, axis=0), seen


def sum_chips(rows, chip, chips):
    count = rows.shape[1] // chips

    def piece(offset):
        start = lax.rem(chip - offset + chips, chips) * count
        return lax.dynamic_slice_in_dim(rows, start, count, axis=1)

    return [piece(0)] + [to_chip(piece(offset), -offset) for offset in range(1, chips)]


def shards(
    tokens,
    cotangent,
    norm_gains,
    router,
    dense_weight,
    expert_weight,
    routes,
    assign,
    dense_order,
    expert_order,
    dense_moment,
    dense_second,
    dense_left,
    dense_right,
    expert_moment,
    expert_second,
    expert_left,
    expert_right,
    gains_moment,
    gains_second,
    router_moment,
    router_second,
):
    ctx_count = lax.axis_size("ctx")
    shard_count = lax.axis_size("shard")
    chips = ctx_count // 2
    micros, rows, width = tokens.shape
    slots = dense_weight.shape[0]
    span = rows // 2
    row_groups = width // BR
    q_groups = HEADS * HD // BC
    kv_groups = 2 * KVH * HD // BC

    expert_inverse = inverse_order(expert_order)
    ctx = lax.axis_index("ctx").astype(jnp.int32)
    me = jnp.stack([ctx, lax.axis_index("shard").astype(jnp.int32)])
    row_ids = jnp.arange(rows, dtype=jnp.int32)
    all_pos = assign[:, row_ids // span] * span + row_ids % span
    key_pos = all_pos.reshape(1, rows * ctx_count)
    rows_pos = all_pos[ctx].reshape(rows, 1)
    router_pad = jnp.pad(router.astype(low_type), ((0, 0), (0, LANES - shard_count)))

    small = (me, expert_inverse, router_pad, key_pos, rows_pos)
    far, pieces, arrays = gather_weights(
        dense_weight.astype(low_type), chips, shard_count, small
    )
    expert_low = after(expert_weight[0].astype(low_type), *far)
    expert_all = [lax.all_gather(expert_low[:, :UPPER], "ctx", axis=0, tiled=True)]

    lanes = jnp.arange(LANES, dtype=jnp.int32)
    hits = jnp.sum((routes[..., None] == lanes).astype(low_type), axis=2)
    cot_rows = jnp.concatenate([cotangent.astype(low_type), hits], axis=2)
    cot_rows = cot_rows.reshape(micros * rows, width + LANES)
    cot_rows = after(cot_rows, *arrays[::2])
    cot_parts = [to_partner(cot_rows, j) for j in range(shard_count)]

    h1, kv, w_in, w_out = project(
        pieces,
        arrays,
        chips,
        shard_count,
        slots,
        dense_order,
        me,
        [tokens[m] for m in range(micros)],
        norm_gains,
    )
    q = make_queries(h1, w_in, micros)
    h1_other = to_ctx(h1, 1)
    obs, logs, x2s, h2s = [], [], [], []
    kv_all = lax.all_gather(after(kv, expert_all[0]), "ctx", axis=0, tiled=True)
    lower = after(expert_low[:, UPPER:], kv_all, q, cot_parts)
    expert_all.append(lax.all_gather(lower, "ctx", axis=0, tiled=True))
    for m in range(micros):
        query = after(q[m], *(cot_parts if m == 0 else obs[m - 1 : m]))
        ob, log_total, x2, h2 = attend(
            m, query, kv_all, rows_pos, key_pos, tokens[m], norm_gains, w_out
        )
        obs.append(ob)
        logs.append(log_total)
        x2s.append(x2)
        h2s.append(h2)
    ob_others = [to_ctx(ob, 1) for ob in obs]

    h_parts = []
    for m in range(micros):
        own = h2s[m] if m == 0 else after(h2s[m], *h_parts[m - 1])
        h_parts.append([own] + [to_partner(own, j) for j in range(1, shard_count)])
    sent = []
    zs, dgs, dus, cs, xs = [], [], [], [], []
    for m in range(micros):
        here = after(me, h2s[-1], h1_other, *ob_others) if m == 0 else after(me, zs[-1])
        made = run_expert(m, expert_inverse, here, router_pad, h_parts[m], cot_parts, expert_all)
        sent.append(made[:shard_count])
        z, dg, du, c, x = made[shard_count:]
        zs.append(z)
        dgs.append(dg)
        dus.append(du)
        cs.append(c)
        xs.append(x)
    backs = [[to_partner(sent[m][j], j) for j in range(shard_count)] for m in range(micros)]

    expert_terms = outer_blocks(
        after(expert_inverse, *backs[0]), width, (0, 0, 1), [xs, cs], [dgs, dus, zs]
    )
    outs = produce(after(expert_inverse, *expert_terms), expert_all, zs, shard_count, width)
    arrived = [to_partner(outs[j], j) for j in range(min(3, shard_count))]
    dxs, das, dqs, stats = [], [], [], []
    dkv_terms = None
    for m in range(micros):
        here = after(me, outs, backs[-1]) if m == 0 else after(me, dqs[-1], arrived[1:])
        dx, da, do, stat = merge(
            here, x2s[m], cotangent[m], h2s[m], norm_gains, router_pad, w_out, backs[m]
        )
        dq, dkv_terms = attend_back(
            m, q[m], kv_all, rows_pos, key_pos, obs[m], logs[m], do, dkv_terms
        )
        dxs.append(dx)
        das.append(da)
        dqs.append(dq)
        stats.append(stat)

    def other_core(parts):
        return [to_ctx(part, 1) for part in parts]

    da_others, dq_others = other_core(das), other_core(dqs)
    first_term = after(expert_terms[0], *backs[-1])
    expert_sums = [lax.psum_scatter(first_term, "ctx", scatter_dimension=0, tiled=True)]
    dkv = lax.psum_scatter(
        after(dkv_terms, expert_sums[0]), "ctx", scatter_dimension=0, tiled=True
    )
    stat_sum = add_wide(stats)
    early = gradient_pieces(
        shard_count,
        after(me, dkv_terms),
        [([h1, h1_other], dqs + dq_others), (das + da_others, obs + ob_others)],
        [q_groups, q_groups],
        False,
        [stat_sum, to_ctx(stat_sum, 1)],
    )
    h1_turned = early[4]
    parts_back = query_back(after(w_in, early[0]), dqs)
    early_rows, early_seen = sum_members(early[:4], parts_back, shard_count)
    chip = ctx // 2
    early_parts = sum_chips(early_rows, chip, chips)
    late = gradient_pieces(
        shard_count,
        after(me, *early_seen),
        [([h1_turned], [dkv, to_ctx(dkv, 1)])],
        [kv_groups],
        True,
        [],
    )
    input_grad, gain_stat = input_back(
        after(tokens, late[0]), norm_gains, w_in, dxs, parts_back, dkv
    )
    late_rows, late_seen = sum_members(late[:4], (input_grad, early_parts), shard_count)
    late_term = after(expert_terms[1], dkv, early_seen)
    expert_sums.append(lax.psum_scatter(late_term, "ctx", scatter_dimension=0, tiled=True))
    last_outs = after(list(outs), *late_seen)
    arrived += [to_partner(last_outs[j], j) for j in range(3, shard_count)]
    early_sum = add_wide(early_parts).astype(low_type)
    expert_grad, expert_new, expert_moment_new, expert_second_new = rotate(
        expert_weight[0], expert_sums, expert_moment[0], expert_second[0], expert_left[0], expert_right[0]
    )
    late_parts = after(sum_chips(late_rows, chip, chips), expert_new)
    late_sum = add_wide(late_parts).astype(low_type)
    all_sums = jnp.concatenate([early_sum, late_sum], axis=0)
    places = jnp.asarray(piece_places(row_groups, q_groups, kv_groups), jnp.int32)[dense_order]
    chosen = (places[:, None] == jnp.arange(all_sums.shape[0])[None, :]).astype(low_type)
    ordered = jnp.dot(chosen, all_sums, preferred_element_type=jnp.float32).astype(low_type)
    devices = ctx_count * shard_count
    piece_width = ordered.shape[1]
    stat_place = row_groups // 2 * 2 * q_groups
    gain_parts = gain_stat[:1].astype(low_type).reshape(-1, piece_width)
    stat_parts = jnp.concatenate([early_sum[stat_place : stat_place + 1], gain_parts], axis=0)
    extra = stat_parts.shape[0]
    ordered = jnp.concatenate(
        [
            ordered.reshape(devices, slots, piece_width),
            jnp.broadcast_to(stat_parts, (devices, extra, piece_width)),
        ],
        axis=1,
    ).reshape(devices * 2, (slots + extra) * piece_width // 2)
    ordered = lax.all_to_all(ordered, ("ctx", "shard"), split_axis=0, concat_axis=0, tiled=True)
    ordered = ordered.reshape(devices, slots + extra, piece_width)
    span = BR // (shard_count * chips)
    stat_block = ordered[:, slots].reshape(chips, 2, shard_count, span, LANES)
    stat_rows = wide(stat_block.transpose(2, 0, 3, 1, 4).reshape(BR * BC)[: (shard_count + 1) * width])
    stat_rows = stat_rows.reshape(shard_count + 1, width)
    gain_row = jnp.sum(wide(ordered[:, slots + 1 :]), axis=0).reshape(width)
    ordered = ordered[:, :slots].reshape(
        chips, 2, shard_count, slots, BR // (shard_count * chips), LANES
    )
    dense_sum = ordered.transpose(3, 2, 0, 4, 1, 5).reshape(slots, BR, BC)
    router_grad = stat_rows[:shard_count].T
    gains_grad = jnp.stack([gain_row, stat_rows[shard_count]])

    dense_grad, dense_new, dense_moment_new, dense_second_new = rotate(
        dense_weight, [dense_sum], dense_moment, dense_second, dense_left, dense_right
    )
    outputs = []
    for m in range(micros):
        total = x2s[m]
        for part in after(arrived, expert_new):
            total = total + wide(part[m * rows : (m + 1) * rows])
        outputs.append(total)

    gains_new, gains_moment_new, gains_second_new = adam(
        norm_gains, gains_grad, gains_moment, gains_second, gain_rate
    )
    router_new, router_moment_new, router_second_new = adam(
        router, router_grad, router_moment, router_second, rate
    )
    return (
        jnp.stack(outputs),
        input_grad,
        dense_grad,
        dense_new,
        dense_moment_new,
        dense_second_new,
        expert_grad[None],
        expert_new[None],
        expert_moment_new[None],
        expert_second_new[None],
        gains_grad,
        gains_new,
        gains_moment_new,
        gains_second_new,
        router_grad,
        router_new,
        router_moment_new,
        router_second_new,
    )


def solution(mesh):
    rows_spec = P("shard", "ctx", None)
    dense_spec = P(("ctx", "shard"), None, None)
    expert_spec = P("shard", "ctx", None, None)
    in_specs = (
        (rows_spec, rows_spec, P(), P(), dense_spec, expert_spec, rows_spec, P(), P(), P())
        + (dense_spec,) * 4
        + (expert_spec,) * 4
        + (P(),) * 4
    )
    out_specs = (rows_spec,) * 2 + (dense_spec,) * 4 + (expert_spec,) * 4 + (P(),) * 8
    return jax.shard_map(shards, mesh=mesh, in_specs=in_specs, out_specs=out_specs, check_vma=False)
```

```python
import functools

import jax
import jax.numpy as jnp
from jax import lax
from jax.experimental import pallas as pl
from jax.experimental.pallas import tpu as pltpu
from jax.sharding import PartitionSpec as P

HEADS = 24
KVH = 8
HD = 64
FF = 1024
BR = 192
BC = 256
LANES = 128
UPPER = 128

norm_eps = 1e-06
beta_one = 0.9
beta_two = 0.95
rate = 0.01
gain_rate = 0.5
adam_eps = 1e-08
masked_score = -1e30
low_type = jnp.bfloat16
MIB = 1 << 20
VMEM_LIMIT = 60 * MIB

NN = (((1,), (0,)), ((), ()))
NT = (((1,), (1,)), ((), ()))
TN = (((0,), (0,)), ((), ()))

in_vmem = pl.BlockSpec(memory_space=pltpu.VMEM)
in_smem = pl.BlockSpec(memory_space=pltpu.SMEM)
in_any = pl.BlockSpec(memory_space=pl.ANY)


def dot(left_side, right_side, dims=NN):
    return lax.dot_general(left_side, right_side, dims, preferred_element_type=jnp.float32)


def call(kernel, out_shapes, in_specs, out_specs, scratch, flops, moved):
    return pl.pallas_call(
        kernel,
        out_shape=out_shapes,
        in_specs=in_specs,
        out_specs=out_specs,
        scratch_shapes=scratch,
        compiler_params=pltpu.CompilerParams(vmem_limit_bytes=VMEM_LIMIT),
        cost_estimate=pl.CostEstimate(flops=flops, bytes_accessed=moved, transcendentals=0),
    )


def shaped(dims, kind):
    return jax.ShapeDtypeStruct(dims, kind)


def inverse_order(slot_order):
    count = slot_order.shape[0]
    numbers = jnp.arange(count, dtype=jnp.int32)
    return jnp.sum(
        jnp.where(slot_order[None, :] == numbers[:, None], numbers[None, :], 0), axis=1
    ).astype(jnp.int32)


def wait_bytes(landed, semaphore):
    pltpu.make_async_copy(landed, landed, semaphore).wait()


def unit_rows(rows, gain):
    inverse = lax.rsqrt(jnp.mean(rows * rows, axis=-1, keepdims=True) + norm_eps)
    return rows * inverse * gain, inverse


def unit_back(rows, gain, inverse, gradient):
    unit = rows * inverse
    scaled = gradient * gain
    inner = jnp.mean(scaled * unit, axis=-1, keepdims=True)
    return inverse * (scaled - unit * inner), jnp.sum(gradient * unit, axis=0, keepdims=True)


def lane_ids(dims):
    return lax.broadcasted_iota(jnp.int32, dims, len(dims) - 1)


def half_turn(tile):
    return pltpu.roll(tile, HD, 1)


def stack_heads(ref, pair, scale=None):
    base = pair * (3 * LANES)
    tiles = [
        ref[:, pl.ds(pl.multiple_of(base + LANES * t, LANES), LANES)].astype(jnp.float32)
        for t in range(3)
    ]
    if scale is not None:
        tiles = [t * scale for t in tiles]
    lower = lane_ids(tiles[0].shape) < HD
    first = [tiles[0], half_turn(tiles[0]), tiles[1]]
    second = [tiles[1], half_turn(tiles[2]), tiles[2]]
    return (
        jnp.concatenate([jnp.where(lower, t, 0.0) for t in first], axis=0),
        jnp.concatenate([jnp.where(lower, 0.0, t) for t in second], axis=0),
    )


def unstack_heads(ref, pair, first, second):
    rows = first.shape[0] // 3
    base = pair * (3 * LANES)
    lower = lane_ids((rows, LANES)) < HD
    tiles = (
        jnp.where(lower, first[:rows], half_turn(first[rows : 2 * rows])),
        jnp.where(lower, first[2 * rows :], second[:rows]),
        jnp.where(lower, half_turn(second[rows : 2 * rows]), second[2 * rows :]),
    )
    for t in range(3):
        ref[:, pl.ds(pl.multiple_of(base + LANES * t, LANES), LANES)] = tiles[t].astype(ref.dtype)


def project_kernel(
    pieces, chips, members, slots, all_groups, micros, order_ref, me_ref, *refs
):
    x_refs = refs[:micros]
    gain_ref = refs[micros]
    piece_refs = refs[micros + 1 : micros + 1 + len(pieces)]
    refs = refs[micros + 1 + len(pieces) :]
    h_ref = refs[0]
    kv_ref, win_ref, wout_ref, held, held_out, sems, out_sems = refs[1:]
    groups = held.shape[1] // BC
    kv_groups = kv_ref.shape[-1] // BC
    rows = x_refs[0].shape[0]
    ctx, shard = me_ref[0], me_ref[1]
    chip, core = lax.div(ctx, 2), lax.rem(ctx, 2)

    for ref, (other_core, offset, first, cut) in zip(piece_refs, pieces):

        @pl.loop(0, ref.shape[0])
        def _(i):
            source = lax.rem(chip - (first + lax.div(i, slots)) + chips, chips) * 2
            source = source + jnp.bitwise_xor(core, other_core)
            source = source * members + jnp.bitwise_xor(shard, offset)
            number = order_ref[source * slots + lax.rem(i, slots)]
            a, b = lax.div(number, all_groups), lax.rem(number, all_groups)
            down = pl.ds(pl.multiple_of(a * BR + cut, 32), ref.shape[1])

            @pl.when(b < groups)
            def _():
                across = pl.ds(pl.multiple_of(b * BC, BC), BC)
                pltpu.make_async_copy(ref.at[i], held.at[down, across], sems.at[b]).start()

            @pl.when(b >= groups)
            def _():
                across = pl.ds(pl.multiple_of((b - groups) * BC, BC), BC)
                pltpu.make_async_copy(ref.at[i], held_out.at[down, across], sems.at[groups]).start()

    for m in range(micros):
        h_ref[m * rows : (m + 1) * rows, :] = unit_rows(x_refs[m][...], gain_ref[0:1])[0].astype(
            low_type
        )
    q_groups = groups - kv_groups

    @pl.loop(0, groups)
    def _(b):
        across = pl.ds(pl.multiple_of(b * BC, BC), BC)
        wait_bytes(held.at[:, across], sems.at[b])

    wait_bytes(held_out, sems.at[groups])
    copies = [
        pltpu.make_async_copy(held, win_ref, out_sems.at[0]),
        pltpu.make_async_copy(held_out, wout_ref, out_sems.at[1]),
    ]
    for copy in copies:
        copy.start()

    @pl.loop(0, kv_groups)
    def _(b):
        across = pl.ds(pl.multiple_of((q_groups + b) * BC, BC), BC)
        made = dot(h_ref[...], held[:, across]).astype(low_type)
        kv_ref[:, pl.ds(pl.multiple_of(b * BC, BC), BC)] = made

    for copy in copies:
        copy.wait()


def project(pieces, arrays, chips, members, slots, order, me, xs, gains):
    micros = len(xs)
    rows, width = xs[0].shape
    in_width = (HEADS + 2 * KVH) * HD
    out_width = HEADS * HD
    kv_width = 2 * KVH * HD
    return call(
        functools.partial(
            project_kernel, pieces, chips, members, slots, (in_width + out_width) // BC, micros
        ),
        tuple(
            [shaped((micros * rows, width), low_type)]
            + [shaped((micros * rows, kv_width), low_type)]
            + [shaped((width, in_width), low_type), shaped((width, out_width), low_type)]
        ),
        [in_smem, in_smem] + [in_vmem] * (micros + 1) + [in_any] * len(arrays),
        (in_vmem, in_vmem, in_any, in_any),
        [
            pltpu.VMEM((width, in_width), low_type),
            pltpu.VMEM((width, out_width), low_type),
            pltpu.SemaphoreType.DMA((in_width // BC + 1,)),
            pltpu.SemaphoreType.DMA((2,)),
        ],
        2 * micros * rows * width * kv_width,
        4 * width * (in_width + out_width),
    )(order, me, *xs, gains, *arrays)


def query_kernel(h_ref, w_ref, *refs):
    q_refs = refs[:-2]
    held, sems = refs[-2:]
    groups = held.shape[1] // BC
    rows = q_refs[0].shape[0]

    def copy(b):
        across = pl.ds(pl.multiple_of(b * BC, BC), BC)
        return pltpu.make_async_copy(w_ref.at[:, across], held.at[:, across], sems.at[b])

    @pl.loop(0, groups)
    def _(b):
        copy(b).start()

    @pl.loop(0, groups)
    def _(b):
        copy(b).wait()
        across = pl.ds(pl.multiple_of(b * BC, BC), BC)
        made = dot(h_ref[...], held[:, across]).astype(low_type)
        for m, ref in enumerate(q_refs):
            ref[:, across] = made[m * rows : (m + 1) * rows]


def make_queries(h, w, micros):
    total, width = h.shape
    q_width = HEADS * HD
    return call(
        query_kernel,
        tuple([shaped((total // micros, q_width), low_type)] * micros),
        [in_vmem, in_any],
        tuple([in_vmem] * micros),
        [pltpu.VMEM((width, q_width), low_type), pltpu.SemaphoreType.DMA((q_width // BC,))],
        2 * total * width * q_width,
        2 * width * q_width,
    )(h, w)


def load_keys(kv_ref, micro, rows, held, sem):
    count = held.shape[0] // rows
    span = kv_ref.shape[0] // count

    @pl.loop(0, count)
    def _(i):
        pltpu.make_async_copy(
            kv_ref.at[pl.ds(pl.multiple_of(i * span + micro * rows, 16), rows)],
            held.at[pl.ds(pl.multiple_of(i * rows, 16), rows)],
            sem,
        ).start()


def attend_kernel(
    micro, q_ref, rpos_ref, kpos_ref, x_ref, gain_ref, w_ref, all_ref,
    ob_ref, log_ref, x2_ref, h2_ref, bias, kv_ref, held, sems,
):
    rows = q_ref.shape[0]
    load_keys(all_ref, micro, rows, kv_ref, sems.at[0])
    pltpu.make_async_copy(w_ref, held, sems.at[1]).start()
    bias[...] = jnp.where(kpos_ref[...] <= rpos_ref[...], 0.0, masked_score)
    log_ref[...] = jnp.zeros_like(log_ref)
    length = kv_ref.shape[0]
    wait_bytes(kv_ref, sems.at[0])

    @pl.loop(0, KVH // 2)
    def _(pair):
        lane = pl.multiple_of(pair * LANES, LANES)
        keys = kv_ref[:, pl.ds(lane, LANES)]
        values = kv_ref[:, pl.ds(pl.multiple_of(lane + KVH * HD, LANES), LANES)]
        stacked = stack_heads(q_ref, pair, HD**-0.5)
        mixed = []
        for part in range(2):
            scores = dot(stacked[part].astype(low_type), keys, NT)
            scores = (scores.reshape(3, rows, length) + bias[...][None]).reshape(3 * rows, length)
            largest = jnp.max(scores, axis=-1, keepdims=True)
            raised = jnp.exp(scores - largest)
            summed = jnp.sum(raised, axis=-1, keepdims=True)
            mixed.append(dot(raised.astype(low_type), values) / summed)
            log_ref[...] = jnp.where(
                lane_ids(log_ref.shape) == 2 * pair + part, largest + jnp.log(summed), log_ref[...]
            )
        unstack_heads(ob_ref, pair, mixed[0], mixed[1])

    wait_bytes(held, sems.at[1])
    for n in range(held.shape[0] // BC):
        cut = slice(n * BC, (n + 1) * BC)
        x2_ref[:, cut] = x_ref[:, cut] + dot(ob_ref[...], held[cut, :], NT)
    h2_ref[...] = unit_rows(x2_ref[...], gain_ref[1:2])[0].astype(low_type)


def attend(micro, q, kv, rows_pos, key_pos, x, gains, w):
    rows, width = q.shape
    length = key_pos.shape[1]
    model = x.shape[1]
    return call(
        functools.partial(attend_kernel, micro),
        (
            shaped((rows, width), low_type),
            shaped((3 * rows, LANES), jnp.float32),
            shaped((rows, model), jnp.float32),
            shaped((rows, model), low_type),
        ),
        [in_vmem] * 5 + [in_any] * 2,
        (in_vmem,) * 4,
        [
            pltpu.VMEM((rows, length), jnp.float32),
            pltpu.VMEM((length, kv.shape[1]), low_type),
            pltpu.VMEM((model, width), low_type),
            pltpu.SemaphoreType.DMA((2,)),
        ],
        16 * rows * length * width,
        8 * MIB,
    )(q, rows_pos, key_pos, x, gains, w, kv)


def router_parts(h2, router, experts):
    logits = dot(h2, router)
    logits = jnp.where(lane_ids(logits.shape) < experts, logits, masked_score)
    raised = jnp.exp(logits - jnp.max(logits, axis=-1, keepdims=True))
    return raised / jnp.sum(raised, axis=-1, keepdims=True)


def expert_kernel(sources, micro, order_ref, me_ref, router_ref, *refs):
    h_parts = refs[:sources]
    c_parts = refs[sources : 2 * sources]
    w_refs = refs[2 * sources : 2 * sources + 2]
    outs = refs[2 * sources + 2 :]
    back_refs = outs[:sources]
    z_ref, dg_ref, du_ref, cs, xs_ref = outs[sources : sources + 5]
    held, chance, load_sem, w_sems = outs[sources + 5 :]
    rows, width = h_parts[0].shape
    row_groups = width // BR
    col_groups = FF // BC
    for j in range(sources):
        pltpu.make_async_copy(h_parts[j], xs_ref.at[pl.ds(j * rows, rows)], load_sem.at[0]).start()
        pltpu.make_async_copy(
            c_parts[j].at[pl.ds(micro * rows, rows)], cs.at[pl.ds(j * rows, rows)], load_sem.at[1]
        ).start()
    for b in range(col_groups):

        @pl.loop(0, row_groups)
        def _(a):
            for k in range(3):
                slot = order_ref[(k * row_groups + a) * col_groups + b]
                for start, ref in zip((0, UPPER), w_refs):
                    down = pl.ds(pl.multiple_of(a * BR + start, 64), ref.shape[1])
                    pltpu.make_async_copy(
                        ref.at[slot], held.at[k, down, pl.ds(b * BC, BC)], w_sems.at[b]
                    ).start()

    wait_bytes(xs_ref, load_sem.at[0])
    wait_bytes(cs, load_sem.at[1])
    me = me_ref[1]
    probs = router_parts(xs_ref[...], router_ref[...], sources)
    hits = cs[:, width:].astype(jnp.float32)
    mine = lane_ids(hits.shape) == me
    hit = jnp.sum(jnp.where(mine, hits, 0.0), axis=-1, keepdims=True)
    weight = jnp.sum(jnp.where(mine, probs, 0.0), axis=-1, keepdims=True) * hit
    chance[...] = jnp.zeros_like(chance)

    @pl.loop(0, col_groups)
    def _(b):
        cut = pl.ds(pl.multiple_of(b * BC, BC), BC)
        wait_bytes(held.at[:, :, cut], w_sems.at[b])
        gate = dot(xs_ref[...], held[0, :, cut])
        up = dot(xs_ref[...], held[1, :, cut])
        down = dot(cs[:, :width], held[2, :, cut])
        sig = jax.nn.sigmoid(gate)
        act = gate * sig
        hidden = act * up
        chance[...] += jnp.sum(down * hidden, axis=-1, keepdims=True)
        z_ref[:, cut] = (hidden * weight).astype(low_type)
        down = down * weight
        dg_ref[:, cut] = (down * up * (sig + act * (1.0 - sig))).astype(low_type)
        du_ref[:, cut] = (down * act).astype(low_type)

    for n in range(width // BC):
        cut = slice(n * BC, (n + 1) * BC)
        back = dot(dg_ref[...], held[0, cut, :], NT) + dot(du_ref[...], held[1, cut, :], NT)
        for j in range(sources):
            back_refs[j][:, cut] = back[j * rows : (j + 1) * rows].astype(low_type)
    told = chance[...] * hit
    high_part = told.astype(low_type)
    low_part = (told - high_part.astype(jnp.float32)).astype(low_type)
    lanes = lane_ids((sources * rows, LANES))
    tail = jnp.where(lanes == 0, high_part, jnp.where(lanes == 1, low_part, jnp.zeros_like(low_part)))
    for j in range(sources):
        back_refs[j][:, width:] = tail[j * rows : (j + 1) * rows]


def run_expert(micro, order, me, router, h_parts, c_parts, ws):
    sources = len(h_parts)
    rows, width = h_parts[0].shape
    total = sources * rows
    return call(
        functools.partial(expert_kernel, sources, micro),
        tuple(
            [shaped((rows, width + LANES), low_type)] * sources
            + [shaped((total, FF), low_type)] * 3
            + [shaped((total, width + LANES), low_type), shaped((total, width), low_type)]
        ),
        [in_smem, in_smem, in_vmem] + [in_any] * (2 * sources + 2),
        tuple([in_vmem] * (sources + 5)),
        [
            pltpu.VMEM((3, width, FF), low_type),
            pltpu.VMEM((total, 1), jnp.float32),
            pltpu.SemaphoreType.DMA((2,)),
            pltpu.SemaphoreType.DMA((FF // BC,)),
        ],
        10 * total * width * FF,
        20 * MIB,
    )(order, me, router, *h_parts, *c_parts, *ws)


def produce_kernel(sources, order_ref, upper_ref, lower_ref, *refs):
    out_refs = refs[-3 - sources : -3]
    z_refs = refs[: -3 - sources]
    zs, held, sem = refs[-3:]
    width = held.shape[0]
    total = z_refs[0].shape[0]
    rows = total // sources
    row_groups, col_groups = width // BR, FF // BC

    @pl.loop(0, row_groups)
    def _(a):
        for b in range(col_groups):
            slot = order_ref[(2 * row_groups + a) * col_groups + b]
            for start, ref in zip((0, UPPER), (upper_ref, lower_ref)):
                down = pl.ds(pl.multiple_of(a * BR + start, 64), ref.shape[1])
                pltpu.make_async_copy(
                    ref.at[slot], held.at[down, pl.ds(b * BC, BC)], sem
                ).start()

    for m, z_ref in enumerate(z_refs):
        zs[m * total : (m + 1) * total] = z_ref[...]
    wait_bytes(held, sem)
    for n in range(width // BC):
        cut = slice(n * BC, (n + 1) * BC)
        made = dot(zs[...], held[cut, :], NT).astype(low_type)
        for m in range(len(z_refs)):
            for j in range(sources):
                start = m * total + j * rows
                out_refs[j][m * rows : (m + 1) * rows, cut] = made[start : start + rows]


def produce(order, ws, zs, sources, width):
    micros = len(zs)
    total = zs[0].shape[0]
    return call(
        functools.partial(produce_kernel, sources),
        tuple([shaped((micros * total // sources, width), low_type)] * sources),
        [in_smem, in_any, in_any] + [in_vmem] * micros,
        tuple([in_vmem] * sources),
        [
            pltpu.VMEM((micros * total, FF), low_type),
            pltpu.VMEM((width, FF), low_type),
            pltpu.SemaphoreType.DMA,
        ],
        2 * micros * total * width * FF,
        8 * MIB,
    )(order, *ws, *zs)


def outer_kernel(groups, col_groups, order_ref, *refs):
    micros = len(refs[:-5]) // (len(groups) + 2)
    lefts = [refs[i * micros : (i + 1) * micros] for i in range(2)]
    rights = [refs[(2 + i) * micros : (3 + i) * micros] for i in range(len(groups))]
    out_refs, (turned, stage, sems) = refs[-5:-3], refs[-3:]
    rows = rights[0][0].shape[0]
    width = turned.shape[1]
    span = 2 * BR
    for side in range(2):
        for m in range(micros):
            for r in range(0, rows, LANES):
                part = lefts[side][m][r : r + LANES, :width]
                turned[side, :, m * rows + r : m * rows + r + LANES] = part.T
    row_groups = width // BR
    steps = [(k, p) for k in range(len(groups)) for p in range(width // span)]
    for n, (k, p) in enumerate(steps):
        slot = n % 2
        if n >= 2:
            wait_bytes(stage.at[slot], sems.at[slot])
        cut = slice(p * span, (p + 1) * span)
        made = 0.0
        for m in range(micros):
            left = turned[groups[k], cut, m * rows : (m + 1) * rows]
            made = made + dot(left, rights[k][m][...])
        stage[slot] = made.astype(low_type)
        for half in range(2):
            for b in range(col_groups):
                number = (k * row_groups + 2 * p + half) * col_groups + b
                place = order_ref[number]
                for side in range(2):
                    pltpu.make_async_copy(
                        stage.at[
                            slot, pl.ds(half * BR, BR), pl.ds(b * BC + side * LANES, LANES)
                        ],
                        out_refs[side].at[place],
                        sems.at[slot],
                    ).start()
    for slot in range(2):
        wait_bytes(stage.at[slot], sems.at[slot])


def outer_blocks(order, width, groups, lefts, rights):
    flat = [part for group in lefts + rights for part in group]
    rows = sum(part.shape[0] for part in rights[0])
    cols = rights[0][0].shape[1]
    blocks = len(groups) * width * cols // (BR * BC)
    return call(
        functools.partial(outer_kernel, groups, cols // BC),
        (shaped((blocks, BR, LANES), low_type),) * 2,
        [in_smem] + [in_vmem] * len(flat),
        (in_any,) * 2,
        [
            pltpu.VMEM((2, width, rows), low_type),
            pltpu.VMEM((2, 2 * BR, cols), low_type),
            pltpu.SemaphoreType.DMA((2,)),
        ],
        2 * rows * blocks * BR * BC,
        blocks * BR * BC * 2 + sum(f.size * 2 for f in flat),
    )(order, *flat)


def xor_plan(members, offset):
    if members != 4:
        return list(range(1, members)), [0]
    first = 1 if offset % 2 else 2
    return [first, 3], [0, 3 - first]


def pieces_kernel(members, counts, cols, turned_first, me_ref, *refs):
    lists = []
    for left_count, right_count in counts:
        lists.append((refs[:left_count], refs[left_count : left_count + right_count]))
        refs = refs[left_count + right_count :]
    stat_refs = refs[: len(refs) - 8] if turned_first else refs[: len(refs) - 10]
    refs = refs[len(stat_refs) :]
    outs, refs = refs[:4], refs[4:]
    extra = refs[0] if not turned_first else None
    turned, rights, stage, sems = refs[0 if turned_first else 1 :][:4]
    ctx, shard = me_ref[0], me_ref[1]
    core = lax.rem(ctx, 2)
    total = turned.shape[2]
    row_groups = turned.shape[1] // BR
    base = 0
    for g, (_, parts) in enumerate(lists):
        start = 0
        for part in parts:
            count = part.shape[0]
            for b in range(cols[g]):
                lane = pl.multiple_of(b * BC + core * LANES, LANES)
                pltpu.make_async_copy(
                    part.at[:, pl.ds(lane, LANES)],
                    rights.at[pl.ds(start, count), pl.ds((base + b) * LANES, LANES)],
                    sems.at[g],
                ).start()
            start += count
        base += cols[g]
    for g, (parts, _) in enumerate(lists):
        if g == 0 and turned_first:
            turned[0] = parts[0][...]
            continue
        start = 0
        for part in parts:
            for r in range(0, part.shape[0], LANES):
                turned[g, :, start : start + LANES] = part[r : r + LANES, :].T
                start += LANES
    if extra is not None:
        extra[...] = turned[0]
    all_cols = sum(cols)
    half_blocks = row_groups // 2 * all_cols
    counts = [half_blocks + (1 if stat_refs else 0), half_blocks]
    span = BR // members
    if stat_refs:
        block = refs[-1]
        block[...] = jnp.zeros_like(block)
        up = stat_refs[0].shape[0] - 8
        for r, row in enumerate(list(range(members)) + [up]):
            total_row = sum(ref[row : row + 1, :] for ref in stat_refs)
            for t in range(total_row.shape[1] // BC):
                place = r * (total_row.shape[1] // BC) + t
                block[place : place + 1, :] = total_row[:, t * BC : (t + 1) * BC]
        lane = pl.multiple_of(core * LANES, LANES)
        for out, hops in zip(outs[:2], xor_plan(members, 1)):
            for place, hop in enumerate(hops):
                down = pl.multiple_of(jnp.bitwise_xor(shard, hop) * span, 8)
                out[place * counts[0] + half_blocks] = block[
                    pl.ds(down, span), pl.ds(lane, LANES)
                ].astype(low_type)
    base = 0
    for g in range(len(lists)):
        wide_cols = cols[g] * LANES
        wait_bytes(rights.at[:, pl.ds(base * LANES, wide_cols)], sems.at[g])
        for a in range(row_groups):
            made = dot(
                turned[g, a * BR : (a + 1) * BR, :],
                rights[:, base * LANES : base * LANES + wide_cols],
            )
            stage[a % 2, :, :wide_cols] = made.astype(stage.dtype)
            half = a // (row_groups // 2)
            first = (a % (row_groups // 2)) * all_cols + base
            for out, hops in zip(outs[2 * half : 2 * half + 2], xor_plan(members, 1 - half)):
                for place, hop in enumerate(hops):
                    down = pl.multiple_of(jnp.bitwise_xor(shard, hop) * span, 16 if span % 16 == 0 else 8)
                    for b in range(cols[g]):
                        out[place * counts[half] + first + b] = stage[
                            a % 2, pl.ds(down, span), b * LANES : (b + 1) * LANES
                        ].astype(low_type)
        base += cols[g]


def gradient_pieces(members, me, groups, cols, turned_first, stats):
    counts = tuple((len(left), len(right)) for left, right in groups)
    flat = [part for left, right in groups for part in left + right]
    total = sum(part.shape[0] for part in groups[0][1])
    width = groups[0][0][0].shape[0 if turned_first else 1]
    row_groups = width // BR
    half_blocks = row_groups // 2 * sum(cols)
    span = BR // members
    stage_type = jnp.float32 if span % 16 else low_type
    outs = []
    for half in range(2):
        count = half_blocks + (1 if stats and half == 0 else 0)
        for hops in xor_plan(members, 1 - half):
            outs.append(shaped((len(hops) * count, span, LANES), low_type))
    out_specs = [in_vmem] * 4
    if not turned_first:
        outs.append(shaped((width, total), low_type))
        out_specs.append(in_vmem)
    in_specs = [in_smem]
    for left, right in groups:
        in_specs += [in_vmem] * len(left) + [in_any] * len(right)
    in_specs += [in_vmem] * len(stats)
    return call(
        functools.partial(pieces_kernel, members, counts, tuple(cols), turned_first),
        tuple(outs),
        in_specs,
        tuple(out_specs),
        [
            pltpu.VMEM((len(groups), width, total), low_type),
            pltpu.VMEM((total, sum(cols) * LANES), low_type),
            pltpu.VMEM((2, BR, max(cols) * LANES), stage_type),
            pltpu.SemaphoreType.DMA((len(groups),)),
        ]
        + ([pltpu.VMEM((BR, BC), jnp.float32)] if stats else []),
        2 * total * width * sum(cols) * LANES,
        16 * MIB,
    )(me, *flat, *stats)


def merge_kernel(
    sources, me_ref, x2_ref, cot_ref, h2_ref, gain_ref, router_ref, w_ref, *refs
):
    back_refs = refs[:sources]
    dx_ref, da_ref, do_ref, stat_ref, held, sem = refs[sources:]
    rows, width = x2_ref.shape
    pltpu.make_async_copy(w_ref, held, sem).start()
    lanes = lane_ids((rows, LANES))
    prob_grad = jnp.zeros((rows, LANES), jnp.float32)
    gathered = jnp.zeros((rows, width), jnp.float32)
    for j in range(sources):
        tail = back_refs[j][:, width:].astype(jnp.float32)
        told = jnp.sum(tail, axis=-1, keepdims=True)
        expert = jnp.bitwise_xor(me_ref[1], j)
        prob_grad = prob_grad + jnp.where(lanes == expert, told, 0.0)
        gathered = gathered + back_refs[j][:, :width].astype(jnp.float32)
    h2 = h2_ref[...]
    probs = router_parts(h2, router_ref[...], sources)
    logit_grad = probs * (prob_grad - jnp.sum(probs * prob_grad, axis=-1, keepdims=True))
    high_part = logit_grad.astype(low_type)
    low_part = (logit_grad - high_part.astype(jnp.float32)).astype(low_type)
    router_grad = dot(high_part, h2, TN) + dot(low_part, h2, TN)
    gathered = gathered + dot(high_part, router_ref[...], NT) + dot(low_part, router_ref[...], NT)
    x2 = x2_ref[...]
    inverse = lax.rsqrt(jnp.mean(x2 * x2, axis=-1, keepdims=True) + norm_eps)
    moe_grad, gain_grad = unit_back(x2, gain_ref[1:2], inverse, gathered)
    after = cot_ref[...] + moe_grad
    dx_ref[...] = after
    da_ref[...] = after.astype(low_type)
    experts_up = stat_ref.shape[0] - 8
    stat_ref[:experts_up] = router_grad[:experts_up]
    stat_ref[experts_up:] = jnp.broadcast_to(gain_grad, (8, width))
    wait_bytes(held, sem)
    for n in range(held.shape[1] // BC):
        cut = slice(n * BC, (n + 1) * BC)
        do_ref[:, cut] = dot(da_ref[...], held[:, cut]).astype(low_type)


def merge(me, x2, cot, h2, gains, router, w, backs):
    rows, width = x2.shape
    sources = len(backs)
    experts_up = -(-sources // 8) * 8
    return call(
        functools.partial(merge_kernel, sources),
        (
            shaped((rows, width), jnp.float32),
            shaped((rows, width), low_type),
            shaped((rows, HEADS * HD), low_type),
            shaped((experts_up + 8, width), jnp.float32),
        ),
        [in_smem] + [in_vmem] * 5 + [in_any] + [in_vmem] * sources,
        (in_vmem,) * 4,
        [pltpu.VMEM((width, HEADS * HD), low_type), pltpu.SemaphoreType.DMA],
        2 * rows * width * HEADS * HD,
        10 * MIB,
    )(me, x2, cot, h2, gains, router, w, *backs)


def attend_back_kernel(
    micro, q_ref, rpos_ref, kpos_ref, ob_ref, log_ref, do_ref, all_ref, *refs
):
    dq_ref, out_ref, bias, kv_ref, grad_ref, sems = refs[-6:]
    rows = q_ref.shape[0]
    load_keys(all_ref, micro, rows, kv_ref, sems.at[0])
    length = kv_ref.shape[0]
    bias[...] = jnp.where(kpos_ref[...] <= rpos_ref[...], 0.0, masked_score)
    wait_bytes(kv_ref, sems.at[0])

    @pl.loop(0, KVH // 2)
    def _(pair):
        lane = pl.multiple_of(pair * LANES, LANES)
        value_lane = pl.multiple_of(lane + KVH * HD, LANES)
        keys = kv_ref[:, pl.ds(lane, LANES)]
        values = kv_ref[:, pl.ds(value_lane, LANES)]
        queries = stack_heads(q_ref, pair, HD**-0.5)
        grads = stack_heads(do_ref, pair)
        mixes = stack_heads(ob_ref, pair)
        query_grads = []
        key_grad = value_grad = None
        for part in range(2):
            query = queries[part].astype(low_type)
            grad = grads[part].astype(low_type)
            log_total = jnp.sum(
                jnp.where(lane_ids(log_ref.shape) == 2 * pair + part, log_ref[...], 0.0),
                axis=-1,
                keepdims=True,
            )
            delta = jnp.sum(grads[part] * mixes[part], axis=-1, keepdims=True)
            scores = dot(query, keys, NT)
            scores = (scores.reshape(3, rows, length) + bias[...][None]).reshape(3 * rows, length)
            chance = jnp.exp(scores - log_total)
            prob_grad = dot(grad, values, NT)
            score_grad = (chance * (prob_grad - delta)).astype(low_type)
            value_term = dot(chance.astype(low_type), grad, TN)
            key_term = dot(score_grad, query, TN)
            key_grad = key_term if part == 0 else key_grad + key_term
            value_grad = value_term if part == 0 else value_grad + value_term
            query_grads.append(dot(score_grad, keys) * HD**-0.5)
        unstack_heads(dq_ref, pair, query_grads[0], query_grads[1])
        grad_ref[:, pl.ds(lane, LANES)] = key_grad.astype(low_type)
        grad_ref[:, pl.ds(value_lane, LANES)] = value_grad.astype(low_type)

    count = length // rows
    span = out_ref.shape[0] // count

    @pl.loop(0, count)
    def _(i):
        pltpu.make_async_copy(
            grad_ref.at[pl.ds(pl.multiple_of(i * rows, 16), rows)],
            out_ref.at[pl.ds(pl.multiple_of(i * span + micro * rows, 16), rows)],
            sems.at[1],
        ).start()

    wait_bytes(grad_ref, sems.at[1])


def attend_back(micro, q, kv, rows_pos, key_pos, ob, log_total, do, shared):
    rows, width = q.shape
    length = key_pos.shape[1]
    operands = [q, rows_pos, key_pos, ob, log_total, do, kv]
    in_specs = [in_vmem] * 6 + [in_any]
    aliases = {}
    if shared is not None:
        aliases = {len(operands): 1}
        operands.append(shared)
        in_specs.append(in_any)
    return pl.pallas_call(
        functools.partial(attend_back_kernel, micro),
        out_shape=(shaped((rows, width), low_type), shaped(kv.shape, low_type)),
        in_specs=in_specs,
        out_specs=(in_vmem, in_any),
        scratch_shapes=[
            pltpu.VMEM((rows, length), jnp.float32),
            pltpu.VMEM((length, kv.shape[1]), low_type),
            pltpu.VMEM((length, kv.shape[1]), low_type),
            pltpu.SemaphoreType.DMA((2,)),
        ],
        input_output_aliases=aliases,
        compiler_params=pltpu.CompilerParams(vmem_limit_bytes=VMEM_LIMIT),
        cost_estimate=pl.CostEstimate(
            flops=40 * rows * length * width, bytes_accessed=8 * MIB, transcendentals=0
        ),
    )(*operands)


def query_back_kernel(w_ref, *refs):
    micros = (len(refs) - 3) // 2
    dq_refs, out_refs = refs[:micros], refs[micros : 2 * micros]
    rows_ref, held, sem = refs[2 * micros :]
    rows = dq_refs[0].shape[0]
    copy = pltpu.make_async_copy(w_ref.at[:, pl.ds(0, held.shape[1])], held, sem)
    copy.start()
    for m in range(micros):
        rows_ref[m * rows : (m + 1) * rows] = dq_refs[m][...]
    copy.wait()
    for n in range(held.shape[0] // BC):
        cut = slice(n * BC, (n + 1) * BC)
        made = dot(rows_ref[...], held[cut, :], NT)
        for m in range(micros):
            out_refs[m][:, cut] = made[m * rows : (m + 1) * rows]


def query_back(w, dqs):
    micros = len(dqs)
    rows, q_width = dqs[0].shape
    width = w.shape[0]
    return call(
        query_back_kernel,
        tuple([shaped((rows, width), jnp.float32)] * micros),
        [in_any] + [in_vmem] * micros,
        tuple([in_vmem] * micros),
        [
            pltpu.VMEM((micros * rows, q_width), low_type),
            pltpu.VMEM((width, q_width), low_type),
            pltpu.SemaphoreType.DMA,
        ],
        2 * micros * rows * width * q_width,
        7 * MIB,
    )(w, *dqs)


def input_kernel(x_ref, gain_ref, w_ref, *refs):
    micros, rows = x_ref.shape[:2]
    dx_refs = refs[:micros]
    part_refs = refs[micros : 2 * micros]
    dkv_ref, out_ref, stat_ref, grad, held, sem = refs[2 * micros :]
    kv_width = held.shape[1]
    copy = pltpu.make_async_copy(
        w_ref.at[:, pl.ds(w_ref.shape[1] - kv_width, kv_width)], held, sem
    )
    copy.start()
    copy.wait()
    for n in range(held.shape[0] // BC):
        cut = slice(n * BC, (n + 1) * BC)
        made = dot(dkv_ref[...], held[cut, :], NT)
        for m in range(micros):
            grad[m, :, cut] = part_refs[m][:, cut] + made[m * rows : (m + 1) * rows]
    total = jnp.zeros((1, x_ref.shape[-1]), jnp.float32)
    for m in range(micros):
        x = x_ref[m]
        inverse = lax.rsqrt(jnp.mean(x * x, axis=-1, keepdims=True) + norm_eps)
        term, gain_grad = unit_back(x, gain_ref[0:1], inverse, grad[m])
        out_ref[m] = dx_refs[m][...] + term
        total = total + gain_grad
    stat_ref[...] = jnp.broadcast_to(total, stat_ref.shape)


def input_back(x, gains, w, dxs, parts, dkv):
    micros, rows, width = x.shape
    kv_width = dkv.shape[1]
    return call(
        input_kernel,
        (shaped(x.shape, jnp.float32), shaped((8, width), jnp.float32)),
        [in_vmem, in_vmem, in_any] + [in_vmem] * (2 * micros + 1),
        (in_vmem,) * 2,
        [
            pltpu.VMEM(x.shape, jnp.float32),
            pltpu.VMEM((width, kv_width), low_type),
            pltpu.SemaphoreType.DMA,
        ],
        2 * micros * rows * width * kv_width,
        14 * MIB,
    )(x, gains, w, *dxs, *parts, dkv)


def rotate_kernel(b_ref, m_ref, s_ref, l_ref, r_ref, *refs):
    grad_ref, new_ref, moment_ref, second_ref = refs[-4:]
    parts = [ref[0].astype(jnp.float32) for ref in refs[:-4]]
    gradient = parts[0] if len(parts) == 1 else jnp.concatenate(parts, axis=1)
    grad_ref[0] = gradient
    left = l_ref[0].astype(low_type)
    right = r_ref[0].astype(low_type)
    rotated = dot(dot(left, gradient.astype(low_type), TN).astype(low_type), right)
    moment = beta_one * m_ref[0] + (1.0 - beta_one) * rotated
    second = beta_two * s_ref[0] + (1.0 - beta_two) * rotated * rotated
    moment_ref[0] = moment
    second_ref[0] = second
    direction = (moment / (jnp.sqrt(second) + adam_eps)).astype(low_type)
    turned = dot(dot(left, direction).astype(low_type), right, NT)
    new_ref[0] = b_ref[0] - rate * turned


def rotate(weight, gradients, moment, second, left, right):
    count = weight.shape[0]

    def spec(rows, cols):
        return pl.BlockSpec((1, rows, cols), lambda i: (i, 0, 0))

    block = spec(BR, BC)
    return pl.pallas_call(
        rotate_kernel,
        grid=(count,),
        out_shape=(shaped(weight.shape, jnp.float32),) * 4,
        in_specs=[block] * 3
        + [spec(BR, BR), spec(BC, BC)]
        + [spec(BR, part.shape[2]) for part in gradients],
        out_specs=(block,) * 4,
        compiler_params=pltpu.CompilerParams(vmem_limit_bytes=VMEM_LIMIT),
        cost_estimate=pl.CostEstimate(
            flops=4 * count * BR * BC * (BR + BC),
            bytes_accessed=count * 2 * MIB,
            transcendentals=0,
        ),
    )(weight, moment, second, left, right, *gradients)


def adam(weight, gradient, moment, second, step_rate):
    moment_new = beta_one * moment + (1.0 - beta_one) * gradient
    second_new = beta_two * second + (1.0 - beta_two) * gradient * gradient
    return (
        weight - step_rate * moment_new / (jnp.sqrt(second_new) + adam_eps),
        moment_new,
        second_new,
    )


def piece_places(row_groups, q_groups, kv_groups):
    all_groups = 2 * q_groups + kv_groups
    out_groups = list(range(q_groups)) + list(range(q_groups + kv_groups, all_groups))
    half = row_groups // 2
    numbers = [a * all_groups + b for a in range(half) for b in out_groups] + [None]
    numbers += [a * all_groups + b for a in range(half, row_groups) for b in out_groups]
    numbers += [a * all_groups + q_groups + b for a in range(row_groups) for b in range(kv_groups)]
    places = [0] * (len(numbers) - 1)
    for place, number in enumerate(numbers):
        if number is not None:
            places[number] = place
    return places


def to_partner(array, offset):
    if offset == 0:
        return array
    count = lax.axis_size("shard")
    return lax.ppermute(array, "shard", [(i, i ^ offset) for i in range(count)])


def to_ctx(array, offset):
    count = lax.axis_size("ctx")
    return lax.ppermute(array, "ctx", [(i, i ^ offset) for i in range(count)])


def to_chip(array, offset):
    count = lax.axis_size("ctx")
    return lax.ppermute(array, "ctx", [(i, (i + 2 * offset) % count) for i in range(count)])


def after(value, *others):
    return lax.optimization_barrier((value, others))[0]


def from_chips(array, chips):
    return [array] + [to_chip(array, offset) for offset in range(1, chips)]


def wide(array):
    return array.astype(jnp.float32)


def sum_to_chips(parts):
    total = wide(parts[0])
    for offset in range(1, len(parts)):
        total = total + wide(to_chip(parts[offset], -offset))
    return total


def gather_weights(blocks, chips, members, small):
    parts = [blocks]
    for _ in range(chips - 1):
        parts.append(to_chip(parts[-1], 1))
    pieces, arrays = [], []
    gate = []

    def add(array, offset, first, cut):
        pieces.append((0, offset, first, cut))
        arrays.append(array)
        pieces.append((1, offset, first, cut))
        arrays.append(to_ctx(after(array, *gate), 1))
        return array

    def spread(group, first):
        add(group, 0, first, 0)
        if members == 4 and first > 0:
            by_one, by_two = to_partner(group, 1), to_partner(group, 2)
            add(by_one, 1, first, 0)
            add(by_two, 2, first, 0)
            half = BR // 2
            add(to_partner(by_one[:, :half], 2), 3, first, 0)
            add(to_partner(by_two[:, half:], 1), 3, first, half)
            return [by_one, by_two]
        got = [to_partner(group, offset) for offset in range(1, members)]
        for offset in range(1, members):
            add(got[offset - 1], offset, first, 0)
        return got

    got = [to_partner(blocks, offset) for offset in range(1, members)]
    first = got + parts[1:3]
    gate.append(got[0])
    add(blocks, 0, 0, 0)
    for offset in range(1, members):
        add(got[offset - 1], offset, 0, 0)
    last = list(got)
    if chips > 1:
        last = spread(after(parts[1], *last), 1)
        gate[:] = last
    if chips > 2:
        group = after(jnp.concatenate(parts[2:], axis=0), *last, *small)
        spread(group, 2)
    return first, pieces, arrays


def add_wide(parts):
    total = wide(parts[0])
    for part in parts[1:]:
        total = total + wide(part)
    return total


def sum_members(made, ready, members):
    sums, seen = [], []
    for half in range(2):
        sent, kept = made[2 * half : 2 * half + 2]
        hops, keeps = xor_plan(members, 1 - half)
        count = kept.shape[0] // len(keeps)
        total = wide(kept[:count])
        if members == 4:
            got = to_partner(sent, hops[0])
            got = got if ready is None else after(got, ready)
            total = total + wide(got[:count])
            relay = (wide(kept[count:]) + wide(got[count:])).astype(low_type)
            second = to_partner(relay, keeps[1])
            seen.append(second)
            total = total + wide(second)
        else:
            for place, hop in enumerate(hops):
                total = total + wide(to_partner(sent[place * count : (place + 1) * count], hop))
        sums.append(total.astype(low_type).reshape(count, -1))
    return jnp.concatenate(sums, axis=0), seen


def sum_chips(rows, chip, chips):
    count = rows.shape[1] // chips

    def piece(offset):
        start = lax.rem(chip - offset + chips, chips) * count
        return lax.dynamic_slice_in_dim(rows, start, count, axis=1)

    return [piece(0)] + [to_chip(piece(offset), -offset) for offset in range(1, chips)]


def shards(
    tokens,
    cotangent,
    norm_gains,
    router,
    dense_weight,
    expert_weight,
    routes,
    assign,
    dense_order,
    expert_order,
    dense_moment,
    dense_second,
    dense_left,
    dense_right,
    expert_moment,
    expert_second,
    expert_left,
    expert_right,
    gains_moment,
    gains_second,
    router_moment,
    router_second,
):
    ctx_count = lax.axis_size("ctx")
    shard_count = lax.axis_size("shard")
    chips = ctx_count // 2
    micros, rows, width = tokens.shape
    slots = dense_weight.shape[0]
    span = rows // 2
    row_groups = width // BR
    q_groups = HEADS * HD // BC
    kv_groups = 2 * KVH * HD // BC

    expert_inverse = inverse_order(expert_order)
    ctx = lax.axis_index("ctx").astype(jnp.int32)
    me = jnp.stack([ctx, lax.axis_index("shard").astype(jnp.int32)])
    row_ids = jnp.arange(rows, dtype=jnp.int32)
    all_pos = assign[:, row_ids // span] * span + row_ids % span
    key_pos = all_pos.reshape(1, rows * ctx_count)
    rows_pos = all_pos[ctx].reshape(rows, 1)
    router_pad = jnp.pad(router.astype(low_type), ((0, 0), (0, LANES - shard_count)))

    small = (me, expert_inverse, router_pad, key_pos, rows_pos)
    far, pieces, arrays = gather_weights(
        dense_weight.astype(low_type), chips, shard_count, small
    )
    expert_low = after(expert_weight[0].astype(low_type), *far)
    expert_all = [lax.all_gather(expert_low[:, :UPPER], "ctx", axis=0, tiled=True)]

    lanes = jnp.arange(LANES, dtype=jnp.int32)
    hits = jnp.sum((routes[..., None] == lanes).astype(low_type), axis=2)
    cot_rows = jnp.concatenate([cotangent.astype(low_type), hits], axis=2)
    cot_rows = cot_rows.reshape(micros * rows, width + LANES)
    cot_rows = after(cot_rows, *arrays[::2])
    cot_parts = [to_partner(cot_rows, j) for j in range(shard_count)]

    h1, kv, w_in, w_out = project(
        pieces,
        arrays,
        chips,
        shard_count,
        slots,
        dense_order,
        me,
        [tokens[m] for m in range(micros)],
        norm_gains,
    )
    q = make_queries(h1, w_in, micros)
    h1_other = to_ctx(h1, 1)
    obs, logs, x2s, h2s = [], [], [], []
    kv_all = lax.all_gather(after(kv, expert_all[0]), "ctx", axis=0, tiled=True)
    lower = after(expert_low[:, UPPER:], kv_all, q, cot_parts)
    expert_all.append(lax.all_gather(lower, "ctx", axis=0, tiled=True))
    for m in range(micros):
        query = after(q[m], *(cot_parts if m == 0 else obs[m - 1 : m]))
        ob, log_total, x2, h2 = attend(
            m, query, kv_all, rows_pos, key_pos, tokens[m], norm_gains, w_out
        )
        obs.append(ob)
        logs.append(log_total)
        x2s.append(x2)
        h2s.append(h2)
    ob_others = [to_ctx(ob, 1) for ob in obs]

    h_parts = []
    for m in range(micros):
        own = h2s[m] if m == 0 else after(h2s[m], *h_parts[m - 1])
        h_parts.append([own] + [to_partner(own, j) for j in range(1, shard_count)])
    sent = []
    zs, dgs, dus, cs, xs = [], [], [], [], []
    for m in range(micros):
        here = after(me, h2s[-1], h1_other, *ob_others) if m == 0 else after(me, zs[-1])
        made = run_expert(m, expert_inverse, here, router_pad, h_parts[m], cot_parts, expert_all)
        sent.append(made[:shard_count])
        z, dg, du, c, x = made[shard_count:]
        zs.append(z)
        dgs.append(dg)
        dus.append(du)
        cs.append(c)
        xs.append(x)
    backs = [[to_partner(sent[m][j], j) for j in range(shard_count)] for m in range(micros)]

    expert_terms = outer_blocks(
        after(expert_inverse, *backs[0]), width, (0, 0, 1), [xs, cs], [dgs, dus, zs]
    )
    outs = produce(after(expert_inverse, *expert_terms), expert_all, zs, shard_count, width)
    arrived = [to_partner(outs[j], j) for j in range(min(3, shard_count))]
    dxs, das, dqs, stats = [], [], [], []
    dkv_terms = None
    for m in range(micros):
        here = after(me, outs, backs[-1]) if m == 0 else after(me, dqs[-1], arrived[1:])
        dx, da, do, stat = merge(
            here, x2s[m], cotangent[m], h2s[m], norm_gains, router_pad, w_out, backs[m]
        )
        dq, dkv_terms = attend_back(
            m, q[m], kv_all, rows_pos, key_pos, obs[m], logs[m], do, dkv_terms
        )
        dxs.append(dx)
        das.append(da)
        dqs.append(dq)
        stats.append(stat)

    def other_core(parts):
        return [to_ctx(part, 1) for part in parts]

    da_others, dq_others = other_core(das), other_core(dqs)
    first_term = after(expert_terms[0], *backs[-1])
    expert_sums = [lax.psum_scatter(first_term, "ctx", scatter_dimension=0, tiled=True)]
    dkv = lax.psum_scatter(
        after(dkv_terms, expert_sums[0]), "ctx", scatter_dimension=0, tiled=True
    )
    stat_sum = add_wide(stats)
    early = gradient_pieces(
        shard_count,
        after(me, dkv_terms),
        [([h1, h1_other], dqs + dq_others), (das + da_others, obs + ob_others)],
        [q_groups, q_groups],
        False,
        [stat_sum, to_ctx(stat_sum, 1)],
    )
    h1_turned = early[4]
    parts_back = query_back(after(w_in, early[0]), dqs)
    early_rows, early_seen = sum_members(early[:4], parts_back, shard_count)
    chip = ctx // 2
    early_parts = sum_chips(early_rows, chip, chips)
    late = gradient_pieces(
        shard_count,
        after(me, *early_seen),
        [([h1_turned], [dkv, to_ctx(dkv, 1)])],
        [kv_groups],
        True,
        [],
    )
    last_outs = after(list(outs), early_seen)
    arrived += [to_partner(last_outs[j], j) for j in range(3, shard_count)]
    input_grad, gain_stat = input_back(
        after(tokens, late[0], arrived[3:]), norm_gains, w_in, dxs, parts_back, dkv
    )
    late_rows, late_seen = sum_members(late[:4], input_grad, shard_count)
    late_term = after(expert_terms[1], dkv, early_seen)
    expert_sums.append(lax.psum_scatter(late_term, "ctx", scatter_dimension=0, tiled=True))
    expert_grad, expert_new, expert_moment_new, expert_second_new = rotate(
        expert_weight[0], expert_sums, expert_moment[0], expert_second[0], expert_left[0], expert_right[0]
    )
    late_parts = sum_chips(late_rows, chip, chips)
    early_parts, late_parts = after((early_parts, late_parts), expert_new)
    early_sum = add_wide(early_parts).astype(low_type)
    late_sum = add_wide(late_parts).astype(low_type)
    all_sums = jnp.concatenate([early_sum, late_sum], axis=0)
    places = jnp.asarray(piece_places(row_groups, q_groups, kv_groups), jnp.int32)[dense_order]
    chosen = (places[:, None] == jnp.arange(all_sums.shape[0])[None, :]).astype(low_type)
    ordered = jnp.dot(chosen, all_sums, preferred_element_type=jnp.float32).astype(low_type)
    devices = ctx_count * shard_count
    piece_width = ordered.shape[1]
    stat_place = row_groups // 2 * 2 * q_groups
    gain_parts = gain_stat[:1].astype(low_type).reshape(-1, piece_width)
    stat_parts = jnp.concatenate([early_sum[stat_place : stat_place + 1], gain_parts], axis=0)
    extra = stat_parts.shape[0]
    ordered = jnp.concatenate(
        [
            ordered.reshape(devices, slots, piece_width),
            jnp.broadcast_to(stat_parts, (devices, extra, piece_width)),
        ],
        axis=1,
    ).reshape(devices * 2, (slots + extra) * piece_width // 2)
    ordered = lax.all_to_all(ordered, ("ctx", "shard"), split_axis=0, concat_axis=0, tiled=True)
    ordered = ordered.reshape(devices, slots + extra, piece_width)
    span = BR // (shard_count * chips)
    stat_block = ordered[:, slots].reshape(chips, 2, shard_count, span, LANES)
    stat_rows = wide(stat_block.transpose(2, 0, 3, 1, 4).reshape(BR * BC)[: (shard_count + 1) * width])
    stat_rows = stat_rows.reshape(shard_count + 1, width)
    gain_row = jnp.sum(wide(ordered[:, slots + 1 :]), axis=0).reshape(width)
    ordered = ordered[:, :slots].reshape(
        chips, 2, shard_count, slots, BR // (shard_count * chips), LANES
    )
    dense_sum = ordered.transpose(3, 2, 0, 4, 1, 5).reshape(slots, BR, BC)
    router_grad = stat_rows[:shard_count].T
    gains_grad = jnp.stack([gain_row, stat_rows[shard_count]])

    dense_grad, dense_new, dense_moment_new, dense_second_new = rotate(
        dense_weight, [dense_sum], dense_moment, dense_second, dense_left, dense_right
    )
    outputs = []
    for m in range(micros):
        total = x2s[m]
        for part in after(arrived, expert_new):
            total = total + wide(part[m * rows : (m + 1) * rows])
        outputs.append(total)

    gains_new, gains_moment_new, gains_second_new = adam(
        norm_gains, gains_grad, gains_moment, gains_second, gain_rate
    )
    router_new, router_moment_new, router_second_new = adam(
        router, router_grad, router_moment, router_second, rate
    )
    return (
        jnp.stack(outputs),
        input_grad,
        dense_grad,
        dense_new,
        dense_moment_new,
        dense_second_new,
        expert_grad[None],
        expert_new[None],
        expert_moment_new[None],
        expert_second_new[None],
        gains_grad,
        gains_new,
        gains_moment_new,
        gains_second_new,
        router_grad,
        router_new,
        router_moment_new,
        router_second_new,
    )


def solution(mesh):
    rows_spec = P("shard", "ctx", None)
    dense_spec = P(("ctx", "shard"), None, None)
    expert_spec = P("shard", "ctx", None, None)
    in_specs = (
        (rows_spec, rows_spec, P(), P(), dense_spec, expert_spec, rows_spec, P(), P(), P())
        + (dense_spec,) * 4
        + (expert_spec,) * 4
        + (P(),) * 4
    )
    out_specs = (rows_spec,) * 2 + (dense_spec,) * 4 + (expert_spec,) * 4 + (P(),) * 8
    return jax.shard_map(shards, mesh=mesh, in_specs=in_specs, out_specs=out_specs, check_vma=False)
```

```python
import functools

import jax
import jax.numpy as jnp
from jax import lax
from jax.experimental import pallas as pl
from jax.experimental.pallas import tpu as pltpu
from jax.sharding import PartitionSpec as P

HEADS = 24
KVH = 8
HD = 64
FF = 1024
BR = 192
BC = 256
LANES = 128
UPPER = 128

norm_eps = 1e-06
beta_one = 0.9
beta_two = 0.95
rate = 0.01
gain_rate = 0.5
adam_eps = 1e-08
masked_score = -1e30
low_type = jnp.bfloat16
MIB = 1 << 20
VMEM_LIMIT = 60 * MIB

NN = (((1,), (0,)), ((), ()))
NT = (((1,), (1,)), ((), ()))
TN = (((0,), (0,)), ((), ()))

in_vmem = pl.BlockSpec(memory_space=pltpu.VMEM)
in_smem = pl.BlockSpec(memory_space=pltpu.SMEM)
in_any = pl.BlockSpec(memory_space=pl.ANY)


def dot(left_side, right_side, dims=NN):
    return lax.dot_general(left_side, right_side, dims, preferred_element_type=jnp.float32)


def call(kernel, out_shapes, in_specs, out_specs, scratch, flops, moved):
    return pl.pallas_call(
        kernel,
        out_shape=out_shapes,
        in_specs=in_specs,
        out_specs=out_specs,
        scratch_shapes=scratch,
        compiler_params=pltpu.CompilerParams(vmem_limit_bytes=VMEM_LIMIT),
        cost_estimate=pl.CostEstimate(flops=flops, bytes_accessed=moved, transcendentals=0),
    )


def shaped(dims, kind):
    return jax.ShapeDtypeStruct(dims, kind)


def inverse_order(slot_order):
    count = slot_order.shape[0]
    numbers = jnp.arange(count, dtype=jnp.int32)
    return jnp.sum(
        jnp.where(slot_order[None, :] == numbers[:, None], numbers[None, :], 0), axis=1
    ).astype(jnp.int32)


def wait_bytes(landed, semaphore):
    pltpu.make_async_copy(landed, landed, semaphore).wait()


def unit_rows(rows, gain):
    inverse = lax.rsqrt(jnp.mean(rows * rows, axis=-1, keepdims=True) + norm_eps)
    return rows * inverse * gain, inverse


def unit_back(rows, gain, inverse, gradient):
    unit = rows * inverse
    scaled = gradient * gain
    inner = jnp.mean(scaled * unit, axis=-1, keepdims=True)
    return inverse * (scaled - unit * inner), jnp.sum(gradient * unit, axis=0, keepdims=True)


def lane_ids(dims):
    return lax.broadcasted_iota(jnp.int32, dims, len(dims) - 1)


def half_turn(tile):
    return pltpu.roll(tile, HD, 1)


def stack_heads(ref, pair, scale=None):
    base = pair * (3 * LANES)
    tiles = [
        ref[:, pl.ds(pl.multiple_of(base + LANES * t, LANES), LANES)].astype(jnp.float32)
        for t in range(3)
    ]
    if scale is not None:
        tiles = [t * scale for t in tiles]
    lower = lane_ids(tiles[0].shape) < HD
    first = [tiles[0], half_turn(tiles[0]), tiles[1]]
    second = [tiles[1], half_turn(tiles[2]), tiles[2]]
    return (
        jnp.concatenate([jnp.where(lower, t, 0.0) for t in first], axis=0),
        jnp.concatenate([jnp.where(lower, 0.0, t) for t in second], axis=0),
    )


def unstack_heads(ref, pair, first, second):
    rows = first.shape[0] // 3
    base = pair * (3 * LANES)
    lower = lane_ids((rows, LANES)) < HD
    tiles = (
        jnp.where(lower, first[:rows], half_turn(first[rows : 2 * rows])),
        jnp.where(lower, first[2 * rows :], second[:rows]),
        jnp.where(lower, half_turn(second[rows : 2 * rows]), second[2 * rows :]),
    )
    for t in range(3):
        ref[:, pl.ds(pl.multiple_of(base + LANES * t, LANES), LANES)] = tiles[t].astype(ref.dtype)


def project_kernel(
    pieces, chips, members, slots, all_groups, micros, order_ref, me_ref, *refs
):
    x_refs = refs[:micros]
    gain_ref = refs[micros]
    piece_refs = refs[micros + 1 : micros + 1 + len(pieces)]
    refs = refs[micros + 1 + len(pieces) :]
    h_ref = refs[0]
    kv_ref, win_ref, wout_ref, held, held_out, sems, out_sems = refs[1:]
    groups = held.shape[1] // BC
    kv_groups = kv_ref.shape[-1] // BC
    rows = x_refs[0].shape[0]
    ctx, shard = me_ref[0], me_ref[1]
    chip, core = lax.div(ctx, 2), lax.rem(ctx, 2)

    for ref, (other_core, offset, first, cut) in zip(piece_refs, pieces):

        @pl.loop(0, ref.shape[0])
        def _(i):
            source = lax.rem(chip - (first + lax.div(i, slots)) + chips, chips) * 2
            source = source + jnp.bitwise_xor(core, other_core)
            source = source * members + jnp.bitwise_xor(shard, offset)
            number = order_ref[source * slots + lax.rem(i, slots)]
            a, b = lax.div(number, all_groups), lax.rem(number, all_groups)
            down = pl.ds(pl.multiple_of(a * BR + cut, 32), ref.shape[1])

            @pl.when(b < groups)
            def _():
                across = pl.ds(pl.multiple_of(b * BC, BC), BC)
                pltpu.make_async_copy(ref.at[i], held.at[down, across], sems.at[b]).start()

            @pl.when(b >= groups)
            def _():
                across = pl.ds(pl.multiple_of((b - groups) * BC, BC), BC)
                pltpu.make_async_copy(ref.at[i], held_out.at[down, across], sems.at[groups]).start()

    for m in range(micros):
        h_ref[m * rows : (m + 1) * rows, :] = unit_rows(x_refs[m][...], gain_ref[0:1])[0].astype(
            low_type
        )
    q_groups = groups - kv_groups

    @pl.loop(0, groups)
    def _(b):
        across = pl.ds(pl.multiple_of(b * BC, BC), BC)
        wait_bytes(held.at[:, across], sems.at[b])

    wait_bytes(held_out, sems.at[groups])
    copies = [
        pltpu.make_async_copy(held, win_ref, out_sems.at[0]),
        pltpu.make_async_copy(held_out, wout_ref, out_sems.at[1]),
    ]
    for copy in copies:
        copy.start()

    @pl.loop(0, kv_groups)
    def _(b):
        across = pl.ds(pl.multiple_of((q_groups + b) * BC, BC), BC)
        made = dot(h_ref[...], held[:, across]).astype(low_type)
        kv_ref[:, pl.ds(pl.multiple_of(b * BC, BC), BC)] = made

    for copy in copies:
        copy.wait()


def project(pieces, arrays, chips, members, slots, order, me, xs, gains):
    micros = len(xs)
    rows, width = xs[0].shape
    in_width = (HEADS + 2 * KVH) * HD
    out_width = HEADS * HD
    kv_width = 2 * KVH * HD
    return call(
        functools.partial(
            project_kernel, pieces, chips, members, slots, (in_width + out_width) // BC, micros
        ),
        tuple(
            [shaped((micros * rows, width), low_type)]
            + [shaped((micros * rows, kv_width), low_type)]
            + [shaped((width, in_width), low_type), shaped((width, out_width), low_type)]
        ),
        [in_smem, in_smem] + [in_vmem] * (micros + 1) + [in_any] * len(arrays),
        (in_vmem, in_vmem, in_any, in_any),
        [
            pltpu.VMEM((width, in_width), low_type),
            pltpu.VMEM((width, out_width), low_type),
            pltpu.SemaphoreType.DMA((in_width // BC + 1,)),
            pltpu.SemaphoreType.DMA((2,)),
        ],
        2 * micros * rows * width * kv_width,
        4 * width * (in_width + out_width),
    )(order, me, *xs, gains, *arrays)


def query_kernel(h_ref, w_ref, *refs):
    q_refs = refs[:-2]
    held, sems = refs[-2:]
    groups = held.shape[1] // BC
    rows = q_refs[0].shape[0]

    def copy(b):
        across = pl.ds(pl.multiple_of(b * BC, BC), BC)
        return pltpu.make_async_copy(w_ref.at[:, across], held.at[:, across], sems.at[b])

    @pl.loop(0, groups)
    def _(b):
        copy(b).start()

    @pl.loop(0, groups)
    def _(b):
        copy(b).wait()
        across = pl.ds(pl.multiple_of(b * BC, BC), BC)
        made = dot(h_ref[...], held[:, across]).astype(low_type)
        for m, ref in enumerate(q_refs):
            ref[:, across] = made[m * rows : (m + 1) * rows]


def make_queries(h, w, micros):
    total, width = h.shape
    q_width = HEADS * HD
    return call(
        query_kernel,
        tuple([shaped((total // micros, q_width), low_type)] * micros),
        [in_vmem, in_any],
        tuple([in_vmem] * micros),
        [pltpu.VMEM((width, q_width), low_type), pltpu.SemaphoreType.DMA((q_width // BC,))],
        2 * total * width * q_width,
        2 * width * q_width,
    )(h, w)


def load_keys(kv_ref, micro, rows, held, sem):
    count = held.shape[0] // rows
    span = kv_ref.shape[0] // count

    @pl.loop(0, count)
    def _(i):
        pltpu.make_async_copy(
            kv_ref.at[pl.ds(pl.multiple_of(i * span + micro * rows, 16), rows)],
            held.at[pl.ds(pl.multiple_of(i * rows, 16), rows)],
            sem,
        ).start()


def attend_kernel(
    micro, q_ref, rpos_ref, kpos_ref, x_ref, gain_ref, w_ref, all_ref,
    ob_ref, log_ref, x2_ref, h2_ref, bias, kv_ref, held, sems,
):
    rows = q_ref.shape[0]
    load_keys(all_ref, micro, rows, kv_ref, sems.at[0])
    pltpu.make_async_copy(w_ref, held, sems.at[1]).start()
    bias[...] = jnp.where(kpos_ref[...] <= rpos_ref[...], 0.0, masked_score)
    log_ref[...] = jnp.zeros_like(log_ref)
    length = kv_ref.shape[0]
    wait_bytes(kv_ref, sems.at[0])

    @pl.loop(0, KVH // 2)
    def _(pair):
        lane = pl.multiple_of(pair * LANES, LANES)
        keys = kv_ref[:, pl.ds(lane, LANES)]
        values = kv_ref[:, pl.ds(pl.multiple_of(lane + KVH * HD, LANES), LANES)]
        stacked = stack_heads(q_ref, pair, HD**-0.5)
        mixed = []
        for part in range(2):
            scores = dot(stacked[part].astype(low_type), keys, NT)
            scores = (scores.reshape(3, rows, length) + bias[...][None]).reshape(3 * rows, length)
            largest = jnp.max(scores, axis=-1, keepdims=True)
            raised = jnp.exp(scores - largest)
            summed = jnp.sum(raised, axis=-1, keepdims=True)
            mixed.append(dot(raised.astype(low_type), values) / summed)
            log_ref[...] = jnp.where(
                lane_ids(log_ref.shape) == 2 * pair + part, largest + jnp.log(summed), log_ref[...]
            )
        unstack_heads(ob_ref, pair, mixed[0], mixed[1])

    wait_bytes(held, sems.at[1])
    for n in range(held.shape[0] // BC):
        cut = slice(n * BC, (n + 1) * BC)
        x2_ref[:, cut] = x_ref[:, cut] + dot(ob_ref[...], held[cut, :], NT)
    h2_ref[...] = unit_rows(x2_ref[...], gain_ref[1:2])[0].astype(low_type)


def attend(micro, q, kv, rows_pos, key_pos, x, gains, w):
    rows, width = q.shape
    length = key_pos.shape[1]
    model = x.shape[1]
    return call(
        functools.partial(attend_kernel, micro),
        (
            shaped((rows, width), low_type),
            shaped((3 * rows, LANES), jnp.float32),
            shaped((rows, model), jnp.float32),
            shaped((rows, model), low_type),
        ),
        [in_vmem] * 5 + [in_any] * 2,
        (in_vmem,) * 4,
        [
            pltpu.VMEM((rows, length), jnp.float32),
            pltpu.VMEM((length, kv.shape[1]), low_type),
            pltpu.VMEM((model, width), low_type),
            pltpu.SemaphoreType.DMA((2,)),
        ],
        16 * rows * length * width,
        8 * MIB,
    )(q, rows_pos, key_pos, x, gains, w, kv)


def router_parts(h2, router, experts):
    logits = dot(h2, router)
    logits = jnp.where(lane_ids(logits.shape) < experts, logits, masked_score)
    raised = jnp.exp(logits - jnp.max(logits, axis=-1, keepdims=True))
    return raised / jnp.sum(raised, axis=-1, keepdims=True)


def expert_kernel(sources, micro, order_ref, me_ref, router_ref, *refs):
    h_parts = refs[:sources]
    c_parts = refs[sources : 2 * sources]
    w_refs = refs[2 * sources : 2 * sources + 2]
    outs = refs[2 * sources + 2 :]
    back_refs = outs[:sources]
    z_ref, dg_ref, du_ref, cs, xs_ref = outs[sources : sources + 5]
    held, chance, load_sem, w_sems = outs[sources + 5 :]
    rows, width = h_parts[0].shape
    row_groups = width // BR
    col_groups = FF // BC
    for j in range(sources):
        pltpu.make_async_copy(h_parts[j], xs_ref.at[pl.ds(j * rows, rows)], load_sem.at[0]).start()
        pltpu.make_async_copy(
            c_parts[j].at[pl.ds(micro * rows, rows)], cs.at[pl.ds(j * rows, rows)], load_sem.at[1]
        ).start()
    for b in range(col_groups):

        @pl.loop(0, row_groups)
        def _(a):
            for k in range(3):
                slot = order_ref[(k * row_groups + a) * col_groups + b]
                for start, ref in zip((0, UPPER), w_refs):
                    down = pl.ds(pl.multiple_of(a * BR + start, 64), ref.shape[1])
                    pltpu.make_async_copy(
                        ref.at[slot], held.at[k, down, pl.ds(b * BC, BC)], w_sems.at[b]
                    ).start()

    wait_bytes(xs_ref, load_sem.at[0])
    wait_bytes(cs, load_sem.at[1])
    me = me_ref[1]
    probs = router_parts(xs_ref[...], router_ref[...], sources)
    hits = cs[:, width:].astype(jnp.float32)
    mine = lane_ids(hits.shape) == me
    hit = jnp.sum(jnp.where(mine, hits, 0.0), axis=-1, keepdims=True)
    weight = jnp.sum(jnp.where(mine, probs, 0.0), axis=-1, keepdims=True) * hit
    chance[...] = jnp.zeros_like(chance)

    @pl.loop(0, col_groups)
    def _(b):
        cut = pl.ds(pl.multiple_of(b * BC, BC), BC)
        wait_bytes(held.at[:, :, cut], w_sems.at[b])
        gate = dot(xs_ref[...], held[0, :, cut])
        up = dot(xs_ref[...], held[1, :, cut])
        down = dot(cs[:, :width], held[2, :, cut])
        sig = jax.nn.sigmoid(gate)
        act = gate * sig
        hidden = act * up
        chance[...] += jnp.sum(down * hidden, axis=-1, keepdims=True)
        z_ref[:, cut] = (hidden * weight).astype(low_type)
        down = down * weight
        dg_ref[:, cut] = (down * up * (sig + act * (1.0 - sig))).astype(low_type)
        du_ref[:, cut] = (down * act).astype(low_type)

    for n in range(width // BC):
        cut = slice(n * BC, (n + 1) * BC)
        back = dot(dg_ref[...], held[0, cut, :], NT) + dot(du_ref[...], held[1, cut, :], NT)
        for j in range(sources):
            back_refs[j][:, cut] = back[j * rows : (j + 1) * rows].astype(low_type)
    told = chance[...] * hit
    high_part = told.astype(low_type)
    low_part = (told - high_part.astype(jnp.float32)).astype(low_type)
    lanes = lane_ids((sources * rows, LANES))
    tail = jnp.where(lanes == 0, high_part, jnp.where(lanes == 1, low_part, jnp.zeros_like(low_part)))
    for j in range(sources):
        back_refs[j][:, width:] = tail[j * rows : (j + 1) * rows]


def run_expert(micro, order, me, router, h_parts, c_parts, ws):
    sources = len(h_parts)
    rows, width = h_parts[0].shape
    total = sources * rows
    return call(
        functools.partial(expert_kernel, sources, micro),
        tuple(
            [shaped((rows, width + LANES), low_type)] * sources
            + [shaped((total, FF), low_type)] * 3
            + [shaped((total, width + LANES), low_type), shaped((total, width), low_type)]
        ),
        [in_smem, in_smem, in_vmem] + [in_any] * (2 * sources + 2),
        tuple([in_vmem] * (sources + 5)),
        [
            pltpu.VMEM((3, width, FF), low_type),
            pltpu.VMEM((total, 1), jnp.float32),
            pltpu.SemaphoreType.DMA((2,)),
            pltpu.SemaphoreType.DMA((FF // BC,)),
        ],
        10 * total * width * FF,
        20 * MIB,
    )(order, me, router, *h_parts, *c_parts, *ws)


def produce_kernel(sources, order_ref, upper_ref, lower_ref, *refs):
    out_refs = refs[-3 - sources : -3]
    z_refs = refs[: -3 - sources]
    zs, held, sem = refs[-3:]
    width = held.shape[0]
    total = z_refs[0].shape[0]
    rows = total // sources
    row_groups, col_groups = width // BR, FF // BC

    @pl.loop(0, row_groups)
    def _(a):
        for b in range(col_groups):
            slot = order_ref[(2 * row_groups + a) * col_groups + b]
            for start, ref in zip((0, UPPER), (upper_ref, lower_ref)):
                down = pl.ds(pl.multiple_of(a * BR + start, 64), ref.shape[1])
                pltpu.make_async_copy(
                    ref.at[slot], held.at[down, pl.ds(b * BC, BC)], sem
                ).start()

    for m, z_ref in enumerate(z_refs):
        zs[m * total : (m + 1) * total] = z_ref[...]
    wait_bytes(held, sem)
    for n in range(width // BC):
        cut = slice(n * BC, (n + 1) * BC)
        made = dot(zs[...], held[cut, :], NT).astype(low_type)
        for m in range(len(z_refs)):
            for j in range(sources):
                start = m * total + j * rows
                out_refs[j][m * rows : (m + 1) * rows, cut] = made[start : start + rows]


def produce(order, ws, zs, sources, width):
    micros = len(zs)
    total = zs[0].shape[0]
    return call(
        functools.partial(produce_kernel, sources),
        tuple([shaped((micros * total // sources, width), low_type)] * sources),
        [in_smem, in_any, in_any] + [in_vmem] * micros,
        tuple([in_vmem] * sources),
        [
            pltpu.VMEM((micros * total, FF), low_type),
            pltpu.VMEM((width, FF), low_type),
            pltpu.SemaphoreType.DMA,
        ],
        2 * micros * total * width * FF,
        8 * MIB,
    )(order, *ws, *zs)


def outer_kernel(groups, col_groups, order_ref, *refs):
    micros = len(refs[:-5]) // (len(groups) + 2)
    lefts = [refs[i * micros : (i + 1) * micros] for i in range(2)]
    rights = [refs[(2 + i) * micros : (3 + i) * micros] for i in range(len(groups))]
    out_refs, (turned, stage, sems) = refs[-5:-3], refs[-3:]
    rows = rights[0][0].shape[0]
    width = turned.shape[1]
    span = 2 * BR
    for side in range(2):
        for m in range(micros):
            for r in range(0, rows, LANES):
                part = lefts[side][m][r : r + LANES, :width]
                turned[side, :, m * rows + r : m * rows + r + LANES] = part.T
    row_groups = width // BR
    steps = [(k, p) for k in range(len(groups)) for p in range(width // span)]
    for n, (k, p) in enumerate(steps):
        slot = n % 2
        if n >= 2:
            wait_bytes(stage.at[slot], sems.at[slot])
        cut = slice(p * span, (p + 1) * span)
        made = 0.0
        for m in range(micros):
            left = turned[groups[k], cut, m * rows : (m + 1) * rows]
            made = made + dot(left, rights[k][m][...])
        stage[slot] = made.astype(low_type)
        for half in range(2):
            for b in range(col_groups):
                number = (k * row_groups + 2 * p + half) * col_groups + b
                place = order_ref[number]
                for side in range(2):
                    pltpu.make_async_copy(
                        stage.at[
                            slot, pl.ds(half * BR, BR), pl.ds(b * BC + side * LANES, LANES)
                        ],
                        out_refs[side].at[place],
                        sems.at[slot],
                    ).start()
    for slot in range(2):
        wait_bytes(stage.at[slot], sems.at[slot])


def outer_blocks(order, width, groups, lefts, rights):
    flat = [part for group in lefts + rights for part in group]
    rows = sum(part.shape[0] for part in rights[0])
    cols = rights[0][0].shape[1]
    blocks = len(groups) * width * cols // (BR * BC)
    return call(
        functools.partial(outer_kernel, groups, cols // BC),
        (shaped((blocks, BR, LANES), low_type),) * 2,
        [in_smem] + [in_vmem] * len(flat),
        (in_any,) * 2,
        [
            pltpu.VMEM((2, width, rows), low_type),
            pltpu.VMEM((2, 2 * BR, cols), low_type),
            pltpu.SemaphoreType.DMA((2,)),
        ],
        2 * rows * blocks * BR * BC,
        blocks * BR * BC * 2 + sum(f.size * 2 for f in flat),
    )(order, *flat)


def xor_plan(members, offset):
    if members != 4:
        return list(range(1, members)), [0]
    first = 1 if offset % 2 else 2
    return [first, 3], [0, 3 - first]


def pieces_kernel(members, counts, cols, turned_first, me_ref, *refs):
    lists = []
    for left_count, right_count in counts:
        lists.append((refs[:left_count], refs[left_count : left_count + right_count]))
        refs = refs[left_count + right_count :]
    stat_refs = refs[: len(refs) - 8] if turned_first else refs[: len(refs) - 10]
    refs = refs[len(stat_refs) :]
    outs, refs = refs[:4], refs[4:]
    extra = refs[0] if not turned_first else None
    turned, rights, stage, sems = refs[0 if turned_first else 1 :][:4]
    ctx, shard = me_ref[0], me_ref[1]
    core = lax.rem(ctx, 2)
    total = turned.shape[2]
    row_groups = turned.shape[1] // BR
    base = 0
    for g, (_, parts) in enumerate(lists):
        start = 0
        for part in parts:
            count = part.shape[0]
            for b in range(cols[g]):
                lane = pl.multiple_of(b * BC + core * LANES, LANES)
                pltpu.make_async_copy(
                    part.at[:, pl.ds(lane, LANES)],
                    rights.at[pl.ds(start, count), pl.ds((base + b) * LANES, LANES)],
                    sems.at[g],
                ).start()
            start += count
        base += cols[g]
    for g, (parts, _) in enumerate(lists):
        if g == 0 and turned_first:
            turned[0] = parts[0][...]
            continue
        start = 0
        for part in parts:
            for r in range(0, part.shape[0], LANES):
                turned[g, :, start : start + LANES] = part[r : r + LANES, :].T
                start += LANES
    if extra is not None:
        extra[...] = turned[0]
    all_cols = sum(cols)
    half_blocks = row_groups // 2 * all_cols
    counts = [half_blocks + (1 if stat_refs else 0), half_blocks]
    span = BR // members
    if stat_refs:
        block = refs[-1]
        block[...] = jnp.zeros_like(block)
        up = stat_refs[0].shape[0] - 8
        for r, row in enumerate(list(range(members)) + [up]):
            total_row = sum(ref[row : row + 1, :] for ref in stat_refs)
            for t in range(total_row.shape[1] // BC):
                place = r * (total_row.shape[1] // BC) + t
                block[place : place + 1, :] = total_row[:, t * BC : (t + 1) * BC]
        lane = pl.multiple_of(core * LANES, LANES)
        for out, hops in zip(outs[:2], xor_plan(members, 1)):
            for place, hop in enumerate(hops):
                down = pl.multiple_of(jnp.bitwise_xor(shard, hop) * span, 8)
                out[place * counts[0] + half_blocks] = block[
                    pl.ds(down, span), pl.ds(lane, LANES)
                ].astype(low_type)
    base = 0
    for g in range(len(lists)):
        wide_cols = cols[g] * LANES
        wait_bytes(rights.at[:, pl.ds(base * LANES, wide_cols)], sems.at[g])
        for a in range(row_groups):
            made = dot(
                turned[g, a * BR : (a + 1) * BR, :],
                rights[:, base * LANES : base * LANES + wide_cols],
            )
            stage[a % 2, :, :wide_cols] = made.astype(stage.dtype)
            half = a // (row_groups // 2)
            first = (a % (row_groups // 2)) * all_cols + base
            for out, hops in zip(outs[2 * half : 2 * half + 2], xor_plan(members, 1 - half)):
                for place, hop in enumerate(hops):
                    down = pl.multiple_of(jnp.bitwise_xor(shard, hop) * span, 16 if span % 16 == 0 else 8)
                    for b in range(cols[g]):
                        out[place * counts[half] + first + b] = stage[
                            a % 2, pl.ds(down, span), b * LANES : (b + 1) * LANES
                        ].astype(low_type)
        base += cols[g]


def gradient_pieces(members, me, groups, cols, turned_first, stats):
    counts = tuple((len(left), len(right)) for left, right in groups)
    flat = [part for left, right in groups for part in left + right]
    total = sum(part.shape[0] for part in groups[0][1])
    width = groups[0][0][0].shape[0 if turned_first else 1]
    row_groups = width // BR
    half_blocks = row_groups // 2 * sum(cols)
    span = BR // members
    stage_type = jnp.float32 if span % 16 else low_type
    outs = []
    for half in range(2):
        count = half_blocks + (1 if stats and half == 0 else 0)
        for hops in xor_plan(members, 1 - half):
            outs.append(shaped((len(hops) * count, span, LANES), low_type))
    out_specs = [in_vmem] * 4
    if not turned_first:
        outs.append(shaped((width, total), low_type))
        out_specs.append(in_vmem)
    in_specs = [in_smem]
    for left, right in groups:
        in_specs += [in_vmem] * len(left) + [in_any] * len(right)
    in_specs += [in_vmem] * len(stats)
    return call(
        functools.partial(pieces_kernel, members, counts, tuple(cols), turned_first),
        tuple(outs),
        in_specs,
        tuple(out_specs),
        [
            pltpu.VMEM((len(groups), width, total), low_type),
            pltpu.VMEM((total, sum(cols) * LANES), low_type),
            pltpu.VMEM((2, BR, max(cols) * LANES), stage_type),
            pltpu.SemaphoreType.DMA((len(groups),)),
        ]
        + ([pltpu.VMEM((BR, BC), jnp.float32)] if stats else []),
        2 * total * width * sum(cols) * LANES,
        16 * MIB,
    )(me, *flat, *stats)


def merge_kernel(
    sources, me_ref, x2_ref, cot_ref, h2_ref, gain_ref, router_ref, w_ref, *refs
):
    back_refs = refs[:sources]
    dx_ref, da_ref, do_ref, stat_ref, held, sem = refs[sources:]
    rows, width = x2_ref.shape
    pltpu.make_async_copy(w_ref, held, sem).start()
    lanes = lane_ids((rows, LANES))
    prob_grad = jnp.zeros((rows, LANES), jnp.float32)
    gathered = jnp.zeros((rows, width), jnp.float32)
    for j in range(sources):
        tail = back_refs[j][:, width:].astype(jnp.float32)
        told = jnp.sum(tail, axis=-1, keepdims=True)
        expert = jnp.bitwise_xor(me_ref[1], j)
        prob_grad = prob_grad + jnp.where(lanes == expert, told, 0.0)
        gathered = gathered + back_refs[j][:, :width].astype(jnp.float32)
    h2 = h2_ref[...]
    probs = router_parts(h2, router_ref[...], sources)
    logit_grad = probs * (prob_grad - jnp.sum(probs * prob_grad, axis=-1, keepdims=True))
    high_part = logit_grad.astype(low_type)
    low_part = (logit_grad - high_part.astype(jnp.float32)).astype(low_type)
    router_grad = dot(high_part, h2, TN) + dot(low_part, h2, TN)
    gathered = gathered + dot(high_part, router_ref[...], NT) + dot(low_part, router_ref[...], NT)
    x2 = x2_ref[...]
    inverse = lax.rsqrt(jnp.mean(x2 * x2, axis=-1, keepdims=True) + norm_eps)
    moe_grad, gain_grad = unit_back(x2, gain_ref[1:2], inverse, gathered)
    after = cot_ref[...] + moe_grad
    dx_ref[...] = after
    da_ref[...] = after.astype(low_type)
    experts_up = stat_ref.shape[0] - 8
    stat_ref[:experts_up] = router_grad[:experts_up]
    stat_ref[experts_up:] = jnp.broadcast_to(gain_grad, (8, width))
    wait_bytes(held, sem)
    for n in range(held.shape[1] // BC):
        cut = slice(n * BC, (n + 1) * BC)
        do_ref[:, cut] = dot(da_ref[...], held[:, cut]).astype(low_type)


def merge(me, x2, cot, h2, gains, router, w, backs):
    rows, width = x2.shape
    sources = len(backs)
    experts_up = -(-sources // 8) * 8
    return call(
        functools.partial(merge_kernel, sources),
        (
            shaped((rows, width), jnp.float32),
            shaped((rows, width), low_type),
            shaped((rows, HEADS * HD), low_type),
            shaped((experts_up + 8, width), jnp.float32),
        ),
        [in_smem] + [in_vmem] * 5 + [in_any] + [in_vmem] * sources,
        (in_vmem,) * 4,
        [pltpu.VMEM((width, HEADS * HD), low_type), pltpu.SemaphoreType.DMA],
        2 * rows * width * HEADS * HD,
        10 * MIB,
    )(me, x2, cot, h2, gains, router, w, *backs)


def attend_back_kernel(
    micro, q_ref, rpos_ref, kpos_ref, ob_ref, log_ref, do_ref, all_ref, *refs
):
    dq_ref, out_ref, bias, kv_ref, grad_ref, sems = refs[-6:]
    rows = q_ref.shape[0]
    load_keys(all_ref, micro, rows, kv_ref, sems.at[0])
    length = kv_ref.shape[0]
    bias[...] = jnp.where(kpos_ref[...] <= rpos_ref[...], 0.0, masked_score)
    wait_bytes(kv_ref, sems.at[0])

    @pl.loop(0, KVH // 2)
    def _(pair):
        lane = pl.multiple_of(pair * LANES, LANES)
        value_lane = pl.multiple_of(lane + KVH * HD, LANES)
        keys = kv_ref[:, pl.ds(lane, LANES)]
        values = kv_ref[:, pl.ds(value_lane, LANES)]
        queries = stack_heads(q_ref, pair, HD**-0.5)
        grads = stack_heads(do_ref, pair)
        mixes = stack_heads(ob_ref, pair)
        query_grads = []
        key_grad = value_grad = None
        for part in range(2):
            query = queries[part].astype(low_type)
            grad = grads[part].astype(low_type)
            log_total = jnp.sum(
                jnp.where(lane_ids(log_ref.shape) == 2 * pair + part, log_ref[...], 0.0),
                axis=-1,
                keepdims=True,
            )
            delta = jnp.sum(grads[part] * mixes[part], axis=-1, keepdims=True)
            scores = dot(query, keys, NT)
            scores = (scores.reshape(3, rows, length) + bias[...][None]).reshape(3 * rows, length)
            chance = jnp.exp(scores - log_total)
            prob_grad = dot(grad, values, NT)
            score_grad = (chance * (prob_grad - delta)).astype(low_type)
            value_term = dot(chance.astype(low_type), grad, TN)
            key_term = dot(score_grad, query, TN)
            key_grad = key_term if part == 0 else key_grad + key_term
            value_grad = value_term if part == 0 else value_grad + value_term
            query_grads.append(dot(score_grad, keys) * HD**-0.5)
        unstack_heads(dq_ref, pair, query_grads[0], query_grads[1])
        grad_ref[:, pl.ds(lane, LANES)] = key_grad.astype(low_type)
        grad_ref[:, pl.ds(value_lane, LANES)] = value_grad.astype(low_type)

    count = length // rows
    span = out_ref.shape[0] // count

    @pl.loop(0, count)
    def _(i):
        pltpu.make_async_copy(
            grad_ref.at[pl.ds(pl.multiple_of(i * rows, 16), rows)],
            out_ref.at[pl.ds(pl.multiple_of(i * span + micro * rows, 16), rows)],
            sems.at[1],
        ).start()

    wait_bytes(grad_ref, sems.at[1])


def attend_back(micro, q, kv, rows_pos, key_pos, ob, log_total, do, shared):
    rows, width = q.shape
    length = key_pos.shape[1]
    operands = [q, rows_pos, key_pos, ob, log_total, do, kv]
    in_specs = [in_vmem] * 6 + [in_any]
    aliases = {}
    if shared is not None:
        aliases = {len(operands): 1}
        operands.append(shared)
        in_specs.append(in_any)
    return pl.pallas_call(
        functools.partial(attend_back_kernel, micro),
        out_shape=(shaped((rows, width), low_type), shaped(kv.shape, low_type)),
        in_specs=in_specs,
        out_specs=(in_vmem, in_any),
        scratch_shapes=[
            pltpu.VMEM((rows, length), jnp.float32),
            pltpu.VMEM((length, kv.shape[1]), low_type),
            pltpu.VMEM((length, kv.shape[1]), low_type),
            pltpu.SemaphoreType.DMA((2,)),
        ],
        input_output_aliases=aliases,
        compiler_params=pltpu.CompilerParams(vmem_limit_bytes=VMEM_LIMIT),
        cost_estimate=pl.CostEstimate(
            flops=40 * rows * length * width, bytes_accessed=8 * MIB, transcendentals=0
        ),
    )(*operands)


def query_back_kernel(w_ref, *refs):
    micros = (len(refs) - 3) // 2
    dq_refs, out_refs = refs[:micros], refs[micros : 2 * micros]
    rows_ref, held, sem = refs[2 * micros :]
    rows = dq_refs[0].shape[0]
    copy = pltpu.make_async_copy(w_ref.at[:, pl.ds(0, held.shape[1])], held, sem)
    copy.start()
    for m in range(micros):
        rows_ref[m * rows : (m + 1) * rows] = dq_refs[m][...]
    copy.wait()
    for n in range(held.shape[0] // BC):
        cut = slice(n * BC, (n + 1) * BC)
        made = dot(rows_ref[...], held[cut, :], NT)
        for m in range(micros):
            out_refs[m][:, cut] = made[m * rows : (m + 1) * rows]


def query_back(w, dqs):
    micros = len(dqs)
    rows, q_width = dqs[0].shape
    width = w.shape[0]
    return call(
        query_back_kernel,
        tuple([shaped((rows, width), jnp.float32)] * micros),
        [in_any] + [in_vmem] * micros,
        tuple([in_vmem] * micros),
        [
            pltpu.VMEM((micros * rows, q_width), low_type),
            pltpu.VMEM((width, q_width), low_type),
            pltpu.SemaphoreType.DMA,
        ],
        2 * micros * rows * width * q_width,
        7 * MIB,
    )(w, *dqs)


def input_kernel(x_ref, gain_ref, w_ref, *refs):
    micros, rows = x_ref.shape[:2]
    dx_refs = refs[:micros]
    part_refs = refs[micros : 2 * micros]
    dkv_ref, out_ref, stat_ref, grad, held, sem = refs[2 * micros :]
    kv_width = held.shape[1]
    copy = pltpu.make_async_copy(
        w_ref.at[:, pl.ds(w_ref.shape[1] - kv_width, kv_width)], held, sem
    )
    copy.start()
    copy.wait()
    for n in range(held.shape[0] // BC):
        cut = slice(n * BC, (n + 1) * BC)
        made = dot(dkv_ref[...], held[cut, :], NT)
        for m in range(micros):
            grad[m, :, cut] = part_refs[m][:, cut] + made[m * rows : (m + 1) * rows]
    total = jnp.zeros((1, x_ref.shape[-1]), jnp.float32)
    for m in range(micros):
        x = x_ref[m]
        inverse = lax.rsqrt(jnp.mean(x * x, axis=-1, keepdims=True) + norm_eps)
        term, gain_grad = unit_back(x, gain_ref[0:1], inverse, grad[m])
        out_ref[m] = dx_refs[m][...] + term
        total = total + gain_grad
    stat_ref[...] = jnp.broadcast_to(total, stat_ref.shape)


def input_back(x, gains, w, dxs, parts, dkv):
    micros, rows, width = x.shape
    kv_width = dkv.shape[1]
    return call(
        input_kernel,
        (shaped(x.shape, jnp.float32), shaped((8, width), jnp.float32)),
        [in_vmem, in_vmem, in_any] + [in_vmem] * (2 * micros + 1),
        (in_vmem,) * 2,
        [
            pltpu.VMEM(x.shape, jnp.float32),
            pltpu.VMEM((width, kv_width), low_type),
            pltpu.SemaphoreType.DMA,
        ],
        2 * micros * rows * width * kv_width,
        14 * MIB,
    )(x, gains, w, *dxs, *parts, dkv)


def rotate_kernel(b_ref, m_ref, s_ref, l_ref, r_ref, *refs):
    grad_ref, new_ref, moment_ref, second_ref = refs[-4:]
    parts = [ref[0].astype(jnp.float32) for ref in refs[:-4]]
    gradient = parts[0] if len(parts) == 1 else jnp.concatenate(parts, axis=1)
    grad_ref[0] = gradient
    left = l_ref[0].astype(low_type)
    right = r_ref[0].astype(low_type)
    rotated = dot(dot(left, gradient.astype(low_type), TN).astype(low_type), right)
    moment = beta_one * m_ref[0] + (1.0 - beta_one) * rotated
    second = beta_two * s_ref[0] + (1.0 - beta_two) * rotated * rotated
    moment_ref[0] = moment
    second_ref[0] = second
    direction = (moment / (jnp.sqrt(second) + adam_eps)).astype(low_type)
    turned = dot(dot(left, direction).astype(low_type), right, NT)
    new_ref[0] = b_ref[0] - rate * turned


def rotate(weight, gradients, moment, second, left, right):
    count = weight.shape[0]

    def spec(rows, cols):
        return pl.BlockSpec((1, rows, cols), lambda i: (i, 0, 0))

    block = spec(BR, BC)
    return pl.pallas_call(
        rotate_kernel,
        grid=(count,),
        out_shape=(shaped(weight.shape, jnp.float32),) * 4,
        in_specs=[block] * 3
        + [spec(BR, BR), spec(BC, BC)]
        + [spec(BR, part.shape[2]) for part in gradients],
        out_specs=(block,) * 4,
        compiler_params=pltpu.CompilerParams(vmem_limit_bytes=VMEM_LIMIT),
        cost_estimate=pl.CostEstimate(
            flops=4 * count * BR * BC * (BR + BC),
            bytes_accessed=count * 2 * MIB,
            transcendentals=0,
        ),
    )(weight, moment, second, left, right, *gradients)


def adam(weight, gradient, moment, second, step_rate):
    moment_new = beta_one * moment + (1.0 - beta_one) * gradient
    second_new = beta_two * second + (1.0 - beta_two) * gradient * gradient
    return (
        weight - step_rate * moment_new / (jnp.sqrt(second_new) + adam_eps),
        moment_new,
        second_new,
    )


def piece_places(row_groups, q_groups, kv_groups):
    all_groups = 2 * q_groups + kv_groups
    out_groups = list(range(q_groups)) + list(range(q_groups + kv_groups, all_groups))
    half = row_groups // 2
    numbers = [a * all_groups + b for a in range(half) for b in out_groups] + [None]
    numbers += [a * all_groups + b for a in range(half, row_groups) for b in out_groups]
    numbers += [a * all_groups + q_groups + b for a in range(row_groups) for b in range(kv_groups)]
    places = [0] * (len(numbers) - 1)
    for place, number in enumerate(numbers):
        if number is not None:
            places[number] = place
    return places


def to_partner(array, offset):
    if offset == 0:
        return array
    count = lax.axis_size("shard")
    return lax.ppermute(array, "shard", [(i, i ^ offset) for i in range(count)])


def to_ctx(array, offset):
    count = lax.axis_size("ctx")
    return lax.ppermute(array, "ctx", [(i, i ^ offset) for i in range(count)])


def to_chip(array, offset):
    count = lax.axis_size("ctx")
    return lax.ppermute(array, "ctx", [(i, (i + 2 * offset) % count) for i in range(count)])


def after(value, *others):
    return lax.optimization_barrier((value, others))[0]


def from_chips(array, chips):
    return [array] + [to_chip(array, offset) for offset in range(1, chips)]


def wide(array):
    return array.astype(jnp.float32)


def sum_to_chips(parts):
    total = wide(parts[0])
    for offset in range(1, len(parts)):
        total = total + wide(to_chip(parts[offset], -offset))
    return total


def gather_weights(blocks, chips, members, small):
    parts = [blocks]
    for _ in range(chips - 1):
        parts.append(to_chip(parts[-1], 1))
    pieces, arrays = [], []
    gate = []

    def add(array, offset, first, cut):
        pieces.append((0, offset, first, cut))
        arrays.append(array)
        pieces.append((1, offset, first, cut))
        arrays.append(to_ctx(after(array, *gate), 1))
        return array

    def spread(group, first):
        add(group, 0, first, 0)
        if members == 4 and first > 0:
            by_one, by_two = to_partner(group, 1), to_partner(group, 2)
            add(by_one, 1, first, 0)
            add(by_two, 2, first, 0)
            half = BR // 2
            add(to_partner(by_one[:, :half], 2), 3, first, 0)
            add(to_partner(by_two[:, half:], 1), 3, first, half)
            return [by_one, by_two]
        got = [to_partner(group, offset) for offset in range(1, members)]
        for offset in range(1, members):
            add(got[offset - 1], offset, first, 0)
        return got

    got = [to_partner(blocks, offset) for offset in range(1, members)]
    first = got + parts[1:3]
    gate.append(got[0])
    add(blocks, 0, 0, 0)
    for offset in range(1, members):
        add(got[offset - 1], offset, 0, 0)
    last = list(got)
    if chips > 1:
        last = spread(after(parts[1], *last), 1)
        gate[:] = last
    if chips > 2:
        group = after(jnp.concatenate(parts[2:], axis=0), *last, *small)
        spread(group, 2)
    return first, pieces, arrays


def add_wide(parts):
    total = wide(parts[0])
    for part in parts[1:]:
        total = total + wide(part)
    return total


def sum_members(made, ready, members):
    sums, seen = [], []
    for half in range(2):
        sent, kept = made[2 * half : 2 * half + 2]
        hops, keeps = xor_plan(members, 1 - half)
        count = kept.shape[0] // len(keeps)
        total = wide(kept[:count])
        if members == 4:
            got = to_partner(sent, hops[0])
            got = got if ready is None else after(got, ready)
            total = total + wide(got[:count])
            relay = (wide(kept[count:]) + wide(got[count:])).astype(low_type)
            second = to_partner(relay, keeps[1])
            seen.append(second)
            total = total + wide(second)
        else:
            for place, hop in enumerate(hops):
                total = total + wide(to_partner(sent[place * count : (place + 1) * count], hop))
        sums.append(total.astype(low_type).reshape(count, -1))
    return jnp.concatenate(sums, axis=0), seen


def sum_chips(rows, chip, chips):
    count = rows.shape[1] // chips

    def piece(offset):
        start = lax.rem(chip - offset + chips, chips) * count
        return lax.dynamic_slice_in_dim(rows, start, count, axis=1)

    return [piece(0)] + [to_chip(piece(offset), -offset) for offset in range(1, chips)]


def shards(
    tokens,
    cotangent,
    norm_gains,
    router,
    dense_weight,
    expert_weight,
    routes,
    assign,
    dense_order,
    expert_order,
    dense_moment,
    dense_second,
    dense_left,
    dense_right,
    expert_moment,
    expert_second,
    expert_left,
    expert_right,
    gains_moment,
    gains_second,
    router_moment,
    router_second,
):
    ctx_count = lax.axis_size("ctx")
    shard_count = lax.axis_size("shard")
    chips = ctx_count // 2
    micros, rows, width = tokens.shape
    slots = dense_weight.shape[0]
    span = rows // 2
    row_groups = width // BR
    q_groups = HEADS * HD // BC
    kv_groups = 2 * KVH * HD // BC

    expert_inverse = inverse_order(expert_order)
    ctx = lax.axis_index("ctx").astype(jnp.int32)
    me = jnp.stack([ctx, lax.axis_index("shard").astype(jnp.int32)])
    row_ids = jnp.arange(rows, dtype=jnp.int32)
    all_pos = assign[:, row_ids // span] * span + row_ids % span
    key_pos = all_pos.reshape(1, rows * ctx_count)
    rows_pos = all_pos[ctx].reshape(rows, 1)
    router_pad = jnp.pad(router.astype(low_type), ((0, 0), (0, LANES - shard_count)))

    small = (me, expert_inverse, router_pad, key_pos, rows_pos)
    far, pieces, arrays = gather_weights(
        dense_weight.astype(low_type), chips, shard_count, small
    )
    expert_low = after(expert_weight[0].astype(low_type), *far)
    expert_all = [lax.all_gather(expert_low[:, :UPPER], "ctx", axis=0, tiled=True)]

    lanes = jnp.arange(LANES, dtype=jnp.int32)
    hits = jnp.sum((routes[..., None] == lanes).astype(low_type), axis=2)
    cot_rows = jnp.concatenate([cotangent.astype(low_type), hits], axis=2)
    cot_rows = cot_rows.reshape(micros * rows, width + LANES)
    cot_rows = after(cot_rows, *arrays[::2])
    cot_parts = [to_partner(cot_rows, j) for j in range(shard_count)]

    h1, kv, w_in, w_out = project(
        pieces,
        arrays,
        chips,
        shard_count,
        slots,
        dense_order,
        me,
        [tokens[m] for m in range(micros)],
        norm_gains,
    )
    q = make_queries(h1, w_in, micros)
    h1_other = to_ctx(h1, 1)
    obs, logs, x2s, h2s = [], [], [], []
    kv_all = lax.all_gather(after(kv, expert_all[0]), "ctx", axis=0, tiled=True)
    lower = after(expert_low[:, UPPER:], kv_all, q, cot_parts)
    expert_all.append(lax.all_gather(lower, "ctx", axis=0, tiled=True))
    for m in range(micros):
        query = after(q[m], *(cot_parts if m == 0 else obs[m - 1 : m]))
        ob, log_total, x2, h2 = attend(
            m, query, kv_all, rows_pos, key_pos, tokens[m], norm_gains, w_out
        )
        obs.append(ob)
        logs.append(log_total)
        x2s.append(x2)
        h2s.append(h2)
    ob_others = [to_ctx(ob, 1) for ob in obs]

    h_parts = []
    for m in range(micros):
        own = h2s[m] if m == 0 else after(h2s[m], *h_parts[m - 1])
        h_parts.append([own] + [to_partner(own, j) for j in range(1, shard_count)])
    sent = []
    zs, dgs, dus, cs, xs = [], [], [], [], []
    for m in range(micros):
        here = after(me, h2s[-1], h1_other, *ob_others) if m == 0 else after(me, zs[-1])
        made = run_expert(m, expert_inverse, here, router_pad, h_parts[m], cot_parts, expert_all)
        sent.append(made[:shard_count])
        z, dg, du, c, x = made[shard_count:]
        zs.append(z)
        dgs.append(dg)
        dus.append(du)
        cs.append(c)
        xs.append(x)
    backs = [[to_partner(sent[m][j], j) for j in range(shard_count)] for m in range(micros)]

    expert_terms = outer_blocks(
        after(expert_inverse, *backs[0]), width, (0, 0, 1), [xs, cs], [dgs, dus, zs]
    )
    outs = produce(after(expert_inverse, *expert_terms), expert_all, zs, shard_count, width)
    arrived = [to_partner(outs[j], j) for j in range(min(3, shard_count))]
    dxs, das, dqs, stats = [], [], [], []
    dkv_terms = None
    for m in range(micros):
        here = after(me, outs, backs[-1]) if m == 0 else after(me, dqs[-1], arrived[1:])
        dx, da, do, stat = merge(
            here, x2s[m], cotangent[m], h2s[m], norm_gains, router_pad, w_out, backs[m]
        )
        dq, dkv_terms = attend_back(
            m, q[m], kv_all, rows_pos, key_pos, obs[m], logs[m], do, dkv_terms
        )
        dxs.append(dx)
        das.append(da)
        dqs.append(dq)
        stats.append(stat)

    def other_core(parts):
        return [to_ctx(part, 1) for part in parts]

    da_others, dq_others = other_core(das), other_core(dqs)
    first_term = after(expert_terms[0], *backs[-1])
    expert_sums = [lax.psum_scatter(first_term, "ctx", scatter_dimension=0, tiled=True)]
    dkv = lax.psum_scatter(
        after(dkv_terms, expert_sums[0]), "ctx", scatter_dimension=0, tiled=True
    )
    stat_sum = add_wide(stats)
    early = gradient_pieces(
        shard_count,
        after(me, dkv_terms),
        [([h1, h1_other], dqs + dq_others), (das + da_others, obs + ob_others)],
        [q_groups, q_groups],
        False,
        [stat_sum, to_ctx(stat_sum, 1)],
    )
    h1_turned = early[4]
    parts_back = query_back(after(w_in, early[0]), dqs)
    early_rows, early_seen = sum_members(early[:4], parts_back, shard_count)
    chip = ctx // 2
    late = gradient_pieces(
        shard_count,
        after(me, *early_seen),
        [([h1_turned], [dkv, to_ctx(dkv, 1)])],
        [kv_groups],
        True,
        [],
    )
    last_outs = after(list(outs), early_seen)
    arrived += [to_partner(last_outs[j], j) for j in range(3, shard_count)]
    input_grad, gain_stat = input_back(
        after(tokens, late[0], arrived[3:]), norm_gains, w_in, dxs, parts_back, dkv
    )
    late_rows, late_seen = sum_members(late[:4], input_grad, shard_count)
    late_term = after(expert_terms[1], dkv, early_seen)
    expert_sums.append(lax.psum_scatter(late_term, "ctx", scatter_dimension=0, tiled=True))
    expert_grad, expert_new, expert_moment_new, expert_second_new = rotate(
        expert_weight[0], expert_sums, expert_moment[0], expert_second[0], expert_left[0], expert_right[0]
    )
    all_rows = after(jnp.concatenate([early_rows, late_rows], axis=0), expert_sums)
    all_parts = after(sum_chips(all_rows, chip, chips), expert_new)
    all_sums = add_wide(all_parts).astype(low_type)
    places = jnp.asarray(piece_places(row_groups, q_groups, kv_groups), jnp.int32)[dense_order]
    chosen = (places[:, None] == jnp.arange(all_sums.shape[0])[None, :]).astype(low_type)
    ordered = jnp.dot(chosen, all_sums, preferred_element_type=jnp.float32).astype(low_type)
    devices = ctx_count * shard_count
    piece_width = ordered.shape[1]
    stat_place = row_groups // 2 * 2 * q_groups
    gain_parts = gain_stat[:1].astype(low_type).reshape(-1, piece_width)
    stat_parts = jnp.concatenate([all_sums[stat_place : stat_place + 1], gain_parts], axis=0)
    extra = stat_parts.shape[0]
    ordered = jnp.concatenate(
        [
            ordered.reshape(devices, slots, piece_width),
            jnp.broadcast_to(stat_parts, (devices, extra, piece_width)),
        ],
        axis=1,
    ).reshape(devices * 2, (slots + extra) * piece_width // 2)
    ordered = lax.all_to_all(ordered, ("ctx", "shard"), split_axis=0, concat_axis=0, tiled=True)
    ordered = ordered.reshape(devices, slots + extra, piece_width)
    span = BR // (shard_count * chips)
    stat_block = ordered[:, slots].reshape(chips, 2, shard_count, span, LANES)
    stat_rows = wide(stat_block.transpose(2, 0, 3, 1, 4).reshape(BR * BC)[: (shard_count + 1) * width])
    stat_rows = stat_rows.reshape(shard_count + 1, width)
    gain_row = jnp.sum(wide(ordered[:, slots + 1 :]), axis=0).reshape(width)
    ordered = ordered[:, :slots].reshape(
        chips, 2, shard_count, slots, BR // (shard_count * chips), LANES
    )
    dense_sum = ordered.transpose(3, 2, 0, 4, 1, 5).reshape(slots, BR, BC)
    router_grad = stat_rows[:shard_count].T
    gains_grad = jnp.stack([gain_row, stat_rows[shard_count]])

    dense_grad, dense_new, dense_moment_new, dense_second_new = rotate(
        dense_weight, [dense_sum], dense_moment, dense_second, dense_left, dense_right
    )
    outputs = []
    for m in range(micros):
        total = x2s[m]
        for part in after(arrived, expert_new):
            total = total + wide(part[m * rows : (m + 1) * rows])
        outputs.append(total)

    gains_new, gains_moment_new, gains_second_new = adam(
        norm_gains, gains_grad, gains_moment, gains_second, gain_rate
    )
    router_new, router_moment_new, router_second_new = adam(
        router, router_grad, router_moment, router_second, rate
    )
    return (
        jnp.stack(outputs),
        input_grad,
        dense_grad,
        dense_new,
        dense_moment_new,
        dense_second_new,
        expert_grad[None],
        expert_new[None],
        expert_moment_new[None],
        expert_second_new[None],
        gains_grad,
        gains_new,
        gains_moment_new,
        gains_second_new,
        router_grad,
        router_new,
        router_moment_new,
        router_second_new,
    )


def solution(mesh):
    rows_spec = P("shard", "ctx", None)
    dense_spec = P(("ctx", "shard"), None, None)
    expert_spec = P("shard", "ctx", None, None)
    in_specs = (
        (rows_spec, rows_spec, P(), P(), dense_spec, expert_spec, rows_spec, P(), P(), P())
        + (dense_spec,) * 4
        + (expert_spec,) * 4
        + (P(),) * 4
    )
    out_specs = (rows_spec,) * 2 + (dense_spec,) * 4 + (expert_spec,) * 4 + (P(),) * 8
    return jax.shard_map(shards, mesh=mesh, in_specs=in_specs, out_specs=out_specs, check_vma=False)
```

```python
import functools

import jax
import jax.numpy as jnp
from jax import lax
from jax.experimental import pallas as pl
from jax.experimental.pallas import tpu as pltpu
from jax.sharding import PartitionSpec as P

HEADS = 24
KVH = 8
HD = 64
FF = 1024
BR = 192
BC = 256
LANES = 128
UPPER = 128

norm_eps = 1e-06
beta_one = 0.9
beta_two = 0.95
rate = 0.01
gain_rate = 0.5
adam_eps = 1e-08
masked_score = -1e30
low_type = jnp.bfloat16
MIB = 1 << 20
VMEM_LIMIT = 60 * MIB

NN = (((1,), (0,)), ((), ()))
NT = (((1,), (1,)), ((), ()))
TN = (((0,), (0,)), ((), ()))

in_vmem = pl.BlockSpec(memory_space=pltpu.VMEM)
in_smem = pl.BlockSpec(memory_space=pltpu.SMEM)
in_any = pl.BlockSpec(memory_space=pl.ANY)


def dot(left_side, right_side, dims=NN):
    return lax.dot_general(left_side, right_side, dims, preferred_element_type=jnp.float32)


def call(kernel, out_shapes, in_specs, out_specs, scratch, flops, moved):
    return pl.pallas_call(
        kernel,
        out_shape=out_shapes,
        in_specs=in_specs,
        out_specs=out_specs,
        scratch_shapes=scratch,
        compiler_params=pltpu.CompilerParams(vmem_limit_bytes=VMEM_LIMIT),
        cost_estimate=pl.CostEstimate(flops=flops, bytes_accessed=moved, transcendentals=0),
    )


def shaped(dims, kind):
    return jax.ShapeDtypeStruct(dims, kind)


def inverse_order(slot_order):
    count = slot_order.shape[0]
    numbers = jnp.arange(count, dtype=jnp.int32)
    return jnp.sum(
        jnp.where(slot_order[None, :] == numbers[:, None], numbers[None, :], 0), axis=1
    ).astype(jnp.int32)


def wait_bytes(landed, semaphore):
    pltpu.make_async_copy(landed, landed, semaphore).wait()


def unit_rows(rows, gain):
    inverse = lax.rsqrt(jnp.mean(rows * rows, axis=-1, keepdims=True) + norm_eps)
    return rows * inverse * gain, inverse


def unit_back(rows, gain, inverse, gradient):
    unit = rows * inverse
    scaled = gradient * gain
    inner = jnp.mean(scaled * unit, axis=-1, keepdims=True)
    return inverse * (scaled - unit * inner), jnp.sum(gradient * unit, axis=0, keepdims=True)


def lane_ids(dims):
    return lax.broadcasted_iota(jnp.int32, dims, len(dims) - 1)


def half_turn(tile):
    return pltpu.roll(tile, HD, 1)


def stack_heads(ref, pair, scale=None):
    base = pair * (3 * LANES)
    tiles = [
        ref[:, pl.ds(pl.multiple_of(base + LANES * t, LANES), LANES)].astype(jnp.float32)
        for t in range(3)
    ]
    if scale is not None:
        tiles = [t * scale for t in tiles]
    lower = lane_ids(tiles[0].shape) < HD
    first = [tiles[0], half_turn(tiles[0]), tiles[1]]
    second = [tiles[1], half_turn(tiles[2]), tiles[2]]
    return (
        jnp.concatenate([jnp.where(lower, t, 0.0) for t in first], axis=0),
        jnp.concatenate([jnp.where(lower, 0.0, t) for t in second], axis=0),
    )


def unstack_heads(ref, pair, first, second):
    rows = first.shape[0] // 3
    base = pair * (3 * LANES)
    lower = lane_ids((rows, LANES)) < HD
    tiles = (
        jnp.where(lower, first[:rows], half_turn(first[rows : 2 * rows])),
        jnp.where(lower, first[2 * rows :], second[:rows]),
        jnp.where(lower, half_turn(second[rows : 2 * rows]), second[2 * rows :]),
    )
    for t in range(3):
        ref[:, pl.ds(pl.multiple_of(base + LANES * t, LANES), LANES)] = tiles[t].astype(ref.dtype)


def project_kernel(
    pieces, chips, members, slots, all_groups, micros, order_ref, me_ref, *refs
):
    x_refs = refs[:micros]
    gain_ref = refs[micros]
    piece_refs = refs[micros + 1 : micros + 1 + len(pieces)]
    refs = refs[micros + 1 + len(pieces) :]
    h_ref = refs[0]
    kv_ref, win_ref, wout_ref, held, held_out, sems, out_sems = refs[1:]
    groups = held.shape[1] // BC
    kv_groups = kv_ref.shape[-1] // BC
    rows = x_refs[0].shape[0]
    ctx, shard = me_ref[0], me_ref[1]
    chip, core = lax.div(ctx, 2), lax.rem(ctx, 2)

    for ref, (other_core, offset, first, cut) in zip(piece_refs, pieces):

        @pl.loop(0, ref.shape[0])
        def _(i):
            source = lax.rem(chip - (first + lax.div(i, slots)) + chips, chips) * 2
            source = source + jnp.bitwise_xor(core, other_core)
            source = source * members + jnp.bitwise_xor(shard, offset)
            number = order_ref[source * slots + lax.rem(i, slots)]
            a, b = lax.div(number, all_groups), lax.rem(number, all_groups)
            down = pl.ds(pl.multiple_of(a * BR + cut, 32), ref.shape[1])

            @pl.when(b < groups)
            def _():
                across = pl.ds(pl.multiple_of(b * BC, BC), BC)
                pltpu.make_async_copy(ref.at[i], held.at[down, across], sems.at[b]).start()

            @pl.when(b >= groups)
            def _():
                across = pl.ds(pl.multiple_of((b - groups) * BC, BC), BC)
                pltpu.make_async_copy(ref.at[i], held_out.at[down, across], sems.at[groups]).start()

    for m in range(micros):
        h_ref[m * rows : (m + 1) * rows, :] = unit_rows(x_refs[m][...], gain_ref[0:1])[0].astype(
            low_type
        )
    q_groups = groups - kv_groups

    @pl.loop(0, groups)
    def _(b):
        across = pl.ds(pl.multiple_of(b * BC, BC), BC)
        wait_bytes(held.at[:, across], sems.at[b])

    wait_bytes(held_out, sems.at[groups])
    copies = [
        pltpu.make_async_copy(held, win_ref, out_sems.at[0]),
        pltpu.make_async_copy(held_out, wout_ref, out_sems.at[1]),
    ]
    for copy in copies:
        copy.start()

    @pl.loop(0, kv_groups)
    def _(b):
        across = pl.ds(pl.multiple_of((q_groups + b) * BC, BC), BC)
        made = dot(h_ref[...], held[:, across]).astype(low_type)
        kv_ref[:, pl.ds(pl.multiple_of(b * BC, BC), BC)] = made

    for copy in copies:
        copy.wait()


def project(pieces, arrays, chips, members, slots, order, me, xs, gains):
    micros = len(xs)
    rows, width = xs[0].shape
    in_width = (HEADS + 2 * KVH) * HD
    out_width = HEADS * HD
    kv_width = 2 * KVH * HD
    return call(
        functools.partial(
            project_kernel, pieces, chips, members, slots, (in_width + out_width) // BC, micros
        ),
        tuple(
            [shaped((micros * rows, width), low_type)]
            + [shaped((micros * rows, kv_width), low_type)]
            + [shaped((width, in_width), low_type), shaped((width, out_width), low_type)]
        ),
        [in_smem, in_smem] + [in_vmem] * (micros + 1) + [in_any] * len(arrays),
        (in_vmem, in_vmem, in_any, in_any),
        [
            pltpu.VMEM((width, in_width), low_type),
            pltpu.VMEM((width, out_width), low_type),
            pltpu.SemaphoreType.DMA((in_width // BC + 1,)),
            pltpu.SemaphoreType.DMA((2,)),
        ],
        2 * micros * rows * width * kv_width,
        4 * width * (in_width + out_width),
    )(order, me, *xs, gains, *arrays)


def query_kernel(h_ref, w_ref, *refs):
    q_refs = refs[:-2]
    held, sems = refs[-2:]
    groups = held.shape[1] // BC
    rows = q_refs[0].shape[0]

    def copy(b):
        across = pl.ds(pl.multiple_of(b * BC, BC), BC)
        return pltpu.make_async_copy(w_ref.at[:, across], held.at[:, across], sems.at[b])

    @pl.loop(0, groups)
    def _(b):
        copy(b).start()

    @pl.loop(0, groups)
    def _(b):
        copy(b).wait()
        across = pl.ds(pl.multiple_of(b * BC, BC), BC)
        made = dot(h_ref[...], held[:, across]).astype(low_type)
        for m, ref in enumerate(q_refs):
            ref[:, across] = made[m * rows : (m + 1) * rows]


def make_queries(h, w, micros):
    total, width = h.shape
    q_width = HEADS * HD
    return call(
        query_kernel,
        tuple([shaped((total // micros, q_width), low_type)] * micros),
        [in_vmem, in_any],
        tuple([in_vmem] * micros),
        [pltpu.VMEM((width, q_width), low_type), pltpu.SemaphoreType.DMA((q_width // BC,))],
        2 * total * width * q_width,
        2 * width * q_width,
    )(h, w)


def load_keys(kv_ref, micro, rows, held, sem):
    count = held.shape[0] // rows
    span = kv_ref.shape[0] // count

    @pl.loop(0, count)
    def _(i):
        pltpu.make_async_copy(
            kv_ref.at[pl.ds(pl.multiple_of(i * span + micro * rows, 16), rows)],
            held.at[pl.ds(pl.multiple_of(i * rows, 16), rows)],
            sem,
        ).start()


def attend_kernel(
    micro, q_ref, rpos_ref, kpos_ref, x_ref, gain_ref, w_ref, all_ref,
    ob_ref, log_ref, x2_ref, h2_ref, bias, kv_ref, held, sems,
):
    rows = q_ref.shape[0]
    load_keys(all_ref, micro, rows, kv_ref, sems.at[0])
    pltpu.make_async_copy(w_ref, held, sems.at[1]).start()
    bias[...] = jnp.where(kpos_ref[...] <= rpos_ref[...], 0.0, masked_score)
    log_ref[...] = jnp.zeros_like(log_ref)
    length = kv_ref.shape[0]
    wait_bytes(kv_ref, sems.at[0])

    @pl.loop(0, KVH // 2)
    def _(pair):
        lane = pl.multiple_of(pair * LANES, LANES)
        keys = kv_ref[:, pl.ds(lane, LANES)]
        values = kv_ref[:, pl.ds(pl.multiple_of(lane + KVH * HD, LANES), LANES)]
        stacked = stack_heads(q_ref, pair, HD**-0.5)
        mixed = []
        for part in range(2):
            scores = dot(stacked[part].astype(low_type), keys, NT)
            scores = (scores.reshape(3, rows, length) + bias[...][None]).reshape(3 * rows, length)
            largest = jnp.max(scores, axis=-1, keepdims=True)
            raised = jnp.exp(scores - largest)
            summed = jnp.sum(raised, axis=-1, keepdims=True)
            mixed.append(dot(raised.astype(low_type), values) / summed)
            log_ref[...] = jnp.where(
                lane_ids(log_ref.shape) == 2 * pair + part, largest + jnp.log(summed), log_ref[...]
            )
        unstack_heads(ob_ref, pair, mixed[0], mixed[1])

    wait_bytes(held, sems.at[1])
    for n in range(held.shape[0] // BC):
        cut = slice(n * BC, (n + 1) * BC)
        x2_ref[:, cut] = x_ref[:, cut] + dot(ob_ref[...], held[cut, :], NT)
    h2_ref[...] = unit_rows(x2_ref[...], gain_ref[1:2])[0].astype(low_type)


def attend(micro, q, kv, rows_pos, key_pos, x, gains, w):
    rows, width = q.shape
    length = key_pos.shape[1]
    model = x.shape[1]
    return call(
        functools.partial(attend_kernel, micro),
        (
            shaped((rows, width), low_type),
            shaped((3 * rows, LANES), jnp.float32),
            shaped((rows, model), jnp.float32),
            shaped((rows, model), low_type),
        ),
        [in_vmem] * 5 + [in_any] * 2,
        (in_vmem,) * 4,
        [
            pltpu.VMEM((rows, length), jnp.float32),
            pltpu.VMEM((length, kv.shape[1]), low_type),
            pltpu.VMEM((model, width), low_type),
            pltpu.SemaphoreType.DMA((2,)),
        ],
        16 * rows * length * width,
        8 * MIB,
    )(q, rows_pos, key_pos, x, gains, w, kv)


def router_parts(h2, router, experts):
    logits = dot(h2, router)
    logits = jnp.where(lane_ids(logits.shape) < experts, logits, masked_score)
    raised = jnp.exp(logits - jnp.max(logits, axis=-1, keepdims=True))
    return raised / jnp.sum(raised, axis=-1, keepdims=True)


def expert_kernel(sources, micro, order_ref, me_ref, router_ref, *refs):
    h_parts = refs[:sources]
    c_parts = refs[sources : 2 * sources]
    w_refs = refs[2 * sources : 2 * sources + 2]
    outs = refs[2 * sources + 2 :]
    back_refs = outs[:sources]
    z_ref, dg_ref, du_ref, cs, xs_ref = outs[sources : sources + 5]
    held, chance, load_sem, w_sems = outs[sources + 5 :]
    rows, width = h_parts[0].shape
    row_groups = width // BR
    col_groups = FF // BC
    for j in range(sources):
        pltpu.make_async_copy(h_parts[j], xs_ref.at[pl.ds(j * rows, rows)], load_sem.at[0]).start()
        pltpu.make_async_copy(
            c_parts[j].at[pl.ds(micro * rows, rows)], cs.at[pl.ds(j * rows, rows)], load_sem.at[1]
        ).start()
    for b in range(col_groups):

        @pl.loop(0, row_groups)
        def _(a):
            for k in range(3):
                slot = order_ref[(k * row_groups + a) * col_groups + b]
                for start, ref in zip((0, UPPER), w_refs):
                    down = pl.ds(pl.multiple_of(a * BR + start, 64), ref.shape[1])
                    pltpu.make_async_copy(
                        ref.at[slot], held.at[k, down, pl.ds(b * BC, BC)], w_sems.at[b]
                    ).start()

    wait_bytes(xs_ref, load_sem.at[0])
    wait_bytes(cs, load_sem.at[1])
    me = me_ref[1]
    probs = router_parts(xs_ref[...], router_ref[...], sources)
    hits = cs[:, width:].astype(jnp.float32)
    mine = lane_ids(hits.shape) == me
    hit = jnp.sum(jnp.where(mine, hits, 0.0), axis=-1, keepdims=True)
    weight = jnp.sum(jnp.where(mine, probs, 0.0), axis=-1, keepdims=True) * hit
    chance[...] = jnp.zeros_like(chance)

    @pl.loop(0, col_groups)
    def _(b):
        cut = pl.ds(pl.multiple_of(b * BC, BC), BC)
        wait_bytes(held.at[:, :, cut], w_sems.at[b])
        gate = dot(xs_ref[...], held[0, :, cut])
        up = dot(xs_ref[...], held[1, :, cut])
        down = dot(cs[:, :width], held[2, :, cut])
        sig = jax.nn.sigmoid(gate)
        act = gate * sig
        hidden = act * up
        chance[...] += jnp.sum(down * hidden, axis=-1, keepdims=True)
        z_ref[:, cut] = (hidden * weight).astype(low_type)
        down = down * weight
        dg_ref[:, cut] = (down * up * (sig + act * (1.0 - sig))).astype(low_type)
        du_ref[:, cut] = (down * act).astype(low_type)

    for n in range(width // BC):
        cut = slice(n * BC, (n + 1) * BC)
        back = dot(dg_ref[...], held[0, cut, :], NT) + dot(du_ref[...], held[1, cut, :], NT)
        for j in range(sources):
            back_refs[j][:, cut] = back[j * rows : (j + 1) * rows].astype(low_type)
    told = chance[...] * hit
    high_part = told.astype(low_type)
    low_part = (told - high_part.astype(jnp.float32)).astype(low_type)
    lanes = lane_ids((sources * rows, LANES))
    tail = jnp.where(lanes == 0, high_part, jnp.where(lanes == 1, low_part, jnp.zeros_like(low_part)))
    for j in range(sources):
        back_refs[j][:, width:] = tail[j * rows : (j + 1) * rows]


def run_expert(micro, order, me, router, h_parts, c_parts, ws):
    sources = len(h_parts)
    rows, width = h_parts[0].shape
    total = sources * rows
    return call(
        functools.partial(expert_kernel, sources, micro),
        tuple(
            [shaped((rows, width + LANES), low_type)] * sources
            + [shaped((total, FF), low_type)] * 3
            + [shaped((total, width + LANES), low_type), shaped((total, width), low_type)]
        ),
        [in_smem, in_smem, in_vmem] + [in_any] * (2 * sources + 2),
        tuple([in_vmem] * (sources + 5)),
        [
            pltpu.VMEM((3, width, FF), low_type),
            pltpu.VMEM((total, 1), jnp.float32),
            pltpu.SemaphoreType.DMA((2,)),
            pltpu.SemaphoreType.DMA((FF // BC,)),
        ],
        10 * total * width * FF,
        20 * MIB,
    )(order, me, router, *h_parts, *c_parts, *ws)


def produce_kernel(sources, order_ref, upper_ref, lower_ref, *refs):
    out_refs = refs[-3 - sources : -3]
    z_refs = refs[: -3 - sources]
    zs, held, sem = refs[-3:]
    width = held.shape[0]
    total = z_refs[0].shape[0]
    rows = total // sources
    row_groups, col_groups = width // BR, FF // BC

    @pl.loop(0, row_groups)
    def _(a):
        for b in range(col_groups):
            slot = order_ref[(2 * row_groups + a) * col_groups + b]
            for start, ref in zip((0, UPPER), (upper_ref, lower_ref)):
                down = pl.ds(pl.multiple_of(a * BR + start, 64), ref.shape[1])
                pltpu.make_async_copy(
                    ref.at[slot], held.at[down, pl.ds(b * BC, BC)], sem
                ).start()

    for m, z_ref in enumerate(z_refs):
        zs[m * total : (m + 1) * total] = z_ref[...]
    wait_bytes(held, sem)
    for n in range(width // BC):
        cut = slice(n * BC, (n + 1) * BC)
        made = dot(zs[...], held[cut, :], NT).astype(low_type)
        for m in range(len(z_refs)):
            for j in range(sources):
                start = m * total + j * rows
                out_refs[j][m * rows : (m + 1) * rows, cut] = made[start : start + rows]


def produce(order, ws, zs, sources, width):
    micros = len(zs)
    total = zs[0].shape[0]
    return call(
        functools.partial(produce_kernel, sources),
        tuple([shaped((micros * total // sources, width), low_type)] * sources),
        [in_smem, in_any, in_any] + [in_vmem] * micros,
        tuple([in_vmem] * sources),
        [
            pltpu.VMEM((micros * total, FF), low_type),
            pltpu.VMEM((width, FF), low_type),
            pltpu.SemaphoreType.DMA,
        ],
        2 * micros * total * width * FF,
        8 * MIB,
    )(order, *ws, *zs)


def outer_kernel(groups, col_groups, order_ref, *refs):
    micros = len(refs[:-5]) // (len(groups) + 2)
    lefts = [refs[i * micros : (i + 1) * micros] for i in range(2)]
    rights = [refs[(2 + i) * micros : (3 + i) * micros] for i in range(len(groups))]
    out_refs, (turned, stage, sems) = refs[-5:-3], refs[-3:]
    rows = rights[0][0].shape[0]
    width = turned.shape[1]
    span = 2 * BR
    for side in range(2):
        for m in range(micros):
            for r in range(0, rows, LANES):
                part = lefts[side][m][r : r + LANES, :width]
                turned[side, :, m * rows + r : m * rows + r + LANES] = part.T
    row_groups = width // BR
    steps = [(k, p) for k in range(len(groups)) for p in range(width // span)]
    for n, (k, p) in enumerate(steps):
        slot = n % 2
        if n >= 2:
            wait_bytes(stage.at[slot], sems.at[slot])
        cut = slice(p * span, (p + 1) * span)
        made = 0.0
        for m in range(micros):
            left = turned[groups[k], cut, m * rows : (m + 1) * rows]
            made = made + dot(left, rights[k][m][...])
        stage[slot] = made.astype(low_type)
        for half in range(2):
            for b in range(col_groups):
                number = (k * row_groups + 2 * p + half) * col_groups + b
                place = order_ref[number]
                for side in range(2):
                    pltpu.make_async_copy(
                        stage.at[
                            slot, pl.ds(half * BR, BR), pl.ds(b * BC + side * LANES, LANES)
                        ],
                        out_refs[side].at[place],
                        sems.at[slot],
                    ).start()
    for slot in range(2):
        wait_bytes(stage.at[slot], sems.at[slot])


def outer_blocks(order, width, groups, lefts, rights):
    flat = [part for group in lefts + rights for part in group]
    rows = sum(part.shape[0] for part in rights[0])
    cols = rights[0][0].shape[1]
    blocks = len(groups) * width * cols // (BR * BC)
    return call(
        functools.partial(outer_kernel, groups, cols // BC),
        (shaped((blocks, BR, LANES), low_type),) * 2,
        [in_smem] + [in_vmem] * len(flat),
        (in_any,) * 2,
        [
            pltpu.VMEM((2, width, rows), low_type),
            pltpu.VMEM((2, 2 * BR, cols), low_type),
            pltpu.SemaphoreType.DMA((2,)),
        ],
        2 * rows * blocks * BR * BC,
        blocks * BR * BC * 2 + sum(f.size * 2 for f in flat),
    )(order, *flat)


def xor_plan(members, offset):
    if members != 4:
        return list(range(1, members)), [0]
    first = 1 if offset % 2 else 2
    return [first, 3], [0, 3 - first]


def pieces_kernel(members, counts, cols, turned_first, me_ref, *refs):
    lists = []
    for left_count, right_count in counts:
        lists.append((refs[:left_count], refs[left_count : left_count + right_count]))
        refs = refs[left_count + right_count :]
    stat_refs = refs[: len(refs) - 8] if turned_first else refs[: len(refs) - 10]
    refs = refs[len(stat_refs) :]
    outs, refs = refs[:4], refs[4:]
    extra = refs[0] if not turned_first else None
    turned, rights, stage, sems = refs[0 if turned_first else 1 :][:4]
    ctx, shard = me_ref[0], me_ref[1]
    core = lax.rem(ctx, 2)
    total = turned.shape[2]
    row_groups = turned.shape[1] // BR
    base = 0
    for g, (_, parts) in enumerate(lists):
        start = 0
        for part in parts:
            count = part.shape[0]
            for b in range(cols[g]):
                lane = pl.multiple_of(b * BC + core * LANES, LANES)
                pltpu.make_async_copy(
                    part.at[:, pl.ds(lane, LANES)],
                    rights.at[pl.ds(start, count), pl.ds((base + b) * LANES, LANES)],
                    sems.at[g],
                ).start()
            start += count
        base += cols[g]
    for g, (parts, _) in enumerate(lists):
        if g == 0 and turned_first:
            turned[0] = parts[0][...]
            continue
        start = 0
        for part in parts:
            for r in range(0, part.shape[0], LANES):
                turned[g, :, start : start + LANES] = part[r : r + LANES, :].T
                start += LANES
    if extra is not None:
        extra[...] = turned[0]
    all_cols = sum(cols)
    half_blocks = row_groups // 2 * all_cols
    counts = [half_blocks + (1 if stat_refs else 0), half_blocks]
    span = BR // members
    if stat_refs:
        block = refs[-1]
        block[...] = jnp.zeros_like(block)
        up = stat_refs[0].shape[0] - 8
        for r, row in enumerate(list(range(members)) + [up]):
            total_row = sum(ref[row : row + 1, :] for ref in stat_refs)
            for t in range(total_row.shape[1] // BC):
                place = r * (total_row.shape[1] // BC) + t
                block[place : place + 1, :] = total_row[:, t * BC : (t + 1) * BC]
        lane = pl.multiple_of(core * LANES, LANES)
        for out, hops in zip(outs[:2], xor_plan(members, 1)):
            for place, hop in enumerate(hops):
                down = pl.multiple_of(jnp.bitwise_xor(shard, hop) * span, 8)
                out[place * counts[0] + half_blocks] = block[
                    pl.ds(down, span), pl.ds(lane, LANES)
                ].astype(low_type)
    base = 0
    for g in range(len(lists)):
        wide_cols = cols[g] * LANES
        wait_bytes(rights.at[:, pl.ds(base * LANES, wide_cols)], sems.at[g])
        for a in range(row_groups):
            made = dot(
                turned[g, a * BR : (a + 1) * BR, :],
                rights[:, base * LANES : base * LANES + wide_cols],
            )
            stage[a % 2, :, :wide_cols] = made.astype(stage.dtype)
            half = a // (row_groups // 2)
            first = (a % (row_groups // 2)) * all_cols + base
            for out, hops in zip(outs[2 * half : 2 * half + 2], xor_plan(members, 1 - half)):
                for place, hop in enumerate(hops):
                    down = pl.multiple_of(jnp.bitwise_xor(shard, hop) * span, 16 if span % 16 == 0 else 8)
                    for b in range(cols[g]):
                        out[place * counts[half] + first + b] = stage[
                            a % 2, pl.ds(down, span), b * LANES : (b + 1) * LANES
                        ].astype(low_type)
        base += cols[g]


def gradient_pieces(members, me, groups, cols, turned_first, stats):
    counts = tuple((len(left), len(right)) for left, right in groups)
    flat = [part for left, right in groups for part in left + right]
    total = sum(part.shape[0] for part in groups[0][1])
    width = groups[0][0][0].shape[0 if turned_first else 1]
    row_groups = width // BR
    half_blocks = row_groups // 2 * sum(cols)
    span = BR // members
    stage_type = jnp.float32 if span % 16 else low_type
    outs = []
    for half in range(2):
        count = half_blocks + (1 if stats and half == 0 else 0)
        for hops in xor_plan(members, 1 - half):
            outs.append(shaped((len(hops) * count, span, LANES), low_type))
    out_specs = [in_vmem] * 4
    if not turned_first:
        outs.append(shaped((width, total), low_type))
        out_specs.append(in_vmem)
    in_specs = [in_smem]
    for left, right in groups:
        in_specs += [in_vmem] * len(left) + [in_any] * len(right)
    in_specs += [in_vmem] * len(stats)
    return call(
        functools.partial(pieces_kernel, members, counts, tuple(cols), turned_first),
        tuple(outs),
        in_specs,
        tuple(out_specs),
        [
            pltpu.VMEM((len(groups), width, total), low_type),
            pltpu.VMEM((total, sum(cols) * LANES), low_type),
            pltpu.VMEM((2, BR, max(cols) * LANES), stage_type),
            pltpu.SemaphoreType.DMA((len(groups),)),
        ]
        + ([pltpu.VMEM((BR, BC), jnp.float32)] if stats else []),
        2 * total * width * sum(cols) * LANES,
        16 * MIB,
    )(me, *flat, *stats)


def merge_kernel(
    sources, me_ref, x2_ref, cot_ref, h2_ref, gain_ref, router_ref, w_ref, *refs
):
    back_refs = refs[:sources]
    dx_ref, da_ref, do_ref, stat_ref, held, sem = refs[sources:]
    rows, width = x2_ref.shape
    pltpu.make_async_copy(w_ref, held, sem).start()
    lanes = lane_ids((rows, LANES))
    prob_grad = jnp.zeros((rows, LANES), jnp.float32)
    gathered = jnp.zeros((rows, width), jnp.float32)
    for j in range(sources):
        tail = back_refs[j][:, width:].astype(jnp.float32)
        told = jnp.sum(tail, axis=-1, keepdims=True)
        expert = jnp.bitwise_xor(me_ref[1], j)
        prob_grad = prob_grad + jnp.where(lanes == expert, told, 0.0)
        gathered = gathered + back_refs[j][:, :width].astype(jnp.float32)
    h2 = h2_ref[...]
    probs = router_parts(h2, router_ref[...], sources)
    logit_grad = probs * (prob_grad - jnp.sum(probs * prob_grad, axis=-1, keepdims=True))
    high_part = logit_grad.astype(low_type)
    low_part = (logit_grad - high_part.astype(jnp.float32)).astype(low_type)
    router_grad = dot(high_part, h2, TN) + dot(low_part, h2, TN)
    gathered = gathered + dot(high_part, router_ref[...], NT) + dot(low_part, router_ref[...], NT)
    x2 = x2_ref[...]
    inverse = lax.rsqrt(jnp.mean(x2 * x2, axis=-1, keepdims=True) + norm_eps)
    moe_grad, gain_grad = unit_back(x2, gain_ref[1:2], inverse, gathered)
    after = cot_ref[...] + moe_grad
    dx_ref[...] = after
    da_ref[...] = after.astype(low_type)
    experts_up = stat_ref.shape[0] - 8
    stat_ref[:experts_up] = router_grad[:experts_up]
    stat_ref[experts_up:] = jnp.broadcast_to(gain_grad, (8, width))
    wait_bytes(held, sem)
    for n in range(held.shape[1] // BC):
        cut = slice(n * BC, (n + 1) * BC)
        do_ref[:, cut] = dot(da_ref[...], held[:, cut]).astype(low_type)


def merge(me, x2, cot, h2, gains, router, w, backs):
    rows, width = x2.shape
    sources = len(backs)
    experts_up = -(-sources // 8) * 8
    return call(
        functools.partial(merge_kernel, sources),
        (
            shaped((rows, width), jnp.float32),
            shaped((rows, width), low_type),
            shaped((rows, HEADS * HD), low_type),
            shaped((experts_up + 8, width), jnp.float32),
        ),
        [in_smem] + [in_vmem] * 5 + [in_any] + [in_vmem] * sources,
        (in_vmem,) * 4,
        [pltpu.VMEM((width, HEADS * HD), low_type), pltpu.SemaphoreType.DMA],
        2 * rows * width * HEADS * HD,
        10 * MIB,
    )(me, x2, cot, h2, gains, router, w, *backs)


def attend_back_kernel(
    micro, q_ref, rpos_ref, kpos_ref, ob_ref, log_ref, do_ref, all_ref, *refs
):
    dq_ref, out_ref, bias, kv_ref, grad_ref, sems = refs[-6:]
    rows = q_ref.shape[0]
    load_keys(all_ref, micro, rows, kv_ref, sems.at[0])
    length = kv_ref.shape[0]
    bias[...] = jnp.where(kpos_ref[...] <= rpos_ref[...], 0.0, masked_score)
    wait_bytes(kv_ref, sems.at[0])

    @pl.loop(0, KVH // 2)
    def _(pair):
        lane = pl.multiple_of(pair * LANES, LANES)
        value_lane = pl.multiple_of(lane + KVH * HD, LANES)
        keys = kv_ref[:, pl.ds(lane, LANES)]
        values = kv_ref[:, pl.ds(value_lane, LANES)]
        queries = stack_heads(q_ref, pair, HD**-0.5)
        grads = stack_heads(do_ref, pair)
        mixes = stack_heads(ob_ref, pair)
        query_grads = []
        key_grad = value_grad = None
        for part in range(2):
            query = queries[part].astype(low_type)
            grad = grads[part].astype(low_type)
            log_total = jnp.sum(
                jnp.where(lane_ids(log_ref.shape) == 2 * pair + part, log_ref[...], 0.0),
                axis=-1,
                keepdims=True,
            )
            delta = jnp.sum(grads[part] * mixes[part], axis=-1, keepdims=True)
            scores = dot(query, keys, NT)
            scores = (scores.reshape(3, rows, length) + bias[...][None]).reshape(3 * rows, length)
            chance = jnp.exp(scores - log_total)
            prob_grad = dot(grad, values, NT)
            score_grad = (chance * (prob_grad - delta)).astype(low_type)
            value_term = dot(chance.astype(low_type), grad, TN)
            key_term = dot(score_grad, query, TN)
            key_grad = key_term if part == 0 else key_grad + key_term
            value_grad = value_term if part == 0 else value_grad + value_term
            query_grads.append(dot(score_grad, keys) * HD**-0.5)
        unstack_heads(dq_ref, pair, query_grads[0], query_grads[1])
        grad_ref[:, pl.ds(lane, LANES)] = key_grad.astype(low_type)
        grad_ref[:, pl.ds(value_lane, LANES)] = value_grad.astype(low_type)

    count = length // rows
    span = out_ref.shape[0] // count

    @pl.loop(0, count)
    def _(i):
        pltpu.make_async_copy(
            grad_ref.at[pl.ds(pl.multiple_of(i * rows, 16), rows)],
            out_ref.at[pl.ds(pl.multiple_of(i * span + micro * rows, 16), rows)],
            sems.at[1],
        ).start()

    wait_bytes(grad_ref, sems.at[1])


def attend_back(micro, q, kv, rows_pos, key_pos, ob, log_total, do, shared):
    rows, width = q.shape
    length = key_pos.shape[1]
    operands = [q, rows_pos, key_pos, ob, log_total, do, kv]
    in_specs = [in_vmem] * 6 + [in_any]
    aliases = {}
    if shared is not None:
        aliases = {len(operands): 1}
        operands.append(shared)
        in_specs.append(in_any)
    return pl.pallas_call(
        functools.partial(attend_back_kernel, micro),
        out_shape=(shaped((rows, width), low_type), shaped(kv.shape, low_type)),
        in_specs=in_specs,
        out_specs=(in_vmem, in_any),
        scratch_shapes=[
            pltpu.VMEM((rows, length), jnp.float32),
            pltpu.VMEM((length, kv.shape[1]), low_type),
            pltpu.VMEM((length, kv.shape[1]), low_type),
            pltpu.SemaphoreType.DMA((2,)),
        ],
        input_output_aliases=aliases,
        compiler_params=pltpu.CompilerParams(vmem_limit_bytes=VMEM_LIMIT),
        cost_estimate=pl.CostEstimate(
            flops=40 * rows * length * width, bytes_accessed=8 * MIB, transcendentals=0
        ),
    )(*operands)


def query_back_kernel(w_ref, *refs):
    micros = (len(refs) - 3) // 2
    dq_refs, out_refs = refs[:micros], refs[micros : 2 * micros]
    rows_ref, held, sem = refs[2 * micros :]
    rows = dq_refs[0].shape[0]
    copy = pltpu.make_async_copy(w_ref.at[:, pl.ds(0, held.shape[1])], held, sem)
    copy.start()
    for m in range(micros):
        rows_ref[m * rows : (m + 1) * rows] = dq_refs[m][...]
    copy.wait()
    for n in range(held.shape[0] // BC):
        cut = slice(n * BC, (n + 1) * BC)
        made = dot(rows_ref[...], held[cut, :], NT)
        for m in range(micros):
            out_refs[m][:, cut] = made[m * rows : (m + 1) * rows]


def query_back(w, dqs):
    micros = len(dqs)
    rows, q_width = dqs[0].shape
    width = w.shape[0]
    return call(
        query_back_kernel,
        tuple([shaped((rows, width), jnp.float32)] * micros),
        [in_any] + [in_vmem] * micros,
        tuple([in_vmem] * micros),
        [
            pltpu.VMEM((micros * rows, q_width), low_type),
            pltpu.VMEM((width, q_width), low_type),
            pltpu.SemaphoreType.DMA,
        ],
        2 * micros * rows * width * q_width,
        7 * MIB,
    )(w, *dqs)


def input_kernel(x_ref, gain_ref, w_ref, *refs):
    micros, rows = x_ref.shape[:2]
    dx_refs = refs[:micros]
    part_refs = refs[micros : 2 * micros]
    dkv_ref, out_ref, stat_ref, grad, held, sem = refs[2 * micros :]
    kv_width = held.shape[1]
    copy = pltpu.make_async_copy(
        w_ref.at[:, pl.ds(w_ref.shape[1] - kv_width, kv_width)], held, sem
    )
    copy.start()
    copy.wait()
    for n in range(held.shape[0] // BC):
        cut = slice(n * BC, (n + 1) * BC)
        made = dot(dkv_ref[...], held[cut, :], NT)
        for m in range(micros):
            grad[m, :, cut] = part_refs[m][:, cut] + made[m * rows : (m + 1) * rows]
    total = jnp.zeros((1, x_ref.shape[-1]), jnp.float32)
    for m in range(micros):
        x = x_ref[m]
        inverse = lax.rsqrt(jnp.mean(x * x, axis=-1, keepdims=True) + norm_eps)
        term, gain_grad = unit_back(x, gain_ref[0:1], inverse, grad[m])
        out_ref[m] = dx_refs[m][...] + term
        total = total + gain_grad
    stat_ref[...] = jnp.broadcast_to(total, stat_ref.shape)


def input_back(x, gains, w, dxs, parts, dkv):
    micros, rows, width = x.shape
    kv_width = dkv.shape[1]
    return call(
        input_kernel,
        (shaped(x.shape, jnp.float32), shaped((8, width), jnp.float32)),
        [in_vmem, in_vmem, in_any] + [in_vmem] * (2 * micros + 1),
        (in_vmem,) * 2,
        [
            pltpu.VMEM(x.shape, jnp.float32),
            pltpu.VMEM((width, kv_width), low_type),
            pltpu.SemaphoreType.DMA,
        ],
        2 * micros * rows * width * kv_width,
        14 * MIB,
    )(x, gains, w, *dxs, *parts, dkv)


def rotate_kernel(b_ref, m_ref, s_ref, l_ref, r_ref, *refs):
    grad_ref, new_ref, moment_ref, second_ref = refs[-4:]
    parts = [ref[0].astype(jnp.float32) for ref in refs[:-4]]
    gradient = parts[0] if len(parts) == 1 else jnp.concatenate(parts, axis=1)
    grad_ref[0] = gradient
    left = l_ref[0].astype(low_type)
    right = r_ref[0].astype(low_type)
    rotated = dot(dot(left, gradient.astype(low_type), TN).astype(low_type), right)
    moment = beta_one * m_ref[0] + (1.0 - beta_one) * rotated
    second = beta_two * s_ref[0] + (1.0 - beta_two) * rotated * rotated
    moment_ref[0] = moment
    second_ref[0] = second
    direction = (moment / (jnp.sqrt(second) + adam_eps)).astype(low_type)
    turned = dot(dot(left, direction).astype(low_type), right, NT)
    new_ref[0] = b_ref[0] - rate * turned


def rotate(weight, gradients, moment, second, left, right):
    count = weight.shape[0]

    def spec(rows, cols):
        return pl.BlockSpec((1, rows, cols), lambda i: (i, 0, 0))

    block = spec(BR, BC)
    return pl.pallas_call(
        rotate_kernel,
        grid=(count,),
        out_shape=(shaped(weight.shape, jnp.float32),) * 4,
        in_specs=[block] * 3
        + [spec(BR, BR), spec(BC, BC)]
        + [spec(BR, part.shape[2]) for part in gradients],
        out_specs=(block,) * 4,
        compiler_params=pltpu.CompilerParams(vmem_limit_bytes=VMEM_LIMIT),
        cost_estimate=pl.CostEstimate(
            flops=4 * count * BR * BC * (BR + BC),
            bytes_accessed=count * 2 * MIB,
            transcendentals=0,
        ),
    )(weight, moment, second, left, right, *gradients)


def adam(weight, gradient, moment, second, step_rate):
    moment_new = beta_one * moment + (1.0 - beta_one) * gradient
    second_new = beta_two * second + (1.0 - beta_two) * gradient * gradient
    return (
        weight - step_rate * moment_new / (jnp.sqrt(second_new) + adam_eps),
        moment_new,
        second_new,
    )


def piece_places(row_groups, q_groups, kv_groups):
    all_groups = 2 * q_groups + kv_groups
    out_groups = list(range(q_groups)) + list(range(q_groups + kv_groups, all_groups))
    half = row_groups // 2
    numbers = [a * all_groups + b for a in range(half) for b in out_groups] + [None]
    numbers += [a * all_groups + b for a in range(half, row_groups) for b in out_groups]
    numbers += [a * all_groups + q_groups + b for a in range(row_groups) for b in range(kv_groups)]
    places = [0] * (len(numbers) - 1)
    for place, number in enumerate(numbers):
        if number is not None:
            places[number] = place
    return places


def to_partner(array, offset):
    if offset == 0:
        return array
    count = lax.axis_size("shard")
    return lax.ppermute(array, "shard", [(i, i ^ offset) for i in range(count)])


def to_ctx(array, offset):
    count = lax.axis_size("ctx")
    return lax.ppermute(array, "ctx", [(i, i ^ offset) for i in range(count)])


def to_chip(array, offset):
    count = lax.axis_size("ctx")
    return lax.ppermute(array, "ctx", [(i, (i + 2 * offset) % count) for i in range(count)])


def after(value, *others):
    return lax.optimization_barrier((value, others))[0]


def from_chips(array, chips):
    return [array] + [to_chip(array, offset) for offset in range(1, chips)]


def wide(array):
    return array.astype(jnp.float32)


def sum_to_chips(parts):
    total = wide(parts[0])
    for offset in range(1, len(parts)):
        total = total + wide(to_chip(parts[offset], -offset))
    return total


def gather_weights(blocks, chips, members, small):
    parts = [blocks]
    for _ in range(chips - 1):
        parts.append(to_chip(parts[-1], 1))
    pieces, arrays = [], []
    gate = []

    def add(array, offset, first, cut):
        pieces.append((0, offset, first, cut))
        arrays.append(array)
        pieces.append((1, offset, first, cut))
        arrays.append(to_ctx(after(array, *gate), 1))
        return array

    def spread(group, first):
        add(group, 0, first, 0)
        if members == 4 and first > 0:
            by_one, by_two = to_partner(group, 1), to_partner(group, 2)
            add(by_one, 1, first, 0)
            add(by_two, 2, first, 0)
            half = BR // 2
            add(to_partner(by_one[:, :half], 2), 3, first, 0)
            add(to_partner(by_two[:, half:], 1), 3, first, half)
            return [by_one, by_two]
        got = [to_partner(group, offset) for offset in range(1, members)]
        for offset in range(1, members):
            add(got[offset - 1], offset, first, 0)
        return got

    got = [to_partner(blocks, offset) for offset in range(1, members)]
    first = got + parts[1:3]
    gate.append(got[0])
    add(blocks, 0, 0, 0)
    for offset in range(1, members):
        add(got[offset - 1], offset, 0, 0)
    last = list(got)
    if chips > 1:
        last = spread(after(parts[1], *last), 1)
        gate[:] = last
    if chips > 2:
        group = after(jnp.concatenate(parts[2:], axis=0), *last, *small)
        spread(group, 2)
    return first, pieces, arrays


def add_wide(parts):
    total = wide(parts[0])
    for part in parts[1:]:
        total = total + wide(part)
    return total


def sum_members(made, ready, members):
    sums, seen, relays = [], [], []
    for half in range(2):
        sent, kept = made[2 * half : 2 * half + 2]
        hops, keeps = xor_plan(members, 1 - half)
        count = kept.shape[0] // len(keeps)
        total = wide(kept[:count])
        if members == 4:
            got = to_partner(sent, hops[0])
            got = got if ready is None else after(got, ready)
            total = total + wide(got[:count])
            relay = (wide(kept[count:]) + wide(got[count:])).astype(low_type)
            second = to_partner(relay, keeps[1])
            relays.append(relay)
            seen.append(second)
            total = total + wide(second)
        else:
            for place, hop in enumerate(hops):
                total = total + wide(to_partner(sent[place * count : (place + 1) * count], hop))
        sums.append(total.astype(low_type).reshape(count, -1))
    return jnp.concatenate(sums, axis=0), seen, relays


def sum_chips(rows, chip, chips):
    count = rows.shape[1] // chips

    def piece(offset):
        start = lax.rem(chip - offset + chips, chips) * count
        return lax.dynamic_slice_in_dim(rows, start, count, axis=1)

    return [piece(0)] + [to_chip(piece(offset), -offset) for offset in range(1, chips)]


def shards(
    tokens,
    cotangent,
    norm_gains,
    router,
    dense_weight,
    expert_weight,
    routes,
    assign,
    dense_order,
    expert_order,
    dense_moment,
    dense_second,
    dense_left,
    dense_right,
    expert_moment,
    expert_second,
    expert_left,
    expert_right,
    gains_moment,
    gains_second,
    router_moment,
    router_second,
):
    ctx_count = lax.axis_size("ctx")
    shard_count = lax.axis_size("shard")
    chips = ctx_count // 2
    micros, rows, width = tokens.shape
    slots = dense_weight.shape[0]
    span = rows // 2
    row_groups = width // BR
    q_groups = HEADS * HD // BC
    kv_groups = 2 * KVH * HD // BC

    expert_inverse = inverse_order(expert_order)
    ctx = lax.axis_index("ctx").astype(jnp.int32)
    me = jnp.stack([ctx, lax.axis_index("shard").astype(jnp.int32)])
    row_ids = jnp.arange(rows, dtype=jnp.int32)
    all_pos = assign[:, row_ids // span] * span + row_ids % span
    key_pos = all_pos.reshape(1, rows * ctx_count)
    rows_pos = all_pos[ctx].reshape(rows, 1)
    router_pad = jnp.pad(router.astype(low_type), ((0, 0), (0, LANES - shard_count)))

    small = (me, expert_inverse, router_pad, key_pos, rows_pos)
    far, pieces, arrays = gather_weights(
        dense_weight.astype(low_type), chips, shard_count, small
    )
    expert_low = after(expert_weight[0].astype(low_type), *far)
    expert_all = [lax.all_gather(expert_low[:, :UPPER], "ctx", axis=0, tiled=True)]

    lanes = jnp.arange(LANES, dtype=jnp.int32)
    hits = jnp.sum((routes[..., None] == lanes).astype(low_type), axis=2)
    cot_rows = jnp.concatenate([cotangent.astype(low_type), hits], axis=2)
    cot_rows = cot_rows.reshape(micros * rows, width + LANES)
    cot_rows = after(cot_rows, *arrays[::2])
    cot_parts = [to_partner(cot_rows, j) for j in range(shard_count)]

    h1, kv, w_in, w_out = project(
        pieces,
        arrays,
        chips,
        shard_count,
        slots,
        dense_order,
        me,
        [tokens[m] for m in range(micros)],
        norm_gains,
    )
    q = make_queries(h1, w_in, micros)
    h1_other = to_ctx(h1, 1)
    obs, logs, x2s, h2s = [], [], [], []
    kv_all = lax.all_gather(after(kv, expert_all[0]), "ctx", axis=0, tiled=True)
    lower = after(expert_low[:, UPPER:], kv_all, q, cot_parts)
    expert_all.append(lax.all_gather(lower, "ctx", axis=0, tiled=True))
    for m in range(micros):
        query = after(q[m], *(cot_parts if m == 0 else obs[m - 1 : m]))
        ob, log_total, x2, h2 = attend(
            m, query, kv_all, rows_pos, key_pos, tokens[m], norm_gains, w_out
        )
        obs.append(ob)
        logs.append(log_total)
        x2s.append(x2)
        h2s.append(h2)
    ob_others = [to_ctx(ob, 1) for ob in obs]

    h_parts = []
    for m in range(micros):
        own = h2s[m] if m == 0 else after(h2s[m], *h_parts[m - 1])
        h_parts.append([own] + [to_partner(own, j) for j in range(1, shard_count)])
    sent = []
    zs, dgs, dus, cs, xs = [], [], [], [], []
    for m in range(micros):
        here = after(me, h2s[-1], h1_other, *ob_others) if m == 0 else after(me, zs[-1])
        made = run_expert(m, expert_inverse, here, router_pad, h_parts[m], cot_parts, expert_all)
        sent.append(made[:shard_count])
        z, dg, du, c, x = made[shard_count:]
        zs.append(z)
        dgs.append(dg)
        dus.append(du)
        cs.append(c)
        xs.append(x)
    backs = [[to_partner(sent[m][j], j) for j in range(shard_count)] for m in range(micros)]

    expert_terms = outer_blocks(
        after(expert_inverse, *backs[0]), width, (0, 0, 1), [xs, cs], [dgs, dus, zs]
    )
    outs = produce(after(expert_inverse, *expert_terms), expert_all, zs, shard_count, width)
    arrived = [to_partner(outs[j], j) for j in range(min(3, shard_count))]
    dxs, das, dqs, stats = [], [], [], []
    dkv_terms = None
    for m in range(micros):
        here = after(me, outs, backs[-1]) if m == 0 else after(me, dqs[-1], arrived[1:])
        dx, da, do, stat = merge(
            here, x2s[m], cotangent[m], h2s[m], norm_gains, router_pad, w_out, backs[m]
        )
        dq, dkv_terms = attend_back(
            m, q[m], kv_all, rows_pos, key_pos, obs[m], logs[m], do, dkv_terms
        )
        dxs.append(dx)
        das.append(da)
        dqs.append(dq)
        stats.append(stat)

    def other_core(parts):
        return [to_ctx(part, 1) for part in parts]

    da_others, dq_others = other_core(das), other_core(dqs)
    first_term = after(expert_terms[0], *backs[-1])
    expert_sums = [lax.psum_scatter(first_term, "ctx", scatter_dimension=0, tiled=True)]
    dkv = lax.psum_scatter(
        after(dkv_terms, expert_sums[0]), "ctx", scatter_dimension=0, tiled=True
    )
    stat_sum = add_wide(stats)
    early = gradient_pieces(
        shard_count,
        after(me, dkv_terms),
        [([h1, h1_other], dqs + dq_others), (das + da_others, obs + ob_others)],
        [q_groups, q_groups],
        False,
        [stat_sum, to_ctx(stat_sum, 1)],
    )
    h1_turned = early[4]
    parts_back = query_back(after(w_in, early[0]), dqs)
    early_rows, early_seen, early_relays = sum_members(early[:4], parts_back, shard_count)
    chip = ctx // 2
    late = gradient_pieces(
        shard_count,
        after(me, *early_seen),
        [([h1_turned], [dkv, to_ctx(dkv, 1)])],
        [kv_groups],
        True,
        [],
    )
    last_outs = after(list(outs), early_seen)
    arrived += [to_partner(last_outs[j], j) for j in range(3, shard_count)]
    input_grad, gain_stat = input_back(
        after(tokens, late[0], arrived[3:]), norm_gains, w_in, dxs, parts_back, dkv
    )
    late_rows, _, _ = sum_members(late[:4], input_grad, shard_count)
    late_term = after(expert_terms[1], dkv, early_relays)
    expert_sums.append(lax.psum_scatter(late_term, "ctx", scatter_dimension=0, tiled=True))
    expert_grad, expert_new, expert_moment_new, expert_second_new = rotate(
        expert_weight[0], expert_sums, expert_moment[0], expert_second[0], expert_left[0], expert_right[0]
    )
    all_rows = after(jnp.concatenate([early_rows, late_rows], axis=0), expert_sums)
    all_parts = after(sum_chips(all_rows, chip, chips), expert_new)
    all_sums = add_wide(all_parts).astype(low_type)
    places = jnp.asarray(piece_places(row_groups, q_groups, kv_groups), jnp.int32)[dense_order]
    chosen = (places[:, None] == jnp.arange(all_sums.shape[0])[None, :]).astype(low_type)
    ordered = jnp.dot(chosen, all_sums, preferred_element_type=jnp.float32).astype(low_type)
    devices = ctx_count * shard_count
    piece_width = ordered.shape[1]
    stat_place = row_groups // 2 * 2 * q_groups
    gain_parts = gain_stat[:1].astype(low_type).reshape(-1, piece_width)
    stat_parts = jnp.concatenate([all_sums[stat_place : stat_place + 1], gain_parts], axis=0)
    extra = stat_parts.shape[0]
    ordered = jnp.concatenate(
        [
            ordered.reshape(devices, slots, piece_width),
            jnp.broadcast_to(stat_parts, (devices, extra, piece_width)),
        ],
        axis=1,
    ).reshape(devices * 2, (slots + extra) * piece_width // 2)
    ordered = lax.all_to_all(ordered, ("ctx", "shard"), split_axis=0, concat_axis=0, tiled=True)
    ordered = ordered.reshape(devices, slots + extra, piece_width)
    span = BR // (shard_count * chips)
    stat_block = ordered[:, slots].reshape(chips, 2, shard_count, span, LANES)
    stat_rows = wide(stat_block.transpose(2, 0, 3, 1, 4).reshape(BR * BC)[: (shard_count + 1) * width])
    stat_rows = stat_rows.reshape(shard_count + 1, width)
    gain_row = jnp.sum(wide(ordered[:, slots + 1 :]), axis=0).reshape(width)
    ordered = ordered[:, :slots].reshape(
        chips, 2, shard_count, slots, BR // (shard_count * chips), LANES
    )
    dense_sum = ordered.transpose(3, 2, 0, 4, 1, 5).reshape(slots, BR, BC)
    router_grad = stat_rows[:shard_count].T
    gains_grad = jnp.stack([gain_row, stat_rows[shard_count]])

    dense_grad, dense_new, dense_moment_new, dense_second_new = rotate(
        dense_weight, [dense_sum], dense_moment, dense_second, dense_left, dense_right
    )
    outputs = []
    for m in range(micros):
        total = x2s[m]
        for part in after(arrived, expert_new):
            total = total + wide(part[m * rows : (m + 1) * rows])
        outputs.append(total)

    gains_new, gains_moment_new, gains_second_new = adam(
        norm_gains, gains_grad, gains_moment, gains_second, gain_rate
    )
    router_new, router_moment_new, router_second_new = adam(
        router, router_grad, router_moment, router_second, rate
    )
    return (
        jnp.stack(outputs),
        input_grad,
        dense_grad,
        dense_new,
        dense_moment_new,
        dense_second_new,
        expert_grad[None],
        expert_new[None],
        expert_moment_new[None],
        expert_second_new[None],
        gains_grad,
        gains_new,
        gains_moment_new,
        gains_second_new,
        router_grad,
        router_new,
        router_moment_new,
        router_second_new,
    )


def solution(mesh):
    rows_spec = P("shard", "ctx", None)
    dense_spec = P(("ctx", "shard"), None, None)
    expert_spec = P("shard", "ctx", None, None)
    in_specs = (
        (rows_spec, rows_spec, P(), P(), dense_spec, expert_spec, rows_spec, P(), P(), P())
        + (dense_spec,) * 4
        + (expert_spec,) * 4
        + (P(),) * 4
    )
    out_specs = (rows_spec,) * 2 + (dense_spec,) * 4 + (expert_spec,) * 4 + (P(),) * 8
    return jax.shard_map(shards, mesh=mesh, in_specs=in_specs, out_specs=out_specs, check_vma=False)
```

```python
import functools

import jax
import jax.numpy as jnp
from jax import lax
from jax.experimental import pallas as pl
from jax.experimental.pallas import tpu as pltpu
from jax.sharding import PartitionSpec as P

HEADS = 24
KVH = 8
HD = 64
FF = 1024
BR = 192
BC = 256
LANES = 128
UPPER = 128

norm_eps = 1e-06
beta_one = 0.9
beta_two = 0.95
rate = 0.01
gain_rate = 0.5
adam_eps = 1e-08
masked_score = -1e30
low_type = jnp.bfloat16
MIB = 1 << 20
VMEM_LIMIT = 60 * MIB

NN = (((1,), (0,)), ((), ()))
NT = (((1,), (1,)), ((), ()))
TN = (((0,), (0,)), ((), ()))

in_vmem = pl.BlockSpec(memory_space=pltpu.VMEM)
in_smem = pl.BlockSpec(memory_space=pltpu.SMEM)
in_any = pl.BlockSpec(memory_space=pl.ANY)


def dot(left_side, right_side, dims=NN):
    return lax.dot_general(left_side, right_side, dims, preferred_element_type=jnp.float32)


def call(kernel, out_shapes, in_specs, out_specs, scratch, flops, moved, limit=VMEM_LIMIT):
    return pl.pallas_call(
        kernel,
        out_shape=out_shapes,
        in_specs=in_specs,
        out_specs=out_specs,
        scratch_shapes=scratch,
        compiler_params=pltpu.CompilerParams(vmem_limit_bytes=limit),
        cost_estimate=pl.CostEstimate(flops=flops, bytes_accessed=moved, transcendentals=0),
    )


def shaped(dims, kind):
    return jax.ShapeDtypeStruct(dims, kind)


def inverse_order(slot_order):
    count = slot_order.shape[0]
    numbers = jnp.arange(count, dtype=jnp.int32)
    return jnp.sum(
        jnp.where(slot_order[None, :] == numbers[:, None], numbers[None, :], 0), axis=1
    ).astype(jnp.int32)


def wait_bytes(landed, semaphore):
    pltpu.make_async_copy(landed, landed, semaphore).wait()


def unit_rows(rows, gain):
    inverse = lax.rsqrt(jnp.mean(rows * rows, axis=-1, keepdims=True) + norm_eps)
    return rows * inverse * gain, inverse


def unit_back(rows, gain, inverse, gradient):
    unit = rows * inverse
    scaled = gradient * gain
    inner = jnp.mean(scaled * unit, axis=-1, keepdims=True)
    return inverse * (scaled - unit * inner), jnp.sum(gradient * unit, axis=0, keepdims=True)


def lane_ids(dims):
    return lax.broadcasted_iota(jnp.int32, dims, len(dims) - 1)


def half_turn(tile):
    return pltpu.roll(tile, HD, 1)


def stack_heads(ref, pair, scale=None):
    base = pair * (3 * LANES)
    tiles = [
        ref[:, pl.ds(pl.multiple_of(base + LANES * t, LANES), LANES)].astype(jnp.float32)
        for t in range(3)
    ]
    if scale is not None:
        tiles = [t * scale for t in tiles]
    lower = lane_ids(tiles[0].shape) < HD
    first = [tiles[0], half_turn(tiles[0]), tiles[1]]
    second = [tiles[1], half_turn(tiles[2]), tiles[2]]
    return (
        jnp.concatenate([jnp.where(lower, t, 0.0) for t in first], axis=0),
        jnp.concatenate([jnp.where(lower, 0.0, t) for t in second], axis=0),
    )


def unstack_heads(ref, pair, first, second):
    rows = first.shape[0] // 3
    base = pair * (3 * LANES)
    lower = lane_ids((rows, LANES)) < HD
    tiles = (
        jnp.where(lower, first[:rows], half_turn(first[rows : 2 * rows])),
        jnp.where(lower, first[2 * rows :], second[:rows]),
        jnp.where(lower, half_turn(second[rows : 2 * rows]), second[2 * rows :]),
    )
    for t in range(3):
        ref[:, pl.ds(pl.multiple_of(base + LANES * t, LANES), LANES)] = tiles[t].astype(ref.dtype)


def project_kernel(
    pieces, chips, members, slots, all_groups, micros, order_ref, me_ref, *refs
):
    x_refs = refs[:micros]
    gain_ref = refs[micros]
    piece_refs = refs[micros + 1 : micros + 1 + len(pieces)]
    refs = refs[micros + 1 + len(pieces) :]
    h_ref = refs[0]
    kv_ref, win_ref, wout_ref, held, held_out, sems, out_sems = refs[1:]
    groups = held.shape[1] // BC
    kv_groups = kv_ref.shape[-1] // BC
    rows = x_refs[0].shape[0]
    ctx, shard = me_ref[0], me_ref[1]
    chip, core = lax.div(ctx, 2), lax.rem(ctx, 2)

    for ref, (other_core, offset, first, cut) in zip(piece_refs, pieces):

        @pl.loop(0, ref.shape[0])
        def _(i):
            source = lax.rem(chip - (first + lax.div(i, slots)) + chips, chips) * 2
            source = source + jnp.bitwise_xor(core, other_core)
            source = source * members + jnp.bitwise_xor(shard, offset)
            number = order_ref[source * slots + lax.rem(i, slots)]
            a, b = lax.div(number, all_groups), lax.rem(number, all_groups)
            down = pl.ds(pl.multiple_of(a * BR + cut, 32), ref.shape[1])

            @pl.when(b < groups)
            def _():
                across = pl.ds(pl.multiple_of(b * BC, BC), BC)
                pltpu.make_async_copy(ref.at[i], held.at[down, across], sems.at[b]).start()

            @pl.when(b >= groups)
            def _():
                across = pl.ds(pl.multiple_of((b - groups) * BC, BC), BC)
                pltpu.make_async_copy(ref.at[i], held_out.at[down, across], sems.at[groups]).start()

    for m in range(micros):
        h_ref[m * rows : (m + 1) * rows, :] = unit_rows(x_refs[m][...], gain_ref[0:1])[0].astype(
            low_type
        )
    q_groups = groups - kv_groups

    @pl.loop(0, groups)
    def _(b):
        across = pl.ds(pl.multiple_of(b * BC, BC), BC)
        wait_bytes(held.at[:, across], sems.at[b])

    wait_bytes(held_out, sems.at[groups])
    copies = [
        pltpu.make_async_copy(held, win_ref, out_sems.at[0]),
        pltpu.make_async_copy(held_out, wout_ref, out_sems.at[1]),
    ]
    for copy in copies:
        copy.start()

    @pl.loop(0, kv_groups)
    def _(b):
        across = pl.ds(pl.multiple_of((q_groups + b) * BC, BC), BC)
        made = dot(h_ref[...], held[:, across]).astype(low_type)
        kv_ref[:, pl.ds(pl.multiple_of(b * BC, BC), BC)] = made

    for copy in copies:
        copy.wait()


def project(pieces, arrays, chips, members, slots, order, me, xs, gains):
    micros = len(xs)
    rows, width = xs[0].shape
    in_width = (HEADS + 2 * KVH) * HD
    out_width = HEADS * HD
    kv_width = 2 * KVH * HD
    return call(
        functools.partial(
            project_kernel, pieces, chips, members, slots, (in_width + out_width) // BC, micros
        ),
        tuple(
            [shaped((micros * rows, width), low_type)]
            + [shaped((micros * rows, kv_width), low_type)]
            + [shaped((width, in_width), low_type), shaped((width, out_width), low_type)]
        ),
        [in_smem, in_smem] + [in_vmem] * (micros + 1) + [in_any] * len(arrays),
        (in_vmem, in_vmem, in_any, in_any),
        [
            pltpu.VMEM((width, in_width), low_type),
            pltpu.VMEM((width, out_width), low_type),
            pltpu.SemaphoreType.DMA((in_width // BC + 1,)),
            pltpu.SemaphoreType.DMA((2,)),
        ],
        2 * micros * rows * width * kv_width,
        4 * width * (in_width + out_width),
    )(order, me, *xs, gains, *arrays)


def query_kernel(h_ref, w_ref, *refs):
    q_refs = refs[:-2]
    held, sems = refs[-2:]
    groups = held.shape[1] // BC
    rows = q_refs[0].shape[0]

    def copy(b):
        across = pl.ds(pl.multiple_of(b * BC, BC), BC)
        return pltpu.make_async_copy(w_ref.at[:, across], held.at[:, across], sems.at[b])

    @pl.loop(0, groups)
    def _(b):
        copy(b).start()

    @pl.loop(0, groups)
    def _(b):
        copy(b).wait()
        across = pl.ds(pl.multiple_of(b * BC, BC), BC)
        made = dot(h_ref[...], held[:, across]).astype(low_type)
        for m, ref in enumerate(q_refs):
            ref[:, across] = made[m * rows : (m + 1) * rows]


def make_queries(h, w, micros):
    total, width = h.shape
    q_width = HEADS * HD
    return call(
        query_kernel,
        tuple([shaped((total // micros, q_width), low_type)] * micros),
        [in_vmem, in_any],
        tuple([in_vmem] * micros),
        [pltpu.VMEM((width, q_width), low_type), pltpu.SemaphoreType.DMA((q_width // BC,))],
        2 * total * width * q_width,
        2 * width * q_width,
    )(h, w)


def load_keys(kv_ref, micro, rows, held, sem):
    count = held.shape[0] // rows
    span = kv_ref.shape[0] // count

    @pl.loop(0, count)
    def _(i):
        pltpu.make_async_copy(
            kv_ref.at[pl.ds(pl.multiple_of(i * span + micro * rows, 16), rows)],
            held.at[pl.ds(pl.multiple_of(i * rows, 16), rows)],
            sem,
        ).start()


def attend_kernel(
    micro, q_ref, rpos_ref, kpos_ref, x_ref, gain_ref, w_ref, all_ref,
    ob_ref, log_ref, x2_ref, h2_ref, bias, kv_ref, held, sems,
):
    rows = q_ref.shape[0]
    load_keys(all_ref, micro, rows, kv_ref, sems.at[0])
    pltpu.make_async_copy(w_ref, held, sems.at[1]).start()
    bias[...] = jnp.where(kpos_ref[...] <= rpos_ref[...], 0.0, masked_score)
    log_ref[...] = jnp.zeros_like(log_ref)
    length = kv_ref.shape[0]
    wait_bytes(kv_ref, sems.at[0])

    @pl.loop(0, KVH // 2)
    def _(pair):
        lane = pl.multiple_of(pair * LANES, LANES)
        keys = kv_ref[:, pl.ds(lane, LANES)]
        values = kv_ref[:, pl.ds(pl.multiple_of(lane + KVH * HD, LANES), LANES)]
        stacked = stack_heads(q_ref, pair, HD**-0.5)
        mixed = []
        for part in range(2):
            scores = dot(stacked[part].astype(low_type), keys, NT)
            scores = (scores.reshape(3, rows, length) + bias[...][None]).reshape(3 * rows, length)
            largest = jnp.max(scores, axis=-1, keepdims=True)
            raised = jnp.exp(scores - largest)
            summed = jnp.sum(raised, axis=-1, keepdims=True)
            mixed.append(dot(raised.astype(low_type), values) / summed)
            log_ref[...] = jnp.where(
                lane_ids(log_ref.shape) == 2 * pair + part, largest + jnp.log(summed), log_ref[...]
            )
        unstack_heads(ob_ref, pair, mixed[0], mixed[1])

    wait_bytes(held, sems.at[1])
    for n in range(held.shape[0] // BC):
        cut = slice(n * BC, (n + 1) * BC)
        x2_ref[:, cut] = x_ref[:, cut] + dot(ob_ref[...], held[cut, :], NT)
    h2_ref[...] = unit_rows(x2_ref[...], gain_ref[1:2])[0].astype(low_type)


def attend(micro, q, kv, rows_pos, key_pos, x, gains, w):
    rows, width = q.shape
    length = key_pos.shape[1]
    model = x.shape[1]
    return call(
        functools.partial(attend_kernel, micro),
        (
            shaped((rows, width), low_type),
            shaped((3 * rows, LANES), jnp.float32),
            shaped((rows, model), jnp.float32),
            shaped((rows, model), low_type),
        ),
        [in_vmem] * 5 + [in_any] * 2,
        (in_vmem,) * 4,
        [
            pltpu.VMEM((rows, length), jnp.float32),
            pltpu.VMEM((length, kv.shape[1]), low_type),
            pltpu.VMEM((model, width), low_type),
            pltpu.SemaphoreType.DMA((2,)),
        ],
        16 * rows * length * width,
        8 * MIB,
    )(q, rows_pos, key_pos, x, gains, w, kv)


def router_parts(h2, router, experts):
    logits = dot(h2, router)
    logits = jnp.where(lane_ids(logits.shape) < experts, logits, masked_score)
    raised = jnp.exp(logits - jnp.max(logits, axis=-1, keepdims=True))
    return raised / jnp.sum(raised, axis=-1, keepdims=True)


def expert_kernel(sources, micro, order_ref, me_ref, router_ref, *refs):
    h_parts = refs[:sources]
    c_parts = refs[sources : 2 * sources]
    w_refs = refs[2 * sources : 2 * sources + 2]
    outs = refs[2 * sources + 2 :]
    back_refs = outs[:sources]
    z_ref, dg_ref, du_ref, cs, xs_ref = outs[sources : sources + 5]
    held, chance, load_sem, w_sems = outs[sources + 5 :]
    rows, width = h_parts[0].shape
    row_groups = width // BR
    col_groups = FF // BC
    for j in range(sources):
        pltpu.make_async_copy(h_parts[j], xs_ref.at[pl.ds(j * rows, rows)], load_sem.at[0]).start()
        pltpu.make_async_copy(
            c_parts[j].at[pl.ds(micro * rows, rows)], cs.at[pl.ds(j * rows, rows)], load_sem.at[1]
        ).start()
    for b in range(col_groups):

        @pl.loop(0, row_groups)
        def _(a):
            for k in range(3):
                slot = order_ref[(k * row_groups + a) * col_groups + b]
                for start, ref in zip((0, UPPER), w_refs):
                    down = pl.ds(pl.multiple_of(a * BR + start, 64), ref.shape[1])
                    pltpu.make_async_copy(
                        ref.at[slot], held.at[k, down, pl.ds(b * BC, BC)], w_sems.at[b]
                    ).start()

    wait_bytes(xs_ref, load_sem.at[0])
    wait_bytes(cs, load_sem.at[1])
    me = me_ref[1]
    probs = router_parts(xs_ref[...], router_ref[...], sources)
    hits = cs[:, width:].astype(jnp.float32)
    mine = lane_ids(hits.shape) == me
    hit = jnp.sum(jnp.where(mine, hits, 0.0), axis=-1, keepdims=True)
    weight = jnp.sum(jnp.where(mine, probs, 0.0), axis=-1, keepdims=True) * hit
    chance[...] = jnp.zeros_like(chance)

    @pl.loop(0, col_groups)
    def _(b):
        cut = pl.ds(pl.multiple_of(b * BC, BC), BC)
        wait_bytes(held.at[:, :, cut], w_sems.at[b])
        gate = dot(xs_ref[...], held[0, :, cut])
        up = dot(xs_ref[...], held[1, :, cut])
        down = dot(cs[:, :width], held[2, :, cut])
        sig = jax.nn.sigmoid(gate)
        act = gate * sig
        hidden = act * up
        chance[...] += jnp.sum(down * hidden, axis=-1, keepdims=True)
        z_ref[:, cut] = (hidden * weight).astype(low_type)
        down = down * weight
        dg_ref[:, cut] = (down * up * (sig + act * (1.0 - sig))).astype(low_type)
        du_ref[:, cut] = (down * act).astype(low_type)

    for n in range(width // BC):
        cut = slice(n * BC, (n + 1) * BC)
        back = dot(dg_ref[...], held[0, cut, :], NT) + dot(du_ref[...], held[1, cut, :], NT)
        for j in range(sources):
            back_refs[j][:, cut] = back[j * rows : (j + 1) * rows].astype(low_type)
    told = chance[...] * hit
    high_part = told.astype(low_type)
    low_part = (told - high_part.astype(jnp.float32)).astype(low_type)
    lanes = lane_ids((sources * rows, LANES))
    tail = jnp.where(lanes == 0, high_part, jnp.where(lanes == 1, low_part, jnp.zeros_like(low_part)))
    for j in range(sources):
        back_refs[j][:, width:] = tail[j * rows : (j + 1) * rows]


def run_expert(micro, order, me, router, h_parts, c_parts, ws):
    sources = len(h_parts)
    rows, width = h_parts[0].shape
    total = sources * rows
    return call(
        functools.partial(expert_kernel, sources, micro),
        tuple(
            [shaped((rows, width + LANES), low_type)] * sources
            + [shaped((total, FF), low_type)] * 3
            + [shaped((total, width + LANES), low_type), shaped((total, width), low_type)]
        ),
        [in_smem, in_smem, in_vmem] + [in_any] * (2 * sources + 2),
        tuple([in_vmem] * (sources + 5)),
        [
            pltpu.VMEM((3, width, FF), low_type),
            pltpu.VMEM((total, 1), jnp.float32),
            pltpu.SemaphoreType.DMA((2,)),
            pltpu.SemaphoreType.DMA((FF // BC,)),
        ],
        10 * total * width * FF,
        20 * MIB,
    )(order, me, router, *h_parts, *c_parts, *ws)


def produce_kernel(sources, order_ref, upper_ref, lower_ref, *refs):
    out_refs = refs[-3 - sources : -3]
    z_refs = refs[: -3 - sources]
    zs, held, sem = refs[-3:]
    width = held.shape[0]
    total = z_refs[0].shape[0]
    rows = total // sources
    row_groups, col_groups = width // BR, FF // BC

    @pl.loop(0, row_groups)
    def _(a):
        for b in range(col_groups):
            slot = order_ref[(2 * row_groups + a) * col_groups + b]
            for start, ref in zip((0, UPPER), (upper_ref, lower_ref)):
                down = pl.ds(pl.multiple_of(a * BR + start, 64), ref.shape[1])
                pltpu.make_async_copy(
                    ref.at[slot], held.at[down, pl.ds(b * BC, BC)], sem
                ).start()

    for m, z_ref in enumerate(z_refs):
        zs[m * total : (m + 1) * total] = z_ref[...]
    wait_bytes(held, sem)
    for n in range(width // BC):
        cut = slice(n * BC, (n + 1) * BC)
        made = dot(zs[...], held[cut, :], NT).astype(low_type)
        for m in range(len(z_refs)):
            for j in range(sources):
                start = m * total + j * rows
                out_refs[j][m * rows : (m + 1) * rows, cut] = made[start : start + rows]


def produce(order, ws, zs, sources, width):
    micros = len(zs)
    total = zs[0].shape[0]
    return call(
        functools.partial(produce_kernel, sources),
        tuple([shaped((micros * total // sources, width), low_type)] * sources),
        [in_smem, in_any, in_any] + [in_vmem] * micros,
        tuple([in_vmem] * sources),
        [
            pltpu.VMEM((micros * total, FF), low_type),
            pltpu.VMEM((width, FF), low_type),
            pltpu.SemaphoreType.DMA,
        ],
        2 * micros * total * width * FF,
        8 * MIB,
    )(order, *ws, *zs)


def outer_kernel(groups, col_groups, order_ref, *refs):
    micros = len(refs[:-5]) // (len(groups) + 2)
    lefts = [refs[i * micros : (i + 1) * micros] for i in range(2)]
    rights = [refs[(2 + i) * micros : (3 + i) * micros] for i in range(len(groups))]
    out_refs, (turned, stage, sems) = refs[-5:-3], refs[-3:]
    rows = rights[0][0].shape[0]
    width = turned.shape[1]
    span = 2 * BR
    for side in range(2):
        for m in range(micros):
            for r in range(0, rows, LANES):
                part = lefts[side][m][r : r + LANES, :width]
                turned[side, :, m * rows + r : m * rows + r + LANES] = part.T
    row_groups = width // BR
    steps = [(k, p) for k in range(len(groups)) for p in range(width // span)]
    for n, (k, p) in enumerate(steps):
        slot = n % 2
        if n >= 2:
            wait_bytes(stage.at[slot], sems.at[slot])
        cut = slice(p * span, (p + 1) * span)
        made = 0.0
        for m in range(micros):
            left = turned[groups[k], cut, m * rows : (m + 1) * rows]
            made = made + dot(left, rights[k][m][...])
        stage[slot] = made.astype(low_type)
        for half in range(2):
            for b in range(col_groups):
                number = (k * row_groups + 2 * p + half) * col_groups + b
                place = order_ref[number]
                for side in range(2):
                    pltpu.make_async_copy(
                        stage.at[
                            slot, pl.ds(half * BR, BR), pl.ds(b * BC + side * LANES, LANES)
                        ],
                        out_refs[side].at[place],
                        sems.at[slot],
                    ).start()
    for slot in range(2):
        wait_bytes(stage.at[slot], sems.at[slot])


def outer_blocks(order, width, groups, lefts, rights):
    flat = [part for group in lefts + rights for part in group]
    rows = sum(part.shape[0] for part in rights[0])
    cols = rights[0][0].shape[1]
    blocks = len(groups) * width * cols // (BR * BC)
    return call(
        functools.partial(outer_kernel, groups, cols // BC),
        (shaped((blocks, BR, LANES), low_type),) * 2,
        [in_smem] + [in_vmem] * len(flat),
        (in_any,) * 2,
        [
            pltpu.VMEM((2, width, rows), low_type),
            pltpu.VMEM((2, 2 * BR, cols), low_type),
            pltpu.SemaphoreType.DMA((2,)),
        ],
        2 * rows * blocks * BR * BC,
        blocks * BR * BC * 2 + sum(f.size * 2 for f in flat),
    )(order, *flat)


def xor_plan(members, offset):
    if members != 4:
        return list(range(1, members)), [0]
    first = 1 if offset % 2 else 2
    return [first, 3], [0, 3 - first]


def pieces_kernel(members, counts, cols, turned_first, me_ref, *refs):
    lists = []
    for left_count, right_count in counts:
        lists.append((refs[:left_count], refs[left_count : left_count + right_count]))
        refs = refs[left_count + right_count :]
    stat_refs = refs[: len(refs) - 8] if turned_first else refs[: len(refs) - 10]
    refs = refs[len(stat_refs) :]
    outs, refs = refs[:4], refs[4:]
    extra = refs[0] if not turned_first else None
    turned, rights, stage, sems = refs[0 if turned_first else 1 :][:4]
    ctx, shard = me_ref[0], me_ref[1]
    core = lax.rem(ctx, 2)
    total = turned.shape[2]
    row_groups = turned.shape[1] // BR
    base = 0
    for g, (_, parts) in enumerate(lists):
        start = 0
        for part in parts:
            count = part.shape[0]
            for b in range(cols[g]):
                lane = pl.multiple_of(b * BC + core * LANES, LANES)
                pltpu.make_async_copy(
                    part.at[:, pl.ds(lane, LANES)],
                    rights.at[pl.ds(start, count), pl.ds((base + b) * LANES, LANES)],
                    sems.at[g],
                ).start()
            start += count
        base += cols[g]
    for g, (parts, _) in enumerate(lists):
        if g == 0 and turned_first:
            turned[0] = parts[0][...]
            continue
        start = 0
        for part in parts:
            for r in range(0, part.shape[0], LANES):
                turned[g, :, start : start + LANES] = part[r : r + LANES, :].T
                start += LANES
    if extra is not None:
        extra[...] = turned[0]
    all_cols = sum(cols)
    half_blocks = row_groups // 2 * all_cols
    counts = [half_blocks + (1 if stat_refs else 0), half_blocks]
    span = BR // members
    if stat_refs:
        block = refs[-1]
        block[...] = jnp.zeros_like(block)
        up = stat_refs[0].shape[0] - 8
        for r, row in enumerate(list(range(members)) + [up]):
            total_row = sum(ref[row : row + 1, :] for ref in stat_refs)
            for t in range(total_row.shape[1] // BC):
                place = r * (total_row.shape[1] // BC) + t
                block[place : place + 1, :] = total_row[:, t * BC : (t + 1) * BC]
        lane = pl.multiple_of(core * LANES, LANES)
        for out, hops in zip(outs[:2], xor_plan(members, 1)):
            for place, hop in enumerate(hops):
                down = pl.multiple_of(jnp.bitwise_xor(shard, hop) * span, 8)
                out[place * counts[0] + half_blocks] = block[
                    pl.ds(down, span), pl.ds(lane, LANES)
                ].astype(low_type)
    base = 0
    for g in range(len(lists)):
        wide_cols = cols[g] * LANES
        wait_bytes(rights.at[:, pl.ds(base * LANES, wide_cols)], sems.at[g])
        for a in range(row_groups):
            made = dot(
                turned[g, a * BR : (a + 1) * BR, :],
                rights[:, base * LANES : base * LANES + wide_cols],
            )
            stage[a % 2, :, :wide_cols] = made.astype(stage.dtype)
            half = a // (row_groups // 2)
            first = (a % (row_groups // 2)) * all_cols + base
            for out, hops in zip(outs[2 * half : 2 * half + 2], xor_plan(members, 1 - half)):
                for place, hop in enumerate(hops):
                    down = pl.multiple_of(jnp.bitwise_xor(shard, hop) * span, 16 if span % 16 == 0 else 8)
                    for b in range(cols[g]):
                        out[place * counts[half] + first + b] = stage[
                            a % 2, pl.ds(down, span), b * LANES : (b + 1) * LANES
                        ].astype(low_type)
        base += cols[g]


def gradient_pieces(members, me, groups, cols, turned_first, stats):
    counts = tuple((len(left), len(right)) for left, right in groups)
    flat = [part for left, right in groups for part in left + right]
    total = sum(part.shape[0] for part in groups[0][1])
    width = groups[0][0][0].shape[0 if turned_first else 1]
    row_groups = width // BR
    half_blocks = row_groups // 2 * sum(cols)
    span = BR // members
    stage_type = jnp.float32 if span % 16 else low_type
    outs = []
    for half in range(2):
        count = half_blocks + (1 if stats and half == 0 else 0)
        for hops in xor_plan(members, 1 - half):
            outs.append(shaped((len(hops) * count, span, LANES), low_type))
    out_specs = [in_vmem] * 4
    if not turned_first:
        outs.append(shaped((width, total), low_type))
        out_specs.append(in_vmem)
    in_specs = [in_smem]
    for left, right in groups:
        in_specs += [in_vmem] * len(left) + [in_any] * len(right)
    in_specs += [in_vmem] * len(stats)
    return call(
        functools.partial(pieces_kernel, members, counts, tuple(cols), turned_first),
        tuple(outs),
        in_specs,
        tuple(out_specs),
        [
            pltpu.VMEM((len(groups), width, total), low_type),
            pltpu.VMEM((total, sum(cols) * LANES), low_type),
            pltpu.VMEM((2, BR, max(cols) * LANES), stage_type),
            pltpu.SemaphoreType.DMA((len(groups),)),
        ]
        + ([pltpu.VMEM((BR, BC), jnp.float32)] if stats else []),
        2 * total * width * sum(cols) * LANES,
        16 * MIB,
    )(me, *flat, *stats)


def merge_kernel(
    sources, me_ref, x2_ref, cot_ref, h2_ref, gain_ref, router_ref, w_ref, *refs
):
    back_refs = refs[:sources]
    dx_ref, da_ref, do_ref, stat_ref, held, sem = refs[sources:]
    rows, width = x2_ref.shape
    pltpu.make_async_copy(w_ref, held, sem).start()
    lanes = lane_ids((rows, LANES))
    prob_grad = jnp.zeros((rows, LANES), jnp.float32)
    gathered = jnp.zeros((rows, width), jnp.float32)
    for j in range(sources):
        tail = back_refs[j][:, width:].astype(jnp.float32)
        told = jnp.sum(tail, axis=-1, keepdims=True)
        expert = jnp.bitwise_xor(me_ref[1], j)
        prob_grad = prob_grad + jnp.where(lanes == expert, told, 0.0)
        gathered = gathered + back_refs[j][:, :width].astype(jnp.float32)
    h2 = h2_ref[...]
    probs = router_parts(h2, router_ref[...], sources)
    logit_grad = probs * (prob_grad - jnp.sum(probs * prob_grad, axis=-1, keepdims=True))
    high_part = logit_grad.astype(low_type)
    low_part = (logit_grad - high_part.astype(jnp.float32)).astype(low_type)
    router_grad = dot(high_part, h2, TN) + dot(low_part, h2, TN)
    gathered = gathered + dot(high_part, router_ref[...], NT) + dot(low_part, router_ref[...], NT)
    x2 = x2_ref[...]
    inverse = lax.rsqrt(jnp.mean(x2 * x2, axis=-1, keepdims=True) + norm_eps)
    moe_grad, gain_grad = unit_back(x2, gain_ref[1:2], inverse, gathered)
    after = cot_ref[...] + moe_grad
    dx_ref[...] = after
    da_ref[...] = after.astype(low_type)
    experts_up = stat_ref.shape[0] - 8
    stat_ref[:experts_up] = router_grad[:experts_up]
    stat_ref[experts_up:] = jnp.broadcast_to(gain_grad, (8, width))
    wait_bytes(held, sem)
    for n in range(held.shape[1] // BC):
        cut = slice(n * BC, (n + 1) * BC)
        do_ref[:, cut] = dot(da_ref[...], held[:, cut]).astype(low_type)


def merge(me, x2, cot, h2, gains, router, w, backs):
    rows, width = x2.shape
    sources = len(backs)
    experts_up = -(-sources // 8) * 8
    return call(
        functools.partial(merge_kernel, sources),
        (
            shaped((rows, width), jnp.float32),
            shaped((rows, width), low_type),
            shaped((rows, HEADS * HD), low_type),
            shaped((experts_up + 8, width), jnp.float32),
        ),
        [in_smem] + [in_vmem] * 5 + [in_any] + [in_vmem] * sources,
        (in_vmem,) * 4,
        [pltpu.VMEM((width, HEADS * HD), low_type), pltpu.SemaphoreType.DMA],
        2 * rows * width * HEADS * HD,
        10 * MIB,
        24 * MIB,
    )(me, x2, cot, h2, gains, router, w, *backs)


def attend_back_kernel(
    micro, q_ref, rpos_ref, kpos_ref, ob_ref, log_ref, do_ref, all_ref, *refs
):
    dq_ref, out_ref, bias, kv_ref, grad_ref, sems = refs[-6:]
    rows = q_ref.shape[0]
    load_keys(all_ref, micro, rows, kv_ref, sems.at[0])
    length = kv_ref.shape[0]
    bias[...] = jnp.where(kpos_ref[...] <= rpos_ref[...], 0.0, masked_score)
    wait_bytes(kv_ref, sems.at[0])

    @pl.loop(0, KVH // 2)
    def _(pair):
        lane = pl.multiple_of(pair * LANES, LANES)
        value_lane = pl.multiple_of(lane + KVH * HD, LANES)
        keys = kv_ref[:, pl.ds(lane, LANES)]
        values = kv_ref[:, pl.ds(value_lane, LANES)]
        queries = stack_heads(q_ref, pair, HD**-0.5)
        grads = stack_heads(do_ref, pair)
        mixes = stack_heads(ob_ref, pair)
        query_grads = []
        key_grad = value_grad = None
        for part in range(2):
            query = queries[part].astype(low_type)
            grad = grads[part].astype(low_type)
            log_total = jnp.sum(
                jnp.where(lane_ids(log_ref.shape) == 2 * pair + part, log_ref[...], 0.0),
                axis=-1,
                keepdims=True,
            )
            delta = jnp.sum(grads[part] * mixes[part], axis=-1, keepdims=True)
            scores = dot(query, keys, NT)
            scores = (scores.reshape(3, rows, length) + bias[...][None]).reshape(3 * rows, length)
            chance = jnp.exp(scores - log_total)
            prob_grad = dot(grad, values, NT)
            score_grad = (chance * (prob_grad - delta)).astype(low_type)
            value_term = dot(chance.astype(low_type), grad, TN)
            key_term = dot(score_grad, query, TN)
            key_grad = key_term if part == 0 else key_grad + key_term
            value_grad = value_term if part == 0 else value_grad + value_term
            query_grads.append(dot(score_grad, keys) * HD**-0.5)
        unstack_heads(dq_ref, pair, query_grads[0], query_grads[1])
        grad_ref[:, pl.ds(lane, LANES)] = key_grad.astype(low_type)
        grad_ref[:, pl.ds(value_lane, LANES)] = value_grad.astype(low_type)

    count = length // rows
    span = out_ref.shape[0] // count

    @pl.loop(0, count)
    def _(i):
        pltpu.make_async_copy(
            grad_ref.at[pl.ds(pl.multiple_of(i * rows, 16), rows)],
            out_ref.at[pl.ds(pl.multiple_of(i * span + micro * rows, 16), rows)],
            sems.at[1],
        ).start()

    wait_bytes(grad_ref, sems.at[1])


def attend_back(micro, q, kv, rows_pos, key_pos, ob, log_total, do, shared):
    rows, width = q.shape
    length = key_pos.shape[1]
    operands = [q, rows_pos, key_pos, ob, log_total, do, kv]
    in_specs = [in_vmem] * 6 + [in_any]
    aliases = {}
    if shared is not None:
        aliases = {len(operands): 1}
        operands.append(shared)
        in_specs.append(in_any)
    return pl.pallas_call(
        functools.partial(attend_back_kernel, micro),
        out_shape=(shaped((rows, width), low_type), shaped(kv.shape, low_type)),
        in_specs=in_specs,
        out_specs=(in_vmem, in_any),
        scratch_shapes=[
            pltpu.VMEM((rows, length), jnp.float32),
            pltpu.VMEM((length, kv.shape[1]), low_type),
            pltpu.VMEM((length, kv.shape[1]), low_type),
            pltpu.SemaphoreType.DMA((2,)),
        ],
        input_output_aliases=aliases,
        compiler_params=pltpu.CompilerParams(vmem_limit_bytes=40 * MIB),
        cost_estimate=pl.CostEstimate(
            flops=40 * rows * length * width, bytes_accessed=8 * MIB, transcendentals=0
        ),
    )(*operands)


def query_back_kernel(w_ref, *refs):
    micros = (len(refs) - 3) // 2
    dq_refs, out_refs = refs[:micros], refs[micros : 2 * micros]
    rows_ref, held, sem = refs[2 * micros :]
    rows = dq_refs[0].shape[0]
    copy = pltpu.make_async_copy(w_ref.at[:, pl.ds(0, held.shape[1])], held, sem)
    copy.start()
    for m in range(micros):
        rows_ref[m * rows : (m + 1) * rows] = dq_refs[m][...]
    copy.wait()
    for n in range(held.shape[0] // BC):
        cut = slice(n * BC, (n + 1) * BC)
        made = dot(rows_ref[...], held[cut, :], NT)
        for m in range(micros):
            out_refs[m][:, cut] = made[m * rows : (m + 1) * rows]


def query_back(w, dqs):
    micros = len(dqs)
    rows, q_width = dqs[0].shape
    width = w.shape[0]
    return call(
        query_back_kernel,
        tuple([shaped((rows, width), jnp.float32)] * micros),
        [in_any] + [in_vmem] * micros,
        tuple([in_vmem] * micros),
        [
            pltpu.VMEM((micros * rows, q_width), low_type),
            pltpu.VMEM((width, q_width), low_type),
            pltpu.SemaphoreType.DMA,
        ],
        2 * micros * rows * width * q_width,
        7 * MIB,
    )(w, *dqs)


def input_kernel(x_ref, gain_ref, w_ref, *refs):
    micros, rows = x_ref.shape[:2]
    dx_refs = refs[:micros]
    part_refs = refs[micros : 2 * micros]
    dkv_ref, out_ref, stat_ref, grad, held, sem = refs[2 * micros :]
    kv_width = held.shape[1]
    copy = pltpu.make_async_copy(
        w_ref.at[:, pl.ds(w_ref.shape[1] - kv_width, kv_width)], held, sem
    )
    copy.start()
    copy.wait()
    for n in range(held.shape[0] // BC):
        cut = slice(n * BC, (n + 1) * BC)
        made = dot(dkv_ref[...], held[cut, :], NT)
        for m in range(micros):
            grad[m, :, cut] = part_refs[m][:, cut] + made[m * rows : (m + 1) * rows]
    total = jnp.zeros((1, x_ref.shape[-1]), jnp.float32)
    for m in range(micros):
        x = x_ref[m]
        inverse = lax.rsqrt(jnp.mean(x * x, axis=-1, keepdims=True) + norm_eps)
        term, gain_grad = unit_back(x, gain_ref[0:1], inverse, grad[m])
        out_ref[m] = dx_refs[m][...] + term
        total = total + gain_grad
    stat_ref[...] = jnp.broadcast_to(total, stat_ref.shape)


def input_back(x, gains, w, dxs, parts, dkv):
    micros, rows, width = x.shape
    kv_width = dkv.shape[1]
    return call(
        input_kernel,
        (shaped(x.shape, jnp.float32), shaped((8, width), jnp.float32)),
        [in_vmem, in_vmem, in_any] + [in_vmem] * (2 * micros + 1),
        (in_vmem,) * 2,
        [
            pltpu.VMEM(x.shape, jnp.float32),
            pltpu.VMEM((width, kv_width), low_type),
            pltpu.SemaphoreType.DMA,
        ],
        2 * micros * rows * width * kv_width,
        14 * MIB,
    )(x, gains, w, *dxs, *parts, dkv)


def rotate_kernel(b_ref, m_ref, s_ref, l_ref, r_ref, *refs):
    grad_ref, new_ref, moment_ref, second_ref = refs[-4:]
    parts = [ref[0].astype(jnp.float32) for ref in refs[:-4]]
    gradient = parts[0] if len(parts) == 1 else jnp.concatenate(parts, axis=1)
    grad_ref[0] = gradient
    left = l_ref[0].astype(low_type)
    right = r_ref[0].astype(low_type)
    rotated = dot(dot(left, gradient.astype(low_type), TN).astype(low_type), right)
    moment = beta_one * m_ref[0] + (1.0 - beta_one) * rotated
    second = beta_two * s_ref[0] + (1.0 - beta_two) * rotated * rotated
    moment_ref[0] = moment
    second_ref[0] = second
    direction = (moment / (jnp.sqrt(second) + adam_eps)).astype(low_type)
    turned = dot(dot(left, direction).astype(low_type), right, NT)
    new_ref[0] = b_ref[0] - rate * turned


def rotate(weight, gradients, moment, second, left, right):
    count = weight.shape[0]

    def spec(rows, cols):
        return pl.BlockSpec((1, rows, cols), lambda i: (i, 0, 0))

    block = spec(BR, BC)
    return pl.pallas_call(
        rotate_kernel,
        grid=(count,),
        out_shape=(shaped(weight.shape, jnp.float32),) * 4,
        in_specs=[block] * 3
        + [spec(BR, BR), spec(BC, BC)]
        + [spec(BR, part.shape[2]) for part in gradients],
        out_specs=(block,) * 4,
        compiler_params=pltpu.CompilerParams(vmem_limit_bytes=VMEM_LIMIT if count > 8 else 16 * MIB),
        cost_estimate=pl.CostEstimate(
            flops=4 * count * BR * BC * (BR + BC),
            bytes_accessed=count * 2 * MIB,
            transcendentals=0,
        ),
    )(weight, moment, second, left, right, *gradients)


def adam(weight, gradient, moment, second, step_rate):
    moment_new = beta_one * moment + (1.0 - beta_one) * gradient
    second_new = beta_two * second + (1.0 - beta_two) * gradient * gradient
    return (
        weight - step_rate * moment_new / (jnp.sqrt(second_new) + adam_eps),
        moment_new,
        second_new,
    )


def piece_places(row_groups, q_groups, kv_groups):
    all_groups = 2 * q_groups + kv_groups
    out_groups = list(range(q_groups)) + list(range(q_groups + kv_groups, all_groups))
    half = row_groups // 2
    numbers = [a * all_groups + b for a in range(half) for b in out_groups] + [None]
    numbers += [a * all_groups + b for a in range(half, row_groups) for b in out_groups]
    numbers += [a * all_groups + q_groups + b for a in range(row_groups) for b in range(kv_groups)]
    places = [0] * (len(numbers) - 1)
    for place, number in enumerate(numbers):
        if number is not None:
            places[number] = place
    return places


def to_partner(array, offset):
    if offset == 0:
        return array
    count = lax.axis_size("shard")
    return lax.ppermute(array, "shard", [(i, i ^ offset) for i in range(count)])


def to_ctx(array, offset):
    count = lax.axis_size("ctx")
    return lax.ppermute(array, "ctx", [(i, i ^ offset) for i in range(count)])


def to_chip(array, offset):
    count = lax.axis_size("ctx")
    return lax.ppermute(array, "ctx", [(i, (i + 2 * offset) % count) for i in range(count)])


def after(value, *others):
    return lax.optimization_barrier((value, others))[0]


def from_chips(array, chips):
    return [array] + [to_chip(array, offset) for offset in range(1, chips)]


def wide(array):
    return array.astype(jnp.float32)


def sum_to_chips(parts):
    total = wide(parts[0])
    for offset in range(1, len(parts)):
        total = total + wide(to_chip(parts[offset], -offset))
    return total


def gather_weights(blocks, chips, members, small):
    parts = [blocks]
    for _ in range(chips - 1):
        parts.append(to_chip(parts[-1], 1))
    pieces, arrays = [], []
    gate = []

    def add(array, offset, first, cut):
        pieces.append((0, offset, first, cut))
        arrays.append(array)
        pieces.append((1, offset, first, cut))
        arrays.append(to_ctx(after(array, *gate), 1))
        return array

    def spread(group, first):
        add(group, 0, first, 0)
        if members == 4 and first > 0:
            by_one, by_two = to_partner(group, 1), to_partner(group, 2)
            add(by_one, 1, first, 0)
            add(by_two, 2, first, 0)
            half = BR // 2
            add(to_partner(by_one[:, :half], 2), 3, first, 0)
            add(to_partner(by_two[:, half:], 1), 3, first, half)
            return [by_one, by_two]
        got = [to_partner(group, offset) for offset in range(1, members)]
        for offset in range(1, members):
            add(got[offset - 1], offset, first, 0)
        return got

    got = [to_partner(blocks, offset) for offset in range(1, members)]
    first = got + parts[1:3]
    gate.append(got[0])
    add(blocks, 0, 0, 0)
    for offset in range(1, members):
        add(got[offset - 1], offset, 0, 0)
    last = list(got)
    if chips > 1:
        last = spread(after(parts[1], *last), 1)
        gate[:] = last
    if chips > 2:
        group = after(jnp.concatenate(parts[2:], axis=0), *last, *small)
        spread(group, 2)
    return first, pieces, arrays


def add_wide(parts):
    total = wide(parts[0])
    for part in parts[1:]:
        total = total + wide(part)
    return total


def sum_members(made, ready, members):
    sums, seen, relays = [], [], []
    for half in range(2):
        sent, kept = made[2 * half : 2 * half + 2]
        hops, keeps = xor_plan(members, 1 - half)
        count = kept.shape[0] // len(keeps)
        total = wide(kept[:count])
        if members == 4:
            got = to_partner(sent, hops[0])
            got = got if ready is None else after(got, ready)
            total = total + wide(got[:count])
            relay = (wide(kept[count:]) + wide(got[count:])).astype(low_type)
            second = to_partner(relay, keeps[1])
            relays.append(relay)
            seen.append(second)
            total = total + wide(second)
        else:
            for place, hop in enumerate(hops):
                total = total + wide(to_partner(sent[place * count : (place + 1) * count], hop))
        sums.append(total.astype(low_type).reshape(count, -1))
    return jnp.concatenate(sums, axis=0), seen, relays


def sum_chips(rows, chip, chips):
    count = rows.shape[1] // chips

    def piece(offset):
        start = lax.rem(chip - offset + chips, chips) * count
        return lax.dynamic_slice_in_dim(rows, start, count, axis=1)

    return [piece(0)] + [to_chip(piece(offset), -offset) for offset in range(1, chips)]


def shards(
    tokens,
    cotangent,
    norm_gains,
    router,
    dense_weight,
    expert_weight,
    routes,
    assign,
    dense_order,
    expert_order,
    dense_moment,
    dense_second,
    dense_left,
    dense_right,
    expert_moment,
    expert_second,
    expert_left,
    expert_right,
    gains_moment,
    gains_second,
    router_moment,
    router_second,
):
    ctx_count = lax.axis_size("ctx")
    shard_count = lax.axis_size("shard")
    chips = ctx_count // 2
    micros, rows, width = tokens.shape
    slots = dense_weight.shape[0]
    span = rows // 2
    row_groups = width // BR
    q_groups = HEADS * HD // BC
    kv_groups = 2 * KVH * HD // BC

    expert_inverse = inverse_order(expert_order)
    ctx = lax.axis_index("ctx").astype(jnp.int32)
    me = jnp.stack([ctx, lax.axis_index("shard").astype(jnp.int32)])
    row_ids = jnp.arange(rows, dtype=jnp.int32)
    all_pos = assign[:, row_ids // span] * span + row_ids % span
    key_pos = all_pos.reshape(1, rows * ctx_count)
    rows_pos = all_pos[ctx].reshape(rows, 1)
    router_pad = jnp.pad(router.astype(low_type), ((0, 0), (0, LANES - shard_count)))

    small = (me, expert_inverse, router_pad, key_pos, rows_pos)
    far, pieces, arrays = gather_weights(
        dense_weight.astype(low_type), chips, shard_count, small
    )
    expert_low = after(expert_weight[0].astype(low_type), *far)
    expert_all = [lax.all_gather(expert_low[:, :UPPER], "ctx", axis=0, tiled=True)]

    lanes = jnp.arange(LANES, dtype=jnp.int32)
    hits = jnp.sum((routes[..., None] == lanes).astype(low_type), axis=2)
    cot_rows = jnp.concatenate([cotangent.astype(low_type), hits], axis=2)
    cot_rows = cot_rows.reshape(micros * rows, width + LANES)
    cot_rows = after(cot_rows, *arrays[::2])
    cot_parts = [to_partner(cot_rows, j) for j in range(shard_count)]

    h1, kv, w_in, w_out = project(
        pieces,
        arrays,
        chips,
        shard_count,
        slots,
        dense_order,
        me,
        [tokens[m] for m in range(micros)],
        norm_gains,
    )
    q = make_queries(h1, w_in, micros)
    h1_other = to_ctx(h1, 1)
    obs, logs, x2s, h2s = [], [], [], []
    kv_all = lax.all_gather(after(kv, expert_all[0]), "ctx", axis=0, tiled=True)
    lower = after(expert_low[:, UPPER:], kv_all, q, cot_parts)
    expert_all.append(lax.all_gather(lower, "ctx", axis=0, tiled=True))
    for m in range(micros):
        query = after(q[m], *(cot_parts if m == 0 else obs[m - 1 : m]))
        ob, log_total, x2, h2 = attend(
            m, query, kv_all, rows_pos, key_pos, tokens[m], norm_gains, w_out
        )
        obs.append(ob)
        logs.append(log_total)
        x2s.append(x2)
        h2s.append(h2)
    ob_others = [to_ctx(ob, 1) for ob in obs]

    h_parts = []
    for m in range(micros):
        own = h2s[m] if m == 0 else after(h2s[m], *h_parts[m - 1])
        h_parts.append([own] + [to_partner(own, j) for j in range(1, shard_count)])
    sent = []
    zs, dgs, dus, cs, xs = [], [], [], [], []
    for m in range(micros):
        here = after(me, h2s[-1], h1_other, *ob_others) if m == 0 else after(me, zs[-1])
        made = run_expert(m, expert_inverse, here, router_pad, h_parts[m], cot_parts, expert_all)
        sent.append(made[:shard_count])
        z, dg, du, c, x = made[shard_count:]
        zs.append(z)
        dgs.append(dg)
        dus.append(du)
        cs.append(c)
        xs.append(x)
    backs = [[to_partner(sent[m][j], j) for j in range(shard_count)] for m in range(micros)]

    expert_terms = outer_blocks(
        after(expert_inverse, *backs[0]), width, (0, 0, 1), [xs, cs], [dgs, dus, zs]
    )
    outs = produce(after(expert_inverse, *expert_terms), expert_all, zs, shard_count, width)
    arrived = [to_partner(outs[j], j) for j in range(min(3, shard_count))]
    dxs, das, dqs, stats = [], [], [], []
    dkv_terms = None
    for m in range(micros):
        here = after(me, outs, backs[-1]) if m == 0 else after(me, dqs[-1], arrived[1:])
        dx, da, do, stat = merge(
            here, x2s[m], cotangent[m], h2s[m], norm_gains, router_pad, w_out, backs[m]
        )
        dq, dkv_terms = attend_back(
            m, q[m], kv_all, rows_pos, key_pos, obs[m], logs[m], do, dkv_terms
        )
        dxs.append(dx)
        das.append(da)
        dqs.append(dq)
        stats.append(stat)

    def other_core(parts):
        return [to_ctx(part, 1) for part in parts]

    da_others, dq_others = other_core(das), other_core(dqs)
    first_term = after(expert_terms[0], *backs[-1])
    expert_sums = [lax.psum_scatter(first_term, "ctx", scatter_dimension=0, tiled=True)]
    dkv = lax.psum_scatter(
        after(dkv_terms, expert_sums[0]), "ctx", scatter_dimension=0, tiled=True
    )
    stat_sum = add_wide(stats)
    early = gradient_pieces(
        shard_count,
        after(me, dkv_terms),
        [([h1, h1_other], dqs + dq_others), (das + da_others, obs + ob_others)],
        [q_groups, q_groups],
        False,
        [stat_sum, to_ctx(stat_sum, 1)],
    )
    h1_turned = early[4]
    parts_back = query_back(after(w_in, early[0]), dqs)
    early_rows, early_seen, early_relays = sum_members(early[:4], parts_back, shard_count)
    chip = ctx // 2
    late = gradient_pieces(
        shard_count,
        after(me, *early_seen),
        [([h1_turned], [dkv, to_ctx(dkv, 1)])],
        [kv_groups],
        True,
        [],
    )
    last_outs = after(list(outs), early_seen)
    arrived += [to_partner(last_outs[j], j) for j in range(3, shard_count)]
    input_grad, gain_stat = input_back(
        after(tokens, late[0], arrived[3:]), norm_gains, w_in, dxs, parts_back, dkv
    )
    late_rows, _, _ = sum_members(late[:4], input_grad, shard_count)
    late_term = after(expert_terms[1], dkv, early_relays)
    expert_sums.append(lax.psum_scatter(late_term, "ctx", scatter_dimension=0, tiled=True))
    expert_grad, expert_new, expert_moment_new, expert_second_new = rotate(
        expert_weight[0], expert_sums, expert_moment[0], expert_second[0], expert_left[0], expert_right[0]
    )
    all_rows = after(jnp.concatenate([early_rows, late_rows], axis=0), expert_sums)
    all_parts = after(sum_chips(all_rows, chip, chips), expert_new)
    all_sums = add_wide(all_parts).astype(low_type)
    places = jnp.asarray(piece_places(row_groups, q_groups, kv_groups), jnp.int32)[dense_order]
    chosen = (places[:, None] == jnp.arange(all_sums.shape[0])[None, :]).astype(low_type)
    ordered = jnp.dot(chosen, all_sums, preferred_element_type=jnp.float32).astype(low_type)
    devices = ctx_count * shard_count
    piece_width = ordered.shape[1]
    stat_place = row_groups // 2 * 2 * q_groups
    gain_parts = gain_stat[:1].astype(low_type).reshape(-1, piece_width)
    stat_parts = jnp.concatenate([all_sums[stat_place : stat_place + 1], gain_parts], axis=0)
    extra = stat_parts.shape[0]
    ordered = jnp.concatenate(
        [
            ordered.reshape(devices, slots, piece_width),
            jnp.broadcast_to(stat_parts, (devices, extra, piece_width)),
        ],
        axis=1,
    ).reshape(devices * 2, (slots + extra) * piece_width // 2)
    ordered = lax.all_to_all(ordered, ("ctx", "shard"), split_axis=0, concat_axis=0, tiled=True)
    ordered = ordered.reshape(devices, slots + extra, piece_width)
    span = BR // (shard_count * chips)
    stat_block = ordered[:, slots].reshape(chips, 2, shard_count, span, LANES)
    stat_rows = wide(stat_block.transpose(2, 0, 3, 1, 4).reshape(BR * BC)[: (shard_count + 1) * width])
    stat_rows = stat_rows.reshape(shard_count + 1, width)
    gain_row = jnp.sum(wide(ordered[:, slots + 1 :]), axis=0).reshape(width)
    ordered = ordered[:, :slots].reshape(
        chips, 2, shard_count, slots, BR // (shard_count * chips), LANES
    )
    dense_sum = ordered.transpose(3, 2, 0, 4, 1, 5).reshape(slots, BR, BC)
    router_grad = stat_rows[:shard_count].T
    gains_grad = jnp.stack([gain_row, stat_rows[shard_count]])

    dense_grad, dense_new, dense_moment_new, dense_second_new = rotate(
        dense_weight, [dense_sum], dense_moment, dense_second, dense_left, dense_right
    )
    outputs = []
    for m in range(micros):
        total = x2s[m]
        for part in after(arrived, expert_new):
            total = total + wide(part[m * rows : (m + 1) * rows])
        outputs.append(total)

    gains_new, gains_moment_new, gains_second_new = adam(
        norm_gains, gains_grad, gains_moment, gains_second, gain_rate
    )
    router_new, router_moment_new, router_second_new = adam(
        router, router_grad, router_moment, router_second, rate
    )
    return (
        jnp.stack(outputs),
        input_grad,
        dense_grad,
        dense_new,
        dense_moment_new,
        dense_second_new,
        expert_grad[None],
        expert_new[None],
        expert_moment_new[None],
        expert_second_new[None],
        gains_grad,
        gains_new,
        gains_moment_new,
        gains_second_new,
        router_grad,
        router_new,
        router_moment_new,
        router_second_new,
    )


def solution(mesh):
    rows_spec = P("shard", "ctx", None)
    dense_spec = P(("ctx", "shard"), None, None)
    expert_spec = P("shard", "ctx", None, None)
    in_specs = (
        (rows_spec, rows_spec, P(), P(), dense_spec, expert_spec, rows_spec, P(), P(), P())
        + (dense_spec,) * 4
        + (expert_spec,) * 4
        + (P(),) * 4
    )
    out_specs = (rows_spec,) * 2 + (dense_spec,) * 4 + (expert_spec,) * 4 + (P(),) * 8
    return jax.shard_map(shards, mesh=mesh, in_specs=in_specs, out_specs=out_specs, check_vma=False)
```
